32 devices in a mesh: groups: 2 (over y), seq: 4 (over x, core), tensor: 4 (over z).
Axes of the slice: x: 2, y: 2, z: 4, core: 2. Of those that a mesh axis runs over, the one named last changes fastest.
Arguments:
- tokens: bfloat16 [6144, 4608], P(('groups', 'seq'), 'tensor'), parts along dimension 0, may hold values from -40 to 40
- seg_ids: int32 [6144], P(('groups', 'seq')), parts along dimension 0, may hold values from 0 to 7, never falling along the last dimension, each value on 1 to 1536 neighbouring positions
- in_gain: float32 [4608], replicated, may hold values from 0.25 to 1.75
- q_weight: bfloat16 [4608, 1024], P(None, 'tensor'), may hold values from -4 to 4
- k_weight: bfloat16 [4608, 512], P(None, 'tensor'), may hold values from -1 to 1
- value_weight: bfloat16 [4608, 512], P(None, 'tensor'), may hold values from -0.09375 to 0.09375
- o_weight: bfloat16 [1024, 4608], P('tensor'), may hold values from -1 to 1
- out_gain: float32 [4608], P('tensor'), may hold values from 0.1 to 1.9
Outputs:
- layer_out: bfloat16 [6144, 4608], P(('groups', 'seq'), 'tensor'), parts along dimension 0
The draws below stay inside these ranges and needn't reach their ends.
There are 2 independent parts, one for each index of `groups`. The reference program is written for one: setup_inputs(seed, part) draws one part's arguments, and reference() takes and returns one part's arrays. A program takes and returns all parts, laid end to end along the dimension named above; an argument that names none is the same for every part. Nothing has to cross between parts.
Inputs may be any that keep to these rules, and one draw needn't show every extreme that they name: `seg_ids`: document numbers never fall along the prompt; each document has at most 1536 tokens, and one has exactly that many.
All inputs are finite; a program needn't handle non-finite values.
Results may differ from the reference program's by a relative error of at most 0.008.
Values may be sent and summed in bfloat16 or wider, within the bound.
No kernel may reach another device: no remote copies, remote signals or barrier semaphores. Data moves between devices by JAX's collectives and lax.ppermute only.
A program may use at most 128 MiB of HBM per device.

```python
import math
import jax
import jax.numpy as jnp
import numpy as np
from jax import lax

MODEL_SIZE = 4608
HEAD_SIZE = 128
KEY_VALUE_HEADS = 4
QUERY_HEADS = 8
PROMPT_TOKENS = 3072
N_TENSOR = 4


def key_projection(key):
    return jax.random.normal(jax.random.fold_in(key, 11), (MODEL_SIZE, KEY_VALUE_HEADS * HEAD_SIZE), jnp.float32) * MODEL_SIZE ** (-0.5)


def draw_k_weight(key, part):
    return jnp.clip(key_projection(key), -1.0, 1.0).astype(jnp.bfloat16)


def draw_q_weight(key, part):
    key = jax.random.fold_in(key, 7)
    base_draw = jax.random.normal(key, (MODEL_SIZE, QUERY_HEADS * HEAD_SIZE), jnp.float32) * MODEL_SIZE ** (-0.5)
    return jnp.clip(base_draw, -4.0, 4.0).astype(jnp.bfloat16)


def draw_tokens(key, part):
    key = jax.random.fold_in(key, 3)
    key_base, key_row, key_col = jax.random.split(key, 3)
    base_draw = jax.random.normal(key_base, (PROMPT_TOKENS, MODEL_SIZE), jnp.float32)
    row_scale = 0.3 * jnp.exp(jax.random.uniform(key_row, (PROMPT_TOKENS, 1), jnp.float32) * math.log(10.0))
    ramp = jnp.exp(math.log(3.0) * jnp.arange(MODEL_SIZE, dtype=jnp.float32) / MODEL_SIZE)[None, :]
    col_scale = ramp * jnp.exp(jax.random.uniform(key_col, (1, MODEL_SIZE), jnp.float32) * math.log(3.0)) / 3.0
    result = base_draw * row_scale * col_scale
    return jnp.clip(result, -40.0, 40.0).astype(jnp.bfloat16)


def draw_o_weight(key, part):
    key = jax.random.fold_in(key, 5)
    key_base, key_spread = jax.random.split(key, 2)
    ramp = jnp.exp(math.log(3.0) * jnp.arange(MODEL_SIZE, dtype=jnp.float32) / MODEL_SIZE)[None, :]
    spread = jnp.exp(jax.random.uniform(key_spread, (1, MODEL_SIZE), jnp.float32, -math.log(2.0), math.log(2.0)))
    result = jax.random.normal(key_base, (QUERY_HEADS * HEAD_SIZE, MODEL_SIZE), jnp.float32) * (QUERY_HEADS * HEAD_SIZE) ** (-0.5) * ramp * spread
    return jnp.clip(result, -1.0, 1.0).astype(jnp.bfloat16)


def levels(own_key, shape, cuts, smallest, top_value):
    factor_of, own = 1.0, jax.random.fold_in(own_key, 6)
    for dim, parts in cuts:
        heights = jnp.exp(jax.random.uniform(jax.random.fold_in(own, dim), (parts,), jnp.float32, smallest / len(cuts), top_value / len(cuts)))
        factor_of = factor_of * jnp.repeat(heights, shape[dim] // parts).reshape([-1 if axis == dim else 1 for axis in range(len(shape))])
    return factor_of


def split_up(count, total, limit, lean):
    loads = [(1 << 20) // math.isqrt(grade ** lean) + 1 for grade in range(2, count + 1)]
    spare, counts = total - limit - (count - 1), [1] * (count - 1)
    while spare > 0:
        free = [i for i in range(count - 1) if counts[i] < limit]
        whole, budget = sum([loads[i] for i in free]), spare
        for i in free:
            extra = min(limit - counts[i], max(1, budget * loads[i] // whole), spare)
            counts[i] = counts[i] + extra
            spare = spare - extra
    return np.array([limit] + counts)


def uneven_parts(key, number_of, total, reach, lean):
    if number_of == 2:
        one = jax.random.randint(key, (), max(1, total - reach), min(reach, total - 1) + 1)
        return jnp.stack([one, total - one])
    tallies = jnp.asarray(split_up(number_of, total, reach, lean), jnp.int32)
    twos = (number_of - 1) // 2
    donor, taker = tallies[1:1 + 2 * twos:2], tallies[2:2 + 2 * twos:2]
    slack = jnp.minimum(donor - 1, reach - taker)
    moved = jax.random.randint(jax.random.fold_in(key, 1), (twos,), 0, 1 << 20) % (slack + 1)
    tallies = tallies.at[1:1 + 2 * twos:2].set(donor - moved).at[2:2 + 2 * twos:2].set(taker + moved)
    return tallies[jax.random.permutation(jax.random.fold_in(key, 2), number_of)]


def normal_values(key, extent, scale, limit, cuts=(), held_as=jnp.bfloat16):
    drawn = scale * jax.random.normal(key, extent, jnp.float32)
    if cuts:
        drawn = drawn * levels(key, extent, cuts, -0.22, 0.18)
    return jnp.clip(drawn, -limit, limit).astype(held_as)


def setup_inputs(seed: int = 0, part: int = 0) -> dict:
    key_of = jax.random.split(jax.random.key(seed), 9)
    part_splits = jax.random.split(jax.random.fold_in(key_of[8], part), 9)
    return {
        "tokens": draw_tokens(jax.random.fold_in(jax.random.fold_in(key_of[8], part), 71), part),
        "seg_ids": jnp.searchsorted(jnp.cumsum(uneven_parts(part_splits[1], 8, PROMPT_TOKENS, PROMPT_TOKENS // 2, 0)), jnp.arange(PROMPT_TOKENS), side="right").astype(jnp.int32),
        "in_gain": jnp.clip(1.0 + 0.15 * jax.random.normal(key_of[2], (MODEL_SIZE,), jnp.float32), 0.25, 1.75),
        "q_weight": draw_q_weight(jax.random.fold_in(key_of[8], 71), part),
        "k_weight": draw_k_weight(jax.random.fold_in(key_of[8], 71), part),
        "value_weight": normal_values(key_of[5], (MODEL_SIZE, KEY_VALUE_HEADS * HEAD_SIZE), MODEL_SIZE ** -0.5, 0.09375, ((1, 4),)),
        "o_weight": draw_o_weight(jax.random.fold_in(key_of[8], 71), part),
        "out_gain": jnp.clip(1.0 + 0.18 * jax.random.normal(key_of[7], (MODEL_SIZE,), jnp.float32), 0.1, 1.9),
    }


epsilon = 1e-06
query_scale = 144.0 ** (-0.5)
rope_base = 10000.0

def apply_rotation(vectors, token_places):
    half_dim = vectors.shape[-1] // 2
    inverse = rope_base ** (-jnp.arange(half_dim, dtype=jnp.float32) / half_dim)
    angles = token_places.astype(jnp.float32)[:, None] * inverse[None, :]
    cosine = jnp.cos(angles)[:, None, :]
    sine_val = jnp.sin(angles)[:, None, :]
    front_half = vectors[..., :half_dim]
    back_half = vectors[..., half_dim:]
    return jnp.concatenate([front_half * cosine - back_half * sine_val, back_half * cosine + front_half * sine_val], axis=-1)

def reference(tokens, seg_ids, in_gain, q_weight, k_weight, value_weight, o_weight, out_gain):
    widened = tokens.astype(jnp.float32)
    mean_sq = lax.optimization_barrier(jnp.mean(widened * widened, axis=1, keepdims=True))
    normed = (widened * lax.rsqrt(mean_sq + epsilon) * in_gain.astype(jnp.float32)[None, :]).astype(jnp.bfloat16)
    query_proj = jnp.dot(normed, q_weight, preferred_element_type=jnp.float32)
    projected_keys = jnp.dot(normed, k_weight, preferred_element_type=jnp.float32)
    projected_values = jnp.dot(normed, value_weight, preferred_element_type=jnp.float32)
    token_places = jnp.arange(PROMPT_TOKENS, dtype=jnp.int32)
    queries = apply_rotation(query_proj.reshape(PROMPT_TOKENS, QUERY_HEADS, HEAD_SIZE), token_places).astype(jnp.bfloat16)
    heads_of_keys = apply_rotation(projected_keys.reshape(PROMPT_TOKENS, KEY_VALUE_HEADS, HEAD_SIZE), token_places).astype(jnp.bfloat16)
    heads_of_values = projected_values.reshape(PROMPT_TOKENS, KEY_VALUE_HEADS, HEAD_SIZE).astype(jnp.bfloat16)
    allowed = (seg_ids[:, None] == seg_ids[None, :]) & (token_places[:, None] >= token_places[None, :])

    def one_head(head_idx):
        query_h = lax.dynamic_index_in_dim(queries, head_idx, 1, keepdims=False)
        kv_idx = (head_idx // 2).astype(jnp.int32)
        key_h = lax.dynamic_index_in_dim(heads_of_keys, kv_idx, 1, keepdims=False)
        value_h = lax.dynamic_index_in_dim(heads_of_values, kv_idx, 1, keepdims=False)
        scores = jnp.dot(query_h, key_h.T, preferred_element_type=jnp.float32) * query_scale
        masked = jnp.where(allowed, scores, -jnp.inf)
        row_max = lax.optimization_barrier(jnp.max(masked, axis=1, keepdims=True))
        expo = jnp.where(allowed, jnp.exp(scores - row_max), 0.0)
        weights = expo.astype(jnp.bfloat16)
        summed = jnp.dot(weights, value_h, preferred_element_type=jnp.float32)
        return (summed / lax.optimization_barrier(jnp.sum(expo, axis=1, keepdims=True))).astype(jnp.bfloat16)
    context = lax.map(one_head, jnp.arange(QUERY_HEADS, dtype=jnp.int32))
    context = jnp.transpose(context, (1, 0, 2)).reshape(PROMPT_TOKENS, QUERY_HEADS * HEAD_SIZE)
    group_cols = QUERY_HEADS * HEAD_SIZE // N_TENSOR
    ctx_groups = jnp.transpose(context.reshape(PROMPT_TOKENS, N_TENSOR, group_cols), (1, 0, 2))
    o_groups = o_weight.reshape(N_TENSOR, group_cols, MODEL_SIZE)

    def add_group(running, operands):
        rounded = jnp.dot(operands[0], operands[1], preferred_element_type=jnp.float32).astype(jnp.bfloat16)
        rounded = lax.optimization_barrier(rounded)
        return (running + rounded.astype(jnp.float32), None)
    branch, _ = lax.scan(add_group, jnp.zeros((PROMPT_TOKENS, MODEL_SIZE), jnp.float32), (ctx_groups, o_groups))
    mean_out = lax.optimization_barrier(jnp.mean(branch * branch, axis=1, keepdims=True))
    layer_out = widened + branch * lax.rsqrt(mean_out + epsilon) * out_gain.astype(jnp.float32)[None, :]
    return layer_out.astype(jnp.bfloat16)
```

```python
import math
from functools import partial

import jax
import jax.numpy as jnp
from jax import lax
from jax.experimental import pallas as pl
from jax.experimental.pallas import tpu as pltpu
from jax.sharding import PartitionSpec as P

HEAD_SIZE = 128
PLANE = ("groups", "seq")

epsilon = 1e-06
query_scale = 144.0 ** (-0.5)
rope_base = 10000.0
NEG = -1e30
Q_TILE = 128
K_TILE = 256


def rotation_table(token_places):
    half_dim = HEAD_SIZE // 2
    inverse = rope_base ** (-jnp.arange(half_dim, dtype=jnp.float32) / half_dim)
    angles = token_places.astype(jnp.float32)[:, None] * inverse[None, :]
    return jnp.cos(angles), jnp.sin(angles)


def rotate(vectors, cosine, sine):
    rows, width = vectors.shape
    half_dim = HEAD_SIZE // 2
    parts = []
    for c in range(0, width, HEAD_SIZE):
        front = vectors[:, c : c + half_dim]
        back = vectors[:, c + half_dim : c + HEAD_SIZE]
        parts += [front * cosine - back * sine, back * cosine + front * sine]
    return jnp.concatenate(parts, axis=1)


def attention_kernel(lo_ref, q_ref, start_ref, *rest, back, group):
    kv_refs = rest[: back + 1]
    out_ref, k_scr, vt_scr = rest[back + 1 :]
    rows = kv_refs[0].shape[0]
    tile = pl.program_id(0)

    @pl.when(tile == 0)
    def _():
        for b in range(back + 1):
            k_scr[b * rows : (b + 1) * rows, :] = kv_refs[b][:, :HEAD_SIZE]
            values = kv_refs[b][:, HEAD_SIZE:].astype(jnp.float32)
            vt_scr[:, b * rows : (b + 1) * rows] = values.T.astype(jnp.bfloat16)

    q = q_ref[...]
    q2 = jnp.concatenate(
        [q[:, g * HEAD_SIZE : (g + 1) * HEAD_SIZE] for g in range(group)], axis=0
    )
    width = group * Q_TILE
    start = jnp.concatenate([start_ref[...]] * group, axis=1)
    first = back * rows + tile * Q_TILE
    place = first + lax.broadcasted_iota(jnp.int32, (1, Q_TILE), 1)
    place = jnp.concatenate([place] * group, axis=1)

    def step(j, state):
        run_max, run_sum, acc = state
        base = pl.multiple_of(j * K_TILE, K_TILE)
        scores = lax.dot_general(
            k_scr[pl.ds(base, K_TILE), :],
            q2,
            (((1,), (1,)), ((), ())),
            preferred_element_type=jnp.float32,
        )
        key_pos = base + lax.broadcasted_iota(jnp.int32, (K_TILE, width), 0)
        allowed = (key_pos >= start) & (key_pos <= place)
        scores = jnp.where(allowed, scores, NEG)
        new_max = jnp.maximum(run_max, jnp.max(scores, axis=0, keepdims=True))
        expo = jnp.exp2(scores - new_max)
        factor = jnp.exp2(run_max - new_max)
        run_sum = run_sum * factor + jnp.sum(expo, axis=0, keepdims=True)
        acc = acc * factor + jnp.dot(
            vt_scr[:, pl.ds(base, K_TILE)],
            expo.astype(jnp.bfloat16),
            preferred_element_type=jnp.float32,
        )
        return new_max, run_sum, acc

    state = (
        jnp.full((1, width), NEG, jnp.float32),
        jnp.zeros((1, width), jnp.float32),
        jnp.zeros((HEAD_SIZE, width), jnp.float32),
    )
    stop = (first + Q_TILE + K_TILE - 1) // K_TILE
    _, run_sum, acc = lax.fori_loop(lo_ref[tile], stop, step, state)
    context = (acc / run_sum).T
    for g in range(group):
        out_ref[:, g * HEAD_SIZE : (g + 1) * HEAD_SIZE] = context[
            g * Q_TILE : (g + 1) * Q_TILE
        ].astype(jnp.bfloat16)


def attend(queries, start, blocks):
    rows, width = queries.shape
    back = len(blocks) - 1
    group = width // HEAD_SIZE
    tiles = rows // Q_TILE
    low = start[::Q_TILE] // K_TILE
    keys = (back + 1) * rows
    whole = lambda i, lo: (0, 0)
    return pl.pallas_call(
        partial(attention_kernel, back=back, group=group),
        out_shape=jax.ShapeDtypeStruct((rows, width), jnp.bfloat16),
        grid_spec=pltpu.PrefetchScalarGridSpec(
            num_scalar_prefetch=1,
            grid=(tiles,),
            in_specs=[
                pl.BlockSpec((Q_TILE, width), lambda i, lo: (i, 0)),
                pl.BlockSpec((1, Q_TILE), lambda i, lo: (0, i)),
            ]
            + [pl.BlockSpec((rows, 2 * HEAD_SIZE), whole) for _ in blocks],
            out_specs=pl.BlockSpec((Q_TILE, width), lambda i, lo: (i, 0)),
            scratch_shapes=[
                pltpu.VMEM((keys, HEAD_SIZE), jnp.bfloat16),
                pltpu.VMEM((HEAD_SIZE, keys), jnp.bfloat16),
            ],
        ),
        compiler_params=pltpu.CompilerParams(vmem_limit_bytes=32 * 1024 * 1024),
        cost_estimate=pl.CostEstimate(
            flops=2 * rows * width * keys, bytes_accessed=4 * rows * width, transcendentals=rows * keys
        ),
        name="attend",
    )(low, queries, start[None, :], *blocks)


def per_device(
    tokens, seg_ids, in_gain, q_weight, k_weight, value_weight, o_weight, out_gain, *, sizes
):
    rows, cols = tokens.shape
    model_width = in_gain.shape[0]
    nz, nseq = sizes["tensor"], sizes["seq"]
    plane = nseq * sizes["groups"]
    z = lax.axis_index("tensor")
    seq = lax.axis_index("seq")
    in_plane = lax.axis_index(PLANE)
    half = nz // 2
    side, within = z // half, z % half
    half_rows = half * cols

    ring = [(i, i // half * half + (i + 1) % half) for i in range(nz)]
    swap = [(i, (i + half) % nz) for i in range(nz)]
    turn = lambda k: [(i, (i + k) % nz) for i in range(nz)]

    x_blocks = [tokens]
    for _ in range(half - 1):
        x_blocks.append(lax.ppermute(x_blocks[-1], "tensor", ring))

    share = half_rows // plane

    def weight_rows(first, count):
        parts = [
            lax.dynamic_slice_in_dim(w, first, count, axis=0)
            for w in (q_weight, k_weight, value_weight)
        ]
        gains = lax.dynamic_slice_in_dim(in_gain, first, count, axis=0)
        joined = jnp.concatenate(parts, axis=1).astype(jnp.float32)
        return (joined * gains[:, None]).astype(jnp.bfloat16)

    sent = weight_rows((1 - side) * half_rows + in_plane * share, share)
    got = lax.ppermute(sent, "tensor", swap)
    far_weight = lax.all_gather(got, PLANE, axis=0, tiled=True)
    near_weight = weight_rows(side * half_rows, half_rows)

    o_rows = o_weight.shape[0]
    o_share = o_rows // plane
    moved = []
    for k in range(1, nz):
        target = (z + k) % nz
        piece = lax.dynamic_slice(
            o_weight, (in_plane * o_share, target * cols), (o_share, cols)
        )
        moved.append(lax.ppermute(piece, "tensor", turn(k)))
    gathered_o = lax.all_gather(jnp.stack(moved), PLANE, axis=1, tiled=True)
    own_o = lax.dynamic_slice_in_dim(o_weight, z * cols, cols, axis=1)
    o_all = jnp.concatenate([own_o, gathered_o.reshape((nz - 1) * o_rows, cols)], axis=0)

    back = -(-(nseq * rows // 2 - 1) // rows)
    all_ids = lax.all_gather(seg_ids, "seq", axis=0, tiled=True)
    start = jnp.sum((all_ids[None, :] < seg_ids[:, None]).astype(jnp.int32), axis=1)
    start = start - (seq - back) * rows

    token_places = seq * rows + jnp.arange(rows, dtype=jnp.int32)
    cosine, sine = rotation_table(token_places)

    squares = sum(
        jnp.sum(jnp.square(b.astype(jnp.float32)), axis=1, keepdims=True) for b in x_blocks
    )
    far_squares = lax.ppermute(squares, "tensor", swap)

    def project(weight):
        total = None
        for k, block in enumerate(x_blocks):
            source = (within + half - k) % half
            part = lax.dynamic_slice_in_dim(weight, source * cols, cols, axis=0)
            term = jnp.dot(block, part, preferred_element_type=jnp.float32)
            total = term if total is None else total + term
        return total

    partial_far = lax.ppermute(project(far_weight).astype(jnp.bfloat16), "tensor", swap)
    projected = project(near_weight) + partial_far.astype(jnp.float32)
    projected = projected * lax.rsqrt((squares + far_squares) / model_width + epsilon)

    q_width, k_width = q_weight.shape[1], k_weight.shape[1]
    scale = query_scale * math.log2(math.e)
    queries = rotate(projected[:, :q_width], cosine * scale, sine * scale).astype(jnp.bfloat16)
    keys = rotate(projected[:, q_width : q_width + k_width], cosine, sine)
    values = projected[:, q_width + k_width :]
    own_kv = jnp.concatenate([keys, values], axis=1).astype(jnp.bfloat16)

    blocks = [own_kv]
    for k in range(1, back + 1):
        blocks.insert(
            0, lax.ppermute(own_kv, "seq", [(i, i + k) for i in range(nseq - k)])
        )
    context = attend(queries, start, blocks)

    contexts = [context] + [lax.ppermute(context, "tensor", turn(k)) for k in range(1, nz)]
    branch = jnp.dot(
        jnp.concatenate(contexts, axis=1), o_all, preferred_element_type=jnp.float32
    )
    own_sq = jnp.sum(branch * branch, axis=1, keepdims=True)
    out_sq = own_sq
    for k in range(1, nz):
        out_sq = out_sq + lax.ppermute(own_sq, "tensor", turn(k))
    layer_out = (
        tokens.astype(jnp.float32)
        + branch * lax.rsqrt(out_sq / model_width + epsilon) * out_gain[None, :]
    )
    return layer_out.astype(jnp.bfloat16)


def solution(mesh):
    return jax.shard_map(
        partial(per_device, sizes=dict(mesh.shape)),
        mesh=mesh,
        in_specs=(
            P(("groups", "seq"), "tensor"),
            P(("groups", "seq")),
            P(),
            P(None, "tensor"),
            P(None, "tensor"),
            P(None, "tensor"),
            P("tensor", None),
            P("tensor"),
        ),
        out_specs=P(("groups", "seq"), "tensor"),
        check_vma=False,
    )
```

```python
import math
from functools import partial

import jax
import jax.numpy as jnp
from jax import lax
from jax.experimental import pallas as pl
from jax.experimental.pallas import tpu as pltpu
from jax.sharding import PartitionSpec as P

HEAD_SIZE = 128
PLANE = ("groups", "seq")

epsilon = 1e-06
query_scale = 144.0 ** (-0.5)
rope_base = 10000.0
NEG = -1e30
Q_TILE = 128
K_TILE = 256
CHUNKS = 2


def rotation_table(token_places):
    half_dim = HEAD_SIZE // 2
    inverse = rope_base ** (-jnp.arange(half_dim, dtype=jnp.float32) / half_dim)
    angles = token_places.astype(jnp.float32)[:, None] * inverse[None, :]
    return jnp.cos(angles), jnp.sin(angles)


def rotate(vectors, cosine, sine):
    rows, width = vectors.shape
    half_dim = HEAD_SIZE // 2
    parts = []
    for c in range(0, width, HEAD_SIZE):
        front = vectors[:, c : c + half_dim]
        back = vectors[:, c + half_dim : c + HEAD_SIZE]
        parts += [front * cosine - back * sine, back * cosine + front * sine]
    return jnp.concatenate(parts, axis=1)


def attention_kernel(lo_ref, q_ref, start_ref, *rest, back, group, offset):
    kv_refs = rest[: back + 1]
    out_ref, k_scr, vt_scr = rest[back + 1 :]
    rows = kv_refs[0].shape[0]
    tile = pl.program_id(0)

    @pl.when(tile == 0)
    def _():
        for b in range(back + 1):
            k_scr[b * rows : (b + 1) * rows, :] = kv_refs[b][:, :HEAD_SIZE]
            values = kv_refs[b][:, HEAD_SIZE:].astype(jnp.float32)
            vt_scr[:, b * rows : (b + 1) * rows] = values.T.astype(jnp.bfloat16)

    q = q_ref[...]
    q2 = jnp.concatenate(
        [q[:, g * HEAD_SIZE : (g + 1) * HEAD_SIZE] for g in range(group)], axis=0
    )
    width = group * Q_TILE
    start = jnp.concatenate([start_ref[...]] * group, axis=1)
    first = back * rows + offset + tile * Q_TILE
    place = first + lax.broadcasted_iota(jnp.int32, (1, Q_TILE), 1)
    place = jnp.concatenate([place] * group, axis=1)

    def score(j):
        base = pl.multiple_of(j * K_TILE, K_TILE)
        return lax.dot_general(
            k_scr[pl.ds(base, K_TILE), :],
            q2,
            (((1,), (1,)), ((), ())),
            preferred_element_type=jnp.float32,
        )

    low = lo_ref[tile]
    stop = (first + Q_TILE + K_TILE - 1) // K_TILE

    def step(j, state):
        scores, run_max, run_sum, acc = state
        following = score(jnp.minimum(j + 1, stop - 1))
        base = pl.multiple_of(j * K_TILE, K_TILE)
        key_pos = base + lax.broadcasted_iota(jnp.int32, (K_TILE, width), 0)
        allowed = (key_pos >= start) & (key_pos <= place)
        scores = jnp.where(allowed, scores, NEG)
        new_max = jnp.maximum(run_max, jnp.max(scores, axis=0, keepdims=True))
        expo = jnp.exp2(scores - new_max)
        factor = jnp.exp2(run_max - new_max)
        run_sum = run_sum * factor + jnp.sum(expo, axis=0, keepdims=True)
        acc = acc * factor + jnp.dot(
            vt_scr[:, pl.ds(base, K_TILE)],
            expo.astype(jnp.bfloat16),
            preferred_element_type=jnp.float32,
        )
        return following, new_max, run_sum, acc

    state = (
        score(low),
        jnp.full((1, width), NEG, jnp.float32),
        jnp.zeros((1, width), jnp.float32),
        jnp.zeros((HEAD_SIZE, width), jnp.float32),
    )
    _, _, run_sum, acc = lax.fori_loop(low, stop, step, state)
    context = (acc / run_sum).T
    for g in range(group):
        out_ref[:, g * HEAD_SIZE : (g + 1) * HEAD_SIZE] = context[
            g * Q_TILE : (g + 1) * Q_TILE
        ].astype(jnp.bfloat16)


def attend(queries, start, blocks, offset):
    rows, width = queries.shape
    block_rows = blocks[0].shape[0]
    back = len(blocks) - 1
    group = width // HEAD_SIZE
    low = start[::Q_TILE] // K_TILE
    keys = (back + 1) * block_rows
    whole = lambda i, lo: (0, 0)
    return pl.pallas_call(
        partial(attention_kernel, back=back, group=group, offset=offset),
        out_shape=jax.ShapeDtypeStruct((rows, width), jnp.bfloat16),
        grid_spec=pltpu.PrefetchScalarGridSpec(
            num_scalar_prefetch=1,
            grid=(rows // Q_TILE,),
            in_specs=[
                pl.BlockSpec((Q_TILE, width), lambda i, lo: (i, 0)),
                pl.BlockSpec((1, Q_TILE), lambda i, lo: (0, i)),
            ]
            + [pl.BlockSpec((block_rows, 2 * HEAD_SIZE), whole) for _ in blocks],
            out_specs=pl.BlockSpec((Q_TILE, width), lambda i, lo: (i, 0)),
            scratch_shapes=[
                pltpu.VMEM((keys, HEAD_SIZE), jnp.bfloat16),
                pltpu.VMEM((HEAD_SIZE, keys), jnp.bfloat16),
            ],
        ),
        compiler_params=pltpu.CompilerParams(vmem_limit_bytes=32 * 1024 * 1024),
        cost_estimate=pl.CostEstimate(
            flops=2 * rows * width * keys, bytes_accessed=4 * rows * width, transcendentals=rows * keys
        ),
        name="attend",
    )(low, queries, start[None, :], *blocks)


def place_kernel(where_ref, own_ref, got_ref, out_ref):
    piece = pl.program_id(0)
    held = pl.num_programs(0) // 2

    @pl.when(piece < held)
    def _():
        out_ref[...] = own_ref[0]

    @pl.when(piece >= held)
    def _():
        out_ref[...] = got_ref[0]


def spread(piece, plane, masks):
    own = piece[None]
    order = [0]
    for mask in masks:
        got = lax.ppermute(own, PLANE, [(i, i ^ mask) for i in range(plane)])
        if mask != masks[-1]:
            own = jnp.concatenate([own, got], axis=0)
        order = order + [k ^ mask for k in order]
    where = jnp.bitwise_xor(lax.axis_index(PLANE), jnp.array(order, jnp.int32))
    held = own.shape[0]
    rows, width = piece.shape
    return pl.pallas_call(
        place_kernel,
        out_shape=jax.ShapeDtypeStruct((plane * rows, width), piece.dtype),
        grid_spec=pltpu.PrefetchScalarGridSpec(
            num_scalar_prefetch=1,
            grid=(plane,),
            in_specs=[
                pl.BlockSpec((1, rows, width), lambda i, to: (jnp.minimum(i, held - 1), 0, 0)),
                pl.BlockSpec((1, rows, width), lambda i, to: (jnp.maximum(i - held, 0), 0, 0)),
            ],
            out_specs=pl.BlockSpec((rows, width), lambda i, to: (to[i], 0)),
        ),
        name="place",
    )(where, own, got)


def per_device(
    tokens, seg_ids, in_gain, q_weight, k_weight, value_weight, o_weight, out_gain, *, sizes
):
    rows, cols = tokens.shape
    model_width = in_gain.shape[0]
    nz, nseq = sizes["tensor"], sizes["seq"]
    plane = nseq * sizes["groups"]
    z = lax.axis_index("tensor")
    seq = lax.axis_index("seq")
    in_plane = lax.axis_index(PLANE)
    half = nz // 2
    side, within = z // half, z % half
    half_rows = half * cols

    ring = [(i, i // half * half + (i + 1) % half) for i in range(nz)]
    swap = [(i, (i + half) % nz) for i in range(nz)]
    turn = lambda k: [(i, (i + k) % nz) for i in range(nz)]
    seq_bits = [1 << b for b in range(1, nseq.bit_length() - 1)]
    group_bits = [nseq << b for b in range(sizes["groups"].bit_length() - 1)]

    share = half_rows // plane
    far_first = (1 - side) * half_rows + in_plane * share
    near_first = side * half_rows

    def weight_rows(weights, first, count):
        parts = [lax.dynamic_slice_in_dim(w, first, count, axis=0) for w in weights]
        gains = lax.dynamic_slice_in_dim(in_gain, first, count, axis=0)
        joined = jnp.concatenate(parts, axis=1).astype(jnp.float32)
        return (joined * gains[:, None]).astype(jnp.bfloat16)

    kv_weights, q_weights = (k_weight, value_weight), (q_weight,)
    far_kv = lax.ppermute(weight_rows(kv_weights, far_first, share), "tensor", swap)
    far_q = lax.ppermute(weight_rows(q_weights, far_first, share), "tensor", swap)
    far_kv = spread(far_kv, plane, seq_bits + group_bits + [1])
    far_q = spread(far_q, plane, group_bits + seq_bits + [1])
    near_kv = weight_rows(kv_weights, near_first, half_rows)
    near_q = weight_rows(q_weights, near_first, half_rows)

    chunk = rows // CHUNKS
    x_chunks = []
    for c in range(CHUNKS):
        x_blocks = [tokens[c * chunk : (c + 1) * chunk]]
        for _ in range(half - 1):
            x_blocks.append(lax.ppermute(x_blocks[-1], "tensor", ring))
        x_chunks.append(x_blocks)

    o_rows = o_weight.shape[0]
    o_share = o_rows // plane
    moved = []
    for k in range(1, nz):
        target = (z + k) % nz
        piece = lax.dynamic_slice(
            o_weight, (in_plane * o_share, target * cols), (o_share, cols)
        )
        moved.append(lax.ppermute(piece, "tensor", turn(k)))
    gathered_o = lax.all_gather(jnp.stack(moved), PLANE, axis=1, tiled=True)
    own_o = lax.dynamic_slice_in_dim(o_weight, z * cols, cols, axis=1)
    o_all = jnp.concatenate([own_o, gathered_o.reshape((nz - 1) * o_rows, cols)], axis=0)

    back = -(-(nseq * rows // 2 - 1) // rows)
    all_ids = lax.all_gather(seg_ids, "seq", axis=0, tiled=True)
    start = jnp.sum((all_ids[None, :] < seg_ids[:, None]).astype(jnp.int32), axis=1)
    start = start - (seq - back) * rows

    token_places = seq * rows + jnp.arange(rows, dtype=jnp.int32)
    cosine, sine = rotation_table(token_places)

    def project(x_blocks, weight):
        total = None
        for k, block in enumerate(x_blocks):
            source = (within + half - k) % half
            part = lax.dynamic_slice_in_dim(weight, source * cols, cols, axis=0)
            term = jnp.dot(block, part, preferred_element_type=jnp.float32)
            total = term if total is None else total + term
        return total

    squares = [
        sum(jnp.sum(jnp.square(b.astype(jnp.float32)), axis=1) for b in x_blocks)
        for x_blocks in x_chunks
    ]
    squares = jnp.concatenate(squares)
    squares = squares + lax.ppermute(squares, "tensor", swap)
    factor = lax.rsqrt(squares / model_width + epsilon)[:, None]

    def projections(far, near):
        sums = []
        for x_blocks in x_chunks:
            other = project(x_blocks, far).astype(jnp.bfloat16)
            other = lax.ppermute(other, "tensor", swap)
            sums.append(project(x_blocks, near) + other.astype(jnp.float32))
        return sums

    projected_kv = jnp.concatenate(projections(far_kv, near_kv), axis=0) * factor
    k_width = k_weight.shape[1]
    keys = rotate(projected_kv[:, :k_width], cosine, sine)
    own_kv = jnp.concatenate([keys, projected_kv[:, k_width:]], axis=1).astype(jnp.bfloat16)
    blocks = [own_kv]
    for k in range(1, back + 1):
        blocks.insert(
            0, lax.ppermute(own_kv, "seq", [(i, i + k) for i in range(nseq - k)])
        )

    scale = query_scale * math.log2(math.e)
    outs = []
    for c, projected_q in enumerate(projections(far_q, near_q)):
        at = slice(c * chunk, (c + 1) * chunk)
        queries = rotate(projected_q * factor[at], cosine[at] * scale, sine[at] * scale)
        context = attend(queries.astype(jnp.bfloat16), start[at], blocks, c * chunk)

        contexts = [context]
        contexts += [lax.ppermute(context, "tensor", turn(k)) for k in range(1, nz)]
        branch = jnp.dot(
            jnp.concatenate(contexts, axis=1), o_all, preferred_element_type=jnp.float32
        )
        own_sq = jnp.sum(branch * branch, axis=1)
        out_sq = own_sq
        for k in range(1, nz):
            out_sq = out_sq + lax.ppermute(own_sq, "tensor", turn(k))
        out = (
            tokens[at].astype(jnp.float32)
            + branch * lax.rsqrt(out_sq / model_width + epsilon)[:, None] * out_gain[None, :]
        )
        outs.append(out.astype(jnp.bfloat16))
    return jnp.concatenate(outs, axis=0)


def solution(mesh):
    return jax.shard_map(
        partial(per_device, sizes=dict(mesh.shape)),
        mesh=mesh,
        in_specs=(
            P(("groups", "seq"), "tensor"),
            P(("groups", "seq")),
            P(),
            P(None, "tensor"),
            P(None, "tensor"),
            P(None, "tensor"),
            P("tensor", None),
            P("tensor"),
        ),
        out_specs=P(("groups", "seq"), "tensor"),
        check_vma=False,
    )
```

```python
import math
from functools import partial

import jax
import jax.numpy as jnp
from jax import lax
from jax.experimental import pallas as pl
from jax.experimental.pallas import tpu as pltpu
from jax.sharding import PartitionSpec as P

HEAD_SIZE = 128
PLANE = ("groups", "seq")

epsilon = 1e-06
query_scale = 144.0 ** (-0.5)
rope_base = 10000.0
NEG = -1e30
Q_TILE = 128
K_TILE = 256
CHUNKS = 2
LANES = 128
TAIL = 16
F32, BF16 = jnp.float32, jnp.bfloat16
ANY = pl.BlockSpec(memory_space=pl.ANY)
HBM = pl.BlockSpec(memory_space=pltpu.HBM)
PARAMS = pltpu.CompilerParams(vmem_limit_bytes=48 * 1024 * 1024)


def shape(dims, dtype):
    return jax.ShapeDtypeStruct(dims, dtype)


def to_row(column):
    return jnp.broadcast_to(column, (column.shape[0], LANES)).T[0:1, :]


def to_column(row):
    return jnp.broadcast_to(row, (LANES, row.shape[1])).T


def rotation_table(token_places):
    half_dim = HEAD_SIZE // 2
    inverse = rope_base ** (-jnp.arange(half_dim, dtype=F32) / half_dim)
    angles = token_places.astype(F32)[:, None] * inverse[None, :]
    cosine, sine = jnp.cos(angles), jnp.sin(angles)
    return jnp.concatenate([cosine, cosine], 1), jnp.concatenate([-sine, sine], 1)


def rotate(vectors, cosine, sine):
    return vectors * cosine + pltpu.roll(vectors, HEAD_SIZE // 2, 1) * sine


def pack_kernel(at_ref, q_ref, k_ref, v_ref, kv_out, q_out, sems):
    share, width = q_out.shape[0], k_ref.shape[1]
    rows = pl.ds(pl.multiple_of(at_ref[0] * share, TAIL), share)
    copies = [
        pltpu.make_async_copy(k_ref.at[rows], kv_out.at[:, pl.ds(0, width)], sems.at[0]),
        pltpu.make_async_copy(v_ref.at[rows], kv_out.at[:, pl.ds(width, width)], sems.at[1]),
        pltpu.make_async_copy(q_ref.at[rows], q_out, sems.at[2]),
    ]
    for copy in copies:
        copy.start()
    for copy in copies:
        copy.wait()


def pack(at, q_weight, k_weight, v_weight, share):
    kv_width = k_weight.shape[1] + v_weight.shape[1]
    return pl.pallas_call(
        pack_kernel,
        out_shape=(shape((share, kv_width), BF16), shape((share, q_weight.shape[1]), BF16)),
        grid_spec=pltpu.PrefetchScalarGridSpec(
            num_scalar_prefetch=1,
            grid=(1,),
            in_specs=[HBM, HBM, HBM],
            out_specs=[ANY, ANY],
            scratch_shapes=[pltpu.SemaphoreType.DMA((3,))],
        ),
        compiler_params=pltpu.CompilerParams(vmem_limit_bytes=62 * 1024 * 1024),
        name="pack",
    )(at, q_weight, k_weight, v_weight)


def join_kernel(first_ref, second_ref, out_ref, sems):
    held = first_ref.shape[0]
    copies = [
        pltpu.make_async_copy(first_ref, out_ref.at[pl.ds(0, held)], sems.at[0]),
        pltpu.make_async_copy(second_ref, out_ref.at[pl.ds(held, held)], sems.at[1]),
    ]
    for copy in copies:
        copy.start()
    for copy in copies:
        copy.wait()


def join(first, second):
    return pl.pallas_call(
        join_kernel,
        out_shape=shape((2 * first.shape[0],) + first.shape[1:], first.dtype),
        in_specs=[ANY, ANY],
        out_specs=ANY,
        scratch_shapes=[pltpu.SemaphoreType.DMA((2,))],
        compiler_params=PARAMS,
        name="join",
    )(first, second)


def spread(piece, plane, masks):
    own = piece[None]
    order = [0]
    for mask in masks:
        got = lax.ppermute(own, PLANE, [(i, i ^ mask) for i in range(plane)])
        order = order + [k ^ mask for k in order]
        if mask != masks[-1]:
            own = join(own, got)
    where = jnp.bitwise_xor(lax.axis_index(PLANE), jnp.array(order, jnp.int32))
    return where, own, got


def prep_kernel(src_ref, gain_ref, *rest):
    x_refs, (out_ref, sq_ref) = rest[:-2], rest[-2:]
    total = 0.0
    for k, x_ref in enumerate(x_refs):
        x = x_ref[...].astype(F32)
        total = total + jnp.sum(x * x, axis=1, keepdims=True)
        out_ref[k] = (x * gain_ref[src_ref[k]]).astype(BF16)
    sq_ref[...] = to_row(total)


def prep(sources, gains, tokens, received, chunk, c):
    count, (nz, _, cols) = len(received) + 1, gains.shape
    return pl.pallas_call(
        prep_kernel,
        out_shape=(shape((count, chunk, cols), BF16), shape((1, chunk), F32)),
        grid_spec=pltpu.PrefetchScalarGridSpec(
            num_scalar_prefetch=1,
            grid=(1,),
            in_specs=[
                pl.BlockSpec((nz, 1, cols), lambda i, s: (0, 0, 0)),
                pl.BlockSpec((chunk, cols), lambda i, s: (c, 0)),
            ]
            + [pl.BlockSpec((chunk, cols), lambda i, s: (0, 0)) for _ in received],
            out_specs=[
                pl.BlockSpec((count, chunk, cols), lambda i, s: (0, 0, 0)),
                pl.BlockSpec((1, chunk), lambda i, s: (0, 0)),
            ],
        ),
        compiler_params=PARAMS,
        name="prep",
    )(sources, gains, tokens, *received)


def far_kernel(where_ref, src_ref, x_ref, *rest, with_sq):
    if with_sq:
        sq_ref, own_ref, got_ref, out_ref, weight, sems = rest
    else:
        own_ref, got_ref, out_ref, weight, sems = rest
    held, share, _ = own_ref.shape
    copies = []
    for i in range(2 * held):
        piece = own_ref.at[i] if i < held else got_ref.at[i - held]
        row = pl.multiple_of(where_ref[i] * share, TAIL)
        copies.append(
            pltpu.make_async_copy(piece, weight.at[pl.ds(row, share)], sems.at[i])
        )
    for copy in copies:
        copy.start()
    for copy in copies:
        copy.wait()
    count, chunk, cols = x_ref.shape
    total = None
    for k in range(count):
        row = pl.multiple_of(src_ref[k] * cols, TAIL)
        term = jnp.dot(x_ref[k], weight[pl.ds(row, cols), :], preferred_element_type=F32)
        total = term if total is None else total + term
    out_ref[:chunk, :] = total.astype(BF16)
    if with_sq:
        width = out_ref.shape[1]
        sq = sq_ref[...]
        high = sq.astype(BF16).astype(F32)
        lines = []
        for part in (high, sq - high):
            for at in range(0, chunk, width):
                line = part[:, at : at + width]
                if line.shape[1] < width:
                    line = jnp.concatenate(
                        [line, jnp.zeros((1, width - line.shape[1]), F32)], axis=1
                    )
                lines.append(line)
        lines.append(jnp.zeros((TAIL - len(lines), width), F32))
        out_ref[chunk:, :] = jnp.concatenate(lines, axis=0).astype(BF16)


def far_product(where, sources, x, pieces, sq):
    own, got = pieces
    held, share, width = own.shape
    count, chunk, cols = x.shape
    with_sq = sq is not None
    rows = chunk + (TAIL if with_sq else 0)
    extra = [pl.BlockSpec((1, chunk), lambda i, w, s: (0, 0))] if with_sq else []
    return pl.pallas_call(
        partial(far_kernel, with_sq=with_sq),
        out_shape=shape((rows, width), BF16),
        grid_spec=pltpu.PrefetchScalarGridSpec(
            num_scalar_prefetch=2,
            grid=(1,),
            in_specs=[pl.BlockSpec((count, chunk, cols), lambda i, w, s: (0, 0, 0))]
            + extra
            + [ANY, ANY],
            out_specs=pl.BlockSpec((rows, width), lambda i, w, s: (0, 0)),
            scratch_shapes=[
                pltpu.VMEM((2 * held * share, width), BF16),
                pltpu.SemaphoreType.DMA((2 * held,)),
            ],
        ),
        compiler_params=PARAMS,
        name="far",
    )(where, sources, x, *([sq] if with_sq else []), own, got)


def near_kernel(src_ref, x_ref, q_ref, k_ref, v_ref, after_ref, kv_out, q_out):
    step = pl.program_id(0)
    x = x_ref[0]
    width = k_ref.shape[1]
    dot = partial(jnp.dot, preferred_element_type=F32)

    @pl.when(step == 0)
    def _():
        kv_out[...] = jnp.zeros_like(kv_out)
        q_out[...] = jnp.zeros_like(q_out)

    kv_out[:, :width] += dot(x, k_ref[...])
    kv_out[:, width:] += dot(x, v_ref[...])
    q_out[...] += dot(x, q_ref[...])


def near_product(blocks, x, q_weight, k_weight, v_weight, after):
    count, chunk, cols = x.shape
    widths = [w.shape[1] for w in (q_weight, k_weight, v_weight)]
    kv_width = widths[1] + widths[2]
    return pl.pallas_call(
        near_kernel,
        out_shape=(shape((chunk, kv_width), F32), shape((chunk, widths[0]), F32)),
        grid_spec=pltpu.PrefetchScalarGridSpec(
            num_scalar_prefetch=1,
            grid=(count,),
            in_specs=[pl.BlockSpec((1, chunk, cols), lambda i, s: (i, 0, 0))]
            + [pl.BlockSpec((cols, w), lambda i, s: (s[i], 0)) for w in widths]
            + [ANY],
            out_specs=[
                pl.BlockSpec((chunk, kv_width), lambda i, s: (0, 0)),
                pl.BlockSpec((chunk, widths[0]), lambda i, s: (0, 0)),
            ],
        ),
        compiler_params=PARAMS,
        name="near",
    )(blocks, x, q_weight, k_weight, v_weight, after)


def keys_kernel(near_ref, far_ref, sq_ref, cos_ref, sin_ref, out_ref, sum_ref, *, model):
    chunk, width = near_ref.shape
    tail = far_ref[chunk:, :].astype(F32)
    lines = -(-chunk // width)
    total = sq_ref[...]
    for part in range(2):
        row = [tail[part * lines + i : part * lines + i + 1, :] for i in range(lines)]
        total = total + jnp.concatenate(row, axis=1)[:, :chunk]
    factor = to_column(lax.rsqrt(total / model + epsilon))
    sum_ref[...] = total
    for c in range(0, width, HEAD_SIZE):
        at = slice(c, c + HEAD_SIZE)
        part = (near_ref[:, at] + far_ref[:chunk, at].astype(F32)) * factor
        if c < width // 2:
            part = rotate(part, cos_ref[...], sin_ref[...])
        out_ref[:, at] = part.astype(BF16)


def keys_values(near, far, sq, cosine, sine, c, model):
    chunk, width = near.shape
    whole = lambda i: (0, 0)
    return pl.pallas_call(
        partial(keys_kernel, model=model),
        out_shape=(shape((chunk, width), BF16), shape((1, chunk), F32)),
        grid=(1,),
        in_specs=[
            pl.BlockSpec(near.shape, whole),
            pl.BlockSpec(far.shape, whole),
            pl.BlockSpec((1, chunk), whole),
            pl.BlockSpec((chunk, HEAD_SIZE), lambda i: (c, 0)),
            pl.BlockSpec((chunk, HEAD_SIZE), lambda i: (c, 0)),
        ],
        out_specs=[pl.BlockSpec((chunk, width), whole), pl.BlockSpec((1, chunk), whole)],
        compiler_params=PARAMS,
        name="keys",
    )(near, far, sq, cosine, sine)


def attention_kernel(
    lo_ref, near_ref, far_ref, sum_ref, cos_ref, sin_ref, start_ref, *rest, back, offset, model
):
    kv_refs, (out_ref, k_scr, vt_scr) = rest[:-3], rest[-3:]
    part_rows = kv_refs[0].shape[0]
    group = near_ref.shape[1] // HEAD_SIZE
    tile = pl.program_id(0)

    @pl.when(tile == 0)
    def _():
        for b, kv_ref in enumerate(kv_refs):
            at = slice(b * part_rows, (b + 1) * part_rows)
            k_scr[at, :] = kv_ref[:, :HEAD_SIZE]
            vt_scr[:, at] = kv_ref[:, HEAD_SIZE:].astype(F32).T.astype(BF16)

    scale = query_scale * math.log2(math.e)
    factor = to_column(lax.rsqrt(sum_ref[...] / model + epsilon) * scale)
    heads = []
    for c in range(0, group * HEAD_SIZE, HEAD_SIZE):
        at = slice(c, c + HEAD_SIZE)
        part = (near_ref[:, at] + far_ref[:, at].astype(F32)) * factor
        heads.append(rotate(part, cos_ref[...], sin_ref[...]).astype(BF16))
    q2 = jnp.concatenate(heads, axis=0)
    width = group * Q_TILE
    start = jnp.concatenate([start_ref[...]] * group, axis=1)
    first = back * part_rows * CHUNKS + offset + tile * Q_TILE
    place = first + lax.broadcasted_iota(jnp.int32, (1, Q_TILE), 1)
    place = jnp.concatenate([place] * group, axis=1)

    def score(j):
        base = pl.multiple_of(j * K_TILE, K_TILE)
        return lax.dot_general(
            k_scr[pl.ds(base, K_TILE), :],
            q2,
            (((1,), (1,)), ((), ())),
            preferred_element_type=F32,
        )

    low = lo_ref[tile]
    stop = (first + Q_TILE + K_TILE - 1) // K_TILE

    def step(j, state):
        scores, run_max, run_sum, acc = state
        following = score(jnp.minimum(j + 1, stop - 1))
        base = pl.multiple_of(j * K_TILE, K_TILE)
        key_pos = base + lax.broadcasted_iota(jnp.int32, (K_TILE, width), 0)
        allowed = (key_pos >= start) & (key_pos <= place)
        scores = jnp.where(allowed, scores, NEG)
        new_max = jnp.maximum(run_max, jnp.max(scores, axis=0, keepdims=True))
        expo = jnp.exp2(scores - new_max)
        factor = jnp.exp2(run_max - new_max)
        run_sum = run_sum * factor + jnp.sum(expo, axis=0, keepdims=True)
        acc = acc * factor + jnp.dot(
            vt_scr[:, pl.ds(base, K_TILE)], expo.astype(BF16), preferred_element_type=F32
        )
        return following, new_max, run_sum, acc

    state = (
        score(low),
        jnp.full((1, width), NEG, F32),
        jnp.zeros((1, width), F32),
        jnp.zeros((HEAD_SIZE, width), F32),
    )
    _, _, run_sum, acc = lax.fori_loop(low, stop, step, state)
    context = (acc / run_sum).T
    for g in range(group):
        out_ref[:, g * HEAD_SIZE : (g + 1) * HEAD_SIZE] = context[
            g * Q_TILE : (g + 1) * Q_TILE
        ].astype(BF16)


def attend(near, far, sums, cosine, sine, start, blocks, c, model):
    rows, width = near.shape
    part_rows = blocks[0].shape[0]
    back = len(blocks) // CHUNKS - 1
    tiles = rows // Q_TILE
    low = start[c * rows : (c + 1) * rows : Q_TILE] // K_TILE
    keys = len(blocks) * part_rows
    return pl.pallas_call(
        partial(attention_kernel, back=back, offset=c * rows, model=model),
        out_shape=shape((rows, width), BF16),
        grid_spec=pltpu.PrefetchScalarGridSpec(
            num_scalar_prefetch=1,
            grid=(tiles,),
            in_specs=[
                pl.BlockSpec((Q_TILE, width), lambda i, lo: (i, 0)),
                pl.BlockSpec((Q_TILE, width), lambda i, lo: (i, 0)),
                pl.BlockSpec((1, Q_TILE), lambda i, lo: (0, i)),
                pl.BlockSpec((Q_TILE, HEAD_SIZE), lambda i, lo: (c * tiles + i, 0)),
                pl.BlockSpec((Q_TILE, HEAD_SIZE), lambda i, lo: (c * tiles + i, 0)),
                pl.BlockSpec((1, Q_TILE), lambda i, lo: (0, c * tiles + i)),
            ]
            + [pl.BlockSpec(b.shape, lambda i, lo: (0, 0)) for b in blocks],
            out_specs=pl.BlockSpec((Q_TILE, width), lambda i, lo: (i, 0)),
            scratch_shapes=[
                pltpu.VMEM((keys, HEAD_SIZE), BF16),
                pltpu.VMEM((HEAD_SIZE, keys), BF16),
            ],
        ),
        compiler_params=PARAMS,
        name="attend",
    )(low, near, far, sums, cosine, sine, start[None, :], *blocks)


def output_kernel(z_ref, own_o_ref, o_ref, *rest):
    ctx_refs, (out_ref, sq_ref, acc) = rest[:-3], rest[-3:]
    step = pl.program_id(0)
    plane, _, share, tile = o_ref.shape
    total = jnp.dot(ctx_refs[0][...], own_o_ref[...], preferred_element_type=F32)
    for k, ctx_ref in enumerate(ctx_refs[1:]):
        weight = o_ref[:, k].reshape(plane * share, tile)
        total = total + jnp.dot(ctx_ref[...], weight, preferred_element_type=F32)
    out_ref[...] = total
    squares = jnp.sum(total * total, axis=1, keepdims=True)
    squares = jnp.broadcast_to(squares, acc.shape)

    @pl.when(step == 0)
    def _():
        acc[...] = squares

    @pl.when(step > 0)
    def _():
        acc[...] += squares

    @pl.when(step == pl.num_programs(0) - 1)
    def _():
        sq_ref[...] = acc[...].T[0:1, :]


def output_product(z, o_weight, gathered, contexts):
    chunk, width = contexts[0].shape
    plane, others, share, cols = gathered.shape
    tiles = 3 if cols % (3 * LANES) == 0 else 1
    tile = cols // tiles
    whole = lambda i, z: (0, 0)
    if cols % LANES:
        o_weight = lax.dynamic_slice_in_dim(o_weight, z[0] * cols, cols, axis=1)
        z = z * 0
    return pl.pallas_call(
        output_kernel,
        out_shape=(shape((chunk, cols), F32), shape((1, chunk), F32)),
        grid_spec=pltpu.PrefetchScalarGridSpec(
            num_scalar_prefetch=1,
            grid=(tiles,),
            in_specs=[
                pl.BlockSpec((width, tile), lambda i, z: (0, z[0] * tiles + i)),
                pl.BlockSpec((plane, others, share, tile), lambda i, z: (0, 0, 0, i)),
            ]
            + [pl.BlockSpec((chunk, width), whole) for _ in contexts],
            out_specs=[
                pl.BlockSpec((chunk, tile), lambda i, z: (0, i)),
                pl.BlockSpec((1, chunk), whole),
            ],
            scratch_shapes=[pltpu.VMEM((chunk, LANES), F32)],
        ),
        compiler_params=PARAMS,
        name="output",
    )(z, o_weight, gathered, *contexts)


def final_kernel(token_ref, branch_ref, gain_ref, *rest, model, others):
    sq_refs, out_ref = rest[:others], rest[-1]
    total = sq_refs[0][...]
    for sq_ref in sq_refs[1:]:
        total = total + sq_ref[...]
    factor = to_column(lax.rsqrt(total / model + epsilon))[:, 0:1]
    out = token_ref[...].astype(F32) + branch_ref[...] * factor * gain_ref[...]
    out_ref[...] = out.astype(BF16)


def finish(tokens, branch, out_gain, sums, previous, c, model):
    chunk, cols = branch.shape
    tiles = chunk // Q_TILE
    in_specs = [
        pl.BlockSpec((Q_TILE, cols), lambda i: (c * tiles + i, 0)),
        pl.BlockSpec((Q_TILE, cols), lambda i: (i, 0)),
        pl.BlockSpec((1, cols), lambda i: (0, 0)),
    ]
    in_specs += [pl.BlockSpec((1, Q_TILE), lambda i: (0, i)) for _ in sums]
    args = [tokens, branch, out_gain, *sums]
    aliases = {}
    if previous is not None:
        aliases = {len(args): 0}
        in_specs.append(ANY)
        args.append(previous)
    return pl.pallas_call(
        partial(final_kernel, model=model, others=len(sums)),
        out_shape=shape(tokens.shape, BF16),
        grid=(tiles,),
        in_specs=in_specs,
        out_specs=pl.BlockSpec((Q_TILE, cols), lambda i: (c * tiles + i, 0)),
        input_output_aliases=aliases,
        compiler_params=PARAMS,
        name="finish",
    )(*args)


def per_device(
    tokens, seg_ids, in_gain, q_weight, k_weight, value_weight, o_weight, out_gain, *, sizes
):
    rows, cols = tokens.shape
    model = in_gain.shape[0]
    nz, nseq = sizes["tensor"], sizes["seq"]
    plane = nseq * sizes["groups"]
    z = lax.axis_index("tensor")
    seq = lax.axis_index("seq")
    in_plane = lax.axis_index(PLANE)
    half = nz // 2
    side, within = z // half, z % half
    half_rows = half * cols

    ring = [(i, i // half * half + (i + 1) % half) for i in range(nz)]
    swap = [(i, (i + half) % nz) for i in range(nz)]
    turn = lambda k: [(i, (i + k) % nz) for i in range(nz)]
    seq_bits = [1 << b for b in range(1, nseq.bit_length() - 1)]
    group_bits = [nseq << b for b in range(sizes["groups"].bit_length() - 1)]

    share = half_rows // plane
    at = jnp.reshape((1 - side) * plane + in_plane, (1,))
    packed_kv, packed_q = pack(at, q_weight, k_weight, value_weight, share)
    far_kv = lax.ppermute(packed_kv, "tensor", swap)
    far_q = lax.ppermute(packed_q, "tensor", swap)
    where_kv, *far_kv = spread(far_kv, plane, seq_bits + group_bits + [1])
    where_q, *far_q = spread(far_q, plane, group_bits + seq_bits + [1])

    chunk = rows // CHUNKS
    sources = (within + half - jnp.arange(half, dtype=jnp.int32)) % half
    blocks_of = side * half + sources
    gains = in_gain.reshape(nz, 1, cols)
    received = []
    for c in range(CHUNKS):
        blocks = []
        held = tokens[c * chunk : (c + 1) * chunk]
        for _ in range(half - 1):
            held = lax.ppermute(held, "tensor", ring)
            blocks.append(held)
        received.append(blocks)

    o_share = o_weight.shape[0] // plane
    moved = []
    for k in range(1, nz):
        target = (z + k) % nz
        piece = lax.dynamic_slice(
            o_weight, (in_plane * o_share, target * cols), (o_share, cols)
        )
        moved.append(lax.ppermute(piece, "tensor", turn(k)))
    gathered_o = lax.all_gather(jnp.stack(moved), PLANE)

    back = -(-(nseq * rows // 2 - 1) // rows)
    earlier = lambda k: [(i, i + k) for i in range(nseq - k)]
    start = jnp.sum((seg_ids[None, :] < seg_ids[:, None]).astype(jnp.int32), axis=1)
    start = start + back * rows
    for k in range(1, back + 1):
        ids = lax.ppermute(seg_ids, "seq", earlier(k))
        ids = jnp.where(seq >= k, ids, -1)
        start = start - jnp.sum((ids[None, :] >= seg_ids[:, None]).astype(jnp.int32), axis=1)

    cosine, sine = rotation_table(seq * rows + jnp.arange(rows, dtype=jnp.int32))

    kv_parts, q_parts = [], []
    for c in range(CHUNKS):
        x, sq = prep(blocks_of, gains, tokens, received[c], chunk, c)
        sent_kv = far_product(where_kv, sources, x, far_kv, sq)
        sent_q = far_product(where_q, sources, x, far_q, None)
        got_kv = lax.ppermute(sent_kv, "tensor", swap)
        got_q = lax.ppermute(sent_q, "tensor", swap)
        near_kv, near_q = near_product(
            blocks_of, x, q_weight, k_weight, value_weight, sent_q
        )
        own_kv, sums = keys_values(near_kv, got_kv, sq, cosine, sine, c, model)
        kv_parts.append(own_kv)
        q_parts.append((near_q, got_q, sums))
    blocks = list(kv_parts)
    for k in range(1, back + 1):
        blocks = [lax.ppermute(part, "seq", earlier(k)) for part in kv_parts] + blocks

    out = None
    z_at = jnp.reshape(z, (1,))
    for c in range(CHUNKS):
        context = attend(*q_parts[c], cosine, sine, start, blocks, c, model)
        contexts = [context]
        contexts += [lax.ppermute(context, "tensor", turn(k)) for k in range(1, nz)]
        branch, own_sq = output_product(z_at, o_weight, gathered_o, contexts)
        sums = [own_sq]
        sums += [lax.ppermute(own_sq, "tensor", turn(k)) for k in range(1, nz)]
        out = finish(tokens, branch, out_gain[None, :], sums, out, c, model)
    return out


def solution(mesh):
    return jax.shard_map(
        partial(per_device, sizes=dict(mesh.shape)),
        mesh=mesh,
        in_specs=(
            P(("groups", "seq"), "tensor"),
            P(("groups", "seq")),
            P(),
            P(None, "tensor"),
            P(None, "tensor"),
            P(None, "tensor"),
            P("tensor", None),
            P("tensor"),
        ),
        out_specs=P(("groups", "seq"), "tensor"),
        check_vma=False,
    )
```

```python
import math
from functools import partial

import jax
import jax.numpy as jnp
from jax import lax
from jax.experimental import pallas as pl
from jax.experimental.pallas import tpu as pltpu
from jax.sharding import PartitionSpec as P

HEAD_SIZE = 128
PLANE = ("groups", "seq")

epsilon = 1e-06
query_scale = 144.0 ** (-0.5)
rope_base = 10000.0
NEG = -1e30
Q_TILE = 128
K_TILE = 256
CHUNKS = 2
LANES = 128
TAIL = 16
F32, BF16 = jnp.float32, jnp.bfloat16
ANY = pl.BlockSpec(memory_space=pl.ANY)
HBM = pl.BlockSpec(memory_space=pltpu.HBM)
PARAMS = pltpu.CompilerParams(vmem_limit_bytes=40 * 1024 * 1024)
ALL_VMEM = pltpu.CompilerParams(vmem_limit_bytes=62 * 1024 * 1024)


def shape(dims, dtype):
    return jax.ShapeDtypeStruct(dims, dtype)


def to_row(column):
    return jnp.broadcast_to(column, (column.shape[0], LANES)).T[0:1, :]


def to_column(row):
    return jnp.broadcast_to(row, (LANES, row.shape[1])).T


def rotation_table(token_places):
    half_dim = HEAD_SIZE // 2
    inverse = rope_base ** (-jnp.arange(half_dim, dtype=F32) / half_dim)
    angles = token_places.astype(F32)[:, None] * inverse[None, :]
    cosine, sine = jnp.cos(angles), jnp.sin(angles)
    return jnp.concatenate([cosine, cosine], 1), jnp.concatenate([-sine, sine], 1)


def rotate(vectors, cosine, sine):
    return vectors * cosine + pltpu.roll(vectors, HEAD_SIZE // 2, 1) * sine


def pack_kernel(at_ref, q_ref, k_ref, v_ref, kv_out, q_out, sems):
    share, width = q_out.shape[0], k_ref.shape[1]
    rows = pl.ds(pl.multiple_of(at_ref[0] * share, TAIL), share)
    copies = [
        pltpu.make_async_copy(k_ref.at[rows], kv_out.at[:, pl.ds(0, width)], sems.at[0]),
        pltpu.make_async_copy(v_ref.at[rows], kv_out.at[:, pl.ds(width, width)], sems.at[1]),
        pltpu.make_async_copy(q_ref.at[rows], q_out, sems.at[2]),
    ]
    for copy in copies:
        copy.start()
    for copy in copies:
        copy.wait()


def pack(at, q_weight, k_weight, v_weight, share):
    kv_width = k_weight.shape[1] + v_weight.shape[1]
    return pl.pallas_call(
        pack_kernel,
        out_shape=(shape((share, kv_width), BF16), shape((share, q_weight.shape[1]), BF16)),
        grid_spec=pltpu.PrefetchScalarGridSpec(
            num_scalar_prefetch=1,
            grid=(1,),
            in_specs=[HBM, HBM, HBM],
            out_specs=[
                pl.BlockSpec((share, kv_width), lambda i, at: (0, 0)),
                pl.BlockSpec((share, q_weight.shape[1]), lambda i, at: (0, 0)),
            ],
            scratch_shapes=[pltpu.SemaphoreType.DMA((3,))],
        ),
        compiler_params=ALL_VMEM,
        name="pack",
    )(at, q_weight, k_weight, v_weight)


def join_kernel(first_ref, second_ref, out_ref, sems):
    held = first_ref.shape[0]
    copies = [
        pltpu.make_async_copy(first_ref, out_ref.at[pl.ds(0, held)], sems.at[0]),
        pltpu.make_async_copy(second_ref, out_ref.at[pl.ds(held, held)], sems.at[1]),
    ]
    for copy in copies:
        copy.start()
    for copy in copies:
        copy.wait()


def join(first, second):
    return pl.pallas_call(
        join_kernel,
        out_shape=shape((2 * first.shape[0],) + first.shape[1:], first.dtype),
        in_specs=[ANY, ANY],
        scratch_shapes=[pltpu.SemaphoreType.DMA((2,))],
        compiler_params=PARAMS,
        name="join",
    )(first, second)


def spread(piece, plane, masks):
    own = piece[None]
    order = [0]
    for mask in masks:
        got = lax.ppermute(own, PLANE, [(i, i ^ mask) for i in range(plane)])
        order = order + [k ^ mask for k in order]
        if mask != masks[-1]:
            own = join(own, got)
    return order, own, got


def prep_kernel(src_ref, gain_ref, *rest):
    x_refs, (out_ref, sq_ref) = rest[:-2], rest[-2:]
    total = 0.0
    for k, x_ref in enumerate(x_refs):
        x = x_ref[...].astype(F32)
        total = total + jnp.sum(x * x, axis=1, keepdims=True)
        out_ref[k] = (x * gain_ref[src_ref[k]]).astype(BF16)
    sq_ref[...] = to_row(total)


def prep(sources, gains, tokens, received, chunk, c):
    count, (nz, _, cols) = len(received) + 1, gains.shape
    return pl.pallas_call(
        prep_kernel,
        out_shape=(shape((count, chunk, cols), BF16), shape((1, chunk), F32)),
        grid_spec=pltpu.PrefetchScalarGridSpec(
            num_scalar_prefetch=1,
            grid=(1,),
            in_specs=[
                pl.BlockSpec((nz, 1, cols), lambda i, s: (0, 0, 0)),
                pl.BlockSpec((chunk, cols), lambda i, s: (c, 0)),
            ]
            + [pl.BlockSpec((chunk, cols), lambda i, s: (0, 0)) for _ in received],
            out_specs=[
                pl.BlockSpec((count, chunk, cols), lambda i, s: (0, 0, 0)),
                pl.BlockSpec((1, chunk), lambda i, s: (0, 0)),
            ],
        ),
        compiler_params=PARAMS,
        name="prep",
    )(sources, gains, tokens, *received)


def far_kernel(place_ref, src_ref, x_ref, sq_ref, *rest, orders):
    pieces, (out_ref, weight, sems) = rest[:-3], rest[-3:]
    copies, column = [], 0
    for order, own_ref, got_ref in zip(orders, pieces[::2], pieces[1::2]):
        held, share, width = own_ref.shape
        for i, mask in enumerate(order):
            piece = own_ref.at[i] if i < held else got_ref.at[i - held]
            row = pl.multiple_of((place_ref[0] ^ mask) * share, TAIL)
            there = weight.at[pl.ds(row, share), pl.ds(column, width)]
            copies.append(pltpu.make_async_copy(piece, there, sems.at[len(copies)]))
        column += width
    for copy in copies:
        copy.start()
    for copy in copies:
        copy.wait()
    count, chunk, cols = x_ref.shape
    total = None
    for k in range(count):
        row = pl.multiple_of(src_ref[k] * cols, TAIL)
        term = jnp.dot(x_ref[k], weight[pl.ds(row, cols), :], preferred_element_type=F32)
        total = term if total is None else total + term
    out_ref[:chunk, :] = total.astype(BF16)
    sq = sq_ref[...]
    high = sq.astype(BF16).astype(F32)
    out_ref[chunk:, :] = lines_of((high, sq - high), out_ref.shape[1])


def lines_of(rows, width):
    lines = []
    for row in rows:
        for at in range(0, row.shape[1], width):
            line = row[:, at : at + width]
            if line.shape[1] < width:
                rest = jnp.zeros((1, width - line.shape[1]), F32)
                line = jnp.concatenate([line, rest], axis=1)
            lines.append(line)
    lines.append(jnp.zeros((TAIL - len(lines), width), F32))
    return jnp.concatenate(lines, axis=0).astype(BF16)


def rows_of(tail, count, length):
    per_row = -(-length // tail.shape[1])
    rows = []
    for r in range(count):
        lines = [tail[r * per_row + i : r * per_row + i + 1, :] for i in range(per_row)]
        rows.append(jnp.concatenate(lines, axis=1)[:, :length])
    return rows


def far_product(place, sources, x, gathered, sq):
    orders = [g[0] for g in gathered]
    pieces = [piece for g in gathered for piece in g[1:]]
    width = sum(g[1].shape[2] for g in gathered)
    share = pieces[0].shape[1]
    count, chunk, cols = x.shape
    return pl.pallas_call(
        partial(far_kernel, orders=orders),
        out_shape=shape((chunk + TAIL, width), BF16),
        grid_spec=pltpu.PrefetchScalarGridSpec(
            num_scalar_prefetch=2,
            grid=(1,),
            in_specs=[
                pl.BlockSpec((count, chunk, cols), lambda i, p, s: (0, 0, 0)),
                pl.BlockSpec((1, chunk), lambda i, p, s: (0, 0)),
            ]
            + [ANY for _ in pieces],
            out_specs=pl.BlockSpec((chunk + TAIL, width), lambda i, p, s: (0, 0)),
            scratch_shapes=[
                pltpu.VMEM((len(orders[0]) * share, width), BF16),
                pltpu.SemaphoreType.DMA((sum(len(o) for o in orders),)),
            ],
        ),
        compiler_params=PARAMS,
        name="far",
    )(place, sources, x, sq, *pieces)


def near_kernel(src_ref, x_ref, k_ref, v_ref, q_ref, after_ref, out_ref):
    x = x_ref[0]

    @pl.when(pl.program_id(0) == 0)
    def _():
        out_ref[...] = jnp.zeros_like(out_ref)

    column = 0
    for ref in (k_ref, v_ref, q_ref):
        at = slice(column, column + ref.shape[1])
        out_ref[:, at] += jnp.dot(x, ref[...], preferred_element_type=F32)
        column += ref.shape[1]


def near_product(blocks, x, weights, after):
    count, chunk, cols = x.shape
    widths = [w.shape[1] for w in weights]
    return pl.pallas_call(
        near_kernel,
        out_shape=shape((chunk, sum(widths)), F32),
        grid_spec=pltpu.PrefetchScalarGridSpec(
            num_scalar_prefetch=1,
            grid=(count,),
            in_specs=[pl.BlockSpec((1, chunk, cols), lambda i, s: (i, 0, 0))]
            + [pl.BlockSpec((cols, w), lambda i, s: (s[i], 0)) for w in widths]
            + [ANY],
            out_specs=pl.BlockSpec((chunk, sum(widths)), lambda i, s: (0, 0)),
        ),
        compiler_params=PARAMS,
        name="near",
    )(blocks, x, *weights, after)


def keys_kernel(near_ref, far_ref, sq_ref, id_ref, cos_ref, sin_ref, out_ref, sum_ref, *, model):
    chunk, width = near_ref.shape
    tail = far_ref[chunk:, :].astype(F32)
    total = sum(rows_of(tail, 2, chunk), sq_ref[...])
    factor = to_column(lax.rsqrt(total / model + epsilon))
    sum_ref[...] = total
    for c in range(0, width, HEAD_SIZE):
        at = slice(c, c + HEAD_SIZE)
        part = (near_ref[:, at] + far_ref[:chunk, at].astype(F32)) * factor
        if c < width // 2:
            part = rotate(part, cos_ref[...], sin_ref[...])
        out_ref[:chunk, at] = part.astype(BF16)
    out_ref[chunk:, :] = lines_of((id_ref[...].astype(F32),), width)


def keys_values(near, far, sq, ids, cosine, sine, c, width, model):
    chunk = near.shape[0]
    whole = lambda i: (0, 0)
    return pl.pallas_call(
        partial(keys_kernel, model=model),
        out_shape=(shape((chunk + TAIL, width), BF16), shape((1, chunk), F32)),
        grid=(1,),
        in_specs=[
            pl.BlockSpec((chunk, width), whole),
            pl.BlockSpec(far.shape, whole),
            pl.BlockSpec((1, chunk), whole),
            pl.BlockSpec((1, chunk), lambda i: (0, c)),
            pl.BlockSpec((chunk, HEAD_SIZE), lambda i: (c, 0)),
            pl.BlockSpec((chunk, HEAD_SIZE), lambda i: (c, 0)),
        ],
        out_specs=[pl.BlockSpec((chunk + TAIL, width), whole), pl.BlockSpec((1, chunk), whole)],
        compiler_params=PARAMS,
        name="keys",
    )(near, far, sq, ids, cosine, sine)


def attention_kernel(
    seq_ref, near_ref, far_ref, sum_ref, cos_ref, sin_ref, id_ref, *rest, back, offset, model
):
    kv_refs, (out_ref, k_scr, vt_scr, id_scr) = rest[:-4], rest[-4:]
    part_rows = kv_refs[0].shape[0] - TAIL
    group = near_ref.shape[1] // HEAD_SIZE
    tile = pl.program_id(0)

    @pl.when(tile == 0)
    def _():
        for b, kv_ref in enumerate(kv_refs):
            at = slice(b * part_rows, (b + 1) * part_rows)
            k_scr[at, :] = kv_ref[:part_rows, :HEAD_SIZE]
            vt_scr[:, at] = kv_ref[:part_rows, HEAD_SIZE:].astype(F32).T.astype(BF16)
            (ids,) = rows_of(kv_ref[part_rows:, :].astype(F32), 1, part_rows)
            exists = b // CHUNKS >= back - seq_ref[0]
            id_scr[at, :] = to_column(jnp.where(exists, ids, -1.0))

    scale = query_scale * math.log2(math.e)
    factor = to_column(lax.rsqrt(sum_ref[...] / model + epsilon) * scale)
    heads = []
    for c in range(0, group * HEAD_SIZE, HEAD_SIZE):
        at = slice(c, c + HEAD_SIZE)
        part = (near_ref[:, at] + far_ref[:, at].astype(F32)) * factor
        heads.append(rotate(part, cos_ref[...], sin_ref[...]).astype(BF16))
    q2 = jnp.concatenate(heads, axis=0)
    width = group * Q_TILE

    before = (id_scr[...] < id_ref[...].astype(F32)).astype(F32)
    start = jnp.sum(before, axis=0, keepdims=True).astype(jnp.int32)
    low = jnp.min(start) // K_TILE
    start = jnp.concatenate([start] * group, axis=1)
    first = back * part_rows * CHUNKS + offset + tile * Q_TILE
    place = first + lax.broadcasted_iota(jnp.int32, (1, Q_TILE), 1)
    place = jnp.concatenate([place] * group, axis=1)

    def score(j):
        base = pl.multiple_of(j * K_TILE, K_TILE)
        return lax.dot_general(
            k_scr[pl.ds(base, K_TILE), :],
            q2,
            (((1,), (1,)), ((), ())),
            preferred_element_type=F32,
        )

    stop = (first + Q_TILE + K_TILE - 1) // K_TILE

    def step(j, state):
        scores, run_max, run_sum, acc = state
        following = score(jnp.minimum(j + 1, stop - 1))
        base = pl.multiple_of(j * K_TILE, K_TILE)
        key_pos = base + lax.broadcasted_iota(jnp.int32, (K_TILE, width), 0)
        allowed = (key_pos >= start) & (key_pos <= place)
        scores = jnp.where(allowed, scores, NEG)
        new_max = jnp.maximum(run_max, jnp.max(scores, axis=0, keepdims=True))
        expo = jnp.exp2(scores - new_max)
        factor = jnp.exp2(run_max - new_max)
        run_sum = run_sum * factor + jnp.sum(expo, axis=0, keepdims=True)
        acc = acc * factor + jnp.dot(
            vt_scr[:, pl.ds(base, K_TILE)], expo.astype(BF16), preferred_element_type=F32
        )
        return following, new_max, run_sum, acc

    state = (
        score(low),
        jnp.full((1, width), NEG, F32),
        jnp.zeros((1, width), F32),
        jnp.zeros((HEAD_SIZE, width), F32),
    )
    _, _, run_sum, acc = lax.fori_loop(low, stop, step, state)
    context = (acc / run_sum).T
    for g in range(group):
        out_ref[:, g * HEAD_SIZE : (g + 1) * HEAD_SIZE] = context[
            g * Q_TILE : (g + 1) * Q_TILE
        ].astype(BF16)


def attend(seq, near, far, sums, cosine, sine, ids, blocks, c, width, model):
    rows = near.shape[0]
    part_rows = blocks[0].shape[0] - TAIL
    back = len(blocks) // CHUNKS - 1
    tiles = rows // Q_TILE
    keys = len(blocks) * part_rows
    last = near.shape[1] // width - 1
    return pl.pallas_call(
        partial(attention_kernel, back=back, offset=c * rows, model=model),
        out_shape=shape((rows, width), BF16),
        grid_spec=pltpu.PrefetchScalarGridSpec(
            num_scalar_prefetch=1,
            grid=(tiles,),
            in_specs=[
                pl.BlockSpec((Q_TILE, width), lambda i, s: (i, last)),
                pl.BlockSpec((Q_TILE, width), lambda i, s: (i, last)),
                pl.BlockSpec((1, Q_TILE), lambda i, s: (0, i)),
                pl.BlockSpec((Q_TILE, HEAD_SIZE), lambda i, s: (c * tiles + i, 0)),
                pl.BlockSpec((Q_TILE, HEAD_SIZE), lambda i, s: (c * tiles + i, 0)),
                pl.BlockSpec((1, Q_TILE), lambda i, s: (0, c * tiles + i)),
            ]
            + [pl.BlockSpec(b.shape, lambda i, s: (0, 0)) for b in blocks],
            out_specs=pl.BlockSpec((Q_TILE, width), lambda i, s: (i, 0)),
            scratch_shapes=[
                pltpu.VMEM((keys, HEAD_SIZE), BF16),
                pltpu.VMEM((HEAD_SIZE, keys), BF16),
                pltpu.VMEM((keys, LANES), F32),
            ],
        ),
        compiler_params=PARAMS,
        name="attend",
    )(seq, near, far, sums, cosine, sine, ids, *blocks)


def output_kernel(z_ref, own_o_ref, o_ref, *rest):
    ctx_refs, (out_ref, sq_ref, acc) = rest[:-3], rest[-3:]
    step = pl.program_id(0)
    plane, _, share, tile = o_ref.shape
    total = jnp.dot(ctx_refs[0][...], own_o_ref[...], preferred_element_type=F32)
    for i, ctx_ref in enumerate(ctx_refs[1:]):
        weight = o_ref[:, z_ref[1 + i]].reshape(plane * share, tile)
        total = total + jnp.dot(ctx_ref[...], weight, preferred_element_type=F32)
    out_ref[...] = total
    squares = jnp.sum(total * total, axis=1, keepdims=True)
    squares = jnp.broadcast_to(squares, acc.shape)

    @pl.when(step == 0)
    def _():
        acc[...] = squares

    @pl.when(step > 0)
    def _():
        acc[...] += squares

    @pl.when(step == pl.num_programs(0) - 1)
    def _():
        sq_ref[...] = acc[...].T[0:1, :]


def output_product(z, o_weight, gathered, contexts):
    chunk, width = contexts[0].shape
    plane, others, share, cols = gathered.shape
    tiles = 3 if cols % (3 * LANES) == 0 else 1
    tile = cols // tiles
    whole = lambda i, z: (0, 0)
    if cols % LANES:
        o_weight = lax.dynamic_slice_in_dim(o_weight, z[0] * cols, cols, axis=1)
        z = z.at[0].set(0)
    return pl.pallas_call(
        output_kernel,
        out_shape=(shape((chunk, cols), F32), shape((1, chunk), F32)),
        grid_spec=pltpu.PrefetchScalarGridSpec(
            num_scalar_prefetch=1,
            grid=(tiles,),
            in_specs=[
                pl.BlockSpec((width, tile), lambda i, z: (0, z[0] * tiles + i)),
                pl.BlockSpec((plane, others, share, tile), lambda i, z: (0, 0, 0, i)),
            ]
            + [pl.BlockSpec((chunk, width), whole) for _ in contexts],
            out_specs=[
                pl.BlockSpec((chunk, tile), lambda i, z: (0, i)),
                pl.BlockSpec((1, chunk), whole),
            ],
            scratch_shapes=[pltpu.VMEM((chunk, LANES), F32)],
        ),
        compiler_params=PARAMS,
        name="output",
    )(z, o_weight, gathered, *contexts)


def final_kernel(token_ref, branch_ref, gain_ref, *rest, model, others):
    sq_refs, out_ref = rest[:others], rest[-1]
    total = sq_refs[0][...]
    for sq_ref in sq_refs[1:]:
        total = total + sq_ref[...]
    factor = to_column(lax.rsqrt(total / model + epsilon))[:, 0:1]
    out = token_ref[...].astype(F32) + branch_ref[...] * factor * gain_ref[...]
    out_ref[...] = out.astype(BF16)


def finish(tokens, branch, out_gain, sums, previous, c, model):
    chunk, cols = branch.shape
    tiles = chunk // Q_TILE
    in_specs = [
        pl.BlockSpec((Q_TILE, cols), lambda i: (c * tiles + i, 0)),
        pl.BlockSpec((Q_TILE, cols), lambda i: (i, 0)),
        pl.BlockSpec((1, cols), lambda i: (0, 0)),
    ]
    in_specs += [pl.BlockSpec((1, Q_TILE), lambda i: (0, i)) for _ in sums]
    args = [tokens, branch, out_gain, *sums]
    aliases = {}
    if previous is not None:
        aliases = {len(args): 0}
        in_specs.append(ANY)
        args.append(previous)
    return pl.pallas_call(
        partial(final_kernel, model=model, others=len(sums)),
        out_shape=shape(tokens.shape, BF16),
        grid=(tiles,),
        in_specs=in_specs,
        out_specs=pl.BlockSpec((Q_TILE, cols), lambda i: (c * tiles + i, 0)),
        input_output_aliases=aliases,
        compiler_params=PARAMS,
        name="finish",
    )(*args)


def per_device(
    tokens, seg_ids, in_gain, q_weight, k_weight, value_weight, o_weight, out_gain, *, sizes
):
    rows, cols = tokens.shape
    model = in_gain.shape[0]
    nz, nseq = sizes["tensor"], sizes["seq"]
    plane = nseq * sizes["groups"]
    z = lax.axis_index("tensor")
    seq = lax.axis_index("seq")
    in_plane = lax.axis_index(PLANE)
    half = nz // 2
    side, within = z // half, z % half
    half_rows = half * cols

    ring = [(i, i // half * half + (i + 1) % half) for i in range(nz)]
    swap = [(i, (i + half) % nz) for i in range(nz)]
    turn = lambda k: [(i, (i + k) % nz) for i in range(nz)]
    seq_bits = [1 << b for b in range(1, nseq.bit_length() - 1)]
    group_bits = [nseq << b for b in range(sizes["groups"].bit_length() - 1)]

    share = half_rows // plane
    at = jnp.reshape((1 - side) * plane + in_plane, (1,))
    packed_kv, packed_q = pack(at, q_weight, k_weight, value_weight, share)
    far_kv = lax.ppermute(packed_kv, "tensor", swap)
    far_q = lax.ppermute(packed_q, "tensor", swap)
    far_kv = spread(far_kv, plane, seq_bits + group_bits + [1])
    far_q = spread(far_q, plane, group_bits + seq_bits + [1])

    chunk = rows // CHUNKS
    sources = (within + half - jnp.arange(half, dtype=jnp.int32)) % half
    blocks_of = side * half + sources
    gains = in_gain.reshape(nz, 1, cols)
    received = []
    for c in range(CHUNKS):
        blocks = []
        held = tokens[c * chunk : (c + 1) * chunk]
        for _ in range(half - 1):
            held = lax.ppermute(held, "tensor", ring)
            blocks.append(held)
        received.append(blocks)

    cosine, sine = rotation_table(seq * rows + jnp.arange(rows, dtype=jnp.int32))
    ids = seg_ids[None, :]
    weights = (k_weight, value_weight, q_weight)
    kv_width = k_weight.shape[1] + value_weight.shape[1]
    place = jnp.reshape(in_plane, (1,))
    prepared, sent = [], []
    for c in range(CHUNKS):
        prepared.append(prep(blocks_of, gains, tokens, received[c], chunk, c))
        sent.append(far_product(place, sources, prepared[c][0], [far_kv, far_q], prepared[c][1]))
    kv_parts, q_parts = [], []
    for c in range(CHUNKS):
        x, sq = prepared[c]
        got = lax.ppermute(sent[c], "tensor", swap)
        near = near_product(blocks_of, x, weights, sent[-1])
        own_kv, sums = keys_values(near, got, sq, ids, cosine, sine, c, kv_width, model)
        kv_parts.append(own_kv)
        q_parts.append((near, got, sums))

    back = -(-(nseq * rows // 2 - 1) // rows)
    blocks = list(kv_parts)
    for k in range(1, back + 1):
        earlier = [(i, i + k) for i in range(nseq - k)]
        blocks = [lax.ppermute(part, "seq", earlier) for part in kv_parts] + blocks

    o_share = o_weight.shape[0] // plane
    last = sent[-1][0, 0]
    wait = (last != last).astype(jnp.int32)
    moved = []
    for k in range(1, nz):
        target = (z + k) % nz
        piece = lax.dynamic_slice(
            o_weight, (in_plane * o_share + wait, target * cols), (o_share, cols)
        )
        moved.append(lax.ppermute(piece, "tensor", turn(k)))
    gathered_o = lax.all_gather(jnp.stack(moved), PLANE)

    out = None
    order = list(range(nz - 1))
    if nz == 4:
        order = [1, 0, 2, jnp.where(z < half, 0, 2)]
    z_at = jnp.stack([z] + [jnp.int32(k) for k in order])
    seq_at = jnp.reshape(seq, (1,))
    q_width = q_weight.shape[1]
    for c in range(CHUNKS):
        context = attend(seq_at, *q_parts[c], cosine, sine, ids, blocks, c, q_width, model)
        if nz == 4:
            opposite = lax.ppermute(context, "tensor", swap)
            right = lax.ppermute(context, "tensor", [(0, 1), (1, 2), (2, 3)])
            left = lax.ppermute(context, "tensor", [(1, 0), (2, 1), (3, 2)])
            far_end = lax.ppermute(opposite, "tensor", [(2, 3), (1, 0)])
            contexts = [context, opposite, right, left, far_end]
        else:
            contexts = [context]
            contexts += [lax.ppermute(context, "tensor", turn(k)) for k in range(1, nz)]
        branch, own_sq = output_product(z_at, o_weight, gathered_o, contexts)
        sums = [own_sq]
        sums += [lax.ppermute(own_sq, "tensor", turn(k)) for k in range(1, nz)]
        out = finish(tokens, branch, out_gain[None, :], sums, out, c, model)
    return out


def solution(mesh):
    return jax.shard_map(
        partial(per_device, sizes=dict(mesh.shape)),
        mesh=mesh,
        in_specs=(
            P(("groups", "seq"), "tensor"),
            P(("groups", "seq")),
            P(),
            P(None, "tensor"),
            P(None, "tensor"),
            P(None, "tensor"),
            P("tensor", None),
            P("tensor"),
        ),
        out_specs=P(("groups", "seq"), "tensor"),
        check_vma=False,
    )
```

```python
import math
from functools import partial

import jax
import jax.numpy as jnp
from jax import lax
from jax.experimental import pallas as pl
from jax.experimental.pallas import tpu as pltpu
from jax.sharding import PartitionSpec as P

HEAD_SIZE = 128
PLANE = ("groups", "seq")

epsilon = 1e-06
query_scale = 144.0 ** (-0.5)
rope_base = 10000.0
NEG = -1e30
Q_TILE = 128
K_TILE = 256
CHUNKS = 2
LANES = 128
TAIL = 16
F32, BF16 = jnp.float32, jnp.bfloat16
ANY = pl.BlockSpec(memory_space=pl.ANY)
HBM = pl.BlockSpec(memory_space=pltpu.HBM)
PARAMS = pltpu.CompilerParams(vmem_limit_bytes=40 * 1024 * 1024)
ALL_VMEM = pltpu.CompilerParams(vmem_limit_bytes=62 * 1024 * 1024)


def shape(dims, dtype):
    return jax.ShapeDtypeStruct(dims, dtype)


def to_row(column):
    return jnp.broadcast_to(column, (column.shape[0], LANES)).T[0:1, :]


def to_column(row):
    return jnp.broadcast_to(row, (LANES, row.shape[1])).T


def rotation_table(token_places):
    half_dim = HEAD_SIZE // 2
    inverse = rope_base ** (-jnp.arange(half_dim, dtype=F32) / half_dim)
    angles = token_places.astype(F32)[:, None] * inverse[None, :]
    cosine, sine = jnp.cos(angles), jnp.sin(angles)
    return jnp.concatenate([cosine, cosine], 1), jnp.concatenate([-sine, sine], 1)


def rotate(vectors, cosine, sine):
    return vectors * cosine + pltpu.roll(vectors, HEAD_SIZE // 2, 1) * sine


def pack_kernel(at_ref, q_ref, k_ref, v_ref, kv_out, q_out, sems):
    share, width = q_out.shape[0], k_ref.shape[1]
    rows = pl.ds(pl.multiple_of(at_ref[0] * share, TAIL), share)
    copies = [
        pltpu.make_async_copy(k_ref.at[rows], kv_out.at[:, pl.ds(0, width)], sems.at[0]),
        pltpu.make_async_copy(v_ref.at[rows], kv_out.at[:, pl.ds(width, width)], sems.at[1]),
        pltpu.make_async_copy(q_ref.at[rows], q_out, sems.at[2]),
    ]
    for copy in copies:
        copy.start()
    for copy in copies:
        copy.wait()


def pack(at, q_weight, k_weight, v_weight, share):
    kv_width = k_weight.shape[1] + v_weight.shape[1]
    return pl.pallas_call(
        pack_kernel,
        out_shape=(shape((share, kv_width), BF16), shape((share, q_weight.shape[1]), BF16)),
        grid_spec=pltpu.PrefetchScalarGridSpec(
            num_scalar_prefetch=1,
            grid=(1,),
            in_specs=[HBM, HBM, HBM],
            out_specs=[
                pl.BlockSpec((share, kv_width), lambda i, at: (0, 0)),
                pl.BlockSpec((share, q_weight.shape[1]), lambda i, at: (0, 0)),
            ],
            scratch_shapes=[pltpu.SemaphoreType.DMA((3,))],
        ),
        compiler_params=ALL_VMEM,
        name="pack",
    )(at, q_weight, k_weight, v_weight)


def join_kernel(first_ref, second_ref, out_ref, sems):
    held = first_ref.shape[0]
    copies = [
        pltpu.make_async_copy(first_ref, out_ref.at[pl.ds(0, held)], sems.at[0]),
        pltpu.make_async_copy(second_ref, out_ref.at[pl.ds(held, held)], sems.at[1]),
    ]
    for copy in copies:
        copy.start()
    for copy in copies:
        copy.wait()


def join(first, second):
    return pl.pallas_call(
        join_kernel,
        out_shape=shape((2 * first.shape[0],) + first.shape[1:], first.dtype),
        in_specs=[ANY, ANY],
        scratch_shapes=[pltpu.SemaphoreType.DMA((2,))],
        compiler_params=PARAMS,
        name="join",
    )(first, second)


def spread(piece, plane, masks):
    own = piece[None]
    order = [0]
    for mask in masks:
        got = lax.ppermute(own, PLANE, [(i, i ^ mask) for i in range(plane)])
        order = order + [k ^ mask for k in order]
        if mask != masks[-1]:
            own = join(own, got)
    return order, own, got


def prep_kernel(first_ref, gain_ref, x_ref, out_ref, sq_ref):
    total = 0.0
    for k in range(x_ref.shape[0]):
        x = x_ref[k].astype(F32)
        total = total + jnp.sum(x * x, axis=1, keepdims=True)
        out_ref[k] = (x * gain_ref[first_ref[0] + k]).astype(BF16)
    sq_ref[...] = to_row(total)


def prep(first, gains, x):
    count, chunk, cols = x.shape
    return pl.pallas_call(
        prep_kernel,
        out_shape=(shape(x.shape, BF16), shape((1, chunk), F32)),
        grid_spec=pltpu.PrefetchScalarGridSpec(
            num_scalar_prefetch=1,
            grid=(1,),
            in_specs=[
                pl.BlockSpec(gains.shape, lambda i, s: (0, 0, 0)),
                pl.BlockSpec(x.shape, lambda i, s: (0, 0, 0)),
            ],
            out_specs=[
                pl.BlockSpec(x.shape, lambda i, s: (0, 0, 0)),
                pl.BlockSpec((1, chunk), lambda i, s: (0, 0)),
            ],
        ),
        compiler_params=PARAMS,
        name="prep",
    )(first, gains, x)


def far_kernel(place_ref, x_ref, sq_ref, after_ref, *rest, orders):
    pieces, (out_ref, weight, sems) = rest[:-3], rest[-3:]
    copies, column = [], 0
    for order, own_ref, got_ref in zip(orders, pieces[::2], pieces[1::2]):
        held, share, width = own_ref.shape
        for i, mask in enumerate(order):
            piece = own_ref.at[i] if i < held else got_ref.at[i - held]
            row = pl.multiple_of((place_ref[0] ^ mask) * share, TAIL)
            there = weight.at[pl.ds(row, share), pl.ds(column, width)]
            copies.append(pltpu.make_async_copy(piece, there, sems.at[len(copies)]))
        column += width
    for copy in copies:
        copy.start()
    for copy in copies:
        copy.wait()
    count, chunk, cols = x_ref.shape
    total = None
    for k in range(count):
        rows = weight[k * cols : (k + 1) * cols, :]
        term = jnp.dot(x_ref[k], rows, preferred_element_type=F32)
        total = term if total is None else total + term
    out_ref[:chunk, :] = total.astype(BF16)
    sq = sq_ref[...]
    high = sq.astype(BF16).astype(F32)
    out_ref[chunk:, :] = lines_of((high, sq - high), out_ref.shape[1])


def lines_of(rows, width):
    lines = []
    for row in rows:
        for at in range(0, row.shape[1], width):
            line = row[:, at : at + width]
            if line.shape[1] < width:
                rest = jnp.zeros((1, width - line.shape[1]), F32)
                line = jnp.concatenate([line, rest], axis=1)
            lines.append(line)
    lines.append(jnp.zeros((TAIL - len(lines), width), F32))
    return jnp.concatenate(lines, axis=0).astype(BF16)


def rows_of(tail, count, length):
    per_row = -(-length // tail.shape[1])
    rows = []
    for r in range(count):
        lines = [tail[r * per_row + i : r * per_row + i + 1, :] for i in range(per_row)]
        rows.append(jnp.concatenate(lines, axis=1)[:, :length])
    return rows


def far_product(place, x, sq, gathered, after):
    orders = [g[0] for g in gathered]
    pieces = [piece for g in gathered for piece in g[1:]]
    width = sum(g[1].shape[2] for g in gathered)
    share = pieces[0].shape[1]
    count, chunk, cols = x.shape
    return pl.pallas_call(
        partial(far_kernel, orders=orders),
        out_shape=shape((chunk + TAIL, width), BF16),
        grid_spec=pltpu.PrefetchScalarGridSpec(
            num_scalar_prefetch=1,
            grid=(1,),
            in_specs=[
                pl.BlockSpec((count, chunk, cols), lambda i, p: (0, 0, 0)),
                pl.BlockSpec((1, chunk), lambda i, p: (0, 0)),
                ANY,
            ]
            + [ANY for _ in pieces],
            out_specs=pl.BlockSpec((chunk + TAIL, width), lambda i, p: (0, 0)),
            scratch_shapes=[
                pltpu.VMEM((len(orders[0]) * share, width), BF16),
                pltpu.SemaphoreType.DMA((sum(len(o) for o in orders),)),
            ],
        ),
        compiler_params=PARAMS,
        name="far",
    )(place, x, sq, after, *pieces)


def near_kernel(first_ref, x_ref, k_ref, v_ref, q_ref, after_ref, out_ref):
    x = x_ref[0]

    @pl.when(pl.program_id(0) == 0)
    def _():
        out_ref[...] = jnp.zeros_like(out_ref)

    column = 0
    for ref in (k_ref, v_ref, q_ref):
        at = slice(column, column + ref.shape[1])
        out_ref[:, at] += jnp.dot(x, ref[...], preferred_element_type=F32)
        column += ref.shape[1]


def near_product(first, x, weights, after):
    count, chunk, cols = x.shape
    widths = [w.shape[1] for w in weights]
    return pl.pallas_call(
        near_kernel,
        out_shape=shape((chunk, sum(widths)), F32),
        grid_spec=pltpu.PrefetchScalarGridSpec(
            num_scalar_prefetch=1,
            grid=(count,),
            in_specs=[pl.BlockSpec((1, chunk, cols), lambda i, s: (i, 0, 0))]
            + [pl.BlockSpec((cols, w), lambda i, s: (s[0] + i, 0)) for w in widths]
            + [ANY],
            out_specs=pl.BlockSpec((chunk, sum(widths)), lambda i, s: (0, 0)),
        ),
        compiler_params=PARAMS,
        name="near",
    )(first, x, *weights, after)


def keys_kernel(
    near_ref, far_ref, sq_ref, id_ref, cos_ref, sin_ref, after_ref, out_ref, sum_ref, *, model
):
    chunk, width = near_ref.shape
    tail = far_ref[chunk:, :].astype(F32)
    total = sum(rows_of(tail, 2, chunk), sq_ref[...])
    factor = to_column(lax.rsqrt(total / model + epsilon))
    sum_ref[...] = total
    for c in range(0, width, HEAD_SIZE):
        at = slice(c, c + HEAD_SIZE)
        part = (near_ref[:, at] + far_ref[:chunk, at].astype(F32)) * factor
        if c < width // 2:
            part = rotate(part, cos_ref[...], sin_ref[...])
        out_ref[:chunk, at] = part.astype(BF16)
    out_ref[chunk:, :] = lines_of((id_ref[...].astype(F32),), width)


def keys_values(near, far, sq, ids, cosine, sine, after, c, width, model):
    chunk = near.shape[0]
    whole = lambda i: (0, 0)
    return pl.pallas_call(
        partial(keys_kernel, model=model),
        out_shape=(shape((chunk + TAIL, width), BF16), shape((1, chunk), F32)),
        grid=(1,),
        in_specs=[
            pl.BlockSpec((chunk, width), whole),
            pl.BlockSpec(far.shape, whole),
            pl.BlockSpec((1, chunk), whole),
            pl.BlockSpec((1, chunk), lambda i: (0, c)),
            pl.BlockSpec((chunk, HEAD_SIZE), lambda i: (c, 0)),
            pl.BlockSpec((chunk, HEAD_SIZE), lambda i: (c, 0)),
            ANY,
        ],
        out_specs=[pl.BlockSpec((chunk + TAIL, width), whole), pl.BlockSpec((1, chunk), whole)],
        compiler_params=PARAMS,
        name="keys",
    )(near, far, sq, ids, cosine, sine, after)


def attention_kernel(
    seq_ref, near_ref, far_ref, sum_ref, cos_ref, sin_ref, id_ref, after_ref, *rest, back, offset, model
):
    kv_refs, (out_ref, k_scr, vt_scr, id_scr) = rest[:-4], rest[-4:]
    part_rows = kv_refs[0].shape[0] - TAIL
    group = near_ref.shape[1] // HEAD_SIZE
    tile = pl.program_id(0)

    @pl.when(tile == 0)
    def _():
        for b, kv_ref in enumerate(kv_refs):
            at = slice(b * part_rows, (b + 1) * part_rows)
            k_scr[at, :] = kv_ref[:part_rows, :HEAD_SIZE]
            vt_scr[:, at] = kv_ref[:part_rows, HEAD_SIZE:].astype(F32).T.astype(BF16)
            (ids,) = rows_of(kv_ref[part_rows:, :].astype(F32), 1, part_rows)
            exists = b // CHUNKS >= back - seq_ref[0]
            id_scr[at, :] = to_column(jnp.where(exists, ids, -1.0))

    scale = query_scale * math.log2(math.e)
    factor = to_column(lax.rsqrt(sum_ref[...] / model + epsilon) * scale)
    heads = []
    for c in range(0, group * HEAD_SIZE, HEAD_SIZE):
        at = slice(c, c + HEAD_SIZE)
        part = (near_ref[:, at] + far_ref[:, at].astype(F32)) * factor
        heads.append(rotate(part, cos_ref[...], sin_ref[...]).astype(BF16))
    q2 = jnp.concatenate(heads, axis=0)
    width = group * Q_TILE

    before = (id_scr[...] < id_ref[...].astype(F32)).astype(F32)
    start = jnp.sum(before, axis=0, keepdims=True).astype(jnp.int32)
    low = jnp.min(start) // K_TILE
    start = jnp.concatenate([start] * group, axis=1)
    first = back * part_rows * CHUNKS + offset + tile * Q_TILE
    place = first + lax.broadcasted_iota(jnp.int32, (1, Q_TILE), 1)
    place = jnp.concatenate([place] * group, axis=1)

    def score(j):
        base = pl.multiple_of(j * K_TILE, K_TILE)
        return lax.dot_general(
            k_scr[pl.ds(base, K_TILE), :],
            q2,
            (((1,), (1,)), ((), ())),
            preferred_element_type=F32,
        )

    stop = (first + Q_TILE + K_TILE - 1) // K_TILE

    def step(j, state):
        scores, run_max, run_sum, acc = state
        following = score(jnp.minimum(j + 1, stop - 1))
        base = pl.multiple_of(j * K_TILE, K_TILE)
        key_pos = base + lax.broadcasted_iota(jnp.int32, (K_TILE, width), 0)
        allowed = (key_pos >= start) & (key_pos <= place)
        scores = jnp.where(allowed, scores, NEG)
        new_max = jnp.maximum(run_max, jnp.max(scores, axis=0, keepdims=True))
        expo = jnp.exp2(scores - new_max)
        factor = jnp.exp2(run_max - new_max)
        run_sum = run_sum * factor + jnp.sum(expo, axis=0, keepdims=True)
        acc = acc * factor + jnp.dot(
            vt_scr[:, pl.ds(base, K_TILE)], expo.astype(BF16), preferred_element_type=F32
        )
        return following, new_max, run_sum, acc

    state = (
        score(low),
        jnp.full((1, width), NEG, F32),
        jnp.zeros((1, width), F32),
        jnp.zeros((HEAD_SIZE, width), F32),
    )
    _, _, run_sum, acc = lax.fori_loop(low, stop, step, state)
    context = (acc / run_sum).T
    for g in range(group):
        out_ref[:, g * HEAD_SIZE : (g + 1) * HEAD_SIZE] = context[
            g * Q_TILE : (g + 1) * Q_TILE
        ].astype(BF16)


def attend(seq, near, far, sums, cosine, sine, ids, after, blocks, c, width, model):
    rows = near.shape[0]
    part_rows = blocks[0].shape[0] - TAIL
    back = len(blocks) // CHUNKS - 1
    tiles = rows // Q_TILE
    keys = len(blocks) * part_rows
    last = near.shape[1] // width - 1
    return pl.pallas_call(
        partial(attention_kernel, back=back, offset=c * rows, model=model),
        out_shape=shape((rows, width), BF16),
        grid_spec=pltpu.PrefetchScalarGridSpec(
            num_scalar_prefetch=1,
            grid=(tiles,),
            in_specs=[
                pl.BlockSpec((Q_TILE, width), lambda i, s: (i, last)),
                pl.BlockSpec((Q_TILE, width), lambda i, s: (i, last)),
                pl.BlockSpec((1, Q_TILE), lambda i, s: (0, i)),
                pl.BlockSpec((Q_TILE, HEAD_SIZE), lambda i, s: (c * tiles + i, 0)),
                pl.BlockSpec((Q_TILE, HEAD_SIZE), lambda i, s: (c * tiles + i, 0)),
                pl.BlockSpec((1, Q_TILE), lambda i, s: (0, c * tiles + i)),
                ANY,
            ]
            + [pl.BlockSpec(b.shape, lambda i, s: (0, 0)) for b in blocks],
            out_specs=pl.BlockSpec((Q_TILE, width), lambda i, s: (i, 0)),
            scratch_shapes=[
                pltpu.VMEM((keys, HEAD_SIZE), BF16),
                pltpu.VMEM((HEAD_SIZE, keys), BF16),
                pltpu.VMEM((keys, LANES), F32),
            ],
        ),
        compiler_params=PARAMS,
        name="attend",
    )(seq, near, far, sums, cosine, sine, ids, after, *blocks)


def output_kernel(z_ref, own_o_ref, o_ref, ctx_ref, after_ref, out_ref, sq_ref, acc):
    step = pl.program_id(0)
    plane, others, share, tile = o_ref.shape
    z = z_ref[0]
    total = jnp.dot(ctx_ref[z], own_o_ref[...], preferred_element_type=F32)
    for k in range(1, others + 1):
        source = lax.rem(z + others + 1 - k, others + 1)
        weight = o_ref[:, k - 1].reshape(plane * share, tile)
        total = total + jnp.dot(ctx_ref[source], weight, preferred_element_type=F32)
    out_ref[...] = total
    squares = jnp.sum(total * total, axis=1, keepdims=True)
    squares = jnp.broadcast_to(squares, acc.shape)

    @pl.when(step == 0)
    def _():
        acc[...] = squares

    @pl.when(step > 0)
    def _():
        acc[...] += squares

    @pl.when(step == pl.num_programs(0) - 1)
    def _():
        sq_ref[...] = acc[...].T[0:1, :]


def output_product(z, o_weight, gathered, contexts, after):
    _, chunk, width = contexts.shape
    plane, others, share, cols = gathered.shape
    tiles = 3 if cols % (3 * LANES) == 0 else 1
    tile = cols // tiles
    column = z
    if cols % LANES:
        o_weight = lax.dynamic_slice_in_dim(o_weight, z[0] * cols, cols, axis=1)
        column = z * 0
    return pl.pallas_call(
        output_kernel,
        out_shape=(shape((chunk, cols), F32), shape((1, chunk), F32)),
        grid_spec=pltpu.PrefetchScalarGridSpec(
            num_scalar_prefetch=1,
            grid=(tiles,),
            in_specs=[
                pl.BlockSpec((width, tile), lambda i, z: (0, z[1] * tiles + i)),
                pl.BlockSpec((plane, others, share, tile), lambda i, z: (0, 0, 0, i)),
                pl.BlockSpec(contexts.shape, lambda i, z: (0, 0, 0)),
                ANY,
            ],
            out_specs=[
                pl.BlockSpec((chunk, tile), lambda i, z: (0, i)),
                pl.BlockSpec((1, chunk), lambda i, z: (0, 0)),
            ],
            scratch_shapes=[pltpu.VMEM((chunk, LANES), F32)],
        ),
        compiler_params=PARAMS,
        name="output",
    )(jnp.concatenate([z, column]), o_weight, gathered, contexts, after)


def final_kernel(token_ref, branch_ref, gain_ref, *rest, model, others):
    sq_refs, out_ref = rest[:others], rest[-1]
    total = sq_refs[0][...]
    for sq_ref in sq_refs[1:]:
        total = total + sq_ref[...]
    factor = to_column(lax.rsqrt(total / model + epsilon))[:, 0:1]
    out = token_ref[...].astype(F32) + branch_ref[...] * factor * gain_ref[...]
    out_ref[...] = out.astype(BF16)


def finish(tokens, branch, out_gain, sums, previous, c, model):
    chunk, cols = branch.shape
    tiles = chunk // Q_TILE
    in_specs = [
        pl.BlockSpec((Q_TILE, cols), lambda i: (c * tiles + i, 0)),
        pl.BlockSpec((Q_TILE, cols), lambda i: (i, 0)),
        pl.BlockSpec((1, cols), lambda i: (0, 0)),
    ]
    in_specs += [pl.BlockSpec((1, Q_TILE), lambda i: (0, i)) for _ in sums]
    args = [tokens, branch, out_gain, *sums]
    aliases = {}
    if previous is not None:
        aliases = {len(args): 0}
        in_specs.append(ANY)
        args.append(previous)
    return pl.pallas_call(
        partial(final_kernel, model=model, others=len(sums)),
        out_shape=shape(tokens.shape, BF16),
        grid=(tiles,),
        in_specs=in_specs,
        out_specs=pl.BlockSpec((Q_TILE, cols), lambda i: (c * tiles + i, 0)),
        input_output_aliases=aliases,
        compiler_params=PARAMS,
        name="finish",
    )(*args)


def per_device(
    tokens, seg_ids, in_gain, q_weight, k_weight, value_weight, o_weight, out_gain, *, sizes
):
    rows, cols = tokens.shape
    model = in_gain.shape[0]
    nz, nseq = sizes["tensor"], sizes["seq"]
    plane = nseq * sizes["groups"]
    z = lax.axis_index("tensor")
    seq = lax.axis_index("seq")
    in_plane = lax.axis_index(PLANE)
    half = nz // 2
    side = z // half
    half_rows = half * cols

    swap = [(i, (i + half) % nz) for i in range(nz)]
    turn = lambda k: [(i, (i + k) % nz) for i in range(nz)]
    seq_bits = [1 << b for b in range(1, nseq.bit_length() - 1)]
    group_bits = [nseq << b for b in range(sizes["groups"].bit_length() - 1)]

    share = half_rows // plane
    at = jnp.reshape((1 - side) * plane + in_plane, (1,))
    packed_kv, packed_q = pack(at, q_weight, k_weight, value_weight, share)
    far_kv = lax.ppermute(packed_kv, "tensor", swap)
    far_q = lax.ppermute(packed_q, "tensor", swap)
    far_kv = spread(far_kv, plane, seq_bits + group_bits + [1])
    far_q = spread(far_q, plane, group_bits + seq_bits + [1])

    chunk = rows // CHUNKS
    halves = [list(range(h, h + half)) for h in (0, half)]
    x_chunks = [
        lax.all_gather(tokens[c * chunk : (c + 1) * chunk], "tensor", axis_index_groups=halves)
        for c in range(CHUNKS)
    ]
    first = jnp.reshape(side * half, (1,))
    gains = in_gain.reshape(nz, 1, cols)

    cosine, sine = rotation_table(seq * rows + jnp.arange(rows, dtype=jnp.int32))
    ids = seg_ids[None, :]
    weights = (k_weight, value_weight, q_weight)
    kv_width = k_weight.shape[1] + value_weight.shape[1]
    place = jnp.reshape(in_plane, (1,))
    prepared, sent = [], []
    for c in range(CHUNKS):
        prepared.append(prep(first, gains, x_chunks[c]))
        after = sent[-1] if sent else place
        sent.append(far_product(place, *prepared[c], [far_kv, far_q], after))
    o_share = o_weight.shape[0] // plane
    last = sent[-1][0, 0]
    wait = (last != last).astype(jnp.int32)
    moved = []
    for k in range(1, nz):
        target = (z + k) % nz
        piece = lax.dynamic_slice(
            o_weight, (in_plane * o_share + wait, target * cols), (o_share, cols)
        )
        moved.append(lax.ppermute(piece, "tensor", turn(k)))
    moved = jnp.stack(moved)
    gathered_o = lax.all_gather(moved, PLANE)

    kv_parts, q_parts = [], []
    for c in range(CHUNKS):
        x, sq = prepared[c]
        got = lax.ppermute(sent[c], "tensor", swap)
        near = near_product(first, x, weights, sent[-1])
        after = kv_parts[-1] if kv_parts else moved
        own_kv, sums = keys_values(
            near, got, sq, ids, cosine, sine, after, c, kv_width, model
        )
        kv_parts.append(own_kv)
        q_parts.append((near, got, sums))

    back = -(-(nseq * rows // 2 - 1) // rows)
    blocks = list(kv_parts)
    for k in range(1, back + 1):
        earlier = [(i, i + k) for i in range(nseq - k)]
        blocks = [lax.ppermute(part, "seq", earlier) for part in kv_parts] + blocks

    out = None
    z_at = jnp.reshape(z, (1,))
    seq_at = jnp.reshape(seq, (1,))
    q_width = q_weight.shape[1]
    context, own_sq = place, place
    for c in range(CHUNKS):
        context = attend(
            seq_at, *q_parts[c], cosine, sine, ids, context, blocks, c, q_width, model
        )
        contexts = lax.all_gather(context, "tensor")
        branch, own_sq = output_product(z_at, o_weight, gathered_o, contexts, own_sq)
        sums = [own_sq]
        sums += [lax.ppermute(own_sq, "tensor", turn(k)) for k in range(1, nz)]
        out = finish(tokens, branch, out_gain[None, :], sums, out, c, model)
    return out


def solution(mesh):
    return jax.shard_map(
        partial(per_device, sizes=dict(mesh.shape)),
        mesh=mesh,
        in_specs=(
            P(("groups", "seq"), "tensor"),
            P(("groups", "seq")),
            P(),
            P(None, "tensor"),
            P(None, "tensor"),
            P(None, "tensor"),
            P("tensor", None),
            P("tensor"),
        ),
        out_specs=P(("groups", "seq"), "tensor"),
        check_vma=False,
    )
```

```python
import math
from functools import partial

import jax
import jax.numpy as jnp
from jax import lax
from jax.experimental import pallas as pl
from jax.experimental.pallas import tpu as pltpu
from jax.sharding import PartitionSpec as P

HEAD_SIZE = 128
PLANE = ("groups", "seq")

epsilon = 1e-06
query_scale = 144.0 ** (-0.5)
rope_base = 10000.0
NEG = -1e30
Q_TILE = 128
K_TILE = 256
CHUNKS = 2
LANES = 128
TAIL = 16
F32, BF16 = jnp.float32, jnp.bfloat16
ANY = pl.BlockSpec(memory_space=pl.ANY)
HBM = pl.BlockSpec(memory_space=pltpu.HBM)
PARAMS = pltpu.CompilerParams(vmem_limit_bytes=40 * 1024 * 1024)
ALL_VMEM = pltpu.CompilerParams(vmem_limit_bytes=62 * 1024 * 1024)


def shape(dims, dtype):
    return jax.ShapeDtypeStruct(dims, dtype)


def to_row(column):
    return jnp.broadcast_to(column, (column.shape[0], LANES)).T[0:1, :]


def to_column(row):
    return jnp.broadcast_to(row, (LANES, row.shape[1])).T


def rotation_table(token_places):
    half_dim = HEAD_SIZE // 2
    inverse = rope_base ** (-jnp.arange(half_dim, dtype=F32) / half_dim)
    angles = token_places.astype(F32)[:, None] * inverse[None, :]
    cosine, sine = jnp.cos(angles), jnp.sin(angles)
    return jnp.concatenate([cosine, cosine], 1), jnp.concatenate([-sine, sine], 1)


def rotate(vectors, cosine, sine):
    return vectors * cosine + pltpu.roll(vectors, HEAD_SIZE // 2, 1) * sine


def pack_kernel(at_ref, q_ref, k_ref, v_ref, kv_out, q_out, sems):
    share, width = q_out.shape[0], k_ref.shape[1]
    rows = pl.ds(pl.multiple_of(at_ref[0] * share, TAIL), share)
    copies = [
        pltpu.make_async_copy(k_ref.at[rows], kv_out.at[:, pl.ds(0, width)], sems.at[0]),
        pltpu.make_async_copy(v_ref.at[rows], kv_out.at[:, pl.ds(width, width)], sems.at[1]),
        pltpu.make_async_copy(q_ref.at[rows], q_out, sems.at[2]),
    ]
    for copy in copies:
        copy.start()
    for copy in copies:
        copy.wait()


def pack(at, q_weight, k_weight, v_weight, share):
    kv_width = k_weight.shape[1] + v_weight.shape[1]
    return pl.pallas_call(
        pack_kernel,
        out_shape=(shape((share, kv_width), BF16), shape((share, q_weight.shape[1]), BF16)),
        grid_spec=pltpu.PrefetchScalarGridSpec(
            num_scalar_prefetch=1,
            grid=(1,),
            in_specs=[HBM, HBM, HBM],
            out_specs=[
                pl.BlockSpec((share, kv_width), lambda i, at: (0, 0)),
                pl.BlockSpec((share, q_weight.shape[1]), lambda i, at: (0, 0)),
            ],
            scratch_shapes=[pltpu.SemaphoreType.DMA((3,))],
        ),
        compiler_params=ALL_VMEM,
        name="pack",
    )(at, q_weight, k_weight, v_weight)


def join_kernel(first_ref, second_ref, out_ref, sems):
    held = first_ref.shape[0]
    copies = [
        pltpu.make_async_copy(first_ref, out_ref.at[pl.ds(0, held)], sems.at[0]),
        pltpu.make_async_copy(second_ref, out_ref.at[pl.ds(held, held)], sems.at[1]),
    ]
    for copy in copies:
        copy.start()
    for copy in copies:
        copy.wait()


def join(first, second):
    return pl.pallas_call(
        join_kernel,
        out_shape=shape((2 * first.shape[0],) + first.shape[1:], first.dtype),
        in_specs=[ANY, ANY],
        scratch_shapes=[pltpu.SemaphoreType.DMA((2,))],
        compiler_params=PARAMS,
        name="join",
    )(first, second)


def spread(piece, plane, masks):
    own = piece[None]
    order = [0]
    for mask in masks:
        got = lax.ppermute(own, PLANE, [(i, i ^ mask) for i in range(plane)])
        order = order + [k ^ mask for k in order]
        if mask != masks[-1]:
            own = join(own, got)
    return order, own, got


def prep_kernel(src_ref, gain_ref, *rest):
    x_refs, (out_ref, sq_ref) = rest[:-2], rest[-2:]
    for k, x_ref in enumerate(x_refs):
        x = x_ref[...].astype(F32)
        squares = jnp.sum(x * x, axis=1, keepdims=True)
        total = squares if k == 0 else total + squares
        out_ref[k] = (x * gain_ref[src_ref[k]]).astype(BF16)
    sq_ref[...] = to_row(total)


def prep(sources, gains, blocks):
    rows, cols = blocks[0].shape
    dims = (len(blocks), rows, cols)
    return pl.pallas_call(
        prep_kernel,
        out_shape=(shape(dims, BF16), shape((1, rows), F32)),
        grid_spec=pltpu.PrefetchScalarGridSpec(
            num_scalar_prefetch=1,
            grid=(1,),
            in_specs=[pl.BlockSpec(gains.shape, lambda i, s: (0, 0, 0))]
            + [pl.BlockSpec((rows, cols), lambda i, s: (0, 0)) for _ in blocks],
            out_specs=[
                pl.BlockSpec(dims, lambda i, s: (0, 0, 0)),
                pl.BlockSpec((1, rows), lambda i, s: (0, 0)),
            ],
        ),
        compiler_params=PARAMS,
        name="prep",
    )(sources, gains, *blocks)


def far_kernel(place_ref, src_ref, x_ref, sq_ref, own_ref, got_ref, *rest, order, with_sq):
    out_ref, weight, sems = rest[-3:]
    held, share, width = own_ref.shape
    copies = []
    for i, mask in enumerate(order):
        piece = own_ref.at[i] if i < held else got_ref.at[i - held]
        row = pl.multiple_of((place_ref[0] ^ mask) * share, TAIL)
        there = weight.at[pl.ds(row, share)]
        copies.append(pltpu.make_async_copy(piece, there, sems.at[i]))
    for copy in copies:
        copy.start()
    for copy in copies:
        copy.wait()
    count, rows, cols = x_ref.shape
    total = None
    for k in range(count):
        row = pl.multiple_of(src_ref[k] * cols, TAIL)
        term = jnp.dot(x_ref[k], weight[pl.ds(row, cols), :], preferred_element_type=F32)
        total = term if total is None else total + term
    out_ref[:rows, :] = total.astype(BF16)
    if with_sq:
        sq = sq_ref[...]
        high = sq.astype(BF16).astype(F32)
        out_ref[rows:, :] = lines_of((high, sq - high), width)


def lines_of(rows, width):
    lines = []
    for row in rows:
        for at in range(0, row.shape[1], width):
            line = row[:, at : at + width]
            if line.shape[1] < width:
                rest = jnp.zeros((1, width - line.shape[1]), F32)
                line = jnp.concatenate([line, rest], axis=1)
            lines.append(line)
    lines.append(jnp.zeros((TAIL - len(lines), width), F32))
    return jnp.concatenate(lines, axis=0).astype(BF16)


def rows_of(tail, count, length):
    per_row = -(-length // tail.shape[1])
    rows = []
    for r in range(count):
        lines = [tail[r * per_row + i : r * per_row + i + 1, :] for i in range(per_row)]
        rows.append(jnp.concatenate(lines, axis=1)[:, :length])
    return rows


def far_product(place, sources, x, sq, gathered, with_sq, after):
    order, own, got = gathered
    _, share, width = own.shape
    rows = x.shape[1]
    out_rows = rows + (TAIL if with_sq else 0)
    return pl.pallas_call(
        partial(far_kernel, order=order, with_sq=with_sq),
        out_shape=shape((out_rows, width), BF16),
        grid_spec=pltpu.PrefetchScalarGridSpec(
            num_scalar_prefetch=2,
            grid=(1,),
            in_specs=[
                pl.BlockSpec(x.shape, lambda i, p, s: (0, 0, 0)),
                pl.BlockSpec((1, rows), lambda i, p, s: (0, 0)),
                ANY,
                ANY,
            ]
            + [ANY for _ in after],
            out_specs=pl.BlockSpec((out_rows, width), lambda i, p, s: (0, 0)),
            scratch_shapes=[
                pltpu.VMEM((len(order) * share, width), BF16),
                pltpu.SemaphoreType.DMA((len(order),)),
            ],
        ),
        compiler_params=PARAMS,
        name="far",
    )(place, sources, x, sq, own, got, *after)


def near_kernel(src_ref, x_ref, k_ref, v_ref, q_ref, after_ref, out_ref):
    x = x_ref[0]

    @pl.when(pl.program_id(0) == 0)
    def _():
        out_ref[...] = jnp.zeros_like(out_ref)

    column = 0
    for ref in (k_ref, v_ref, q_ref):
        at = slice(column, column + ref.shape[1])
        out_ref[:, at] += jnp.dot(x, ref[...], preferred_element_type=F32)
        column += ref.shape[1]


def near_product(sources, x, weights, after):
    count, chunk, cols = x.shape
    widths = [w.shape[1] for w in weights]
    return pl.pallas_call(
        near_kernel,
        out_shape=shape((chunk, sum(widths)), F32),
        grid_spec=pltpu.PrefetchScalarGridSpec(
            num_scalar_prefetch=1,
            grid=(count,),
            in_specs=[pl.BlockSpec((1, chunk, cols), lambda i, s: (i, 0, 0))]
            + [pl.BlockSpec((cols, w), lambda i, s: (s[i], 0)) for w in widths]
            + [ANY],
            out_specs=pl.BlockSpec((chunk, sum(widths)), lambda i, s: (0, 0)),
        ),
        compiler_params=PARAMS,
        name="near",
    )(sources, x, *weights, after)


def keys_kernel(
    near_ref, far_ref, sq_ref, id_ref, cos_ref, sin_ref, out_ref, sum_ref, *, model
):
    chunk, width = near_ref.shape
    tail = far_ref[chunk:, :].astype(F32)
    total = sum(rows_of(tail, 2, chunk), sq_ref[...])
    factor = to_column(lax.rsqrt(total / model + epsilon))
    sum_ref[...] = total
    for c in range(0, width, HEAD_SIZE):
        at = slice(c, c + HEAD_SIZE)
        part = (near_ref[:, at] + far_ref[:chunk, at].astype(F32)) * factor
        if c < width // 2:
            part = rotate(part, cos_ref[...], sin_ref[...])
        out_ref[:chunk, at] = part.astype(BF16)
    out_ref[chunk:, :] = lines_of((id_ref[...].astype(F32),), width)


def keys_values(near, far, sq, ids, cosine, sine, width, model):
    chunk = near.shape[0]
    whole = lambda i: (0, 0)
    return pl.pallas_call(
        partial(keys_kernel, model=model),
        out_shape=(shape((chunk + TAIL, width), BF16), shape((1, chunk), F32)),
        grid=(1,),
        in_specs=[
            pl.BlockSpec((chunk, width), whole),
            pl.BlockSpec(far.shape, whole),
            pl.BlockSpec((1, chunk), whole),
            pl.BlockSpec((1, chunk), whole),
            pl.BlockSpec((chunk, HEAD_SIZE), whole),
            pl.BlockSpec((chunk, HEAD_SIZE), whole),
        ],
        out_specs=[pl.BlockSpec((chunk + TAIL, width), whole), pl.BlockSpec((1, chunk), whole)],
        compiler_params=PARAMS,
        name="keys",
    )(near, far, sq, ids, cosine, sine)


def attention_kernel(
    seq_ref, near_ref, far_ref, sum_ref, cos_ref, sin_ref, id_ref, after_ref, *rest, back, offset, model
):
    kv_refs, (out_ref, k_scr, vt_scr, id_scr) = rest[:-4], rest[-4:]
    part_rows = kv_refs[0].shape[0] - TAIL
    group = near_ref.shape[1] // HEAD_SIZE
    tile = pl.program_id(0)

    @pl.when(tile == 0)
    def _():
        for b, kv_ref in enumerate(kv_refs):
            at = slice(b * part_rows, (b + 1) * part_rows)
            k_scr[at, :] = kv_ref[:part_rows, :HEAD_SIZE]
            vt_scr[:, at] = kv_ref[:part_rows, HEAD_SIZE:].astype(F32).T.astype(BF16)
            (ids,) = rows_of(kv_ref[part_rows:, :].astype(F32), 1, part_rows)
            exists = b >= back - seq_ref[0]
            id_scr[at, :] = to_column(jnp.where(exists, ids, -1.0))

    scale = query_scale * math.log2(math.e)
    factor = to_column(lax.rsqrt(sum_ref[...] / model + epsilon) * scale)
    heads = []
    for c in range(0, group * HEAD_SIZE, HEAD_SIZE):
        at = slice(c, c + HEAD_SIZE)
        part = (near_ref[:, at] + far_ref[:, at].astype(F32)) * factor
        heads.append(rotate(part, cos_ref[...], sin_ref[...]).astype(BF16))
    q2 = jnp.concatenate(heads, axis=0)
    width = group * Q_TILE

    before = (id_scr[...] < id_ref[...].astype(F32)).astype(F32)
    start = jnp.sum(before, axis=0, keepdims=True).astype(jnp.int32)
    low = jnp.min(start) // K_TILE
    start = jnp.concatenate([start] * group, axis=1)
    first = back * part_rows + offset + tile * Q_TILE
    place = first + lax.broadcasted_iota(jnp.int32, (1, Q_TILE), 1)
    place = jnp.concatenate([place] * group, axis=1)

    def score(j):
        base = pl.multiple_of(j * K_TILE, K_TILE)
        return lax.dot_general(
            k_scr[pl.ds(base, K_TILE), :],
            q2,
            (((1,), (1,)), ((), ())),
            preferred_element_type=F32,
        )

    stop = (first + Q_TILE + K_TILE - 1) // K_TILE

    def step(j, state):
        scores, run_max, run_sum, acc = state
        following = score(jnp.minimum(j + 1, stop - 1))
        base = pl.multiple_of(j * K_TILE, K_TILE)
        key_pos = base + lax.broadcasted_iota(jnp.int32, (K_TILE, width), 0)
        allowed = (key_pos >= start) & (key_pos <= place)
        scores = jnp.where(allowed, scores, NEG)
        new_max = jnp.maximum(run_max, jnp.max(scores, axis=0, keepdims=True))
        expo = jnp.exp2(scores - new_max)
        factor = jnp.exp2(run_max - new_max)
        run_sum = run_sum * factor + jnp.sum(expo, axis=0, keepdims=True)
        acc = acc * factor + jnp.dot(
            vt_scr[:, pl.ds(base, K_TILE)], expo.astype(BF16), preferred_element_type=F32
        )
        return following, new_max, run_sum, acc

    state = (
        score(low),
        jnp.full((1, width), NEG, F32),
        jnp.zeros((1, width), F32),
        jnp.zeros((HEAD_SIZE, width), F32),
    )
    _, _, run_sum, acc = lax.fori_loop(low, stop, step, state)
    context = (acc / run_sum).T
    for g in range(group):
        out_ref[:, g * HEAD_SIZE : (g + 1) * HEAD_SIZE] = context[
            g * Q_TILE : (g + 1) * Q_TILE
        ].astype(BF16)


def attend(seq, near, far, sums, cosine, sine, ids, after, blocks, c, model):
    rows = near.shape[0] // CHUNKS
    width = far.shape[1]
    part_rows = blocks[0].shape[0] - TAIL
    back = len(blocks) - 1
    tiles = rows // Q_TILE
    keys = len(blocks) * part_rows
    last = near.shape[1] // width - 1
    return pl.pallas_call(
        partial(attention_kernel, back=back, offset=c * rows, model=model),
        out_shape=shape((rows, width), BF16),
        grid_spec=pltpu.PrefetchScalarGridSpec(
            num_scalar_prefetch=1,
            grid=(tiles,),
            in_specs=[
                pl.BlockSpec((Q_TILE, width), lambda i, s: (c * tiles + i, last)),
                pl.BlockSpec((Q_TILE, width), lambda i, s: (c * tiles + i, 0)),
                pl.BlockSpec((1, Q_TILE), lambda i, s: (0, c * tiles + i)),
                pl.BlockSpec((Q_TILE, HEAD_SIZE), lambda i, s: (c * tiles + i, 0)),
                pl.BlockSpec((Q_TILE, HEAD_SIZE), lambda i, s: (c * tiles + i, 0)),
                pl.BlockSpec((1, Q_TILE), lambda i, s: (0, c * tiles + i)),
                ANY,
            ]
            + [pl.BlockSpec(b.shape, lambda i, s: (0, 0)) for b in blocks],
            out_specs=pl.BlockSpec((Q_TILE, width), lambda i, s: (i, 0)),
            scratch_shapes=[
                pltpu.VMEM((keys, HEAD_SIZE), BF16),
                pltpu.VMEM((HEAD_SIZE, keys), BF16),
                pltpu.VMEM((keys, LANES), F32),
            ],
        ),
        compiler_params=PARAMS,
        cost_estimate=pl.CostEstimate(
            flops=4 * rows * width * keys,
            bytes_accessed=4 * keys * width,
            transcendentals=rows * keys * width // HEAD_SIZE,
        ),
        name="attend",
    )(seq, near, far, sums, cosine, sine, ids, after, *blocks)


def output_kernel(at_ref, own_o_ref, o_ref, *rest):
    ctx_refs, (after_ref, out_ref, sq_ref, acc) = rest[:-4], rest[-4:]
    step = pl.program_id(0)
    plane, _, share, tile = o_ref.shape
    total = jnp.dot(ctx_refs[0][...], own_o_ref[...], preferred_element_type=F32)
    for i, ctx_ref in enumerate(ctx_refs[1:]):
        weight = o_ref[:, at_ref[1 + i]].reshape(plane * share, tile)
        total = total + jnp.dot(ctx_ref[...], weight, preferred_element_type=F32)
    out_ref[...] = total
    squares = jnp.sum(total * total, axis=1, keepdims=True)
    squares = jnp.broadcast_to(squares, acc.shape)

    @pl.when(step == 0)
    def _():
        acc[...] = squares

    @pl.when(step > 0)
    def _():
        acc[...] += squares

    @pl.when(step == pl.num_programs(0) - 1)
    def _():
        sq_ref[...] = acc[...].T[0:1, :]


def output_product(column, order, o_weight, gathered, contexts, after):
    chunk, width = contexts[0].shape
    plane, others, share, cols = gathered.shape
    tiles = 3 if cols % (3 * LANES) == 0 else 1
    tile = cols // tiles
    if cols % LANES:
        o_weight = lax.dynamic_slice_in_dim(o_weight, column * cols, cols, axis=1)
        column = jnp.int32(0)
    return pl.pallas_call(
        output_kernel,
        out_shape=(shape((chunk, cols), F32), shape((1, chunk), F32)),
        grid_spec=pltpu.PrefetchScalarGridSpec(
            num_scalar_prefetch=1,
            grid=(tiles,),
            in_specs=[
                pl.BlockSpec((width, tile), lambda i, at: (0, at[0] * tiles + i)),
                pl.BlockSpec((plane, others, share, tile), lambda i, at: (0, 0, 0, i)),
            ]
            + [pl.BlockSpec((chunk, width), lambda i, at: (0, 0)) for _ in contexts]
            + [ANY],
            out_specs=[
                pl.BlockSpec((chunk, tile), lambda i, at: (0, i)),
                pl.BlockSpec((1, chunk), lambda i, at: (0, 0)),
            ],
            scratch_shapes=[pltpu.VMEM((chunk, LANES), F32)],
        ),
        compiler_params=PARAMS,
        name="output",
    )(jnp.stack([column] + order), o_weight, gathered, *contexts, after)


def final_kernel(token_ref, branch_ref, gain_ref, *rest, model, others):
    sq_refs, out_ref = rest[:others], rest[-1]
    total = sq_refs[0][...]
    for sq_ref in sq_refs[1:]:
        total = total + sq_ref[...]
    factor = to_column(lax.rsqrt(total / model + epsilon))[:, 0:1]
    out = token_ref[...].astype(F32) + branch_ref[...] * factor * gain_ref[...]
    out_ref[...] = out.astype(BF16)


def finish(tokens, branch, out_gain, sums, previous, c, model):
    chunk, cols = branch.shape
    tiles = chunk // Q_TILE
    in_specs = [
        pl.BlockSpec((Q_TILE, cols), lambda i: (c * tiles + i, 0)),
        pl.BlockSpec((Q_TILE, cols), lambda i: (i, 0)),
        pl.BlockSpec((1, cols), lambda i: (0, 0)),
    ]
    in_specs += [pl.BlockSpec((1, Q_TILE), lambda i: (0, i)) for _ in sums]
    args = [tokens, branch, out_gain, *sums]
    aliases = {}
    if previous is not None:
        aliases = {len(args): 0}
        in_specs.append(ANY)
        args.append(previous)
    return pl.pallas_call(
        partial(final_kernel, model=model, others=len(sums)),
        out_shape=shape(tokens.shape, BF16),
        grid=(tiles,),
        in_specs=in_specs,
        out_specs=pl.BlockSpec((Q_TILE, cols), lambda i: (c * tiles + i, 0)),
        input_output_aliases=aliases,
        compiler_params=PARAMS,
        name="finish",
    )(*args)


def per_device(
    tokens, seg_ids, in_gain, q_weight, k_weight, value_weight, o_weight, out_gain, *, sizes
):
    rows, cols = tokens.shape
    model = in_gain.shape[0]
    nz, nseq = sizes["tensor"], sizes["seq"]
    plane = nseq * sizes["groups"]
    z = lax.axis_index("tensor")
    seq = lax.axis_index("seq")
    in_plane = lax.axis_index(PLANE)
    half = nz // 2
    side, within = z // half, z % half
    half_rows = half * cols

    ring = [(i, i // half * half + (i + 1) % half) for i in range(nz)]
    swap = [(i, (i + half) % nz) for i in range(nz)]
    turn = lambda k: [(i, (i + k) % nz) for i in range(nz)]
    seq_bits = [1 << b for b in range(1, nseq.bit_length() - 1)]
    group_bits = [nseq << b for b in range(sizes["groups"].bit_length() - 1)]

    share = half_rows // plane
    at = jnp.reshape((1 - side) * plane + in_plane, (1,))
    packed_kv, packed_q = pack(at, q_weight, k_weight, value_weight, share)
    far_kv = lax.ppermute(packed_kv, "tensor", swap)
    far_q = lax.ppermute(packed_q, "tensor", swap)
    far_kv = spread(far_kv, plane, seq_bits + group_bits + [1])
    far_q = spread(far_q, plane, group_bits + seq_bits + [1])

    sources = (within + half - jnp.arange(half, dtype=jnp.int32)) % half
    blocks = [tokens]
    for _ in range(half - 1):
        blocks.append(lax.ppermute(blocks[-1], "tensor", ring))
    gains = in_gain.reshape(nz, 1, cols)
    x, sq = prep(side * half + sources, gains, blocks)

    place = jnp.reshape(in_plane, (1,))
    sent_kv = far_product(place, sources, x, sq, far_kv, True, [])
    got_kv = lax.ppermute(sent_kv, "tensor", swap)
    weights = (k_weight, value_weight, q_weight)
    near = near_product(side * half + sources, x, weights, sent_kv)

    sent_q = far_product(place, sources, x, sq, far_q, False, [near])
    got_q = lax.ppermute(sent_q, "tensor", swap)
    cosine, sine = rotation_table(seq * rows + jnp.arange(rows, dtype=jnp.int32))
    ids = seg_ids[None, :]
    kv_width = k_weight.shape[1] + value_weight.shape[1]
    own_kv, sums = keys_values(near, got_kv, sq, ids, cosine, sine, kv_width, model)

    back = -(-(nseq * rows // 2 - 1) // rows)
    kv_blocks = [own_kv]
    for k in range(1, back + 1):
        earlier = [(i, i + k) for i in range(nseq - k)]
        kv_blocks.insert(0, lax.ppermute(own_kv, "seq", earlier))

    o_share = o_weight.shape[0] // plane
    wait = (got_kv[0, 0] != got_kv[0, 0]).astype(jnp.int32)
    moved = []
    for k in range(1, nz):
        target = (z + k) % nz
        piece = lax.dynamic_slice(
            o_weight, (in_plane * o_share + wait, target * cols), (o_share, cols)
        )
        moved.append(lax.ppermute(piece, "tensor", turn(k)))
    gathered_o = lax.all_gather(jnp.stack(moved), PLANE)

    out = None
    seq_at = jnp.reshape(seq, (1,))
    context, own_sq = place, place
    for c in range(CHUNKS):
        context = attend(
            seq_at, near, got_q, sums, cosine, sine, ids, context, kv_blocks, c, model
        )
        if nz == 4:
            pairs = [(i, i ^ 1) for i in range(nz)]
            opposite = lax.ppermute(context, "tensor", swap)
            beside = lax.ppermute(context, "tensor", pairs)
            across = lax.ppermute(opposite, "tensor", pairs)
            contexts = [context, opposite, beside, across]
            order = [jnp.int32(1), 2 - 2 * (z % 2), 2 * (z % 2)]
        else:
            contexts = [context]
            contexts += [lax.ppermute(context, "tensor", turn(k)) for k in range(1, nz)]
            order = [jnp.int32(k) for k in range(nz - 1)]
        branch, own_sq = output_product(z, order, o_weight, gathered_o, contexts, own_sq)
        squares = [own_sq]
        squares += [lax.ppermute(own_sq, "tensor", turn(k)) for k in range(1, nz)]
        out = finish(tokens, branch, out_gain[None, :], squares, out, c, model)
    return out


def solution(mesh):
    return jax.shard_map(
        partial(per_device, sizes=dict(mesh.shape)),
        mesh=mesh,
        in_specs=(
            P(("groups", "seq"), "tensor"),
            P(("groups", "seq")),
            P(),
            P(None, "tensor"),
            P(None, "tensor"),
            P(None, "tensor"),
            P("tensor", None),
            P("tensor"),
        ),
        out_specs=P(("groups", "seq"), "tensor"),
        check_vma=False,
    )
```

```python
import math
from functools import partial

import jax
import jax.numpy as jnp
from jax import lax
from jax.experimental import pallas as pl
from jax.experimental.pallas import tpu as pltpu
from jax.sharding import PartitionSpec as P

HEAD_SIZE = 128
PLANE = ("groups", "seq")

epsilon = 1e-06
query_scale = 144.0 ** (-0.5)
rope_base = 10000.0
NEG = -1e30
Q_TILE = 128
K_TILE = 256
CHUNKS = 2
LANES = 128
TAIL = 16
F32, BF16 = jnp.float32, jnp.bfloat16
ANY = pl.BlockSpec(memory_space=pl.ANY)
HBM = pl.BlockSpec(memory_space=pltpu.HBM)
PARAMS = pltpu.CompilerParams(vmem_limit_bytes=40 * 1024 * 1024)
ALL_VMEM = pltpu.CompilerParams(vmem_limit_bytes=62 * 1024 * 1024)


def shape(dims, dtype):
    return jax.ShapeDtypeStruct(dims, dtype)


def to_row(column):
    return jnp.broadcast_to(column, (column.shape[0], LANES)).T[0:1, :]


def to_column(row):
    return jnp.broadcast_to(row, (LANES, row.shape[1])).T


def rotation_table(token_places):
    half_dim = HEAD_SIZE // 2
    inverse = rope_base ** (-jnp.arange(half_dim, dtype=F32) / half_dim)
    angles = token_places.astype(F32)[:, None] * inverse[None, :]
    cosine, sine = jnp.cos(angles), jnp.sin(angles)
    return jnp.concatenate([cosine, cosine], 1), jnp.concatenate([-sine, sine], 1)


def rotate(vectors, cosine, sine):
    return vectors * cosine + pltpu.roll(vectors, HEAD_SIZE // 2, 1) * sine


def pack_kernel(at_ref, q_ref, k_ref, v_ref, x_ref, kv_out, q_out, x_out, sems):
    share, width = q_out.shape[0], k_ref.shape[1]
    rows = pl.ds(pl.multiple_of(at_ref[0] * share, TAIL), share)
    copies = [
        pltpu.make_async_copy(k_ref.at[rows], kv_out.at[:, pl.ds(0, width)], sems.at[0]),
        pltpu.make_async_copy(v_ref.at[rows], kv_out.at[:, pl.ds(width, width)], sems.at[1]),
        pltpu.make_async_copy(q_ref.at[rows], q_out, sems.at[2]),
        pltpu.make_async_copy(x_ref.at[pl.ds(0, x_out.shape[0])], x_out, sems.at[3]),
    ]
    for copy in copies:
        copy.start()
    for copy in copies:
        copy.wait()


def pack(at, q_weight, k_weight, v_weight, share, tokens, rows):
    kv_width = k_weight.shape[1] + v_weight.shape[1]
    dims = [(share, kv_width), (share, q_weight.shape[1]), (rows, tokens.shape[1])]
    return pl.pallas_call(
        pack_kernel,
        out_shape=tuple(shape(d, BF16) for d in dims),
        grid_spec=pltpu.PrefetchScalarGridSpec(
            num_scalar_prefetch=1,
            grid=(1,),
            in_specs=[HBM, HBM, HBM, HBM],
            out_specs=[pl.BlockSpec(d, lambda i, at: (0, 0)) for d in dims],
            scratch_shapes=[pltpu.SemaphoreType.DMA((4,))],
        ),
        compiler_params=ALL_VMEM,
        name="pack",
    )(at, q_weight, k_weight, v_weight, tokens)


def stage_kernel(*refs, pairs, first, count):
    outputs = pairs + (1 if count else 0)
    ins, outs, sems = refs[: -outputs - 1], refs[-outputs - 1 : -1], refs[-1]
    copies = []
    for p in range(pairs):
        held = ins[2 * p].shape[0]
        for side in range(2):
            there = outs[p].at[pl.ds(side * held, held)]
            copies.append(
                pltpu.make_async_copy(ins[2 * p + side], there, sems.at[len(copies)])
            )
    if count:
        rows = ins[2 * pairs].at[pl.ds(first, count)]
        copies.append(pltpu.make_async_copy(rows, outs[-1], sems.at[len(copies)]))
    for copy in copies:
        copy.start()
    for copy in copies:
        copy.wait()


def stage(joined, tokens, first, count, after):
    dims = [(2 * pair[0].shape[0],) + pair[0].shape[1:] for pair in joined]
    if count:
        dims.append((count, tokens.shape[1]))
    return pl.pallas_call(
        partial(stage_kernel, pairs=len(joined), first=first, count=count),
        out_shape=tuple(shape(d, BF16) for d in dims),
        in_specs=[ANY] * (2 * len(joined) + 1 + len(after)),
        scratch_shapes=[pltpu.SemaphoreType.DMA((2 * len(joined) + 1,))],
        compiler_params=PARAMS,
        name="stage",
    )(*[piece for pair in joined for piece in pair], tokens, *after)


def prep_kernel(src_ref, gain_ref, *rest, cuts):
    x_refs, (out_ref, sq_ref) = rest[:-2], rest[-2:]
    squares, at = [], 0
    for k, pieces in enumerate(cuts):
        column, row = [], 0
        for x_ref in x_refs[at : at + pieces]:
            x = x_ref[...].astype(F32)
            column.append(jnp.sum(x * x, axis=1, keepdims=True))
            out_ref[k, row : row + x.shape[0]] = (x * gain_ref[src_ref[k]]).astype(BF16)
            row += x.shape[0]
        squares.append(jnp.concatenate(column, axis=0))
        at += pieces
    sq_ref[...] = to_row(sum(squares[1:], squares[0]))


def prep(sources, gains, blocks):
    rows, cols = blocks[0][0].shape
    dims = (len(blocks), rows, cols)
    pieces = [piece for block in blocks for piece in block]
    return pl.pallas_call(
        partial(prep_kernel, cuts=[len(block) for block in blocks]),
        out_shape=(shape(dims, BF16), shape((1, rows), F32)),
        grid_spec=pltpu.PrefetchScalarGridSpec(
            num_scalar_prefetch=1,
            grid=(1,),
            in_specs=[pl.BlockSpec(gains.shape, lambda i, s: (0, 0, 0))]
            + [pl.BlockSpec(piece.shape, lambda i, s: (0, 0)) for piece in pieces],
            out_specs=[
                pl.BlockSpec(dims, lambda i, s: (0, 0, 0)),
                pl.BlockSpec((1, rows), lambda i, s: (0, 0)),
            ],
        ),
        compiler_params=PARAMS,
        name="prep",
    )(sources, gains, *pieces)


def far_kernel(place_ref, src_ref, x_ref, sq_ref, own_ref, got_ref, *rest, order, with_sq):
    out_ref, weight, sems = rest[-3:]
    held, share, width = own_ref.shape
    copies = []
    for i, mask in enumerate(order):
        piece = own_ref.at[i] if i < held else got_ref.at[i - held]
        row = pl.multiple_of((place_ref[0] ^ mask) * share, TAIL)
        there = weight.at[pl.ds(row, share)]
        copies.append(pltpu.make_async_copy(piece, there, sems.at[i]))
    for copy in copies:
        copy.start()
    for copy in copies:
        copy.wait()
    count, rows, cols = x_ref.shape
    total = None
    for k in range(count):
        row = pl.multiple_of(src_ref[k] * cols, TAIL)
        term = jnp.dot(x_ref[k], weight[pl.ds(row, cols), :], preferred_element_type=F32)
        total = term if total is None else total + term
    out_ref[:rows, :] = total.astype(BF16)
    if with_sq:
        sq = sq_ref[...]
        high = sq.astype(BF16).astype(F32)
        out_ref[rows:, :] = lines_of((high, sq - high), width)


def lines_of(rows, width):
    lines = []
    for row in rows:
        for at in range(0, row.shape[1], width):
            line = row[:, at : at + width]
            if line.shape[1] < width:
                rest = jnp.zeros((1, width - line.shape[1]), F32)
                line = jnp.concatenate([line, rest], axis=1)
            lines.append(line)
    lines.append(jnp.zeros((TAIL - len(lines), width), F32))
    return jnp.concatenate(lines, axis=0).astype(BF16)


def rows_of(tail, count, length):
    per_row = -(-length // tail.shape[1])
    rows = []
    for r in range(count):
        lines = [tail[r * per_row + i : r * per_row + i + 1, :] for i in range(per_row)]
        rows.append(jnp.concatenate(lines, axis=1)[:, :length])
    return rows


def far_product(place, sources, x, sq, gathered, with_sq, after):
    order, own, got = gathered
    _, share, width = own.shape
    rows = x.shape[1]
    out_rows = rows + (TAIL if with_sq else 0)
    return pl.pallas_call(
        partial(far_kernel, order=order, with_sq=with_sq),
        out_shape=shape((out_rows, width), BF16),
        grid_spec=pltpu.PrefetchScalarGridSpec(
            num_scalar_prefetch=2,
            grid=(1,),
            in_specs=[
                pl.BlockSpec(x.shape, lambda i, p, s: (0, 0, 0)),
                pl.BlockSpec((1, rows), lambda i, p, s: (0, 0)),
                ANY,
                ANY,
            ]
            + [ANY for _ in after],
            out_specs=pl.BlockSpec((out_rows, width), lambda i, p, s: (0, 0)),
            scratch_shapes=[
                pltpu.VMEM((len(order) * share, width), BF16),
                pltpu.SemaphoreType.DMA((len(order),)),
            ],
        ),
        compiler_params=PARAMS,
        name="far",
    )(place, sources, x, sq, own, got, *after)


def near_kernel(src_ref, x_ref, k_ref, v_ref, q_ref, after_ref, out_ref):
    x = x_ref[0]

    @pl.when(pl.program_id(0) == 0)
    def _():
        out_ref[...] = jnp.zeros_like(out_ref)

    column = 0
    for ref in (k_ref, v_ref, q_ref):
        at = slice(column, column + ref.shape[1])
        out_ref[:, at] += jnp.dot(x, ref[...], preferred_element_type=F32)
        column += ref.shape[1]


def near_product(sources, x, weights, after):
    count, chunk, cols = x.shape
    widths = [w.shape[1] for w in weights]
    return pl.pallas_call(
        near_kernel,
        out_shape=shape((chunk, sum(widths)), F32),
        grid_spec=pltpu.PrefetchScalarGridSpec(
            num_scalar_prefetch=1,
            grid=(count,),
            in_specs=[pl.BlockSpec((1, chunk, cols), lambda i, s: (i, 0, 0))]
            + [pl.BlockSpec((cols, w), lambda i, s: (s[i], 0)) for w in widths]
            + [ANY],
            out_specs=pl.BlockSpec((chunk, sum(widths)), lambda i, s: (0, 0)),
        ),
        compiler_params=PARAMS,
        name="near",
    )(sources, x, *weights, after)


def keys_kernel(
    near_ref, far_ref, sq_ref, id_ref, cos_ref, sin_ref, after_ref, out_ref, sum_ref, *, model
):
    chunk, width = near_ref.shape
    tail = far_ref[chunk:, :].astype(F32)
    total = sum(rows_of(tail, 2, chunk), sq_ref[...])
    factor = to_column(lax.rsqrt(total / model + epsilon))
    sum_ref[...] = total
    for c in range(0, width, HEAD_SIZE):
        at = slice(c, c + HEAD_SIZE)
        part = (near_ref[:, at] + far_ref[:chunk, at].astype(F32)) * factor
        if c < width // 2:
            part = rotate(part, cos_ref[...], sin_ref[...])
        out_ref[:chunk, at] = part.astype(BF16)
    out_ref[chunk:, :] = lines_of((id_ref[...].astype(F32),), width)


def keys_values(near, far, sq, ids, cosine, sine, after, width, model):
    chunk = near.shape[0]
    whole = lambda i: (0, 0)
    return pl.pallas_call(
        partial(keys_kernel, model=model),
        out_shape=(shape((chunk + TAIL, width), BF16), shape((1, chunk), F32)),
        grid=(1,),
        in_specs=[
            pl.BlockSpec((chunk, width), whole),
            pl.BlockSpec(far.shape, whole),
            pl.BlockSpec((1, chunk), whole),
            pl.BlockSpec((1, chunk), whole),
            pl.BlockSpec((chunk, HEAD_SIZE), whole),
            pl.BlockSpec((chunk, HEAD_SIZE), whole),
            ANY,
        ],
        out_specs=[pl.BlockSpec((chunk + TAIL, width), whole), pl.BlockSpec((1, chunk), whole)],
        compiler_params=PARAMS,
        name="keys",
    )(near, far, sq, ids, cosine, sine, after)


def attention_kernel(
    seq_ref, near_ref, far_ref, sum_ref, cos_ref, sin_ref, id_ref, after_ref, *rest, back, offset, model
):
    kv_refs, (out_ref, k_scr, vt_scr, id_scr) = rest[:-4], rest[-4:]
    part_rows = kv_refs[0].shape[0] - TAIL
    group = near_ref.shape[1] // HEAD_SIZE
    tile = pl.program_id(0)

    @pl.when(tile == 0)
    def _():
        for b, kv_ref in enumerate(kv_refs):
            at = slice(b * part_rows, (b + 1) * part_rows)
            k_scr[at, :] = kv_ref[:part_rows, :HEAD_SIZE]
            vt_scr[:, at] = kv_ref[:part_rows, HEAD_SIZE:].astype(F32).T.astype(BF16)
            (ids,) = rows_of(kv_ref[part_rows:, :].astype(F32), 1, part_rows)
            exists = b >= back - seq_ref[0]
            id_scr[at, :] = to_column(jnp.where(exists, ids, -1.0))

    scale = query_scale * math.log2(math.e)
    factor = to_column(lax.rsqrt(sum_ref[...] / model + epsilon) * scale)
    heads = []
    for c in range(0, group * HEAD_SIZE, HEAD_SIZE):
        at = slice(c, c + HEAD_SIZE)
        part = (near_ref[:, at] + far_ref[:, at].astype(F32)) * factor
        heads.append(rotate(part, cos_ref[...], sin_ref[...]).astype(BF16))
    q2 = jnp.concatenate(heads, axis=0)
    width = group * Q_TILE

    before = (id_scr[...] < id_ref[...].astype(F32)).astype(F32)
    start = jnp.sum(before, axis=0, keepdims=True).astype(jnp.int32)
    low = jnp.min(start) // K_TILE
    start = jnp.concatenate([start] * group, axis=1)
    first = back * part_rows + offset + tile * Q_TILE
    place = first + lax.broadcasted_iota(jnp.int32, (1, Q_TILE), 1)
    place = jnp.concatenate([place] * group, axis=1)

    def score(j):
        base = pl.multiple_of(j * K_TILE, K_TILE)
        return lax.dot_general(
            k_scr[pl.ds(base, K_TILE), :],
            q2,
            (((1,), (1,)), ((), ())),
            preferred_element_type=F32,
        )

    stop = (first + Q_TILE + K_TILE - 1) // K_TILE

    def step(j, state):
        scores, run_max, run_sum, acc = state
        following = score(jnp.minimum(j + 1, stop - 1))
        base = pl.multiple_of(j * K_TILE, K_TILE)
        key_pos = base + lax.broadcasted_iota(jnp.int32, (K_TILE, width), 0)
        allowed = (key_pos >= start) & (key_pos <= place)
        scores = jnp.where(allowed, scores, NEG)
        new_max = jnp.maximum(run_max, jnp.max(scores, axis=0, keepdims=True))
        expo = jnp.exp2(scores - new_max)
        factor = jnp.exp2(run_max - new_max)
        run_sum = run_sum * factor + jnp.sum(expo, axis=0, keepdims=True)
        acc = acc * factor + jnp.dot(
            vt_scr[:, pl.ds(base, K_TILE)], expo.astype(BF16), preferred_element_type=F32
        )
        return following, new_max, run_sum, acc

    state = (
        score(low),
        jnp.full((1, width), NEG, F32),
        jnp.zeros((1, width), F32),
        jnp.zeros((HEAD_SIZE, width), F32),
    )
    _, _, run_sum, acc = lax.fori_loop(low, stop, step, state)
    context = (acc / run_sum).T
    for g in range(group):
        out_ref[:, g * HEAD_SIZE : (g + 1) * HEAD_SIZE] = context[
            g * Q_TILE : (g + 1) * Q_TILE
        ].astype(BF16)


def attend(seq, near, far, sums, cosine, sine, ids, after, blocks, c, model):
    rows = near.shape[0] // CHUNKS
    width = far.shape[1]
    part_rows = blocks[0].shape[0] - TAIL
    back = len(blocks) - 1
    tiles = rows // Q_TILE
    keys = len(blocks) * part_rows
    last = near.shape[1] // width - 1
    return pl.pallas_call(
        partial(attention_kernel, back=back, offset=c * rows, model=model),
        out_shape=shape((rows, width), BF16),
        grid_spec=pltpu.PrefetchScalarGridSpec(
            num_scalar_prefetch=1,
            grid=(tiles,),
            in_specs=[
                pl.BlockSpec((Q_TILE, width), lambda i, s: (c * tiles + i, last)),
                pl.BlockSpec((Q_TILE, width), lambda i, s: (c * tiles + i, 0)),
                pl.BlockSpec((1, Q_TILE), lambda i, s: (0, c * tiles + i)),
                pl.BlockSpec((Q_TILE, HEAD_SIZE), lambda i, s: (c * tiles + i, 0)),
                pl.BlockSpec((Q_TILE, HEAD_SIZE), lambda i, s: (c * tiles + i, 0)),
                pl.BlockSpec((1, Q_TILE), lambda i, s: (0, c * tiles + i)),
                ANY,
            ]
            + [pl.BlockSpec(b.shape, lambda i, s: (0, 0)) for b in blocks],
            out_specs=pl.BlockSpec((Q_TILE, width), lambda i, s: (i, 0)),
            scratch_shapes=[
                pltpu.VMEM((keys, HEAD_SIZE), BF16),
                pltpu.VMEM((HEAD_SIZE, keys), BF16),
                pltpu.VMEM((keys, LANES), F32),
            ],
        ),
        compiler_params=PARAMS,
        cost_estimate=pl.CostEstimate(
            flops=4 * rows * width * keys,
            bytes_accessed=4 * keys * width,
            transcendentals=rows * keys * width // HEAD_SIZE,
        ),
        name="attend",
    )(seq, near, far, sums, cosine, sine, ids, after, *blocks)


def output_kernel(at_ref, own_o_ref, o_ref, *rest):
    ctx_refs, (after_ref, out_ref, sq_ref, acc) = rest[:-4], rest[-4:]
    step = pl.program_id(0)
    plane, _, share, tile = o_ref.shape
    total = jnp.dot(ctx_refs[0][...], own_o_ref[...], preferred_element_type=F32)
    for i, ctx_ref in enumerate(ctx_refs[1:]):
        weight = o_ref[:, at_ref[1 + i]].reshape(plane * share, tile)
        total = total + jnp.dot(ctx_ref[...], weight, preferred_element_type=F32)
    out_ref[...] = total
    squares = jnp.sum(total * total, axis=1, keepdims=True)
    squares = jnp.broadcast_to(squares, acc.shape)

    @pl.when(step == 0)
    def _():
        acc[...] = squares

    @pl.when(step > 0)
    def _():
        acc[...] += squares

    @pl.when(step == pl.num_programs(0) - 1)
    def _():
        sq_ref[...] = acc[...].T[0:1, :]


def output_product(column, order, o_weight, gathered, contexts, after):
    chunk, width = contexts[0].shape
    plane, others, share, cols = gathered.shape
    tiles = 3 if cols % (3 * LANES) == 0 else 1
    tile = cols // tiles
    if cols % LANES:
        o_weight = lax.dynamic_slice_in_dim(o_weight, column * cols, cols, axis=1)
        column = jnp.int32(0)
    return pl.pallas_call(
        output_kernel,
        out_shape=(shape((chunk, cols), F32), shape((1, chunk), F32)),
        grid_spec=pltpu.PrefetchScalarGridSpec(
            num_scalar_prefetch=1,
            grid=(tiles,),
            in_specs=[
                pl.BlockSpec((width, tile), lambda i, at: (0, at[0] * tiles + i)),
                pl.BlockSpec((plane, others, share, tile), lambda i, at: (0, 0, 0, i)),
            ]
            + [pl.BlockSpec((chunk, width), lambda i, at: (0, 0)) for _ in contexts]
            + [ANY],
            out_specs=[
                pl.BlockSpec((chunk, tile), lambda i, at: (0, i)),
                pl.BlockSpec((1, chunk), lambda i, at: (0, 0)),
            ],
            scratch_shapes=[pltpu.VMEM((chunk, LANES), F32)],
        ),
        compiler_params=PARAMS,
        name="output",
    )(jnp.stack([column] + order), o_weight, gathered, *contexts, after)


def final_kernel(token_ref, branch_ref, gain_ref, *rest, model, others):
    sq_refs, out_ref = rest[:others], rest[-1]
    total = sq_refs[0][...]
    for sq_ref in sq_refs[1:]:
        total = total + sq_ref[...]
    factor = to_column(lax.rsqrt(total / model + epsilon))[:, 0:1]
    out = token_ref[...].astype(F32) + branch_ref[...] * factor * gain_ref[...]
    out_ref[...] = out.astype(BF16)


def finish(tokens, branch, out_gain, sums, previous, c, model):
    chunk, cols = branch.shape
    tiles = chunk // Q_TILE
    in_specs = [
        pl.BlockSpec((Q_TILE, cols), lambda i: (c * tiles + i, 0)),
        pl.BlockSpec((Q_TILE, cols), lambda i: (i, 0)),
        pl.BlockSpec((1, cols), lambda i: (0, 0)),
    ]
    in_specs += [pl.BlockSpec((1, Q_TILE), lambda i: (0, i)) for _ in sums]
    args = [tokens, branch, out_gain, *sums]
    aliases = {}
    if previous is not None:
        aliases = {len(args): 0}
        in_specs.append(ANY)
        args.append(previous)
    return pl.pallas_call(
        partial(final_kernel, model=model, others=len(sums)),
        out_shape=shape(tokens.shape, BF16),
        grid=(tiles,),
        in_specs=in_specs,
        out_specs=pl.BlockSpec((Q_TILE, cols), lambda i: (c * tiles + i, 0)),
        input_output_aliases=aliases,
        compiler_params=PARAMS,
        name="finish",
    )(*args)


def per_device(
    tokens, seg_ids, in_gain, q_weight, k_weight, value_weight, o_weight, out_gain, *, sizes
):
    rows, cols = tokens.shape
    model = in_gain.shape[0]
    nz, nseq = sizes["tensor"], sizes["seq"]
    plane = nseq * sizes["groups"]
    z = lax.axis_index("tensor")
    seq = lax.axis_index("seq")
    in_plane = lax.axis_index(PLANE)
    half = nz // 2
    side, within = z // half, z % half
    half_rows = half * cols

    ring = [(i, i // half * half + (i + 1) % half) for i in range(nz)]
    swap = [(i, (i + half) % nz) for i in range(nz)]
    turn = lambda k: [(i, (i + k) % nz) for i in range(nz)]
    seq_bits = [1 << b for b in range(1, nseq.bit_length() - 1)]
    group_bits = [nseq << b for b in range(sizes["groups"].bit_length() - 1)]

    share = half_rows // plane
    at = jnp.reshape((1 - side) * plane + in_plane, (1,))
    inner = seq_bits + group_bits
    masks_kv, masks_q = inner + [1], inner[::-1] + [1]
    steps = len(masks_kv)
    piece = rows // (steps + 1) // TAIL * TAIL
    counts = [rows - steps * piece] + [piece] * steps
    if counts[0] > piece:
        counts = [rows - steps * (piece + TAIL)] + [piece + TAIL] * steps
    packed_kv, packed_q, cut = pack(
        at, q_weight, k_weight, value_weight, share, tokens, counts[0]
    )
    own_kv = lax.ppermute(packed_kv, "tensor", swap)[None]
    own_q = lax.ppermute(packed_q, "tensor", swap)[None]
    received = [lax.ppermute(cut, "tensor", ring)]
    order_kv, order_q, first = [0], [0], counts[0]
    for step, (mask_kv, mask_q) in enumerate(zip(masks_kv, masks_q)):
        if step == 0:
            (cut,) = stage([], tokens, first, counts[1], [own_kv, own_q, received[0]])
        else:
            own_kv, own_q, cut = stage(
                [(own_kv, far_kv), (own_q, far_q)],
                tokens,
                first,
                counts[step + 1],
                [received[-1]],
            )
        first += counts[step + 1]
        far_kv = lax.ppermute(own_kv, PLANE, [(i, i ^ mask_kv) for i in range(plane)])
        far_q = lax.ppermute(own_q, PLANE, [(i, i ^ mask_q) for i in range(plane)])
        received.append(lax.ppermute(cut, "tensor", ring))
        order_kv = order_kv + [k ^ mask_kv for k in order_kv]
        order_q = order_q + [k ^ mask_q for k in order_q]
    far_kv, far_q = (order_kv, own_kv, far_kv), (order_q, own_q, far_q)

    sources = (within + half - jnp.arange(half, dtype=jnp.int32)) % half
    blocks = [[tokens], received]
    for _ in range(half - 2):
        blocks.append([lax.ppermute(part, "tensor", ring) for part in blocks[-1]])
    gains = in_gain.reshape(nz, 1, cols)
    x, sq = prep(side * half + sources, gains, blocks)

    place = jnp.reshape(in_plane, (1,))
    sent_kv = far_product(place, sources, x, sq, far_kv, True, [far_q[2]])
    got_kv = lax.ppermute(sent_kv, "tensor", swap)
    weights = (k_weight, value_weight, q_weight)
    near = near_product(side * half + sources, x, weights, sent_kv)

    sent_q = far_product(place, sources, x, sq, far_q, False, [near])
    got_q = lax.ppermute(sent_q, "tensor", swap)
    cosine, sine = rotation_table(seq * rows + jnp.arange(rows, dtype=jnp.int32))
    ids = seg_ids[None, :]
    kv_width = k_weight.shape[1] + value_weight.shape[1]
    own_kv, sums = keys_values(
        near, got_kv, sq, ids, cosine, sine, sent_q, kv_width, model
    )

    back = -(-(nseq * rows // 2 - 1) // rows)
    kv_blocks = [own_kv]
    for k in range(1, back + 1):
        earlier = [(i, i + k) for i in range(nseq - k)]
        kv_blocks.insert(0, lax.ppermute(own_kv, "seq", earlier))

    o_share = o_weight.shape[0] // plane
    last = got_kv[0, 0] + sent_q[0, 0]
    wait = (last != last).astype(jnp.int32)
    moved = []
    for k in range(1, nz):
        target = (z + k) % nz
        piece = lax.dynamic_slice(
            o_weight, (in_plane * o_share + wait, target * cols), (o_share, cols)
        )
        moved.append(lax.ppermute(piece, "tensor", turn(k)))
    gathered_o = lax.all_gather(jnp.stack(moved), PLANE)

    out = None
    seq_at = jnp.reshape(seq, (1,))
    context, own_sq = place, place
    for c in range(CHUNKS):
        context = attend(
            seq_at, near, got_q, sums, cosine, sine, ids, context, kv_blocks, c, model
        )
        if nz == 4:
            pairs = [(i, i ^ 1) for i in range(nz)]
            opposite = lax.ppermute(context, "tensor", swap)
            beside = lax.ppermute(context, "tensor", pairs)
            across = lax.ppermute(opposite, "tensor", pairs)
            contexts = [context, opposite, beside, across]
            order = [jnp.int32(1), 2 - 2 * (z % 2), 2 * (z % 2)]
        else:
            contexts = [context]
            contexts += [lax.ppermute(context, "tensor", turn(k)) for k in range(1, nz)]
            order = [jnp.int32(k) for k in range(nz - 1)]
        branch, own_sq = output_product(z, order, o_weight, gathered_o, contexts, own_sq)
        squares = [own_sq]
        squares += [lax.ppermute(own_sq, "tensor", turn(k)) for k in range(1, nz)]
        out = finish(tokens, branch, out_gain[None, :], squares, out, c, model)
    return out


def solution(mesh):
    return jax.shard_map(
        partial(per_device, sizes=dict(mesh.shape)),
        mesh=mesh,
        in_specs=(
            P(("groups", "seq"), "tensor"),
            P(("groups", "seq")),
            P(),
            P(None, "tensor"),
            P(None, "tensor"),
            P(None, "tensor"),
            P("tensor", None),
            P("tensor"),
        ),
        out_specs=P(("groups", "seq"), "tensor"),
        check_vma=False,
    )
```

```python
import math
from functools import partial

import jax
import jax.numpy as jnp
from jax import lax
from jax.experimental import pallas as pl
from jax.experimental.pallas import tpu as pltpu
from jax.sharding import PartitionSpec as P

HEAD_SIZE = 128
PLANE = ("groups", "seq")

epsilon = 1e-06
query_scale = 144.0 ** (-0.5)
rope_base = 10000.0
NEG = -1e30
Q_TILE = 128
K_TILE = 256
CHUNKS = 2
LANES = 128
TAIL = 16
F32, BF16 = jnp.float32, jnp.bfloat16
ANY = pl.BlockSpec(memory_space=pl.ANY)
HBM = pl.BlockSpec(memory_space=pltpu.HBM)
VMEM = pl.BlockSpec(memory_space=pltpu.VMEM)
DOCUMENTS = 8
PARAMS = pltpu.CompilerParams(vmem_limit_bytes=24 * 1024 * 1024)
ALL_VMEM = pltpu.CompilerParams(vmem_limit_bytes=62 * 1024 * 1024)


def shape(dims, dtype):
    return jax.ShapeDtypeStruct(dims, dtype)


def to_row(column):
    return jnp.broadcast_to(column, (column.shape[0], LANES)).T[0:1, :]


def to_column(row):
    return jnp.broadcast_to(row, (LANES, row.shape[1])).T


def rotation_table(token_places):
    half_dim = HEAD_SIZE // 2
    inverse = rope_base ** (-jnp.arange(half_dim, dtype=F32) / half_dim)
    angles = token_places.astype(F32)[:, None] * inverse[None, :]
    cosine, sine = jnp.cos(angles), jnp.sin(angles)
    return jnp.concatenate([cosine, cosine], 1), jnp.concatenate([-sine, sine], 1)


def rotate(vectors, cosine, sine):
    return vectors * cosine + pltpu.roll(vectors, HEAD_SIZE // 2, 1) * sine


def pack_kernel(at_ref, q_ref, k_ref, v_ref, x_ref, kv_out, q_out, x_out, sems):
    share, width = q_out.shape[0], k_ref.shape[1]
    rows = pl.ds(pl.multiple_of(at_ref[0] * share, TAIL), share)
    copies = [
        pltpu.make_async_copy(k_ref.at[rows], kv_out.at[:, pl.ds(0, width)], sems.at[0]),
        pltpu.make_async_copy(v_ref.at[rows], kv_out.at[:, pl.ds(width, width)], sems.at[1]),
        pltpu.make_async_copy(q_ref.at[rows], q_out, sems.at[2]),
        pltpu.make_async_copy(x_ref.at[pl.ds(0, x_out.shape[0])], x_out, sems.at[3]),
    ]
    for copy in copies:
        copy.start()
    for copy in copies:
        copy.wait()


def pack(at, q_weight, k_weight, v_weight, share, tokens, rows):
    kv_width = k_weight.shape[1] + v_weight.shape[1]
    dims = [(share, kv_width), (share, q_weight.shape[1]), (rows, tokens.shape[1])]
    return pl.pallas_call(
        pack_kernel,
        out_shape=tuple(shape(d, BF16) for d in dims),
        grid_spec=pltpu.PrefetchScalarGridSpec(
            num_scalar_prefetch=1,
            grid=(1,),
            in_specs=[HBM, HBM, HBM, HBM],
            out_specs=[pl.BlockSpec(d, lambda i, at: (0, 0)) for d in dims],
            scratch_shapes=[pltpu.SemaphoreType.DMA((4,))],
        ),
        compiler_params=ALL_VMEM,
        name="pack",
    )(at, q_weight, k_weight, v_weight, tokens)


def stage_kernel(*refs, pairs, first, count):
    outputs = pairs + (1 if count else 0)
    ins, outs, sems = refs[: -outputs - 1], refs[-outputs - 1 : -1], refs[-1]
    copies = []
    for p in range(pairs):
        held = ins[2 * p].shape[0]
        for side in range(2):
            there = outs[p].at[pl.ds(side * held, held)]
            copies.append(
                pltpu.make_async_copy(ins[2 * p + side], there, sems.at[len(copies)])
            )
    if count:
        rows = ins[2 * pairs].at[pl.ds(first, count)]
        copies.append(pltpu.make_async_copy(rows, outs[-1], sems.at[len(copies)]))
    for copy in copies:
        copy.start()
    for copy in copies:
        copy.wait()


def stage(joined, tokens, first, count, after):
    dims = [(2 * pair[0].shape[0],) + pair[0].shape[1:] for pair in joined]
    if count:
        dims.append((count, tokens.shape[1]))
    return pl.pallas_call(
        partial(stage_kernel, pairs=len(joined), first=first, count=count),
        out_shape=tuple(shape(d, BF16) for d in dims),
        in_specs=[ANY] * (2 * len(joined) + 1 + len(after)),
        scratch_shapes=[pltpu.SemaphoreType.DMA((2 * len(joined) + 1,))],
        compiler_params=PARAMS,
        name="stage",
    )(*[piece for pair in joined for piece in pair], tokens, *after)


def cut_kernel(at_ref, o_ref, after_ref, *rest):
    outs, sems = rest[:-1], rest[-1]
    copies = []
    for i, out in enumerate(outs):
        rows = pl.ds(pl.multiple_of(at_ref[0], TAIL), out.shape[0])
        columns = pl.ds(pl.multiple_of(at_ref[1 + i], LANES), out.shape[1])
        copies.append(pltpu.make_async_copy(o_ref.at[rows, columns], out, sems.at[i]))
    for copy in copies:
        copy.start()
    for copy in copies:
        copy.wait()


def cut_pieces(row, columns, o_weight, share, cols, after):
    if cols % LANES:
        return [lax.dynamic_slice(o_weight, (row, c), (share, cols)) for c in columns]
    return pl.pallas_call(
        cut_kernel,
        out_shape=tuple(shape((share, cols), BF16) for _ in columns),
        grid_spec=pltpu.PrefetchScalarGridSpec(
            num_scalar_prefetch=1,
            grid=(1,),
            in_specs=[ANY, ANY],
            out_specs=[VMEM for _ in columns],
            scratch_shapes=[pltpu.SemaphoreType.DMA((len(columns),))],
        ),
        compiler_params=PARAMS,
        name="cut",
    )(jnp.stack([row] + columns), o_weight, after)


def prep_kernel(src_ref, gain_ref, *rest, cuts):
    x_refs, (out_ref, sq_ref) = rest[:-2], rest[-2:]
    squares, at = [], 0
    for k, pieces in enumerate(cuts):
        column, row = [], 0
        for x_ref in x_refs[at : at + pieces]:
            x = x_ref[...].astype(F32)
            column.append(jnp.sum(x * x, axis=1, keepdims=True))
            out_ref[k, row : row + x.shape[0]] = (x * gain_ref[src_ref[k]]).astype(BF16)
            row += x.shape[0]
        squares.append(jnp.concatenate(column, axis=0))
        at += pieces
    sq_ref[...] = to_row(sum(squares[1:], squares[0]))


def prep(sources, gains, blocks):
    rows, cols = blocks[0][0].shape
    dims = (len(blocks), rows, cols)
    pieces = [piece for block in blocks for piece in block]
    return pl.pallas_call(
        partial(prep_kernel, cuts=[len(block) for block in blocks]),
        out_shape=(shape(dims, BF16), shape((1, rows), F32)),
        grid_spec=pltpu.PrefetchScalarGridSpec(
            num_scalar_prefetch=1,
            grid=(1,),
            in_specs=[VMEM] + [VMEM for _ in pieces],
            out_specs=[VMEM, VMEM],
        ),
        compiler_params=PARAMS,
        name="prep",
    )(sources, gains, *pieces)


def far_kernel(place_ref, src_ref, x_ref, sq_ref, own_ref, got_ref, *rest, order, with_sq):
    out_ref, weight, sems = rest[-3:]
    held, share, width = own_ref.shape
    copies = []
    for i, mask in enumerate(order):
        piece = own_ref.at[i] if i < held else got_ref.at[i - held]
        row = pl.multiple_of((place_ref[0] ^ mask) * share, TAIL)
        there = weight.at[pl.ds(row, share)]
        copies.append(pltpu.make_async_copy(piece, there, sems.at[i]))
    for copy in copies:
        copy.start()
    for copy in copies:
        copy.wait()
    count, rows, cols = x_ref.shape
    total = None
    for k in range(count):
        row = pl.multiple_of(src_ref[k] * cols, TAIL)
        term = jnp.dot(x_ref[k], weight[pl.ds(row, cols), :], preferred_element_type=F32)
        total = term if total is None else total + term
    out_ref[:rows, :] = total.astype(BF16)
    if with_sq:
        sq = sq_ref[...]
        high = sq.astype(BF16).astype(F32)
        out_ref[rows:, :] = lines_of((high, sq - high), width)


def lines_of(rows, width):
    lines = []
    for row in rows:
        for at in range(0, row.shape[1], width):
            line = row[:, at : at + width]
            if line.shape[1] < width:
                rest = jnp.zeros((1, width - line.shape[1]), F32)
                line = jnp.concatenate([line, rest], axis=1)
            lines.append(line)
    lines.append(jnp.zeros((TAIL - len(lines), width), F32))
    return jnp.concatenate(lines, axis=0).astype(BF16)


def rows_of(tail, count, length):
    per_row = -(-length // tail.shape[1])
    rows = []
    for r in range(count):
        lines = [tail[r * per_row + i : r * per_row + i + 1, :] for i in range(per_row)]
        rows.append(jnp.concatenate(lines, axis=1)[:, :length])
    return rows


def far_product(place, sources, x, sq, gathered, with_sq, after):
    order, own, got = gathered
    _, share, width = own.shape
    rows = x.shape[1]
    out_rows = rows + (TAIL if with_sq else 0)
    return pl.pallas_call(
        partial(far_kernel, order=order, with_sq=with_sq),
        out_shape=shape((out_rows, width), BF16),
        grid_spec=pltpu.PrefetchScalarGridSpec(
            num_scalar_prefetch=2,
            grid=(1,),
            in_specs=[VMEM, VMEM, ANY, ANY] + [ANY for _ in after],
            out_specs=VMEM,
            scratch_shapes=[
                pltpu.VMEM((len(order) * share, width), BF16),
                pltpu.SemaphoreType.DMA((len(order),)),
            ],
        ),
        compiler_params=PARAMS,
        name="far",
    )(place, sources, x, sq, own, got, *after)


def near_kernel(src_ref, x_ref, k_ref, v_ref, q_ref, after_ref, out_ref):
    x = x_ref[pl.program_id(0)]

    @pl.when(pl.program_id(0) == 0)
    def _():
        out_ref[...] = jnp.zeros_like(out_ref)

    column = 0
    for ref in (k_ref, v_ref, q_ref):
        at = slice(column, column + ref.shape[1])
        out_ref[:, at] += jnp.dot(x, ref[...], preferred_element_type=F32)
        column += ref.shape[1]


def near_product(sources, x, weights, after):
    count, chunk, cols = x.shape
    widths = [w.shape[1] for w in weights]
    return pl.pallas_call(
        near_kernel,
        out_shape=shape((chunk, sum(widths)), F32),
        grid_spec=pltpu.PrefetchScalarGridSpec(
            num_scalar_prefetch=1,
            grid=(count,),
            in_specs=[VMEM]
            + [pl.BlockSpec((cols, w), lambda i, s: (s[i], 0)) for w in widths]
            + [ANY],
            out_specs=VMEM,
        ),
        compiler_params=PARAMS,
        name="near",
    )(sources, x, *weights, after)


def keys_kernel(
    near_ref, far_ref, sq_ref, id_ref, cos_ref, sin_ref, after_ref, out_ref, sum_ref, *, model
):
    rows, width = near_ref.shape[0], far_ref.shape[1]
    tail = far_ref[rows:, :].astype(F32)
    total = sum(rows_of(tail, 2, rows), sq_ref[...])
    factor = to_column(lax.rsqrt(total / model + epsilon))
    sum_ref[...] = total
    keys, values = slice(0, HEAD_SIZE), slice(HEAD_SIZE, 2 * HEAD_SIZE)
    part = (near_ref[:, keys] + far_ref[:rows, keys].astype(F32)) * factor
    part = rotate(part, cos_ref[...], sin_ref[...]).astype(BF16)
    out_ref[: rows // 2, keys] = part[: rows // 2]
    out_ref[: rows // 2, values] = part[rows // 2 :]
    part = (near_ref[:, values] + far_ref[:rows, values].astype(F32)) * factor
    part = part.T.astype(BF16)
    for i, at in enumerate(range(0, rows, width)):
        row = rows // 2 + i * HEAD_SIZE
        out_ref[row : row + HEAD_SIZE, :] = part[:, at : at + width]
    out_ref[rows:, :] = lines_of((id_ref[...].astype(F32),), width)


def keys_values(near, far, sq, ids, cosine, sine, after, model):
    return pl.pallas_call(
        partial(keys_kernel, model=model),
        out_shape=(shape(far.shape, BF16), shape(sq.shape, F32)),
        in_specs=[VMEM] * 6 + [ANY],
        out_specs=[VMEM, VMEM],
        compiler_params=PARAMS,
        name="keys",
    )(near, far, sq, ids, cosine, sine, after)


def attention_kernel(
    seq_ref, near_ref, far_ref, sum_ref, cos_ref, sin_ref, id_ref, after_ref, *rest, back, offset, model
):
    kv_refs, (out_ref, k_scr, vt_scr, count_scr) = rest[:-4], rest[-4:]
    part_rows, message = kv_refs[0].shape[0] - TAIL, kv_refs[0].shape[1]
    group = near_ref.shape[1] // HEAD_SIZE
    tile = pl.program_id(0)

    @pl.when(tile == 0)
    def _():
        counts = [jnp.zeros((1, 1), F32) for _ in range(DOCUMENTS)]
        for b, kv_ref in enumerate(kv_refs):
            row, half = b * part_rows, part_rows // 2
            k_scr[row : row + half, :] = kv_ref[:half, :HEAD_SIZE]
            k_scr[row + half : row + part_rows, :] = kv_ref[:half, HEAD_SIZE:]
            for i, at in enumerate(range(0, part_rows, message)):
                first = half + i * HEAD_SIZE
                vt_scr[:, row + at : row + at + message] = kv_ref[first : first + HEAD_SIZE, :]
            (ids,) = rows_of(kv_ref[part_rows:, :].astype(F32), 1, part_rows)
            exists = b >= back - seq_ref[0]
            ids = jnp.where(exists, ids, -1.0)
            for d in range(DOCUMENTS):
                below = (ids < d).astype(F32)
                counts[d] = counts[d] + jnp.sum(below, axis=1, keepdims=True)
        for d in range(DOCUMENTS):
            count_scr[d : d + 1, :] = jnp.broadcast_to(counts[d], (1, LANES))

    scale = query_scale * math.log2(math.e)
    factor = to_column(lax.rsqrt(sum_ref[...] / model + epsilon) * scale)
    heads = []
    for c in range(0, group * HEAD_SIZE, HEAD_SIZE):
        at = slice(c, c + HEAD_SIZE)
        part = (near_ref[:, at] + far_ref[:, at].astype(F32)) * factor
        heads.append(rotate(part, cos_ref[...], sin_ref[...]).astype(BF16))
    q2 = jnp.concatenate(heads, axis=0)
    width = group * Q_TILE

    start = jnp.zeros((1, Q_TILE), F32)
    for d in range(DOCUMENTS):
        start = jnp.where(id_ref[...] == d, count_scr[d : d + 1, :], start)
    start = start.astype(jnp.int32)
    low = jnp.min(start) // K_TILE
    start = jnp.concatenate([start] * group, axis=1)
    first = back * part_rows + offset + tile * Q_TILE
    place = first + lax.broadcasted_iota(jnp.int32, (1, Q_TILE), 1)
    place = jnp.concatenate([place] * group, axis=1)

    def score(j):
        base = pl.multiple_of(j * K_TILE, K_TILE)
        return lax.dot_general(
            k_scr[pl.ds(base, K_TILE), :],
            q2,
            (((1,), (1,)), ((), ())),
            preferred_element_type=F32,
        )

    stop = (first + Q_TILE + K_TILE - 1) // K_TILE

    def step(j, state):
        scores, run_max, run_sum, acc = state
        following = score(jnp.minimum(j + 1, stop - 1))
        base = pl.multiple_of(j * K_TILE, K_TILE)
        key_pos = base + lax.broadcasted_iota(jnp.int32, (K_TILE, width), 0)
        allowed = (key_pos >= start) & (key_pos <= place)
        scores = jnp.where(allowed, scores, NEG)
        new_max = jnp.maximum(run_max, jnp.max(scores, axis=0, keepdims=True))
        expo = jnp.exp2(scores - new_max)
        factor = jnp.exp2(run_max - new_max)
        run_sum = run_sum * factor + jnp.sum(expo, axis=0, keepdims=True)
        acc = acc * factor + jnp.dot(
            vt_scr[:, pl.ds(base, K_TILE)], expo.astype(BF16), preferred_element_type=F32
        )
        return following, new_max, run_sum, acc

    state = (
        score(low),
        jnp.full((1, width), NEG, F32),
        jnp.zeros((1, width), F32),
        jnp.zeros((HEAD_SIZE, width), F32),
    )
    _, _, run_sum, acc = lax.fori_loop(low, stop, step, state)
    context = (acc / run_sum).T
    for g in range(group):
        out_ref[:, g * HEAD_SIZE : (g + 1) * HEAD_SIZE] = context[
            g * Q_TILE : (g + 1) * Q_TILE
        ].astype(BF16)


def attend(seq, near, far, sums, cosine, sine, ids, after, blocks, c, model):
    rows = near.shape[0] // CHUNKS
    width = far.shape[1]
    part_rows = blocks[0].shape[0] - TAIL
    back = len(blocks) - 1
    tiles = rows // Q_TILE
    keys = len(blocks) * part_rows
    last = near.shape[1] // width - 1
    return pl.pallas_call(
        partial(attention_kernel, back=back, offset=c * rows, model=model),
        out_shape=shape((rows, width), BF16),
        grid_spec=pltpu.PrefetchScalarGridSpec(
            num_scalar_prefetch=1,
            grid=(tiles,),
            in_specs=[
                pl.BlockSpec((Q_TILE, width), lambda i, s: (c * tiles + i, last)),
                pl.BlockSpec((Q_TILE, width), lambda i, s: (c * tiles + i, 0)),
                pl.BlockSpec((1, Q_TILE), lambda i, s: (0, c * tiles + i)),
                pl.BlockSpec((Q_TILE, HEAD_SIZE), lambda i, s: (c * tiles + i, 0)),
                pl.BlockSpec((Q_TILE, HEAD_SIZE), lambda i, s: (c * tiles + i, 0)),
                pl.BlockSpec((1, Q_TILE), lambda i, s: (0, c * tiles + i)),
                ANY,
            ]
            + [VMEM for _ in blocks],
            out_specs=pl.BlockSpec((Q_TILE, width), lambda i, s: (i, 0)),
            scratch_shapes=[
                pltpu.VMEM((keys, HEAD_SIZE), BF16),
                pltpu.VMEM((HEAD_SIZE, keys), BF16),
                pltpu.VMEM((DOCUMENTS, LANES), F32),
            ],
        ),
        compiler_params=PARAMS,
        cost_estimate=pl.CostEstimate(
            flops=4 * rows * width * keys,
            bytes_accessed=4 * keys * width,
            transcendentals=rows * keys * width // HEAD_SIZE,
        ),
        name="attend",
    )(seq, near, far, sums, cosine, sine, ids, after, *blocks)


def output_kernel(at_ref, own_o_ref, o_ref, *rest):
    ctx_refs, (after_ref, out_ref, sq_ref, acc) = rest[:-4], rest[-4:]
    step = pl.program_id(0)
    plane, _, share, tile = o_ref.shape
    total = jnp.dot(ctx_refs[0][...], own_o_ref[...], preferred_element_type=F32)
    for i, ctx_ref in enumerate(ctx_refs[1:]):
        weight = o_ref[:, at_ref[1 + i]].reshape(plane * share, tile)
        total = total + jnp.dot(ctx_ref[...], weight, preferred_element_type=F32)
    out_ref[...] = total
    squares = jnp.sum(total * total, axis=1, keepdims=True)
    squares = jnp.broadcast_to(squares, acc.shape)

    @pl.when(step == 0)
    def _():
        acc[...] = squares

    @pl.when(step > 0)
    def _():
        acc[...] += squares

    @pl.when(step == pl.num_programs(0) - 1)
    def _():
        sq_ref[...] = acc[...].T[0:1, :]


def output_product(column, order, o_weight, gathered, contexts, after):
    chunk, width = contexts[0].shape
    plane, others, share, cols = gathered.shape
    tiles = 3 if cols % (3 * LANES) == 0 else 1
    tile = cols // tiles
    if cols % LANES:
        o_weight = lax.dynamic_slice_in_dim(o_weight, column * cols, cols, axis=1)
        column = jnp.int32(0)
    return pl.pallas_call(
        output_kernel,
        out_shape=(shape((chunk, cols), F32), shape((1, chunk), F32)),
        grid_spec=pltpu.PrefetchScalarGridSpec(
            num_scalar_prefetch=1,
            grid=(tiles,),
            in_specs=[
                pl.BlockSpec((width, tile), lambda i, at: (0, at[0] * tiles + i)),
                pl.BlockSpec((plane, others, share, tile), lambda i, at: (0, 0, 0, i)),
            ]
            + [pl.BlockSpec((chunk, width), lambda i, at: (0, 0)) for _ in contexts]
            + [ANY],
            out_specs=[
                pl.BlockSpec((chunk, tile), lambda i, at: (0, i)),
                pl.BlockSpec((1, chunk), lambda i, at: (0, 0)),
            ],
            scratch_shapes=[pltpu.VMEM((chunk, LANES), F32)],
        ),
        compiler_params=PARAMS,
        name="output",
    )(jnp.stack([column] + order), o_weight, gathered, *contexts, after)


def final_kernel(token_ref, branch_ref, gain_ref, *rest, model, others):
    sq_refs, out_ref = rest[:others], rest[-1]
    total = sq_refs[0][...]
    for sq_ref in sq_refs[1:]:
        total = total + sq_ref[...]
    factor = to_column(lax.rsqrt(total / model + epsilon))[:, 0:1]
    out = token_ref[...].astype(F32) + branch_ref[...] * factor * gain_ref[...]
    out_ref[...] = out.astype(BF16)


def finish(tokens, branch, out_gain, sums, previous, c, model):
    chunk, cols = branch.shape
    tiles = chunk // Q_TILE
    in_specs = [
        pl.BlockSpec((Q_TILE, cols), lambda i: (c * tiles + i, 0)),
        pl.BlockSpec((Q_TILE, cols), lambda i: (i, 0)),
        pl.BlockSpec((1, cols), lambda i: (0, 0)),
    ]
    in_specs += [pl.BlockSpec((1, Q_TILE), lambda i: (0, i)) for _ in sums]
    args = [tokens, branch, out_gain, *sums]
    aliases = {}
    if previous is not None:
        aliases = {len(args): 0}
        in_specs.append(ANY)
        args.append(previous)
    return pl.pallas_call(
        partial(final_kernel, model=model, others=len(sums)),
        out_shape=shape(tokens.shape, BF16),
        grid=(tiles,),
        in_specs=in_specs,
        out_specs=pl.BlockSpec((Q_TILE, cols), lambda i: (c * tiles + i, 0)),
        input_output_aliases=aliases,
        compiler_params=PARAMS,
        name="finish",
    )(*args)


def per_device(
    tokens, seg_ids, in_gain, q_weight, k_weight, value_weight, o_weight, out_gain, *, sizes
):
    rows, cols = tokens.shape
    model = in_gain.shape[0]
    nz, nseq = sizes["tensor"], sizes["seq"]
    plane = nseq * sizes["groups"]
    z = lax.axis_index("tensor")
    seq = lax.axis_index("seq")
    in_plane = lax.axis_index(PLANE)
    half = nz // 2
    side, within = z // half, z % half
    half_rows = half * cols

    ring = [(i, i // half * half + (i + 1) % half) for i in range(nz)]
    swap = [(i, (i + half) % nz) for i in range(nz)]
    turn = lambda k: [(i, (i + k) % nz) for i in range(nz)]
    seq_bits = [1 << b for b in range(1, nseq.bit_length() - 1)]
    group_bits = [nseq << b for b in range(sizes["groups"].bit_length() - 1)]

    share = half_rows // plane
    at = jnp.reshape((1 - side) * plane + in_plane, (1,))
    inner = seq_bits + group_bits
    masks_kv, masks_q = inner + [1], inner[::-1] + [1]
    steps = len(masks_kv)
    piece = rows // (steps + 1) // TAIL * TAIL
    counts = [rows - steps * piece] + [piece] * steps
    if counts[0] > piece:
        counts = [rows - steps * (piece + TAIL)] + [piece + TAIL] * steps
    packed_kv, packed_q, cut = pack(
        at, q_weight, k_weight, value_weight, share, tokens, counts[0]
    )
    own_kv = lax.ppermute(packed_kv, "tensor", swap)[None]
    own_q = lax.ppermute(packed_q, "tensor", swap)[None]
    received = [lax.ppermute(cut, "tensor", ring)]
    order_kv, order_q, first = [0], [0], counts[0]
    for step, (mask_kv, mask_q) in enumerate(zip(masks_kv, masks_q)):
        if step == 0:
            (cut,) = stage([], tokens, first, counts[1], [own_kv, own_q, received[0]])
        else:
            own_kv, own_q, cut = stage(
                [(own_kv, far_kv), (own_q, far_q)],
                tokens,
                first,
                counts[step + 1],
                [received[-1]],
            )
        first += counts[step + 1]
        far_kv = lax.ppermute(own_kv, PLANE, [(i, i ^ mask_kv) for i in range(plane)])
        far_q = lax.ppermute(own_q, PLANE, [(i, i ^ mask_q) for i in range(plane)])
        received.append(lax.ppermute(cut, "tensor", ring))
        order_kv = order_kv + [k ^ mask_kv for k in order_kv]
        order_q = order_q + [k ^ mask_q for k in order_q]
    o_share = o_weight.shape[0] // plane
    columns = [(z + k) % nz * cols for k in range(1, nz)]
    pieces = cut_pieces(in_plane * o_share, columns, o_weight, o_share, cols, own_q)
    moved = [lax.ppermute(p, "tensor", turn(k + 1)) for k, p in enumerate(pieces)]
    moved = jnp.stack(moved)
    gathered_o = lax.all_gather(moved, PLANE)
    far_kv, far_q = (order_kv, own_kv, far_kv), (order_q, own_q, far_q)

    sources = (within + half - jnp.arange(half, dtype=jnp.int32)) % half
    blocks = [[tokens], received]
    for _ in range(half - 2):
        blocks.append([lax.ppermute(part, "tensor", ring) for part in blocks[-1]])
    gains = in_gain.reshape(nz, 1, cols)
    x, sq = prep(side * half + sources, gains, blocks)

    place = jnp.reshape(in_plane, (1,))
    sent_kv = far_product(place, sources, x, sq, far_kv, True, [far_q[2], moved])
    got_kv = lax.ppermute(sent_kv, "tensor", swap)
    weights = (k_weight, value_weight, q_weight)

    sent_q = far_product(place, sources, x, sq, far_q, False, [sent_kv])
    got_q = lax.ppermute(sent_q, "tensor", swap)
    near = near_product(side * half + sources, x, weights, sent_q)
    cosine, sine = rotation_table(seq * rows + jnp.arange(rows, dtype=jnp.int32))
    ids = seg_ids[None, :]
    own_kv, sums = keys_values(near, got_kv, sq, ids, cosine, sine, sent_q, model)

    back = -(-(nseq * rows // 2 - 1) // rows)
    kv_blocks = [own_kv]
    for k in range(1, back + 1):
        earlier = [(i, i + k) for i in range(nseq - k)]
        kv_blocks.insert(0, lax.ppermute(own_kv, "seq", earlier))

    out = None
    seq_at = jnp.reshape(seq, (1,))
    context, own_sq = gathered_o, place
    for c in range(CHUNKS):
        context = attend(
            seq_at, near, got_q, sums, cosine, sine, ids, context, kv_blocks, c, model
        )
        if nz == 4:
            pairs = [(i, i ^ 1) for i in range(nz)]
            opposite = lax.ppermute(context, "tensor", swap)
            beside = lax.ppermute(context, "tensor", pairs)
            across = lax.ppermute(opposite, "tensor", pairs)
            contexts = [context, opposite, beside, across]
            order = [jnp.int32(1), 2 - 2 * (z % 2), 2 * (z % 2)]
        else:
            contexts = [context]
            contexts += [lax.ppermute(context, "tensor", turn(k)) for k in range(1, nz)]
            order = [jnp.int32(k) for k in range(nz - 1)]
        branch, own_sq = output_product(z, order, o_weight, gathered_o, contexts, own_sq)
        squares = [own_sq]
        squares += [lax.ppermute(own_sq, "tensor", turn(k)) for k in range(1, nz)]
        out = finish(tokens, branch, out_gain[None, :], squares, out, c, model)
    return out


def solution(mesh):
    return jax.shard_map(
        partial(per_device, sizes=dict(mesh.shape)),
        mesh=mesh,
        in_specs=(
            P(("groups", "seq"), "tensor"),
            P(("groups", "seq")),
            P(),
            P(None, "tensor"),
            P(None, "tensor"),
            P(None, "tensor"),
            P("tensor", None),
            P("tensor"),
        ),
        out_specs=P(("groups", "seq"), "tensor"),
        check_vma=False,
    )
```

```python
import math
from functools import partial

import jax
import jax.numpy as jnp
from jax import lax
from jax.experimental import pallas as pl
from jax.experimental.pallas import tpu as pltpu
from jax.sharding import PartitionSpec as P

HEAD_SIZE = 128
PLANE = ("groups", "seq")

epsilon = 1e-06
query_scale = 144.0 ** (-0.5)
rope_base = 10000.0
NEG = -1e30
Q_TILE = 128
K_TILE = 256
CHUNKS = 2
LANES = 128
TAIL = 16
F32, BF16 = jnp.float32, jnp.bfloat16
ANY = pl.BlockSpec(memory_space=pl.ANY)
HBM = pl.BlockSpec(memory_space=pltpu.HBM)
VMEM = pl.BlockSpec(memory_space=pltpu.VMEM)
DOCUMENTS = 8
PARAMS = pltpu.CompilerParams(vmem_limit_bytes=48 * 1024 * 1024)
ALL_VMEM = pltpu.CompilerParams(vmem_limit_bytes=62 * 1024 * 1024)


def shape(dims, dtype):
    return jax.ShapeDtypeStruct(dims, dtype)


def to_row(column):
    return jnp.broadcast_to(column, (column.shape[0], LANES)).T[0:1, :]


def to_column(row):
    return jnp.broadcast_to(row, (LANES, row.shape[1])).T


def rotation_table(token_places):
    half_dim = HEAD_SIZE // 2
    inverse = rope_base ** (-jnp.arange(half_dim, dtype=F32) / half_dim)
    angles = token_places.astype(F32)[:, None] * inverse[None, :]
    cosine, sine = jnp.cos(angles), jnp.sin(angles)
    return jnp.concatenate([cosine, cosine], 1), jnp.concatenate([-sine, sine], 1)


def rotate(vectors, cosine, sine):
    return vectors * cosine + pltpu.roll(vectors, HEAD_SIZE // 2, 1) * sine


def pack_kernel(at_ref, q_ref, k_ref, v_ref, x_ref, kv_out, q_out, x_out, sems):
    share, width = q_out.shape[0], k_ref.shape[1]
    rows = pl.ds(pl.multiple_of(at_ref[0] * share, TAIL), share)
    copies = [
        pltpu.make_async_copy(k_ref.at[rows], kv_out.at[:, pl.ds(0, width)], sems.at[0]),
        pltpu.make_async_copy(v_ref.at[rows], kv_out.at[:, pl.ds(width, width)], sems.at[1]),
        pltpu.make_async_copy(q_ref.at[rows], q_out, sems.at[2]),
        pltpu.make_async_copy(x_ref.at[pl.ds(0, x_out.shape[0])], x_out, sems.at[3]),
    ]
    for copy in copies:
        copy.start()
    for copy in copies:
        copy.wait()


def pack(at, q_weight, k_weight, v_weight, share, tokens, rows):
    kv_width = k_weight.shape[1] + v_weight.shape[1]
    dims = [(share, kv_width), (share, q_weight.shape[1]), (rows, tokens.shape[1])]
    return pl.pallas_call(
        pack_kernel,
        out_shape=tuple(shape(d, BF16) for d in dims),
        grid_spec=pltpu.PrefetchScalarGridSpec(
            num_scalar_prefetch=1,
            grid=(1,),
            in_specs=[HBM, HBM, HBM, HBM],
            out_specs=[pl.BlockSpec(d, lambda i, at: (0, 0)) for d in dims],
            scratch_shapes=[pltpu.SemaphoreType.DMA((4,))],
        ),
        compiler_params=ALL_VMEM,
        name="pack",
    )(at, q_weight, k_weight, v_weight, tokens)


def stage_kernel(*refs, pairs, first, count):
    outputs = pairs + (1 if count else 0)
    ins, outs, sems = refs[: -outputs - 1], refs[-outputs - 1 : -1], refs[-1]
    copies = []
    for p in range(pairs):
        held = ins[2 * p].shape[0]
        for side in range(2):
            there = outs[p].at[pl.ds(side * held, held)]
            copies.append(
                pltpu.make_async_copy(ins[2 * p + side], there, sems.at[len(copies)])
            )
    if count:
        rows = ins[2 * pairs].at[pl.ds(first, count)]
        copies.append(pltpu.make_async_copy(rows, outs[-1], sems.at[len(copies)]))
    for copy in copies:
        copy.start()
    for copy in copies:
        copy.wait()


def stage(joined, tokens, first, count, after):
    dims = [(2 * pair[0].shape[0],) + pair[0].shape[1:] for pair in joined]
    if count:
        dims.append((count, tokens.shape[1]))
    return pl.pallas_call(
        partial(stage_kernel, pairs=len(joined), first=first, count=count),
        out_shape=tuple(shape(d, BF16) for d in dims),
        in_specs=[ANY] * (2 * len(joined) + 1 + len(after)),
        scratch_shapes=[pltpu.SemaphoreType.DMA((2 * len(joined) + 1,))],
        compiler_params=PARAMS,
        name="stage",
    )(*[piece for pair in joined for piece in pair], tokens, *after)


def cut_kernel(at_ref, o_ref, after_ref, *rest):
    outs, sems = rest[:-1], rest[-1]
    copies = []
    for i, out in enumerate(outs):
        rows = pl.ds(pl.multiple_of(at_ref[0], TAIL), out.shape[0])
        columns = pl.ds(pl.multiple_of(at_ref[1 + i], LANES), out.shape[1])
        copies.append(pltpu.make_async_copy(o_ref.at[rows, columns], out, sems.at[i]))
    for copy in copies:
        copy.start()
    for copy in copies:
        copy.wait()


def cut_pieces(row, columns, o_weight, share, cols, after):
    if cols % LANES:
        return [lax.dynamic_slice(o_weight, (row, c), (share, cols)) for c in columns]
    return pl.pallas_call(
        cut_kernel,
        out_shape=tuple(shape((share, cols), BF16) for _ in columns),
        grid_spec=pltpu.PrefetchScalarGridSpec(
            num_scalar_prefetch=1,
            grid=(1,),
            in_specs=[ANY, ANY],
            out_specs=[VMEM for _ in columns],
            scratch_shapes=[pltpu.SemaphoreType.DMA((len(columns),))],
        ),
        compiler_params=PARAMS,
        name="cut",
    )(jnp.stack([row] + columns), o_weight, after)


def prep_kernel(src_ref, gain_ref, *rest, cuts):
    x_refs, (out_ref, sq_ref) = rest[:-2], rest[-2:]
    squares, at = [], 0
    for k, pieces in enumerate(cuts):
        column, row = [], 0
        for x_ref in x_refs[at : at + pieces]:
            x = x_ref[...].astype(F32)
            column.append(jnp.sum(x * x, axis=1, keepdims=True))
            out_ref[k, row : row + x.shape[0]] = (x * gain_ref[src_ref[k]]).astype(BF16)
            row += x.shape[0]
        squares.append(jnp.concatenate(column, axis=0))
        at += pieces
    sq_ref[...] = to_row(sum(squares[1:], squares[0]))


def prep(sources, gains, blocks):
    rows, cols = blocks[0][0].shape
    dims = (len(blocks), rows, cols)
    pieces = [piece for block in blocks for piece in block]
    return pl.pallas_call(
        partial(prep_kernel, cuts=[len(block) for block in blocks]),
        out_shape=(shape(dims, BF16), shape((1, rows), F32)),
        grid_spec=pltpu.PrefetchScalarGridSpec(
            num_scalar_prefetch=1,
            grid=(1,),
            in_specs=[pl.BlockSpec(gains.shape, lambda i, s: (0, 0, 0))]
            + [pl.BlockSpec(piece.shape, lambda i, s: (0, 0)) for piece in pieces],
            out_specs=[
                pl.BlockSpec(dims, lambda i, s: (0, 0, 0)),
                pl.BlockSpec((1, rows), lambda i, s: (0, 0)),
            ],
        ),
        compiler_params=PARAMS,
        name="prep",
    )(sources, gains, *pieces)


def far_kernel(place_ref, src_ref, x_ref, sq_ref, own_ref, got_ref, *rest, order, with_sq):
    out_ref, weight, sems = rest[-3:]
    held, share, width = own_ref.shape
    copies = []
    for i, mask in enumerate(order):
        piece = own_ref.at[i] if i < held else got_ref.at[i - held]
        row = pl.multiple_of((place_ref[0] ^ mask) * share, TAIL)
        there = weight.at[pl.ds(row, share)]
        copies.append(pltpu.make_async_copy(piece, there, sems.at[i]))
    for copy in copies:
        copy.start()
    for copy in copies:
        copy.wait()
    count, rows, cols = x_ref.shape
    total = None
    for k in range(count):
        row = pl.multiple_of(src_ref[k] * cols, TAIL)
        term = jnp.dot(x_ref[k], weight[pl.ds(row, cols), :], preferred_element_type=F32)
        total = term if total is None else total + term
    out_ref[:rows, :] = total.astype(BF16)
    if with_sq:
        sq = sq_ref[...]
        high = sq.astype(BF16).astype(F32)
        out_ref[rows:, :] = lines_of((high, sq - high), width)


def lines_of(rows, width):
    lines = []
    for row in rows:
        for at in range(0, row.shape[1], width):
            line = row[:, at : at + width]
            if line.shape[1] < width:
                rest = jnp.zeros((1, width - line.shape[1]), F32)
                line = jnp.concatenate([line, rest], axis=1)
            lines.append(line)
    lines.append(jnp.zeros((TAIL - len(lines), width), F32))
    return jnp.concatenate(lines, axis=0).astype(BF16)


def rows_of(tail, count, length):
    per_row = -(-length // tail.shape[1])
    rows = []
    for r in range(count):
        lines = [tail[r * per_row + i : r * per_row + i + 1, :] for i in range(per_row)]
        rows.append(jnp.concatenate(lines, axis=1)[:, :length])
    return rows


def far_product(place, sources, x, sq, gathered, with_sq, after):
    order, own, got = gathered
    _, share, width = own.shape
    rows = x.shape[1]
    out_rows = rows + (TAIL if with_sq else 0)
    return pl.pallas_call(
        partial(far_kernel, order=order, with_sq=with_sq),
        out_shape=shape((out_rows, width), BF16),
        grid_spec=pltpu.PrefetchScalarGridSpec(
            num_scalar_prefetch=2,
            grid=(1,),
            in_specs=[
                pl.BlockSpec(x.shape, lambda i, p, s: (0, 0, 0)),
                pl.BlockSpec((1, rows), lambda i, p, s: (0, 0)),
                ANY,
                ANY,
            ]
            + [ANY for _ in after],
            out_specs=pl.BlockSpec((out_rows, width), lambda i, p, s: (0, 0)),
            scratch_shapes=[
                pltpu.VMEM((len(order) * share, width), BF16),
                pltpu.SemaphoreType.DMA((len(order),)),
            ],
        ),
        compiler_params=PARAMS,
        name="far",
    )(place, sources, x, sq, own, got, *after)


def near_kernel(src_ref, x_ref, k_ref, v_ref, q_ref, after_ref, out_ref):
    x = x_ref[0]

    @pl.when(pl.program_id(0) == 0)
    def _():
        out_ref[...] = jnp.zeros_like(out_ref)

    column = 0
    for ref in (k_ref, v_ref, q_ref):
        at = slice(column, column + ref.shape[1])
        out_ref[:, at] += jnp.dot(x, ref[...], preferred_element_type=F32)
        column += ref.shape[1]


def near_product(sources, x, weights, after):
    count, chunk, cols = x.shape
    widths = [w.shape[1] for w in weights]
    return pl.pallas_call(
        near_kernel,
        out_shape=shape((chunk, sum(widths)), F32),
        grid_spec=pltpu.PrefetchScalarGridSpec(
            num_scalar_prefetch=1,
            grid=(count,),
            in_specs=[pl.BlockSpec((1, chunk, cols), lambda i, s: (i, 0, 0))]
            + [pl.BlockSpec((cols, w), lambda i, s: (s[i], 0)) for w in widths]
            + [ANY],
            out_specs=pl.BlockSpec((chunk, sum(widths)), lambda i, s: (0, 0)),
        ),
        compiler_params=PARAMS,
        name="near",
    )(sources, x, *weights, after)


def keys_kernel(
    near_ref, far_ref, sq_ref, id_ref, cos_ref, sin_ref, after_ref, k_out, vt_out, sum_ref, *, model
):
    rows = near_ref.shape[0]
    tail = far_ref[rows:, :].astype(F32)
    total = sum(rows_of(tail, 2, rows), sq_ref[...])
    factor = to_column(lax.rsqrt(total / model + epsilon))
    sum_ref[...] = total
    keys, values = slice(0, HEAD_SIZE), slice(HEAD_SIZE, 2 * HEAD_SIZE)
    part = (near_ref[:, keys] + far_ref[:rows, keys].astype(F32)) * factor
    k_out[:rows, :] = rotate(part, cos_ref[...], sin_ref[...]).astype(BF16)
    k_out[rows:, :] = lines_of((id_ref[...].astype(F32),), HEAD_SIZE)
    part = (near_ref[:, values] + far_ref[:rows, values].astype(F32)) * factor
    vt_out[...] = part.T.astype(BF16)


def keys_values(near, far, sq, ids, cosine, sine, after, model):
    rows, width = near.shape[0], far.shape[1]
    whole = lambda i: (0, 0)
    dims = [(rows + TAIL, HEAD_SIZE), (HEAD_SIZE, rows), (1, rows)]
    return pl.pallas_call(
        partial(keys_kernel, model=model),
        out_shape=tuple(shape(d, t) for d, t in zip(dims, (BF16, BF16, F32))),
        grid=(1,),
        in_specs=[pl.BlockSpec((rows, width), whole)]
        + [pl.BlockSpec(a.shape, whole) for a in (far, sq, ids, cosine, sine)]
        + [ANY],
        out_specs=[pl.BlockSpec(d, whole) for d in dims],
        compiler_params=PARAMS,
        name="keys",
    )(near, far, sq, ids, cosine, sine, after)


def attention_kernel(
    seq_ref, near_ref, far_ref, sum_ref, cos_ref, sin_ref, id_ref, after_ref, *rest, back, offset, model
):
    kv_refs, (out_ref, k_scr, vt_scr, count_scr) = rest[:-4], rest[-4:]
    part_rows = kv_refs[1].shape[1]
    group = near_ref.shape[1] // HEAD_SIZE
    tile = pl.program_id(0)

    @pl.when(tile == 0)
    def _():
        counts = [jnp.zeros((1, 1), F32) for _ in range(DOCUMENTS)]
        for b, (k_ref, vt_ref) in enumerate(zip(kv_refs[::2], kv_refs[1::2])):
            at = slice(b * part_rows, (b + 1) * part_rows)
            k_scr[at, :] = k_ref[:part_rows, :]
            vt_scr[:, at] = vt_ref[...]
            (ids,) = rows_of(k_ref[part_rows:, :].astype(F32), 1, part_rows)
            exists = b >= back - seq_ref[0]
            ids = jnp.where(exists, ids, -1.0)
            for d in range(DOCUMENTS):
                below = (ids < d).astype(F32)
                counts[d] = counts[d] + jnp.sum(below, axis=1, keepdims=True)
        for d in range(DOCUMENTS):
            count_scr[d : d + 1, :] = jnp.broadcast_to(counts[d], (1, LANES))

    scale = query_scale * math.log2(math.e)
    factor = to_column(lax.rsqrt(sum_ref[...] / model + epsilon) * scale)
    heads = []
    for c in range(0, group * HEAD_SIZE, HEAD_SIZE):
        at = slice(c, c + HEAD_SIZE)
        part = (near_ref[:, at] + far_ref[:, at].astype(F32)) * factor
        heads.append(rotate(part, cos_ref[...], sin_ref[...]).astype(BF16))
    q2 = jnp.concatenate(heads, axis=0)
    width = group * Q_TILE

    start = jnp.zeros((1, Q_TILE), F32)
    for d in range(DOCUMENTS):
        start = jnp.where(id_ref[...] == d, count_scr[d : d + 1, :], start)
    start = start.astype(jnp.int32)
    low = jnp.min(start) // K_TILE
    start = jnp.concatenate([start] * group, axis=1)
    first = back * part_rows + offset + tile * Q_TILE
    place = first + lax.broadcasted_iota(jnp.int32, (1, Q_TILE), 1)
    place = jnp.concatenate([place] * group, axis=1)

    def score(j):
        base = pl.multiple_of(j * K_TILE, K_TILE)
        return lax.dot_general(
            k_scr[pl.ds(base, K_TILE), :],
            q2,
            (((1,), (1,)), ((), ())),
            preferred_element_type=F32,
        )

    stop = (first + Q_TILE + K_TILE - 1) // K_TILE

    def step(j, state):
        scores, run_max, run_sum, acc = state
        following = score(jnp.minimum(j + 1, stop - 1))
        base = pl.multiple_of(j * K_TILE, K_TILE)
        key_pos = base + lax.broadcasted_iota(jnp.int32, (K_TILE, width), 0)
        allowed = (key_pos >= start) & (key_pos <= place)
        scores = jnp.where(allowed, scores, NEG)
        new_max = jnp.maximum(run_max, jnp.max(scores, axis=0, keepdims=True))
        expo = jnp.exp2(scores - new_max)
        factor = jnp.exp2(run_max - new_max)
        run_sum = run_sum * factor + jnp.sum(expo, axis=0, keepdims=True)
        acc = acc * factor + jnp.dot(
            vt_scr[:, pl.ds(base, K_TILE)], expo.astype(BF16), preferred_element_type=F32
        )
        return following, new_max, run_sum, acc

    state = (
        score(low),
        jnp.full((1, width), NEG, F32),
        jnp.zeros((1, width), F32),
        jnp.zeros((HEAD_SIZE, width), F32),
    )
    _, _, run_sum, acc = lax.fori_loop(low, stop, step, state)
    context = (acc / run_sum).T
    for g in range(group):
        out_ref[:, g * HEAD_SIZE : (g + 1) * HEAD_SIZE] = context[
            g * Q_TILE : (g + 1) * Q_TILE
        ].astype(BF16)


def attend(seq, near, far, sums, cosine, sine, ids, after, blocks, c, model):
    rows = near.shape[0] // CHUNKS
    width = far.shape[1]
    back = len(blocks) - 1
    tiles = rows // Q_TILE
    keys = len(blocks) * near.shape[0]
    blocks = [part for block in blocks for part in block]
    last = near.shape[1] // width - 1
    return pl.pallas_call(
        partial(attention_kernel, back=back, offset=c * rows, model=model),
        out_shape=shape((rows, width), BF16),
        grid_spec=pltpu.PrefetchScalarGridSpec(
            num_scalar_prefetch=1,
            grid=(tiles,),
            in_specs=[
                pl.BlockSpec((Q_TILE, width), lambda i, s: (c * tiles + i, last)),
                pl.BlockSpec((Q_TILE, width), lambda i, s: (c * tiles + i, 0)),
                pl.BlockSpec((1, Q_TILE), lambda i, s: (0, c * tiles + i)),
                pl.BlockSpec((Q_TILE, HEAD_SIZE), lambda i, s: (c * tiles + i, 0)),
                pl.BlockSpec((Q_TILE, HEAD_SIZE), lambda i, s: (c * tiles + i, 0)),
                pl.BlockSpec((1, Q_TILE), lambda i, s: (0, c * tiles + i)),
                ANY,
            ]
            + [pl.BlockSpec(b.shape, lambda i, s: (0, 0)) for b in blocks],
            out_specs=pl.BlockSpec((Q_TILE, width), lambda i, s: (i, 0)),
            scratch_shapes=[
                pltpu.VMEM((keys, HEAD_SIZE), BF16),
                pltpu.VMEM((HEAD_SIZE, keys), BF16),
                pltpu.VMEM((DOCUMENTS, LANES), F32),
            ],
        ),
        compiler_params=PARAMS,
        cost_estimate=pl.CostEstimate(
            flops=4 * rows * width * keys,
            bytes_accessed=4 * keys * width,
            transcendentals=rows * keys * width // HEAD_SIZE,
        ),
        name="attend",
    )(seq, near, far, sums, cosine, sine, ids, after, *blocks)


def output_kernel(at_ref, own_o_ref, o_ref, *rest):
    ctx_refs, (after_ref, out_ref, sq_ref, acc) = rest[:-4], rest[-4:]
    step = pl.program_id(0)
    plane, _, share, tile = o_ref.shape
    total = jnp.dot(ctx_refs[0][...], own_o_ref[...], preferred_element_type=F32)
    for i, ctx_ref in enumerate(ctx_refs[1:]):
        weight = o_ref[:, at_ref[1 + i]].reshape(plane * share, tile)
        total = total + jnp.dot(ctx_ref[...], weight, preferred_element_type=F32)
    out_ref[...] = total
    squares = jnp.sum(total * total, axis=1, keepdims=True)
    squares = jnp.broadcast_to(squares, acc.shape)

    @pl.when(step == 0)
    def _():
        acc[...] = squares

    @pl.when(step > 0)
    def _():
        acc[...] += squares

    @pl.when(step == pl.num_programs(0) - 1)
    def _():
        sq_ref[...] = acc[...].T[0:1, :]


def output_product(column, order, o_weight, gathered, contexts, after):
    chunk, width = contexts[0].shape
    plane, others, share, cols = gathered.shape
    tiles = 3 if cols % (3 * LANES) == 0 else 1
    tile = cols // tiles
    if cols % LANES:
        o_weight = lax.dynamic_slice_in_dim(o_weight, column * cols, cols, axis=1)
        column = jnp.int32(0)
    return pl.pallas_call(
        output_kernel,
        out_shape=(shape((chunk, cols), F32), shape((1, chunk), F32)),
        grid_spec=pltpu.PrefetchScalarGridSpec(
            num_scalar_prefetch=1,
            grid=(tiles,),
            in_specs=[
                pl.BlockSpec((width, tile), lambda i, at: (0, at[0] * tiles + i)),
                pl.BlockSpec((plane, others, share, tile), lambda i, at: (0, 0, 0, i)),
            ]
            + [pl.BlockSpec((chunk, width), lambda i, at: (0, 0)) for _ in contexts]
            + [ANY],
            out_specs=[
                pl.BlockSpec((chunk, tile), lambda i, at: (0, i)),
                pl.BlockSpec((1, chunk), lambda i, at: (0, 0)),
            ],
            scratch_shapes=[pltpu.VMEM((chunk, LANES), F32)],
        ),
        compiler_params=PARAMS,
        name="output",
    )(jnp.stack([column] + order), o_weight, gathered, *contexts, after)


def final_kernel(token_ref, branch_ref, gain_ref, *rest, model, others):
    sq_refs, out_ref = rest[:others], rest[-1]
    total = sq_refs[0][...]
    for sq_ref in sq_refs[1:]:
        total = total + sq_ref[...]
    factor = to_column(lax.rsqrt(total / model + epsilon))[:, 0:1]
    out = token_ref[...].astype(F32) + branch_ref[...] * factor * gain_ref[...]
    out_ref[...] = out.astype(BF16)


def finish(tokens, branch, out_gain, sums, previous, c, model):
    chunk, cols = branch.shape
    tiles = chunk // Q_TILE
    in_specs = [
        pl.BlockSpec((Q_TILE, cols), lambda i: (c * tiles + i, 0)),
        pl.BlockSpec((Q_TILE, cols), lambda i: (i, 0)),
        pl.BlockSpec((1, cols), lambda i: (0, 0)),
    ]
    in_specs += [pl.BlockSpec((1, Q_TILE), lambda i: (0, i)) for _ in sums]
    args = [tokens, branch, out_gain, *sums]
    aliases = {}
    if previous is not None:
        aliases = {len(args): 0}
        in_specs.append(ANY)
        args.append(previous)
    return pl.pallas_call(
        partial(final_kernel, model=model, others=len(sums)),
        out_shape=shape(tokens.shape, BF16),
        grid=(tiles,),
        in_specs=in_specs,
        out_specs=pl.BlockSpec((Q_TILE, cols), lambda i: (c * tiles + i, 0)),
        input_output_aliases=aliases,
        compiler_params=PARAMS,
        name="finish",
    )(*args)


def per_device(
    tokens, seg_ids, in_gain, q_weight, k_weight, value_weight, o_weight, out_gain, *, sizes
):
    rows, cols = tokens.shape
    model = in_gain.shape[0]
    nz, nseq = sizes["tensor"], sizes["seq"]
    plane = nseq * sizes["groups"]
    z = lax.axis_index("tensor")
    seq = lax.axis_index("seq")
    in_plane = lax.axis_index(PLANE)
    half = nz // 2
    side, within = z // half, z % half
    half_rows = half * cols

    ring = [(i, i // half * half + (i + 1) % half) for i in range(nz)]
    swap = [(i, (i + half) % nz) for i in range(nz)]
    turn = lambda k: [(i, (i + k) % nz) for i in range(nz)]
    seq_bits = [1 << b for b in range(1, nseq.bit_length() - 1)]
    group_bits = [nseq << b for b in range(sizes["groups"].bit_length() - 1)]

    share = half_rows // plane
    at = jnp.reshape((1 - side) * plane + in_plane, (1,))
    inner = seq_bits + group_bits
    masks_kv, masks_q = inner + [1], inner[::-1] + [1]
    steps = len(masks_kv)
    piece = rows // (steps + 1) // TAIL * TAIL
    counts = [rows - steps * piece] + [piece] * steps
    if counts[0] > piece:
        counts = [rows - steps * (piece + TAIL)] + [piece + TAIL] * steps
    packed_kv, packed_q, cut = pack(
        at, q_weight, k_weight, value_weight, share, tokens, counts[0]
    )
    own_kv = lax.ppermute(packed_kv, "tensor", swap)[None]
    own_q = lax.ppermute(packed_q, "tensor", swap)[None]
    received = [lax.ppermute(cut, "tensor", ring)]
    order_kv, order_q, first = [0], [0], counts[0]
    for step, (mask_kv, mask_q) in enumerate(zip(masks_kv, masks_q)):
        if step == 0:
            (cut,) = stage([], tokens, first, counts[1], [own_kv, own_q, received[0]])
        else:
            own_kv, own_q, cut = stage(
                [(own_kv, far_kv), (own_q, far_q)],
                tokens,
                first,
                counts[step + 1],
                received[-2:-1],
            )
        first += counts[step + 1]
        far_kv = lax.ppermute(own_kv, PLANE, [(i, i ^ mask_kv) for i in range(plane)])
        far_q = lax.ppermute(own_q, PLANE, [(i, i ^ mask_q) for i in range(plane)])
        received.append(lax.ppermute(cut, "tensor", ring))
        order_kv = order_kv + [k ^ mask_kv for k in order_kv]
        order_q = order_q + [k ^ mask_q for k in order_q]
    far_kv, far_q = (order_kv, own_kv, far_kv), (order_q, own_q, far_q)

    sources = (within + half - jnp.arange(half, dtype=jnp.int32)) % half
    blocks = [[tokens], received]
    for _ in range(half - 2):
        blocks.append([lax.ppermute(part, "tensor", ring) for part in blocks[-1]])
    gains = in_gain.reshape(nz, 1, cols)
    x, sq = prep(side * half + sources, gains, blocks)

    place = jnp.reshape(in_plane, (1,))
    sent_kv = far_product(place, sources, x, sq, far_kv, True, [far_q[2]])
    got_kv = lax.ppermute(sent_kv, "tensor", swap)
    weights = (k_weight, value_weight, q_weight)

    sent_q = far_product(place, sources, x, sq, far_q, False, [sent_kv])
    got_q = lax.ppermute(sent_q, "tensor", swap)
    near = near_product(side * half + sources, x, weights, sent_q)
    cosine, sine = rotation_table(seq * rows + jnp.arange(rows, dtype=jnp.int32))
    ids = seg_ids[None, :]
    *own_kv, sums = keys_values(near, got_kv, sq, ids, cosine, sine, sent_q, model)

    back = -(-(nseq * rows // 2 - 1) // rows)
    kv_blocks = [own_kv]
    for k in range(1, back + 1):
        earlier = [(i, i + k) for i in range(nseq - k)]
        kv_blocks.insert(0, [lax.ppermute(part, "seq", earlier) for part in own_kv])

    o_share = o_weight.shape[0] // plane
    columns = [(z + k) % nz * cols for k in range(1, nz)]
    pieces = cut_pieces(in_plane * o_share, columns, o_weight, o_share, cols, own_kv[0])
    moved = [lax.ppermute(p, "tensor", turn(k + 1)) for k, p in enumerate(pieces)]
    moved = jnp.stack(moved)
    gathered_o = lax.all_gather(moved, PLANE)

    out = None
    seq_at = jnp.reshape(seq, (1,))
    context, own_sq = moved, place
    for c in range(CHUNKS):
        context = attend(
            seq_at, near, got_q, sums, cosine, sine, ids, context, kv_blocks, c, model
        )
        if nz == 4:
            pairs = [(i, i ^ 1) for i in range(nz)]
            opposite = lax.ppermute(context, "tensor", swap)
            beside = lax.ppermute(context, "tensor", pairs)
            across = lax.ppermute(opposite, "tensor", pairs)
            contexts = [context, opposite, beside, across]
            order = [jnp.int32(1), 2 - 2 * (z % 2), 2 * (z % 2)]
        else:
            contexts = [context]
            contexts += [lax.ppermute(context, "tensor", turn(k)) for k in range(1, nz)]
            order = [jnp.int32(k) for k in range(nz - 1)]
        branch, own_sq = output_product(z, order, o_weight, gathered_o, contexts, own_sq)
        squares = [own_sq]
        squares += [lax.ppermute(own_sq, "tensor", turn(k)) for k in range(1, nz)]
        out = finish(tokens, branch, out_gain[None, :], squares, out, c, model)
    return out


def solution(mesh):
    return jax.shard_map(
        partial(per_device, sizes=dict(mesh.shape)),
        mesh=mesh,
        in_specs=(
            P(("groups", "seq"), "tensor"),
            P(("groups", "seq")),
            P(),
            P(None, "tensor"),
            P(None, "tensor"),
            P(None, "tensor"),
            P("tensor", None),
            P("tensor"),
        ),
        out_specs=P(("groups", "seq"), "tensor"),
        check_vma=False,
    )
```

```python
import math
from functools import partial

import jax
import jax.numpy as jnp
from jax import lax
from jax.experimental import pallas as pl
from jax.experimental.pallas import tpu as pltpu
from jax.sharding import PartitionSpec as P

HEAD_SIZE = 128
PLANE = ("groups", "seq")

epsilon = 1e-06
query_scale = 144.0 ** (-0.5)
rope_base = 10000.0
NEG = -1e30
Q_TILE = 128
K_TILE = 256
CHUNKS = 2
LANES = 128
TAIL = 16
F32, BF16 = jnp.float32, jnp.bfloat16
ANY = pl.BlockSpec(memory_space=pl.ANY)
HBM = pl.BlockSpec(memory_space=pltpu.HBM)
VMEM = pl.BlockSpec(memory_space=pltpu.VMEM)
DOCUMENTS = 8
PARAMS = pltpu.CompilerParams(vmem_limit_bytes=48 * 1024 * 1024)
ALL_VMEM = pltpu.CompilerParams(vmem_limit_bytes=62 * 1024 * 1024)


def shape(dims, dtype):
    return jax.ShapeDtypeStruct(dims, dtype)


def to_row(column):
    return jnp.broadcast_to(column, (column.shape[0], LANES)).T[0:1, :]


def to_column(row):
    return jnp.broadcast_to(row, (LANES, row.shape[1])).T


def rotation_table(token_places):
    half_dim = HEAD_SIZE // 2
    inverse = rope_base ** (-jnp.arange(half_dim, dtype=F32) / half_dim)
    angles = token_places.astype(F32)[:, None] * inverse[None, :]
    cosine, sine = jnp.cos(angles), jnp.sin(angles)
    return jnp.concatenate([cosine, cosine], 1), jnp.concatenate([-sine, sine], 1)


def rotate(vectors, cosine, sine):
    return vectors * cosine + pltpu.roll(vectors, HEAD_SIZE // 2, 1) * sine


def pack_kernel(at_ref, q_ref, k_ref, v_ref, x_ref, kv_out, q_out, x_out, sems):
    share, width = q_out.shape[0], k_ref.shape[1]
    rows = pl.ds(pl.multiple_of(at_ref[0] * share, TAIL), share)
    copies = [
        pltpu.make_async_copy(k_ref.at[rows], kv_out.at[:, pl.ds(0, width)], sems.at[0]),
        pltpu.make_async_copy(v_ref.at[rows], kv_out.at[:, pl.ds(width, width)], sems.at[1]),
        pltpu.make_async_copy(q_ref.at[rows], q_out, sems.at[2]),
        pltpu.make_async_copy(x_ref.at[pl.ds(0, x_out.shape[0])], x_out, sems.at[3]),
    ]
    for copy in copies:
        copy.start()
    for copy in copies:
        copy.wait()


def pack(at, q_weight, k_weight, v_weight, share, tokens, rows):
    kv_width = k_weight.shape[1] + v_weight.shape[1]
    dims = [(share, kv_width), (share, q_weight.shape[1]), (rows, tokens.shape[1])]
    return pl.pallas_call(
        pack_kernel,
        out_shape=tuple(shape(d, BF16) for d in dims),
        grid_spec=pltpu.PrefetchScalarGridSpec(
            num_scalar_prefetch=1,
            grid=(1,),
            in_specs=[HBM, HBM, HBM, HBM],
            out_specs=[pl.BlockSpec(d, lambda i, at: (0, 0)) for d in dims],
            scratch_shapes=[pltpu.SemaphoreType.DMA((4,))],
        ),
        compiler_params=ALL_VMEM,
        name="pack",
    )(at, q_weight, k_weight, v_weight, tokens)


def stage_kernel(*refs, pairs, first, count):
    outputs = pairs + (1 if count else 0)
    ins, outs, sems = refs[: -outputs - 1], refs[-outputs - 1 : -1], refs[-1]
    copies = []
    for p in range(pairs):
        held = ins[2 * p].shape[0]
        for side in range(2):
            there = outs[p].at[pl.ds(side * held, held)]
            copies.append(
                pltpu.make_async_copy(ins[2 * p + side], there, sems.at[len(copies)])
            )
    if count:
        rows = ins[2 * pairs].at[pl.ds(first, count)]
        copies.append(pltpu.make_async_copy(rows, outs[-1], sems.at[len(copies)]))
    for copy in copies:
        copy.start()
    for copy in copies:
        copy.wait()


def stage(joined, tokens, first, count, after):
    dims = [(2 * pair[0].shape[0],) + pair[0].shape[1:] for pair in joined]
    if count:
        dims.append((count, tokens.shape[1]))
    return pl.pallas_call(
        partial(stage_kernel, pairs=len(joined), first=first, count=count),
        out_shape=tuple(shape(d, BF16) for d in dims),
        in_specs=[ANY] * (2 * len(joined) + 1 + len(after)),
        scratch_shapes=[pltpu.SemaphoreType.DMA((2 * len(joined) + 1,))],
        compiler_params=PARAMS,
        name="stage",
    )(*[piece for pair in joined for piece in pair], tokens, *after)


def cut_kernel(at_ref, o_ref, after_ref, *rest):
    outs, sems = rest[:-1], rest[-1]
    copies = []
    for i, out in enumerate(outs):
        rows = pl.ds(pl.multiple_of(at_ref[0], TAIL), out.shape[0])
        columns = pl.ds(pl.multiple_of(at_ref[1 + i], LANES), out.shape[1])
        copies.append(pltpu.make_async_copy(o_ref.at[rows, columns], out, sems.at[i]))
    for copy in copies:
        copy.start()
    for copy in copies:
        copy.wait()


def cut_pieces(row, columns, o_weight, share, cols, after):
    if cols % LANES:
        return [lax.dynamic_slice(o_weight, (row, c), (share, cols)) for c in columns]
    return pl.pallas_call(
        cut_kernel,
        out_shape=tuple(shape((share, cols), BF16) for _ in columns),
        grid_spec=pltpu.PrefetchScalarGridSpec(
            num_scalar_prefetch=1,
            grid=(1,),
            in_specs=[ANY, ANY],
            out_specs=[VMEM for _ in columns],
            scratch_shapes=[pltpu.SemaphoreType.DMA((len(columns),))],
        ),
        compiler_params=PARAMS,
        name="cut",
    )(jnp.stack([row] + columns), o_weight, after)


def lay_kernel(place_ref, own_ref, got_ref, out_ref, sems, *, order):
    held, others, share, _ = own_ref.shape
    copies = []
    for i, mask in enumerate(order):
        piece = own_ref.at[i] if i < held else got_ref.at[i - held]
        row = pl.multiple_of((place_ref[0] ^ mask) * share, TAIL)
        there = out_ref.at[:, pl.ds(row, share)]
        copies.append(pltpu.make_async_copy(piece, there, sems.at[i]))
    for copy in copies:
        copy.start()
    for copy in copies:
        copy.wait()


def lay_pieces(place, order, own, got):
    _, others, share, cols = own.shape
    dims = (others, len(order) * share, cols)
    return pl.pallas_call(
        partial(lay_kernel, order=order),
        out_shape=shape(dims, BF16),
        grid_spec=pltpu.PrefetchScalarGridSpec(
            num_scalar_prefetch=1,
            grid=(1,),
            in_specs=[ANY, ANY],
            out_specs=pl.BlockSpec(dims, lambda i, p: (0, 0, 0)),
            scratch_shapes=[pltpu.SemaphoreType.DMA((len(order),))],
        ),
        compiler_params=PARAMS,
        name="lay",
    )(place, own, got)


def place_weights(place_ref, own_ref, got_ref, weight, sems, order):
    held, share, _ = own_ref.shape
    copies = []
    for i, mask in enumerate(order):
        piece = own_ref.at[i] if i < held else got_ref.at[i - held]
        row = pl.multiple_of((place_ref[0] ^ mask) * share, TAIL)
        there = weight.at[pl.ds(row, share)]
        copies.append(pltpu.make_async_copy(piece, there, sems.at[i]))
    for copy in copies:
        copy.start()
    return copies


def far_sum(src_ref, x_ref, weight):
    count, _, cols = x_ref.shape
    total = None
    for k in range(count):
        row = pl.multiple_of(src_ref[k] * cols, TAIL)
        term = jnp.dot(x_ref[k], weight[pl.ds(row, cols), :], preferred_element_type=F32)
        total = term if total is None else total + term
    return total


def far_kv_kernel(place_ref, src_ref, gain_ref, own_ref, got_ref, *rest, order, cuts):
    x_refs, (out_ref, x_out, sq_ref, weight, sems) = rest[: sum(cuts)], rest[-5:]
    copies = place_weights(place_ref, own_ref, got_ref, weight, sems, order)
    rows = x_out.shape[1]
    columns, at = [], 0
    for k, pieces in enumerate(cuts):
        gain = gain_ref[place_ref[1] + src_ref[k]]
        column, row = [], 0
        for x_ref in x_refs[at : at + pieces]:
            x = x_ref[...].astype(F32)
            column.append(jnp.sum(x * x, axis=1, keepdims=True))
            x_out[k, row : row + x.shape[0]] = (x * gain).astype(BF16)
            row += x.shape[0]
        columns.append(jnp.concatenate(column, axis=0))
        at += pieces
    sq = to_row(sum(columns[1:], columns[0]))
    sq_ref[...] = sq
    for copy in copies:
        copy.wait()
    out_ref[:rows, :] = far_sum(src_ref, x_out, weight).astype(BF16)
    high = sq.astype(BF16).astype(F32)
    out_ref[rows:, :] = lines_of((high, sq - high), out_ref.shape[1])


def far_kv_product(place, sources, gains, blocks, gathered, after):
    order, own, got = gathered
    _, share, width = own.shape
    rows, cols = blocks[0][0].shape
    pieces = [piece for block in blocks for piece in block]
    dims = [(rows + TAIL, width), (len(blocks), rows, cols), (1, rows)]
    whole = lambda d: pl.BlockSpec(d, lambda i, p, s: (0,) * len(d))
    return pl.pallas_call(
        partial(far_kv_kernel, order=order, cuts=[len(block) for block in blocks]),
        out_shape=tuple(shape(d, t) for d, t in zip(dims, (BF16, BF16, F32))),
        grid_spec=pltpu.PrefetchScalarGridSpec(
            num_scalar_prefetch=2,
            grid=(1,),
            in_specs=[whole(gains.shape), ANY, ANY]
            + [whole(piece.shape) for piece in pieces]
            + [ANY for _ in after],
            out_specs=[whole(d) for d in dims],
            scratch_shapes=[
                pltpu.VMEM((len(order) * share, width), BF16),
                pltpu.SemaphoreType.DMA((len(order),)),
            ],
        ),
        compiler_params=PARAMS,
        name="far_kv",
    )(place, sources, gains, own, got, *pieces, *after)


def far_kernel(place_ref, src_ref, x_ref, own_ref, got_ref, *rest, order):
    out_ref, weight, sems = rest[-3:]
    for copy in place_weights(place_ref, own_ref, got_ref, weight, sems, order):
        copy.wait()
    out_ref[...] = far_sum(src_ref, x_ref, weight).astype(BF16)


def lines_of(rows, width):
    lines = []
    for row in rows:
        for at in range(0, row.shape[1], width):
            line = row[:, at : at + width]
            if line.shape[1] < width:
                rest = jnp.zeros((1, width - line.shape[1]), F32)
                line = jnp.concatenate([line, rest], axis=1)
            lines.append(line)
    lines.append(jnp.zeros((TAIL - len(lines), width), F32))
    return jnp.concatenate(lines, axis=0).astype(BF16)


def rows_of(tail, count, length):
    per_row = -(-length // tail.shape[1])
    rows = []
    for r in range(count):
        lines = [tail[r * per_row + i : r * per_row + i + 1, :] for i in range(per_row)]
        rows.append(jnp.concatenate(lines, axis=1)[:, :length])
    return rows


def far_product(place, sources, x, gathered, after):
    order, own, got = gathered
    _, share, width = own.shape
    rows = x.shape[1]
    return pl.pallas_call(
        partial(far_kernel, order=order),
        out_shape=shape((rows, width), BF16),
        grid_spec=pltpu.PrefetchScalarGridSpec(
            num_scalar_prefetch=2,
            grid=(1,),
            in_specs=[pl.BlockSpec(x.shape, lambda i, p, s: (0, 0, 0)), ANY, ANY]
            + [ANY for _ in after],
            out_specs=pl.BlockSpec((rows, width), lambda i, p, s: (0, 0)),
            scratch_shapes=[
                pltpu.VMEM((len(order) * share, width), BF16),
                pltpu.SemaphoreType.DMA((len(order),)),
            ],
        ),
        compiler_params=PARAMS,
        name="far",
    )(place, sources, x, own, got, *after)


def near_kernel(src_ref, x_ref, k_ref, v_ref, q_ref, after_ref, out_ref):
    x = x_ref[0]

    @pl.when(pl.program_id(0) == 0)
    def _():
        out_ref[...] = jnp.zeros_like(out_ref)

    column = 0
    for ref in (k_ref, v_ref, q_ref):
        at = slice(column, column + ref.shape[1])
        out_ref[:, at] += jnp.dot(x, ref[...], preferred_element_type=F32)
        column += ref.shape[1]


def near_product(sources, x, weights, after):
    count, chunk, cols = x.shape
    widths = [w.shape[1] for w in weights]
    return pl.pallas_call(
        near_kernel,
        out_shape=shape((chunk, sum(widths)), F32),
        grid_spec=pltpu.PrefetchScalarGridSpec(
            num_scalar_prefetch=1,
            grid=(count,),
            in_specs=[pl.BlockSpec((1, chunk, cols), lambda i, s: (i, 0, 0))]
            + [pl.BlockSpec((cols, w), lambda i, s: (s[i], 0)) for w in widths]
            + [ANY],
            out_specs=pl.BlockSpec((chunk, sum(widths)), lambda i, s: (0, 0)),
        ),
        compiler_params=PARAMS,
        name="near",
    )(sources, x, *weights, after)


def keys_kernel(
    near_ref, far_ref, sq_ref, id_ref, cos_ref, sin_ref, *rest, model
):
    k_out, vt_out, sum_ref = rest[-3:]
    rows = near_ref.shape[0]
    tail = far_ref[rows:, :].astype(F32)
    total = sum(rows_of(tail, 2, rows), sq_ref[...])
    factor = to_column(lax.rsqrt(total / model + epsilon))
    sum_ref[...] = total
    keys, values = slice(0, HEAD_SIZE), slice(HEAD_SIZE, 2 * HEAD_SIZE)
    part = (near_ref[:, keys] + far_ref[:rows, keys].astype(F32)) * factor
    k_out[:rows, :] = rotate(part, cos_ref[...], sin_ref[...]).astype(BF16)
    k_out[rows:, :] = lines_of((id_ref[...].astype(F32),), HEAD_SIZE)
    part = (near_ref[:, values] + far_ref[:rows, values].astype(F32)) * factor
    vt_out[...] = part.T.astype(BF16)


def keys_values(near, far, sq, ids, cosine, sine, after, model):
    rows, width = near.shape[0], far.shape[1]
    whole = lambda i: (0, 0)
    dims = [(rows + TAIL, HEAD_SIZE), (HEAD_SIZE, rows), (1, rows)]
    return pl.pallas_call(
        partial(keys_kernel, model=model),
        out_shape=tuple(shape(d, t) for d, t in zip(dims, (BF16, BF16, F32))),
        grid=(1,),
        in_specs=[pl.BlockSpec((rows, width), whole)]
        + [pl.BlockSpec(a.shape, whole) for a in (far, sq, ids, cosine, sine)]
        + [ANY for _ in after],
        out_specs=[pl.BlockSpec(d, whole) for d in dims],
        compiler_params=PARAMS,
        name="keys",
    )(near, far, sq, ids, cosine, sine, *after)


def attention_kernel(
    seq_ref, near_ref, far_ref, sum_ref, cos_ref, sin_ref, id_ref, after_ref, *rest, back, offset, model
):
    kv_refs, (out_ref, k_scr, vt_scr, count_scr) = rest[:-4], rest[-4:]
    part_rows = kv_refs[1].shape[1]
    group = near_ref.shape[1] // HEAD_SIZE
    tile = pl.program_id(0)

    @pl.when(tile == 0)
    def _():
        counts = [jnp.zeros((1, 1), F32) for _ in range(DOCUMENTS)]
        for b, (k_ref, vt_ref) in enumerate(zip(kv_refs[::2], kv_refs[1::2])):
            at = slice(b * part_rows, (b + 1) * part_rows)
            k_scr[at, :] = k_ref[:part_rows, :]
            vt_scr[:, at] = vt_ref[...]
            (ids,) = rows_of(k_ref[part_rows:, :].astype(F32), 1, part_rows)
            exists = b >= back - seq_ref[0]
            ids = jnp.where(exists, ids, -1.0)
            for d in range(DOCUMENTS):
                below = (ids < d).astype(F32)
                counts[d] = counts[d] + jnp.sum(below, axis=1, keepdims=True)
        for d in range(DOCUMENTS):
            count_scr[d : d + 1, :] = jnp.broadcast_to(counts[d], (1, LANES))

    scale = query_scale * math.log2(math.e)
    factor = to_column(lax.rsqrt(sum_ref[...] / model + epsilon) * scale)
    heads = []
    for c in range(0, group * HEAD_SIZE, HEAD_SIZE):
        at = slice(c, c + HEAD_SIZE)
        part = (near_ref[:, at] + far_ref[:, at].astype(F32)) * factor
        heads.append(rotate(part, cos_ref[...], sin_ref[...]).astype(BF16))
    q2 = jnp.concatenate(heads, axis=0)
    width = group * Q_TILE

    start = jnp.zeros((1, Q_TILE), F32)
    for d in range(DOCUMENTS):
        start = jnp.where(id_ref[...] == d, count_scr[d : d + 1, :], start)
    start = start.astype(jnp.int32)
    low = jnp.min(start) // K_TILE
    start = jnp.concatenate([start] * group, axis=1)
    first = back * part_rows + offset + tile * Q_TILE
    place = first + lax.broadcasted_iota(jnp.int32, (1, Q_TILE), 1)
    place = jnp.concatenate([place] * group, axis=1)

    def score(j):
        base = pl.multiple_of(j * K_TILE, K_TILE)
        return lax.dot_general(
            k_scr[pl.ds(base, K_TILE), :],
            q2,
            (((1,), (1,)), ((), ())),
            preferred_element_type=F32,
        )

    stop = (first + Q_TILE + K_TILE - 1) // K_TILE

    def step(j, state):
        scores, run_max, run_sum, acc = state
        following = score(jnp.minimum(j + 1, stop - 1))
        base = pl.multiple_of(j * K_TILE, K_TILE)
        key_pos = base + lax.broadcasted_iota(jnp.int32, (K_TILE, width), 0)
        allowed = (key_pos >= start) & (key_pos <= place)
        scores = jnp.where(allowed, scores, NEG)
        new_max = jnp.maximum(run_max, jnp.max(scores, axis=0, keepdims=True))
        expo = jnp.exp2(scores - new_max)
        factor = jnp.exp2(run_max - new_max)
        run_sum = run_sum * factor + jnp.sum(expo, axis=0, keepdims=True)
        acc = acc * factor + jnp.dot(
            vt_scr[:, pl.ds(base, K_TILE)], expo.astype(BF16), preferred_element_type=F32
        )
        return following, new_max, run_sum, acc

    state = (
        score(low),
        jnp.full((1, width), NEG, F32),
        jnp.zeros((1, width), F32),
        jnp.zeros((HEAD_SIZE, width), F32),
    )
    _, _, run_sum, acc = lax.fori_loop(low, stop, step, state)
    context = (acc / run_sum).T
    for g in range(group):
        out_ref[:, g * HEAD_SIZE : (g + 1) * HEAD_SIZE] = context[
            g * Q_TILE : (g + 1) * Q_TILE
        ].astype(BF16)


def attend(seq, near, far, sums, cosine, sine, ids, after, blocks, c, model):
    rows = near.shape[0] // CHUNKS
    width = far.shape[1]
    back = len(blocks) - 1
    tiles = rows // Q_TILE
    keys = len(blocks) * near.shape[0]
    blocks = [part for block in blocks for part in block]
    last = near.shape[1] // width - 1
    return pl.pallas_call(
        partial(attention_kernel, back=back, offset=c * rows, model=model),
        out_shape=shape((rows, width), BF16),
        grid_spec=pltpu.PrefetchScalarGridSpec(
            num_scalar_prefetch=1,
            grid=(tiles,),
            in_specs=[
                pl.BlockSpec((Q_TILE, width), lambda i, s: (c * tiles + i, last)),
                pl.BlockSpec((Q_TILE, width), lambda i, s: (c * tiles + i, 0)),
                pl.BlockSpec((1, Q_TILE), lambda i, s: (0, c * tiles + i)),
                pl.BlockSpec((Q_TILE, HEAD_SIZE), lambda i, s: (c * tiles + i, 0)),
                pl.BlockSpec((Q_TILE, HEAD_SIZE), lambda i, s: (c * tiles + i, 0)),
                pl.BlockSpec((1, Q_TILE), lambda i, s: (0, c * tiles + i)),
                ANY,
            ]
            + [pl.BlockSpec(b.shape, lambda i, s: (0, 0)) for b in blocks],
            out_specs=pl.BlockSpec((Q_TILE, width), lambda i, s: (i, 0)),
            scratch_shapes=[
                pltpu.VMEM((keys, HEAD_SIZE), BF16),
                pltpu.VMEM((HEAD_SIZE, keys), BF16),
                pltpu.VMEM((DOCUMENTS, LANES), F32),
            ],
        ),
        compiler_params=PARAMS,
        cost_estimate=pl.CostEstimate(
            flops=4 * rows * width * keys,
            bytes_accessed=4 * keys * width,
            transcendentals=rows * keys * width // HEAD_SIZE,
        ),
        name="attend",
    )(seq, near, far, sums, cosine, sine, ids, after, *blocks)


def output_kernel(at_ref, own_o_ref, o_ref, *rest):
    ctx_refs, (after_ref, out_ref, sq_ref, acc) = rest[:-4], rest[-4:]
    step = pl.program_id(0)
    total = jnp.dot(ctx_refs[0][...], own_o_ref[...], preferred_element_type=F32)
    for i, ctx_ref in enumerate(ctx_refs[1:]):
        weight = o_ref[at_ref[1 + i]]
        total = total + jnp.dot(ctx_ref[...], weight, preferred_element_type=F32)
    out_ref[...] = total
    squares = jnp.sum(total * total, axis=1, keepdims=True)
    squares = jnp.broadcast_to(squares, acc.shape)

    @pl.when(step == 0)
    def _():
        acc[...] = squares

    @pl.when(step > 0)
    def _():
        acc[...] += squares

    @pl.when(step == pl.num_programs(0) - 1)
    def _():
        sq_ref[...] = acc[...].T[0:1, :]


def output_product(column, order, o_weight, gathered, contexts, after):
    chunk, width = contexts[0].shape
    others, _, cols = gathered.shape
    tiles = 3 if cols % (3 * LANES) == 0 else 1
    tile = cols // tiles
    if cols % LANES:
        o_weight = lax.dynamic_slice_in_dim(o_weight, column * cols, cols, axis=1)
        column = jnp.int32(0)
    return pl.pallas_call(
        output_kernel,
        out_shape=(shape((chunk, cols), F32), shape((1, chunk), F32)),
        grid_spec=pltpu.PrefetchScalarGridSpec(
            num_scalar_prefetch=1,
            grid=(tiles,),
            in_specs=[
                pl.BlockSpec((width, tile), lambda i, at: (0, at[0] * tiles + i)),
                pl.BlockSpec((others, width, tile), lambda i, at: (0, 0, i)),
            ]
            + [pl.BlockSpec((chunk, width), lambda i, at: (0, 0)) for _ in contexts]
            + [ANY],
            out_specs=[
                pl.BlockSpec((chunk, tile), lambda i, at: (0, i)),
                pl.BlockSpec((1, chunk), lambda i, at: (0, 0)),
            ],
            scratch_shapes=[pltpu.VMEM((chunk, LANES), F32)],
        ),
        compiler_params=PARAMS,
        name="output",
    )(jnp.stack([column] + order), o_weight, gathered, *contexts, after)


def final_kernel(token_ref, branch_ref, gain_ref, *rest, model, others):
    sq_refs, out_ref = rest[:others], rest[-1]
    total = sq_refs[0][...]
    for sq_ref in sq_refs[1:]:
        total = total + sq_ref[...]
    factor = to_column(lax.rsqrt(total / model + epsilon))[:, 0:1]
    out = token_ref[...].astype(F32) + branch_ref[...] * factor * gain_ref[...]
    out_ref[...] = out.astype(BF16)


def finish(tokens, branch, out_gain, sums, previous, c, model):
    chunk, cols = branch.shape
    tiles = chunk // Q_TILE
    in_specs = [
        pl.BlockSpec((Q_TILE, cols), lambda i: (c * tiles + i, 0)),
        pl.BlockSpec((Q_TILE, cols), lambda i: (i, 0)),
        pl.BlockSpec((1, cols), lambda i: (0, 0)),
    ]
    in_specs += [pl.BlockSpec((1, Q_TILE), lambda i: (0, i)) for _ in sums]
    args = [tokens, branch, out_gain, *sums]
    aliases = {}
    if previous is not None:
        aliases = {len(args): 0}
        in_specs.append(ANY)
        args.append(previous)
    return pl.pallas_call(
        partial(final_kernel, model=model, others=len(sums)),
        out_shape=shape(tokens.shape, BF16),
        grid=(tiles,),
        in_specs=in_specs,
        out_specs=pl.BlockSpec((Q_TILE, cols), lambda i: (c * tiles + i, 0)),
        input_output_aliases=aliases,
        compiler_params=PARAMS,
        name="finish",
    )(*args)


def per_device(
    tokens, seg_ids, in_gain, q_weight, k_weight, value_weight, o_weight, out_gain, *, sizes
):
    rows, cols = tokens.shape
    model = in_gain.shape[0]
    nz, nseq = sizes["tensor"], sizes["seq"]
    plane = nseq * sizes["groups"]
    z = lax.axis_index("tensor")
    seq = lax.axis_index("seq")
    in_plane = lax.axis_index(PLANE)
    half = nz // 2
    side, within = z // half, z % half
    half_rows = half * cols

    ring = [(i, i // half * half + (i + 1) % half) for i in range(nz)]
    swap = [(i, (i + half) % nz) for i in range(nz)]
    turn = lambda k: [(i, (i + k) % nz) for i in range(nz)]
    seq_bits = [1 << b for b in range(1, nseq.bit_length() - 1)]
    group_bits = [nseq << b for b in range(sizes["groups"].bit_length() - 1)]

    share = half_rows // plane
    at = jnp.reshape((1 - side) * plane + in_plane, (1,))
    inner = seq_bits + group_bits
    masks_kv, masks_q = inner + [1], inner[::-1] + [1]
    last = len(masks_kv) - 1
    third = rows // 3 // TAIL * TAIL
    counts = [rows - 2 * third, third, third]
    packed_kv, packed_q, cut = pack(
        at, q_weight, k_weight, value_weight, share, tokens, counts[0]
    )
    own_kv = lax.ppermute(packed_kv, "tensor", swap)[None]
    own_q = lax.ppermute(packed_q, "tensor", swap)[None]
    received = [lax.ppermute(cut, "tensor", ring)]
    order_kv, order_q, first = [0], [0], counts[0]
    for step, (mask_kv, mask_q) in enumerate(zip(masks_kv, masks_q)):
        after, count = [], 0
        if step == 0:
            pairs, after = [], [own_kv, own_q, received[0]]
        else:
            pairs = [(own_kv, far_kv), (own_q, far_q)]
        if step < 2:
            count = counts[1 + step]
        if step == last:
            o_share = o_weight.shape[0] // plane
            columns = [(z + k) % nz * cols for k in range(1, nz)]
            pieces = cut_pieces(in_plane * o_share, columns, o_weight, o_share, cols, own_kv)
            moved = [lax.ppermute(p, "tensor", turn(k + 1)) for k, p in enumerate(pieces)]
            own_o = jnp.stack(moved)[None]
            after = [received[1], own_o]
        outs = stage(pairs, tokens, first, count, after)
        if pairs:
            own_kv, own_q = outs[:2]
        if count:
            received.append(lax.ppermute(outs[-1], "tensor", ring))
        first += count
        far_kv = lax.ppermute(own_kv, PLANE, [(i, i ^ mask_kv) for i in range(plane)])
        far_q = lax.ppermute(own_q, PLANE, [(i, i ^ mask_q) for i in range(plane)])
        order_kv = order_kv + [k ^ mask_kv for k in order_kv]
        order_q = order_q + [k ^ mask_q for k in order_q]
    far_kv, far_q = (order_kv, own_kv, far_kv), (order_q, own_q, far_q)

    def double(own, step, after):
        if step > 0:
            (own,) = stage([own], tokens, 0, 0, after)
        return own, lax.ppermute(own, PLANE, [(i, i ^ masks_kv[step]) for i in range(plane)])

    pair_o = double(own_o, 0, [])
    for step in range(1, last - 1):
        pair_o = double(pair_o, step, [])

    sources = (within + half - jnp.arange(half, dtype=jnp.int32)) % half
    blocks = [[tokens], received]
    for _ in range(half - 2):
        blocks.append([lax.ppermute(part, "tensor", ring) for part in blocks[-1]])
    gains = in_gain.reshape(nz, 1, cols)
    place = jnp.stack([in_plane, side * half])
    sent_kv, x, sq = far_kv_product(
        place, sources, gains, blocks, far_kv, [far_q[2], pair_o[1]]
    )
    got_kv = lax.ppermute(sent_kv, "tensor", swap)
    pair_o = double(pair_o, last - 1, [sent_kv])
    weights = (k_weight, value_weight, q_weight)

    sent_q = far_product(place, sources, x, far_q, [sent_kv])
    got_q = lax.ppermute(sent_q, "tensor", swap)
    near = near_product(side * half + sources, x, weights, sent_q)
    cosine, sine = rotation_table(seq * rows + jnp.arange(rows, dtype=jnp.int32))
    ids = seg_ids[None, :]
    *own_kv, sums = keys_values(
        near, got_kv, sq, ids, cosine, sine, [sent_q, pair_o[1]], model
    )
    pair_o = double(pair_o, last, [own_kv[0]])
    gathered_o = lay_pieces(place, order_kv, *pair_o)

    back = -(-(nseq * rows // 2 - 1) // rows)
    kv_blocks = [own_kv]
    for k in range(1, back + 1):
        earlier = [(i, i + k) for i in range(nseq - k)]
        kv_blocks.insert(0, [lax.ppermute(part, "seq", earlier) for part in own_kv])

    out = None
    seq_at = jnp.reshape(seq, (1,))
    after, own_sq = pair_o[1], place
    for c in range(CHUNKS):
        context = attend(
            seq_at, near, got_q, sums, cosine, sine, ids, after, kv_blocks, c, model
        )
        if nz == 4:
            pairs = [(i, i ^ 1) for i in range(nz)]
            opposite = lax.ppermute(context, "tensor", swap)
            beside = lax.ppermute(context, "tensor", pairs)
            across = lax.ppermute(opposite, "tensor", pairs)
            contexts, after = [context, opposite, beside, across], beside
            order = [jnp.int32(1), 2 - 2 * (z % 2), 2 * (z % 2)]
        else:
            contexts, after = [context], context
            contexts += [lax.ppermute(context, "tensor", turn(k)) for k in range(1, nz)]
            order = [jnp.int32(k) for k in range(nz - 1)]
        branch, own_sq = output_product(z, order, o_weight, gathered_o, contexts, own_sq)
        squares = [own_sq]
        squares += [lax.ppermute(own_sq, "tensor", turn(k)) for k in range(1, nz)]
        out = finish(tokens, branch, out_gain[None, :], squares, out, c, model)
    return out


def solution(mesh):
    return jax.shard_map(
        partial(per_device, sizes=dict(mesh.shape)),
        mesh=mesh,
        in_specs=(
            P(("groups", "seq"), "tensor"),
            P(("groups", "seq")),
            P(),
            P(None, "tensor"),
            P(None, "tensor"),
            P(None, "tensor"),
            P("tensor", None),
            P("tensor"),
        ),
        out_specs=P(("groups", "seq"), "tensor"),
        check_vma=False,
    )
```

```python
import math
from functools import partial

import jax
import jax.numpy as jnp
from jax import lax
from jax.experimental import pallas as pl
from jax.experimental.pallas import tpu as pltpu
from jax.sharding import PartitionSpec as P

HEAD_SIZE = 128
PLANE = ("groups", "seq")

epsilon = 1e-06
query_scale = 144.0 ** (-0.5)
rope_base = 10000.0
NEG = -1e30
Q_TILE = 128
K_TILE = 256
CHUNKS = 2
LANES = 128
TAIL = 16
F32, BF16 = jnp.float32, jnp.bfloat16
ANY = pl.BlockSpec(memory_space=pl.ANY)
HBM = pl.BlockSpec(memory_space=pltpu.HBM)
VMEM = pl.BlockSpec(memory_space=pltpu.VMEM)
DOCUMENTS = 8
PARAMS = pltpu.CompilerParams(vmem_limit_bytes=48 * 1024 * 1024)
ALL_VMEM = pltpu.CompilerParams(vmem_limit_bytes=62 * 1024 * 1024)


def shape(dims, dtype):
    return jax.ShapeDtypeStruct(dims, dtype)


def to_row(column):
    return jnp.broadcast_to(column, (column.shape[0], LANES)).T[0:1, :]


def to_column(row):
    return jnp.broadcast_to(row, (LANES, row.shape[1])).T


def rotation_table(token_places):
    half_dim = HEAD_SIZE // 2
    inverse = rope_base ** (-jnp.arange(half_dim, dtype=F32) / half_dim)
    angles = token_places.astype(F32)[:, None] * inverse[None, :]
    cosine, sine = jnp.cos(angles), jnp.sin(angles)
    return jnp.concatenate([cosine, cosine], 1), jnp.concatenate([-sine, sine], 1)


def rotate(vectors, cosine, sine):
    return vectors * cosine + pltpu.roll(vectors, HEAD_SIZE // 2, 1) * sine


def pack_kernel(at_ref, q_ref, k_ref, v_ref, x_ref, kv_out, q_out, x_out, sems):
    share, width = q_out.shape[0], k_ref.shape[1]
    rows = pl.ds(pl.multiple_of(at_ref[0] * share, TAIL), share)
    copies = [
        pltpu.make_async_copy(k_ref.at[rows], kv_out.at[:, pl.ds(0, width)], sems.at[0]),
        pltpu.make_async_copy(v_ref.at[rows], kv_out.at[:, pl.ds(width, width)], sems.at[1]),
        pltpu.make_async_copy(q_ref.at[rows], q_out, sems.at[2]),
        pltpu.make_async_copy(x_ref.at[pl.ds(0, x_out.shape[0])], x_out, sems.at[3]),
    ]
    for copy in copies:
        copy.start()
    for copy in copies:
        copy.wait()


def pack(at, q_weight, k_weight, v_weight, share, tokens, rows):
    kv_width = k_weight.shape[1] + v_weight.shape[1]
    dims = [(share, kv_width), (share, q_weight.shape[1]), (rows, tokens.shape[1])]
    return pl.pallas_call(
        pack_kernel,
        out_shape=tuple(shape(d, BF16) for d in dims),
        grid_spec=pltpu.PrefetchScalarGridSpec(
            num_scalar_prefetch=1,
            grid=(1,),
            in_specs=[HBM, HBM, HBM, HBM],
            out_specs=[pl.BlockSpec(d, lambda i, at: (0, 0)) for d in dims],
            scratch_shapes=[pltpu.SemaphoreType.DMA((4,))],
        ),
        compiler_params=ALL_VMEM,
        name="pack",
    )(at, q_weight, k_weight, v_weight, tokens)


def stage_kernel(*refs, pairs, first, count):
    outputs = pairs + (1 if count else 0)
    ins, outs, sems = refs[: -outputs - 1], refs[-outputs - 1 : -1], refs[-1]
    copies = []
    for p in range(pairs):
        held = ins[2 * p].shape[0]
        for side in range(2):
            there = outs[p].at[pl.ds(side * held, held)]
            copies.append(
                pltpu.make_async_copy(ins[2 * p + side], there, sems.at[len(copies)])
            )
    if count:
        rows = ins[2 * pairs].at[pl.ds(first, count)]
        copies.append(pltpu.make_async_copy(rows, outs[-1], sems.at[len(copies)]))
    for copy in copies:
        copy.start()
    for copy in copies:
        copy.wait()


def stage(joined, tokens, first, count, after):
    dims = [(2 * pair[0].shape[0],) + pair[0].shape[1:] for pair in joined]
    if count:
        dims.append((count, tokens.shape[1]))
    return pl.pallas_call(
        partial(stage_kernel, pairs=len(joined), first=first, count=count),
        out_shape=tuple(shape(d, BF16) for d in dims),
        in_specs=[ANY] * (2 * len(joined) + 1 + len(after)),
        scratch_shapes=[pltpu.SemaphoreType.DMA((2 * len(joined) + 1,))],
        compiler_params=PARAMS,
        name="stage",
    )(*[piece for pair in joined for piece in pair], tokens, *after)


def cut_kernel(at_ref, o_ref, after_ref, *rest):
    outs, sems = rest[:-1], rest[-1]
    copies = []
    for i, out in enumerate(outs):
        rows = pl.ds(pl.multiple_of(at_ref[0], TAIL), out.shape[0])
        columns = pl.ds(pl.multiple_of(at_ref[1 + i], LANES), out.shape[1])
        copies.append(pltpu.make_async_copy(o_ref.at[rows, columns], out, sems.at[i]))
    for copy in copies:
        copy.start()
    for copy in copies:
        copy.wait()


def cut_pieces(row, columns, o_weight, share, cols, after):
    if cols % LANES:
        return [lax.dynamic_slice(o_weight, (row, c), (share, cols)) for c in columns]
    return pl.pallas_call(
        cut_kernel,
        out_shape=tuple(shape((share, cols), BF16) for _ in columns),
        grid_spec=pltpu.PrefetchScalarGridSpec(
            num_scalar_prefetch=1,
            grid=(1,),
            in_specs=[ANY, ANY],
            out_specs=[VMEM for _ in columns],
            scratch_shapes=[pltpu.SemaphoreType.DMA((len(columns),))],
        ),
        compiler_params=PARAMS,
        name="cut",
    )(jnp.stack([row] + columns), o_weight, after)


def lay_kernel(place_ref, own_ref, got_ref, out_ref, sems, *, order):
    held, others, share, _ = own_ref.shape
    copies = []
    for i, mask in enumerate(order):
        piece = own_ref.at[i] if i < held else got_ref.at[i - held]
        row = pl.multiple_of((place_ref[0] ^ mask) * share, TAIL)
        there = out_ref.at[:, pl.ds(row, share)]
        copies.append(pltpu.make_async_copy(piece, there, sems.at[i]))
    for copy in copies:
        copy.start()
    for copy in copies:
        copy.wait()


def lay_pieces(place, order, own, got):
    _, others, share, cols = own.shape
    dims = (others, len(order) * share, cols)
    return pl.pallas_call(
        partial(lay_kernel, order=order),
        out_shape=shape(dims, BF16),
        grid_spec=pltpu.PrefetchScalarGridSpec(
            num_scalar_prefetch=1,
            grid=(1,),
            in_specs=[ANY, ANY],
            out_specs=pl.BlockSpec(dims, lambda i, p: (0, 0, 0)),
            scratch_shapes=[pltpu.SemaphoreType.DMA((len(order),))],
        ),
        compiler_params=PARAMS,
        name="lay",
    )(place, own, got)


def place_weights(place_ref, own_ref, got_ref, weight, sems, order):
    held, share, _ = own_ref.shape
    copies = []
    for i, mask in enumerate(order):
        piece = own_ref.at[i] if i < held else got_ref.at[i - held]
        row = pl.multiple_of((place_ref[0] ^ mask) * share, TAIL)
        there = weight.at[pl.ds(row, share)]
        copies.append(pltpu.make_async_copy(piece, there, sems.at[i]))
    for copy in copies:
        copy.start()
    return copies


def far_sum(src_ref, x_ref, weight):
    count, _, cols = x_ref.shape
    total = None
    for k in range(count):
        row = pl.multiple_of(src_ref[k] * cols, TAIL)
        term = jnp.dot(x_ref[k], weight[pl.ds(row, cols), :], preferred_element_type=F32)
        total = term if total is None else total + term
    return total


def far_kv_kernel(place_ref, src_ref, gain_ref, own_ref, got_ref, *rest, order, cuts):
    x_refs, (out_ref, x_out, sq_ref, weight, sems) = rest[: sum(cuts)], rest[-5:]
    copies = place_weights(place_ref, own_ref, got_ref, weight, sems, order)
    rows = x_out.shape[1]
    columns, at = [], 0
    for k, pieces in enumerate(cuts):
        gain = gain_ref[place_ref[1] + src_ref[k]]
        column, row = [], 0
        for x_ref in x_refs[at : at + pieces]:
            x = x_ref[...].astype(F32)
            column.append(jnp.sum(x * x, axis=1, keepdims=True))
            x_out[k, row : row + x.shape[0]] = (x * gain).astype(BF16)
            row += x.shape[0]
        columns.append(jnp.concatenate(column, axis=0))
        at += pieces
    sq = to_row(sum(columns[1:], columns[0]))
    sq_ref[...] = sq
    for copy in copies:
        copy.wait()
    out_ref[:rows, :] = far_sum(src_ref, x_out, weight).astype(BF16)
    high = sq.astype(BF16).astype(F32)
    out_ref[rows:, :] = lines_of((high, sq - high), out_ref.shape[1])


def far_kv_product(place, sources, gains, blocks, gathered, after):
    order, own, got = gathered
    _, share, width = own.shape
    rows, cols = blocks[0][0].shape
    pieces = [piece for block in blocks for piece in block]
    dims = [(rows + TAIL, width), (len(blocks), rows, cols), (1, rows)]
    whole = lambda d: pl.BlockSpec(d, lambda i, p, s: (0,) * len(d))
    return pl.pallas_call(
        partial(far_kv_kernel, order=order, cuts=[len(block) for block in blocks]),
        out_shape=tuple(shape(d, t) for d, t in zip(dims, (BF16, BF16, F32))),
        grid_spec=pltpu.PrefetchScalarGridSpec(
            num_scalar_prefetch=2,
            grid=(1,),
            in_specs=[whole(gains.shape), ANY, ANY]
            + [whole(piece.shape) for piece in pieces]
            + [ANY for _ in after],
            out_specs=[whole(d) for d in dims],
            scratch_shapes=[
                pltpu.VMEM((len(order) * share, width), BF16),
                pltpu.SemaphoreType.DMA((len(order),)),
            ],
        ),
        compiler_params=PARAMS,
        name="far_kv",
    )(place, sources, gains, own, got, *pieces, *after)


def far_kernel(place_ref, src_ref, x_ref, own_ref, got_ref, *rest, order):
    out_ref, weight, sems = rest[-3:]
    for copy in place_weights(place_ref, own_ref, got_ref, weight, sems, order):
        copy.wait()
    out_ref[...] = far_sum(src_ref, x_ref, weight).astype(BF16)


def lines_of(rows, width):
    lines = []
    for row in rows:
        for at in range(0, row.shape[1], width):
            line = row[:, at : at + width]
            if line.shape[1] < width:
                rest = jnp.zeros((1, width - line.shape[1]), F32)
                line = jnp.concatenate([line, rest], axis=1)
            lines.append(line)
    lines.append(jnp.zeros((TAIL - len(lines), width), F32))
    return jnp.concatenate(lines, axis=0).astype(BF16)


def rows_of(tail, count, length):
    per_row = -(-length // tail.shape[1])
    rows = []
    for r in range(count):
        lines = [tail[r * per_row + i : r * per_row + i + 1, :] for i in range(per_row)]
        rows.append(jnp.concatenate(lines, axis=1)[:, :length])
    return rows


def far_product(place, sources, x, gathered, after):
    order, own, got = gathered
    _, share, width = own.shape
    rows = x.shape[1]
    return pl.pallas_call(
        partial(far_kernel, order=order),
        out_shape=shape((rows, width), BF16),
        grid_spec=pltpu.PrefetchScalarGridSpec(
            num_scalar_prefetch=2,
            grid=(1,),
            in_specs=[pl.BlockSpec(x.shape, lambda i, p, s: (0, 0, 0)), ANY, ANY]
            + [ANY for _ in after],
            out_specs=pl.BlockSpec((rows, width), lambda i, p, s: (0, 0)),
            scratch_shapes=[
                pltpu.VMEM((len(order) * share, width), BF16),
                pltpu.SemaphoreType.DMA((len(order),)),
            ],
        ),
        compiler_params=PARAMS,
        name="far",
    )(place, sources, x, own, got, *after)


def near_kernel(src_ref, x_ref, k_ref, v_ref, q_ref, *rest):
    out_ref = rest[-1]
    x = x_ref[0]

    @pl.when(pl.program_id(0) == 0)
    def _():
        out_ref[...] = jnp.zeros_like(out_ref)

    column = 0
    for ref in (k_ref, v_ref, q_ref):
        at = slice(column, column + ref.shape[1])
        out_ref[:, at] += jnp.dot(x, ref[...], preferred_element_type=F32)
        column += ref.shape[1]


def near_product(sources, x, weights, after):
    count, chunk, cols = x.shape
    widths = [w.shape[1] for w in weights]
    return pl.pallas_call(
        near_kernel,
        out_shape=shape((chunk, sum(widths)), F32),
        grid_spec=pltpu.PrefetchScalarGridSpec(
            num_scalar_prefetch=1,
            grid=(count,),
            in_specs=[pl.BlockSpec((1, chunk, cols), lambda i, s: (i, 0, 0))]
            + [pl.BlockSpec((cols, w), lambda i, s: (s[i], 0)) for w in widths]
            + [ANY for _ in after],
            out_specs=pl.BlockSpec((chunk, sum(widths)), lambda i, s: (0, 0)),
        ),
        compiler_params=PARAMS,
        name="near",
    )(sources, x, *weights, *after)


def keys_kernel(near_ref, far_ref, sq_ref, id_ref, cos_ref, sin_ref, *rest, model):
    out_ref, sum_ref = rest[-2:]
    rows, width = near_ref.shape[0], far_ref.shape[1]
    tail = far_ref[rows:, :].astype(F32)
    total = sum(rows_of(tail, 2, rows), sq_ref[...])
    factor = to_column(lax.rsqrt(total / model + epsilon))
    sum_ref[...] = total
    keys, values = slice(0, HEAD_SIZE), slice(HEAD_SIZE, 2 * HEAD_SIZE)
    part = (near_ref[:, keys] + far_ref[:rows, keys].astype(F32)) * factor
    part = rotate(part, cos_ref[...], sin_ref[...]).astype(BF16)
    out_ref[: rows // 2, keys] = part[: rows // 2]
    out_ref[: rows // 2, values] = part[rows // 2 :]
    part = (near_ref[:, values] + far_ref[:rows, values].astype(F32)) * factor
    part = part.T.astype(BF16)
    for i, at in enumerate(range(0, rows, width)):
        row = rows // 2 + i * HEAD_SIZE
        out_ref[row : row + HEAD_SIZE, :] = part[:, at : at + width]
    out_ref[rows:, :] = lines_of((id_ref[...].astype(F32),), width)


def keys_values(near, far, sq, ids, cosine, sine, after, model):
    rows, width = near.shape[0], far.shape[1]
    whole = lambda i: (0, 0)
    return pl.pallas_call(
        partial(keys_kernel, model=model),
        out_shape=(shape(far.shape, BF16), shape(sq.shape, F32)),
        grid=(1,),
        in_specs=[pl.BlockSpec((rows, width), whole)]
        + [pl.BlockSpec(a.shape, whole) for a in (far, sq, ids, cosine, sine)]
        + [ANY for _ in after],
        out_specs=[pl.BlockSpec(far.shape, whole), pl.BlockSpec(sq.shape, whole)],
        compiler_params=PARAMS,
        name="keys",
    )(near, far, sq, ids, cosine, sine, *after)


def queries_kernel(near_ref, far_ref, sum_ref, cos_ref, sin_ref, out_ref, *, model):
    scale = query_scale * math.log2(math.e)
    factor = to_column(lax.rsqrt(sum_ref[...] / model + epsilon) * scale)
    for c in range(0, out_ref.shape[1], HEAD_SIZE):
        at = slice(c, c + HEAD_SIZE)
        part = (near_ref[:, at] + far_ref[:, at].astype(F32)) * factor
        out_ref[:, at] = rotate(part, cos_ref[...], sin_ref[...]).astype(BF16)


def finished_queries(near, far, sums, cosine, sine, model):
    rows, width = far.shape
    last = near.shape[1] // width - 1
    whole = lambda i: (0, 0)
    return pl.pallas_call(
        partial(queries_kernel, model=model),
        out_shape=shape((rows, width), BF16),
        grid=(1,),
        in_specs=[pl.BlockSpec((rows, width), lambda i: (0, last))]
        + [pl.BlockSpec(a.shape, whole) for a in (far, sums, cosine, sine)],
        out_specs=pl.BlockSpec((rows, width), whole),
        compiler_params=PARAMS,
        cost_estimate=pl.CostEstimate(flops=5 * 10**10, bytes_accessed=10**8, transcendentals=0),
        name="queries",
    )(near, far, sums, cosine, sine)


def attention_kernel(seq_ref, q_ref, id_ref, after_ref, *rest, back, offset):
    kv_refs, (out_ref, k_scr, vt_scr, count_scr) = rest[:-4], rest[-4:]
    part_rows, message = kv_refs[0].shape[0] - TAIL, kv_refs[0].shape[1]
    group = q_ref.shape[1] // HEAD_SIZE
    tile = pl.program_id(0)

    @pl.when(tile == 0)
    def _():
        counts = [jnp.zeros((1, 1), F32) for _ in range(DOCUMENTS)]
        for b, kv_ref in enumerate(kv_refs):
            row, half = b * part_rows, part_rows // 2
            k_scr[row : row + half, :] = kv_ref[:half, :HEAD_SIZE]
            k_scr[row + half : row + part_rows, :] = kv_ref[:half, HEAD_SIZE:]
            for i, at in enumerate(range(0, part_rows, message)):
                first = half + i * HEAD_SIZE
                vt_scr[:, row + at : row + at + message] = kv_ref[first : first + HEAD_SIZE, :]
            (ids,) = rows_of(kv_ref[part_rows:, :].astype(F32), 1, part_rows)
            exists = b >= back - seq_ref[0]
            ids = jnp.where(exists, ids, -1.0)
            for d in range(DOCUMENTS):
                below = (ids < d).astype(F32)
                counts[d] = counts[d] + jnp.sum(below, axis=1, keepdims=True)
        for d in range(DOCUMENTS):
            count_scr[d : d + 1, :] = jnp.broadcast_to(counts[d], (1, LANES))

    heads = [q_ref[:, c : c + HEAD_SIZE] for c in range(0, group * HEAD_SIZE, HEAD_SIZE)]
    q2 = jnp.concatenate(heads, axis=0)
    width = group * Q_TILE

    start = jnp.zeros((1, Q_TILE), F32)
    for d in range(DOCUMENTS):
        start = jnp.where(id_ref[...] == d, count_scr[d : d + 1, :], start)
    start = start.astype(jnp.int32)
    low = jnp.min(start) // K_TILE
    start = jnp.concatenate([start] * group, axis=1)
    first = back * part_rows + offset + tile * Q_TILE
    place = first + lax.broadcasted_iota(jnp.int32, (1, Q_TILE), 1)
    place = jnp.concatenate([place] * group, axis=1)

    def score(j):
        base = pl.multiple_of(j * K_TILE, K_TILE)
        return lax.dot_general(
            k_scr[pl.ds(base, K_TILE), :],
            q2,
            (((1,), (1,)), ((), ())),
            preferred_element_type=F32,
        )

    stop = (first + Q_TILE + K_TILE - 1) // K_TILE

    def step(j, state):
        scores, run_max, run_sum, acc = state
        following = score(jnp.minimum(j + 1, stop - 1))
        base = pl.multiple_of(j * K_TILE, K_TILE)
        key_pos = base + lax.broadcasted_iota(jnp.int32, (K_TILE, width), 0)
        allowed = (key_pos >= start) & (key_pos <= place)
        scores = jnp.where(allowed, scores, NEG)
        new_max = jnp.maximum(run_max, jnp.max(scores, axis=0, keepdims=True))
        expo = jnp.exp2(scores - new_max)
        factor = jnp.exp2(run_max - new_max)
        run_sum = run_sum * factor + jnp.sum(expo, axis=0, keepdims=True)
        acc = acc * factor + jnp.dot(
            vt_scr[:, pl.ds(base, K_TILE)], expo.astype(BF16), preferred_element_type=F32
        )
        return following, new_max, run_sum, acc

    state = (
        score(low),
        jnp.full((1, width), NEG, F32),
        jnp.zeros((1, width), F32),
        jnp.zeros((HEAD_SIZE, width), F32),
    )
    _, _, run_sum, acc = lax.fori_loop(low, stop, step, state)
    context = (acc / run_sum).T
    for g in range(group):
        out_ref[:, g * HEAD_SIZE : (g + 1) * HEAD_SIZE] = context[
            g * Q_TILE : (g + 1) * Q_TILE
        ].astype(BF16)


def attend(seq, queries, ids, after, blocks, c):
    rows, width = queries.shape[0] // CHUNKS, queries.shape[1]
    back = len(blocks) - 1
    tiles = rows // Q_TILE
    keys = len(blocks) * queries.shape[0]
    return pl.pallas_call(
        partial(attention_kernel, back=back, offset=c * rows),
        out_shape=shape((rows, width), BF16),
        grid_spec=pltpu.PrefetchScalarGridSpec(
            num_scalar_prefetch=1,
            grid=(tiles,),
            in_specs=[
                pl.BlockSpec((Q_TILE, width), lambda i, s: (c * tiles + i, 0)),
                pl.BlockSpec((1, Q_TILE), lambda i, s: (0, c * tiles + i)),
                ANY,
            ]
            + [pl.BlockSpec(b.shape, lambda i, s: (0, 0)) for b in blocks],
            out_specs=pl.BlockSpec((Q_TILE, width), lambda i, s: (i, 0)),
            scratch_shapes=[
                pltpu.VMEM((keys, HEAD_SIZE), BF16),
                pltpu.VMEM((HEAD_SIZE, keys), BF16),
                pltpu.VMEM((DOCUMENTS, LANES), F32),
            ],
        ),
        compiler_params=PARAMS,
        cost_estimate=pl.CostEstimate(
            flops=4 * rows * width * keys,
            bytes_accessed=4 * keys * width,
            transcendentals=rows * keys * width // HEAD_SIZE,
        ),
        name="attend",
    )(seq, queries, ids, after, *blocks)


def output_kernel(at_ref, own_o_ref, o_ref, *rest):
    ctx_refs, (before_ref, out_ref, sq_ref, acc) = rest[:-4], rest[-4:]
    step = pl.program_id(0)
    total = jnp.dot(ctx_refs[0][...], own_o_ref[...], preferred_element_type=F32)
    for i, ctx_ref in enumerate(ctx_refs[1:]):
        weight = o_ref[at_ref[1 + i]]
        total = total + jnp.dot(ctx_ref[...], weight, preferred_element_type=F32)
    out_ref[...] = total
    squares = jnp.sum(total * total, axis=1, keepdims=True)
    squares = jnp.broadcast_to(squares, acc.shape)

    @pl.when(step == 0)
    def _():
        acc[...] = squares

    @pl.when(step > 0)
    def _():
        acc[...] += squares

    @pl.when(step == pl.num_programs(0) - 1)
    def _():
        done = sq_ref.shape[1] - acc.shape[0]
        if done:
            sq_ref[:, :done] = before_ref[...]
        sq_ref[:, done:] = acc[...].T[0:1, :]


def output_product(column, order, o_weight, gathered, contexts, before, c):
    chunk, width = contexts[0].shape
    others, _, cols = gathered.shape
    tiles = 3 if cols % (3 * LANES) == 0 else 1
    tile = cols // tiles
    if cols % LANES:
        o_weight = lax.dynamic_slice_in_dim(o_weight, column * cols, cols, axis=1)
        column = jnp.int32(0)
    return pl.pallas_call(
        output_kernel,
        out_shape=(shape((chunk, cols), F32), shape((1, (c + 1) * chunk), F32)),
        grid_spec=pltpu.PrefetchScalarGridSpec(
            num_scalar_prefetch=1,
            grid=(tiles,),
            in_specs=[
                pl.BlockSpec((width, tile), lambda i, at: (0, at[0] * tiles + i)),
                pl.BlockSpec((others, width, tile), lambda i, at: (0, 0, i)),
            ]
            + [pl.BlockSpec((chunk, width), lambda i, at: (0, 0)) for _ in contexts]
            + [pl.BlockSpec(before.shape, lambda i, at: (0, 0))],
            out_specs=[
                pl.BlockSpec((chunk, tile), lambda i, at: (0, i)),
                pl.BlockSpec((1, (c + 1) * chunk), lambda i, at: (0, 0)),
            ],
            scratch_shapes=[pltpu.VMEM((chunk, LANES), F32)],
        ),
        compiler_params=PARAMS,
        name="output",
    )(jnp.stack([column] + order), o_weight, gathered, *contexts, before)


def final_kernel(token_ref, gain_ref, *rest, model):
    branch_refs, sq_refs, out_ref = rest[:CHUNKS], rest[CHUNKS:-1], rest[-1]
    total = sq_refs[0][...]
    for sq_ref in sq_refs[1:]:
        total = total + sq_ref[...]
    factor = to_column(lax.rsqrt(total / model + epsilon))[:, 0:1]
    for c in range(CHUNKS):

        @pl.when(pl.program_id(0) * CHUNKS // pl.num_programs(0) == c)
        def _():
            out = token_ref[...].astype(F32) + branch_refs[c][...] * factor * gain_ref[...]
            out_ref[...] = out.astype(BF16)


def finish(tokens, branches, out_gain, sums, model):
    rows, cols = tokens.shape
    tiles = rows // CHUNKS // Q_TILE
    held = lambda c: lambda i: (jnp.clip(i - c * tiles, 0, tiles - 1), 0)
    return pl.pallas_call(
        partial(final_kernel, model=model),
        out_shape=shape(tokens.shape, BF16),
        grid=(CHUNKS * tiles,),
        in_specs=[
            pl.BlockSpec((Q_TILE, cols), lambda i: (i, 0)),
            pl.BlockSpec((1, cols), lambda i: (0, 0)),
        ]
        + [pl.BlockSpec((Q_TILE, cols), held(c)) for c in range(CHUNKS)]
        + [pl.BlockSpec((1, Q_TILE), lambda i: (0, i)) for _ in sums],
        out_specs=pl.BlockSpec((Q_TILE, cols), lambda i: (i, 0)),
        compiler_params=PARAMS,
        name="finish",
    )(tokens, out_gain, *branches, *sums)


def per_device(
    tokens, seg_ids, in_gain, q_weight, k_weight, value_weight, o_weight, out_gain, *, sizes
):
    rows, cols = tokens.shape
    model = in_gain.shape[0]
    nz, nseq = sizes["tensor"], sizes["seq"]
    plane = nseq * sizes["groups"]
    z = lax.axis_index("tensor")
    seq = lax.axis_index("seq")
    in_plane = lax.axis_index(PLANE)
    half = nz // 2
    side, within = z // half, z % half
    half_rows = half * cols

    ring = [(i, i // half * half + (i + 1) % half) for i in range(nz)]
    swap = [(i, (i + half) % nz) for i in range(nz)]
    turn = lambda k: [(i, (i + k) % nz) for i in range(nz)]
    seq_bits = [1 << b for b in range(1, nseq.bit_length() - 1)]
    group_bits = [nseq << b for b in range(sizes["groups"].bit_length() - 1)]

    share = half_rows // plane
    at = jnp.reshape((1 - side) * plane + in_plane, (1,))
    inner = seq_bits + group_bits
    masks_kv, masks_q = inner + [1], inner[::-1] + [1]
    last = len(masks_kv) - 1
    eighth = rows // 48 * 8
    counts = [eighth, rows // 2 + TAIL, rows - eighth - rows // 2 - TAIL]
    packed_kv, packed_q, cut = pack(
        at, q_weight, k_weight, value_weight, share, tokens, counts[0]
    )
    own_kv = lax.ppermute(packed_kv, "tensor", swap)[None]
    own_q = lax.ppermute(packed_q, "tensor", swap)[None]
    received = [lax.ppermute(cut, "tensor", ring)]
    order_kv, order_q, first = [0], [0], counts[0]
    for step, (mask_kv, mask_q) in enumerate(zip(masks_kv, masks_q)):
        after, count = [], 0
        if step == 0:
            pairs, after = [], [own_kv, own_q, received[0]]
        else:
            pairs = [(own_kv, far_kv), (own_q, far_q)]
        if step < 2:
            count = counts[1 + step]
        if step == last:
            after = [received[1]]
        outs = stage(pairs, tokens, first, count, after)
        if pairs:
            own_kv, own_q = outs[:2]
        if count:
            received.append(lax.ppermute(outs[-1], "tensor", ring))
        first += count
        far_kv = lax.ppermute(own_kv, PLANE, [(i, i ^ mask_kv) for i in range(plane)])
        far_q = lax.ppermute(own_q, PLANE, [(i, i ^ mask_q) for i in range(plane)])
        order_kv = order_kv + [k ^ mask_kv for k in order_kv]
        order_q = order_q + [k ^ mask_q for k in order_q]
    far_kv, far_q = (order_kv, own_kv, far_kv), (order_q, own_q, far_q)

    o_share = o_weight.shape[0] // plane
    columns = [(z + k) % nz * cols for k in range(1, nz)]
    pieces = cut_pieces(in_plane * o_share, columns, o_weight, o_share, cols, own_kv)
    moved = [lax.ppermute(p, "tensor", turn(k + 1)) for k, p in enumerate(pieces)]
    own_o = jnp.stack(moved)[None]

    def double(own, step, after):
        if step > 0:
            (own,) = stage([own], tokens, 0, 0, after)
        return own, lax.ppermute(own, PLANE, [(i, i ^ masks_kv[step]) for i in range(plane)])

    sources = (within + half - jnp.arange(half, dtype=jnp.int32)) % half
    blocks = [[tokens], received]
    for _ in range(half - 2):
        blocks.append([lax.ppermute(part, "tensor", ring) for part in blocks[-1]])
    gains = in_gain.reshape(nz, 1, cols)
    place = jnp.stack([in_plane, side * half])
    sent_kv, x, sq = far_kv_product(
        place, sources, gains, blocks, far_kv, [far_q[2], own_o]
    )
    got_kv = lax.ppermute(sent_kv, "tensor", swap)
    pair_o = double(own_o, 0, [])
    for step in range(1, last - 1):
        pair_o = double(pair_o, step, [])
    weights = (k_weight, value_weight, q_weight)

    sent_q = far_product(place, sources, x, far_q, [sent_kv])
    got_q = lax.ppermute(sent_q, "tensor", swap)
    near = near_product(side * half + sources, x, weights, [sent_q, pair_o[1]])
    pair_o = double(pair_o, last - 1, [near])
    cosine, sine = rotation_table(seq * rows + jnp.arange(rows, dtype=jnp.int32))
    ids = seg_ids[None, :]
    own_kv, sums = keys_values(
        near, got_kv, sq, ids, cosine, sine, [sent_q], model
    )
    pair_o = double(pair_o, last, [own_kv])
    gathered_o = lay_pieces(place, order_kv, *pair_o)

    back = -(-(nseq * rows // 2 - 1) // rows)
    kv_blocks = [own_kv]
    for k in range(1, back + 1):
        earlier = [(i, i + k) for i in range(nseq - k)]
        kv_blocks.insert(0, lax.ppermute(own_kv, "seq", earlier))

    queries = finished_queries(near, got_q, sums, cosine, sine, model)
    seq_at = jnp.reshape(seq, (1,))
    branches, own_sq, after = [], sums, own_kv
    for c in range(CHUNKS):
        context = attend(seq_at, queries, ids, after, kv_blocks, c)
        after = gathered_o
        if nz == 4:
            pairs = [(i, i ^ 1) for i in range(nz)]
            opposite = lax.ppermute(context, "tensor", swap)
            beside = lax.ppermute(context, "tensor", pairs)
            across = lax.ppermute(opposite, "tensor", pairs)
            contexts = [context, opposite, beside, across]
            order = [jnp.int32(1), 2 - 2 * (z % 2), 2 * (z % 2)]
        else:
            contexts = [context]
            contexts += [lax.ppermute(context, "tensor", turn(k)) for k in range(1, nz)]
            order = [jnp.int32(k) for k in range(nz - 1)]
        branch, own_sq = output_product(
            z, order, o_weight, gathered_o, contexts, own_sq, c
        )
        branches.append(branch)
    squares = [own_sq]
    squares += [lax.ppermute(own_sq, "tensor", turn(k)) for k in range(1, nz)]
    return finish(tokens, branches, out_gain[None, :], squares, model)


def solution(mesh):
    return jax.shard_map(
        partial(per_device, sizes=dict(mesh.shape)),
        mesh=mesh,
        in_specs=(
            P(("groups", "seq"), "tensor"),
            P(("groups", "seq")),
            P(),
            P(None, "tensor"),
            P(None, "tensor"),
            P(None, "tensor"),
            P("tensor", None),
            P("tensor"),
        ),
        out_specs=P(("groups", "seq"), "tensor"),
        check_vma=False,
    )
```

```python
import math
from functools import partial

import jax
import jax.numpy as jnp
from jax import lax
from jax.experimental import pallas as pl
from jax.experimental.pallas import tpu as pltpu
from jax.sharding import PartitionSpec as P

HEAD_SIZE = 128
PLANE = ("groups", "seq")

epsilon = 1e-06
query_scale = 144.0 ** (-0.5)
rope_base = 10000.0
NEG = -1e30
Q_TILE = 128
K_TILE = 256
CHUNKS = 2
LANES = 128
TAIL = 16
F32, BF16 = jnp.float32, jnp.bfloat16
ANY = pl.BlockSpec(memory_space=pl.ANY)
HBM = pl.BlockSpec(memory_space=pltpu.HBM)
VMEM = pl.BlockSpec(memory_space=pltpu.VMEM)
DOCUMENTS = 8
HIDE = 5 * 10**10
PARAMS = pltpu.CompilerParams(vmem_limit_bytes=48 * 1024 * 1024)
ALL_VMEM = pltpu.CompilerParams(vmem_limit_bytes=62 * 1024 * 1024)


def shape(dims, dtype):
    return jax.ShapeDtypeStruct(dims, dtype)


def to_row(column):
    return jnp.broadcast_to(column, (column.shape[0], LANES)).T[0:1, :]


def to_column(row):
    return jnp.broadcast_to(row, (LANES, row.shape[1])).T


def rotation_table(token_places):
    half_dim = HEAD_SIZE // 2
    inverse = rope_base ** (-jnp.arange(half_dim, dtype=F32) / half_dim)
    angles = token_places.astype(F32)[:, None] * inverse[None, :]
    cosine, sine = jnp.cos(angles), jnp.sin(angles)
    return jnp.concatenate([cosine, cosine], 1), jnp.concatenate([-sine, sine], 1)


def rotate(vectors, cosine, sine):
    return vectors * cosine + pltpu.roll(vectors, HEAD_SIZE // 2, 1) * sine


def pack_kernel(at_ref, q_ref, k_ref, v_ref, x_ref, kv_out, q_out, x_out, sems):
    share, width = q_out.shape[0], k_ref.shape[1]
    rows = pl.ds(pl.multiple_of(at_ref[0] * share, TAIL), share)
    copies = [
        pltpu.make_async_copy(k_ref.at[rows], kv_out.at[:, pl.ds(0, width)], sems.at[0]),
        pltpu.make_async_copy(v_ref.at[rows], kv_out.at[:, pl.ds(width, width)], sems.at[1]),
        pltpu.make_async_copy(q_ref.at[rows], q_out, sems.at[2]),
        pltpu.make_async_copy(x_ref.at[pl.ds(0, x_out.shape[0])], x_out, sems.at[3]),
    ]
    for copy in copies:
        copy.start()
    for copy in copies:
        copy.wait()


def pack(at, q_weight, k_weight, v_weight, share, tokens, rows):
    kv_width = k_weight.shape[1] + v_weight.shape[1]
    dims = [(share, kv_width), (share, q_weight.shape[1]), (rows, tokens.shape[1])]
    return pl.pallas_call(
        pack_kernel,
        out_shape=tuple(shape(d, BF16) for d in dims),
        grid_spec=pltpu.PrefetchScalarGridSpec(
            num_scalar_prefetch=1,
            grid=(1,),
            in_specs=[HBM, HBM, HBM, HBM],
            out_specs=[pl.BlockSpec(d, lambda i, at: (0, 0)) for d in dims],
            scratch_shapes=[pltpu.SemaphoreType.DMA((4,))],
        ),
        compiler_params=ALL_VMEM,
        name="pack",
    )(at, q_weight, k_weight, v_weight, tokens)


def stage_kernel(*refs, pairs, first, count):
    outputs = pairs + (1 if count else 0)
    ins, outs, sems = refs[: -outputs - 1], refs[-outputs - 1 : -1], refs[-1]
    copies = []
    for p in range(pairs):
        held = ins[2 * p].shape[0]
        for side in range(2):
            there = outs[p].at[pl.ds(side * held, held)]
            copies.append(
                pltpu.make_async_copy(ins[2 * p + side], there, sems.at[len(copies)])
            )
    if count:
        rows = ins[2 * pairs].at[pl.ds(first, count)]
        copies.append(pltpu.make_async_copy(rows, outs[-1], sems.at[len(copies)]))
    for copy in copies:
        copy.start()
    for copy in copies:
        copy.wait()


def stage(joined, tokens, first, count, after, flops=0):
    dims = [(2 * pair[0].shape[0],) + pair[0].shape[1:] for pair in joined]
    if count:
        dims.append((count, tokens.shape[1]))
    return pl.pallas_call(
        partial(stage_kernel, pairs=len(joined), first=first, count=count),
        out_shape=tuple(shape(d, BF16) for d in dims),
        in_specs=[ANY] * (2 * len(joined) + 1 + len(after)),
        scratch_shapes=[pltpu.SemaphoreType.DMA((2 * len(joined) + 1,))],
        compiler_params=PARAMS,
        cost_estimate=pl.CostEstimate(flops=flops, bytes_accessed=flops // 500, transcendentals=0),
        name="stage",
    )(*[piece for pair in joined for piece in pair], tokens, *after)


def cut_kernel(at_ref, o_ref, after_ref, *rest):
    outs, sems = rest[:-1], rest[-1]
    copies = []
    for i, out in enumerate(outs):
        rows = pl.ds(pl.multiple_of(at_ref[0], TAIL), out.shape[0])
        columns = pl.ds(pl.multiple_of(at_ref[1 + i], LANES), out.shape[1])
        copies.append(pltpu.make_async_copy(o_ref.at[rows, columns], out, sems.at[i]))
    for copy in copies:
        copy.start()
    for copy in copies:
        copy.wait()


def cut_pieces(row, columns, o_weight, share, cols, after):
    if cols % LANES:
        return [lax.dynamic_slice(o_weight, (row, c), (share, cols)) for c in columns]
    return pl.pallas_call(
        cut_kernel,
        out_shape=tuple(shape((share, cols), BF16) for _ in columns),
        grid_spec=pltpu.PrefetchScalarGridSpec(
            num_scalar_prefetch=1,
            grid=(1,),
            in_specs=[ANY, ANY],
            out_specs=[VMEM for _ in columns],
            scratch_shapes=[pltpu.SemaphoreType.DMA((len(columns),))],
        ),
        compiler_params=PARAMS,
        name="cut",
    )(jnp.stack([row] + columns), o_weight, after)


def lay_kernel(place_ref, own_ref, got_ref, out_ref, sems, *, order):
    held, others, share, _ = own_ref.shape
    copies = []
    for i, mask in enumerate(order):
        piece = own_ref.at[i] if i < held else got_ref.at[i - held]
        row = pl.multiple_of((place_ref[0] ^ mask) * share, TAIL)
        there = out_ref.at[:, pl.ds(row, share)]
        copies.append(pltpu.make_async_copy(piece, there, sems.at[i]))
    for copy in copies:
        copy.start()
    for copy in copies:
        copy.wait()


def lay_pieces(place, order, own, got):
    _, others, share, cols = own.shape
    dims = (others, len(order) * share, cols)
    return pl.pallas_call(
        partial(lay_kernel, order=order),
        out_shape=shape(dims, BF16),
        grid_spec=pltpu.PrefetchScalarGridSpec(
            num_scalar_prefetch=1,
            grid=(1,),
            in_specs=[ANY, ANY],
            out_specs=pl.BlockSpec(dims, lambda i, p: (0, 0, 0)),
            scratch_shapes=[pltpu.SemaphoreType.DMA((len(order),))],
        ),
        compiler_params=PARAMS,
        name="lay",
    )(place, own, got)


def place_weights(place_ref, own_ref, got_ref, weight, sems, order):
    held, share, _ = own_ref.shape
    copies = []
    for i, mask in enumerate(order):
        piece = own_ref.at[i] if i < held else got_ref.at[i - held]
        row = pl.multiple_of((place_ref[0] ^ mask) * share, TAIL)
        there = weight.at[pl.ds(row, share)]
        copies.append(pltpu.make_async_copy(piece, there, sems.at[i]))
    for copy in copies:
        copy.start()
    return copies


def far_sum(src_ref, x_ref, weight):
    count, _, cols = x_ref.shape
    total = None
    for k in range(count):
        row = pl.multiple_of(src_ref[k] * cols, TAIL)
        term = jnp.dot(x_ref[k], weight[pl.ds(row, cols), :], preferred_element_type=F32)
        total = term if total is None else total + term
    return total


def far_kv_kernel(place_ref, src_ref, gain_ref, own_ref, got_ref, *rest, order, cuts):
    x_refs, (out_ref, x_out, sq_ref, weight, sems) = rest[: sum(cuts)], rest[-5:]
    copies = place_weights(place_ref, own_ref, got_ref, weight, sems, order)
    rows = x_out.shape[1]
    columns, at = [], 0
    for k, pieces in enumerate(cuts):
        gain = gain_ref[place_ref[1] + src_ref[k]]
        column, row = [], 0
        for x_ref in x_refs[at : at + pieces]:
            x = x_ref[...].astype(F32)
            column.append(jnp.sum(x * x, axis=1, keepdims=True))
            x_out[k, row : row + x.shape[0]] = (x * gain).astype(BF16)
            row += x.shape[0]
        columns.append(jnp.concatenate(column, axis=0))
        at += pieces
    sq = to_row(sum(columns[1:], columns[0]))
    sq_ref[...] = sq
    for copy in copies:
        copy.wait()
    out_ref[:rows, :] = far_sum(src_ref, x_out, weight).astype(BF16)
    high = sq.astype(BF16).astype(F32)
    out_ref[rows:, :] = lines_of((high, sq - high), out_ref.shape[1])


def far_kv_product(place, sources, gains, blocks, gathered, after):
    order, own, got = gathered
    _, share, width = own.shape
    rows, cols = blocks[0][0].shape
    pieces = [piece for block in blocks for piece in block]
    dims = [(rows + TAIL, width), (len(blocks), rows, cols), (1, rows)]
    whole = lambda d: pl.BlockSpec(d, lambda i, p, s: (0,) * len(d))
    return pl.pallas_call(
        partial(far_kv_kernel, order=order, cuts=[len(block) for block in blocks]),
        out_shape=tuple(shape(d, t) for d, t in zip(dims, (BF16, BF16, F32))),
        grid_spec=pltpu.PrefetchScalarGridSpec(
            num_scalar_prefetch=2,
            grid=(1,),
            in_specs=[whole(gains.shape), ANY, ANY]
            + [whole(piece.shape) for piece in pieces]
            + [ANY for _ in after],
            out_specs=[whole(d) for d in dims],
            scratch_shapes=[
                pltpu.VMEM((len(order) * share, width), BF16),
                pltpu.SemaphoreType.DMA((len(order),)),
            ],
        ),
        compiler_params=PARAMS,
        name="far_kv",
    )(place, sources, gains, own, got, *pieces, *after)


def far_kernel(place_ref, src_ref, x_ref, own_ref, got_ref, *rest, order):
    out_ref, weight, sems = rest[-3:]
    for copy in place_weights(place_ref, own_ref, got_ref, weight, sems, order):
        copy.wait()
    out_ref[...] = far_sum(src_ref, x_ref, weight).astype(BF16)


def lines_of(rows, width):
    lines = []
    for row in rows:
        for at in range(0, row.shape[1], width):
            line = row[:, at : at + width]
            if line.shape[1] < width:
                rest = jnp.zeros((1, width - line.shape[1]), F32)
                line = jnp.concatenate([line, rest], axis=1)
            lines.append(line)
    lines.append(jnp.zeros((TAIL - len(lines), width), F32))
    return jnp.concatenate(lines, axis=0).astype(BF16)


def rows_of(tail, count, length):
    per_row = -(-length // tail.shape[1])
    rows = []
    for r in range(count):
        lines = [tail[r * per_row + i : r * per_row + i + 1, :] for i in range(per_row)]
        rows.append(jnp.concatenate(lines, axis=1)[:, :length])
    return rows


def far_product(place, sources, x, gathered, after):
    order, own, got = gathered
    _, share, width = own.shape
    rows = x.shape[1]
    return pl.pallas_call(
        partial(far_kernel, order=order),
        out_shape=shape((rows, width), BF16),
        grid_spec=pltpu.PrefetchScalarGridSpec(
            num_scalar_prefetch=2,
            grid=(1,),
            in_specs=[pl.BlockSpec(x.shape, lambda i, p, s: (0, 0, 0)), ANY, ANY]
            + [ANY for _ in after],
            out_specs=pl.BlockSpec((rows, width), lambda i, p, s: (0, 0)),
            scratch_shapes=[
                pltpu.VMEM((len(order) * share, width), BF16),
                pltpu.SemaphoreType.DMA((len(order),)),
            ],
        ),
        compiler_params=PARAMS,
        name="far",
    )(place, sources, x, own, got, *after)


def near_kernel(src_ref, x_ref, k_ref, v_ref, q_ref, *rest):
    out_ref = rest[-1]
    x = x_ref[0]

    @pl.when(pl.program_id(0) == 0)
    def _():
        out_ref[...] = jnp.zeros_like(out_ref)

    column = 0
    for ref in (k_ref, v_ref, q_ref):
        at = slice(column, column + ref.shape[1])
        out_ref[:, at] += jnp.dot(x, ref[...], preferred_element_type=F32)
        column += ref.shape[1]


def near_product(sources, x, weights, after):
    count, chunk, cols = x.shape
    widths = [w.shape[1] for w in weights]
    return pl.pallas_call(
        near_kernel,
        out_shape=shape((chunk, sum(widths)), F32),
        grid_spec=pltpu.PrefetchScalarGridSpec(
            num_scalar_prefetch=1,
            grid=(count,),
            in_specs=[pl.BlockSpec((1, chunk, cols), lambda i, s: (i, 0, 0))]
            + [pl.BlockSpec((cols, w), lambda i, s: (s[i], 0)) for w in widths]
            + [ANY for _ in after],
            out_specs=pl.BlockSpec((chunk, sum(widths)), lambda i, s: (0, 0)),
        ),
        compiler_params=PARAMS,
        name="near",
    )(sources, x, *weights, *after)


def keys_kernel(near_ref, far_ref, sq_ref, id_ref, cos_ref, sin_ref, *rest, model):
    out_ref, sum_ref = rest[-2:]
    rows, width = near_ref.shape[0], far_ref.shape[1]
    tail = far_ref[rows:, :].astype(F32)
    total = sum(rows_of(tail, 2, rows), sq_ref[...])
    factor = to_column(lax.rsqrt(total / model + epsilon))
    sum_ref[...] = total
    keys, values = slice(0, HEAD_SIZE), slice(HEAD_SIZE, 2 * HEAD_SIZE)
    part = (near_ref[:, keys] + far_ref[:rows, keys].astype(F32)) * factor
    part = rotate(part, cos_ref[...], sin_ref[...]).astype(BF16)
    out_ref[: rows // 2, keys] = part[: rows // 2]
    out_ref[: rows // 2, values] = part[rows // 2 :]
    part = (near_ref[:, values] + far_ref[:rows, values].astype(F32)) * factor
    part = part.T.astype(BF16)
    for i, at in enumerate(range(0, rows, width)):
        row = rows // 2 + i * HEAD_SIZE
        out_ref[row : row + HEAD_SIZE, :] = part[:, at : at + width]
    out_ref[rows:, :] = lines_of((id_ref[...].astype(F32),), width)


def keys_values(near, far, sq, ids, cosine, sine, after, model):
    rows, width = near.shape[0], far.shape[1]
    whole = lambda i: (0, 0)
    return pl.pallas_call(
        partial(keys_kernel, model=model),
        out_shape=(shape(far.shape, BF16), shape(sq.shape, F32)),
        grid=(1,),
        in_specs=[pl.BlockSpec((rows, width), whole)]
        + [pl.BlockSpec(a.shape, whole) for a in (far, sq, ids, cosine, sine)]
        + [ANY for _ in after],
        out_specs=[pl.BlockSpec(far.shape, whole), pl.BlockSpec(sq.shape, whole)],
        compiler_params=PARAMS,
        name="keys",
    )(near, far, sq, ids, cosine, sine, *after)


def queries_kernel(near_ref, far_ref, sum_ref, cos_ref, sin_ref, out_ref, *, model):
    scale = query_scale * math.log2(math.e)
    factor = to_column(lax.rsqrt(sum_ref[...] / model + epsilon) * scale)
    for c in range(0, out_ref.shape[1], HEAD_SIZE):
        at = slice(c, c + HEAD_SIZE)
        part = (near_ref[:, at] + far_ref[:, at].astype(F32)) * factor
        out_ref[:, at] = rotate(part, cos_ref[...], sin_ref[...]).astype(BF16)


def finished_queries(near, far, sums, cosine, sine, model):
    rows, width = far.shape
    last = near.shape[1] // width - 1
    whole = lambda i: (0, 0)
    return pl.pallas_call(
        partial(queries_kernel, model=model),
        out_shape=shape((rows, width), BF16),
        grid=(1,),
        in_specs=[pl.BlockSpec((rows, width), lambda i: (0, last))]
        + [pl.BlockSpec(a.shape, whole) for a in (far, sums, cosine, sine)],
        out_specs=pl.BlockSpec((rows, width), whole),
        compiler_params=PARAMS,
        cost_estimate=pl.CostEstimate(flops=HIDE, bytes_accessed=10**8, transcendentals=0),
        name="queries",
    )(near, far, sums, cosine, sine)


def attention_kernel(seq_ref, q_ref, id_ref, after_ref, *rest, back, offset):
    kv_refs, (out_ref, k_scr, vt_scr, count_scr) = rest[:-4], rest[-4:]
    part_rows, message = kv_refs[0].shape[0] - TAIL, kv_refs[0].shape[1]
    group = q_ref.shape[1] // HEAD_SIZE
    tile = pl.program_id(0)

    @pl.when(tile == 0)
    def _():
        counts = [jnp.zeros((1, 1), F32) for _ in range(DOCUMENTS)]
        for b, kv_ref in enumerate(kv_refs):
            row, half = b * part_rows, part_rows // 2
            k_scr[row : row + half, :] = kv_ref[:half, :HEAD_SIZE]
            k_scr[row + half : row + part_rows, :] = kv_ref[:half, HEAD_SIZE:]
            for i, at in enumerate(range(0, part_rows, message)):
                first = half + i * HEAD_SIZE
                vt_scr[:, row + at : row + at + message] = kv_ref[first : first + HEAD_SIZE, :]
            (ids,) = rows_of(kv_ref[part_rows:, :].astype(F32), 1, part_rows)
            exists = b >= back - seq_ref[0]
            ids = jnp.where(exists, ids, -1.0)
            for d in range(DOCUMENTS):
                below = (ids < d).astype(F32)
                counts[d] = counts[d] + jnp.sum(below, axis=1, keepdims=True)
        for d in range(DOCUMENTS):
            count_scr[d : d + 1, :] = jnp.broadcast_to(counts[d], (1, LANES))

    heads = [q_ref[:, c : c + HEAD_SIZE] for c in range(0, group * HEAD_SIZE, HEAD_SIZE)]
    q2 = jnp.concatenate(heads, axis=0)
    width = group * Q_TILE

    start = jnp.zeros((1, Q_TILE), F32)
    for d in range(DOCUMENTS):
        start = jnp.where(id_ref[...] == d, count_scr[d : d + 1, :], start)
    start = start.astype(jnp.int32)
    low = jnp.min(start) // K_TILE
    start = jnp.concatenate([start] * group, axis=1)
    first = back * part_rows + offset + tile * Q_TILE
    place = first + lax.broadcasted_iota(jnp.int32, (1, Q_TILE), 1)
    place = jnp.concatenate([place] * group, axis=1)

    def score(j):
        base = pl.multiple_of(j * K_TILE, K_TILE)
        return lax.dot_general(
            k_scr[pl.ds(base, K_TILE), :],
            q2,
            (((1,), (1,)), ((), ())),
            preferred_element_type=F32,
        )

    stop = (first + Q_TILE + K_TILE - 1) // K_TILE

    def step(j, state):
        scores, run_max, run_sum, acc = state
        following = score(jnp.minimum(j + 1, stop - 1))
        base = pl.multiple_of(j * K_TILE, K_TILE)
        key_pos = base + lax.broadcasted_iota(jnp.int32, (K_TILE, width), 0)
        allowed = (key_pos >= start) & (key_pos <= place)
        scores = jnp.where(allowed, scores, NEG)
        new_max = jnp.maximum(run_max, jnp.max(scores, axis=0, keepdims=True))
        expo = jnp.exp2(scores - new_max)
        factor = jnp.exp2(run_max - new_max)
        run_sum = run_sum * factor + jnp.sum(expo, axis=0, keepdims=True)
        acc = acc * factor + jnp.dot(
            vt_scr[:, pl.ds(base, K_TILE)], expo.astype(BF16), preferred_element_type=F32
        )
        return following, new_max, run_sum, acc

    state = (
        score(low),
        jnp.full((1, width), NEG, F32),
        jnp.zeros((1, width), F32),
        jnp.zeros((HEAD_SIZE, width), F32),
    )
    _, _, run_sum, acc = lax.fori_loop(low, stop, step, state)
    context = (acc / run_sum).T
    for g in range(group):
        out_ref[:, g * HEAD_SIZE : (g + 1) * HEAD_SIZE] = context[
            g * Q_TILE : (g + 1) * Q_TILE
        ].astype(BF16)


def attend(seq, queries, ids, after, blocks, c):
    rows, width = queries.shape[0] // CHUNKS, queries.shape[1]
    back = len(blocks) - 1
    tiles = rows // Q_TILE
    keys = len(blocks) * queries.shape[0]
    return pl.pallas_call(
        partial(attention_kernel, back=back, offset=c * rows),
        out_shape=shape((rows, width), BF16),
        grid_spec=pltpu.PrefetchScalarGridSpec(
            num_scalar_prefetch=1,
            grid=(tiles,),
            in_specs=[
                pl.BlockSpec((Q_TILE, width), lambda i, s: (c * tiles + i, 0)),
                pl.BlockSpec((1, Q_TILE), lambda i, s: (0, c * tiles + i)),
                ANY,
            ]
            + [pl.BlockSpec(b.shape, lambda i, s: (0, 0)) for b in blocks],
            out_specs=pl.BlockSpec((Q_TILE, width), lambda i, s: (i, 0)),
            scratch_shapes=[
                pltpu.VMEM((keys, HEAD_SIZE), BF16),
                pltpu.VMEM((HEAD_SIZE, keys), BF16),
                pltpu.VMEM((DOCUMENTS, LANES), F32),
            ],
        ),
        compiler_params=PARAMS,
        cost_estimate=pl.CostEstimate(
            flops=4 * rows * width * keys,
            bytes_accessed=4 * keys * width,
            transcendentals=rows * keys * width // HEAD_SIZE,
        ),
        name="attend",
    )(seq, queries, ids, after, *blocks)


def first_output_kernel(at_ref, own_o_ref, o_ref, *rest):
    ctx_refs, out_ref = rest[:-2], rest[-1]
    total = jnp.dot(ctx_refs[0][...], own_o_ref[...], preferred_element_type=F32)
    for i, ctx_ref in enumerate(ctx_refs[1:]):
        total = total + jnp.dot(ctx_ref[...], o_ref[at_ref[1 + i]], preferred_element_type=F32)
    out_ref[...] = total


def last_output_kernel(at_ref, part_ref, o_ref, *rest):
    ctx_refs, (before_ref, out_ref, sq_ref, acc) = rest[:-4], rest[-4:]
    step = pl.program_id(0)
    total = part_ref[...]
    for i, ctx_ref in enumerate(ctx_refs):
        total = total + jnp.dot(ctx_ref[...], o_ref[at_ref[i]], preferred_element_type=F32)
    out_ref[...] = total
    squares = jnp.sum(total * total, axis=1, keepdims=True)
    squares = jnp.broadcast_to(squares, acc.shape)

    @pl.when(step == 0)
    def _():
        acc[...] = squares

    @pl.when(step > 0)
    def _():
        acc[...] += squares

    @pl.when(step == pl.num_programs(0) - 1)
    def _():
        done = sq_ref.shape[1] - acc.shape[0]
        if done:
            sq_ref[:, :done] = before_ref[...]
        sq_ref[:, done:] = acc[...].T[0:1, :]


def column_tiles(cols):
    tiles = 3 if cols % (3 * LANES) == 0 else 1
    return tiles, cols // tiles


def first_output(column, order, o_weight, gathered, contexts, after):
    chunk, width = contexts[0].shape
    others, _, cols = gathered.shape
    tiles, tile = column_tiles(cols)
    if cols % LANES:
        o_weight = lax.dynamic_slice_in_dim(o_weight, column * cols, cols, axis=1)
        column = jnp.int32(0)
    return pl.pallas_call(
        first_output_kernel,
        out_shape=shape((chunk, cols), F32),
        grid_spec=pltpu.PrefetchScalarGridSpec(
            num_scalar_prefetch=1,
            grid=(tiles,),
            in_specs=[
                pl.BlockSpec((width, tile), lambda i, at: (0, at[0] * tiles + i)),
                pl.BlockSpec((others, width, tile), lambda i, at: (0, 0, i)),
            ]
            + [pl.BlockSpec((chunk, width), lambda i, at: (0, 0)) for _ in contexts]
            + [ANY],
            out_specs=pl.BlockSpec((chunk, tile), lambda i, at: (0, i)),
        ),
        compiler_params=PARAMS,
        cost_estimate=pl.CostEstimate(flops=HIDE, bytes_accessed=10**8, transcendentals=0),
        name="first_output",
    )(jnp.stack([column] + order), o_weight, gathered, *contexts, after)


def last_output(order, part, gathered, contexts, before, c):
    chunk, width = contexts[0].shape
    others, _, cols = gathered.shape
    tiles, tile = column_tiles(cols)
    return pl.pallas_call(
        last_output_kernel,
        out_shape=(shape((chunk, cols), F32), shape((1, (c + 1) * chunk), F32)),
        grid_spec=pltpu.PrefetchScalarGridSpec(
            num_scalar_prefetch=1,
            grid=(tiles,),
            in_specs=[
                pl.BlockSpec((chunk, tile), lambda i, at: (0, i)),
                pl.BlockSpec((others, width, tile), lambda i, at: (0, 0, i)),
            ]
            + [pl.BlockSpec((chunk, width), lambda i, at: (0, 0)) for _ in contexts]
            + [pl.BlockSpec(before.shape, lambda i, at: (0, 0))],
            out_specs=[
                pl.BlockSpec((chunk, tile), lambda i, at: (0, i)),
                pl.BlockSpec((1, (c + 1) * chunk), lambda i, at: (0, 0)),
            ],
            scratch_shapes=[pltpu.VMEM((chunk, LANES), F32)],
        ),
        compiler_params=PARAMS,
        name="last_output",
    )(jnp.stack(order), part, gathered, *contexts, before)


def final_kernel(token_ref, gain_ref, *rest, model):
    branch_refs, sq_refs, out_ref = rest[:CHUNKS], rest[CHUNKS:-1], rest[-1]
    total = sq_refs[0][...]
    for sq_ref in sq_refs[1:]:
        total = total + sq_ref[...]
    factor = to_column(lax.rsqrt(total / model + epsilon))[:, 0:1]
    for c in range(CHUNKS):

        @pl.when(pl.program_id(0) * CHUNKS // pl.num_programs(0) == c)
        def _():
            out = token_ref[...].astype(F32) + branch_refs[c][...] * factor * gain_ref[...]
            out_ref[...] = out.astype(BF16)


def finish(tokens, branches, out_gain, sums, model):
    rows, cols = tokens.shape
    tiles = rows // CHUNKS // Q_TILE
    held = lambda c: lambda i: (jnp.clip(i - c * tiles, 0, tiles - 1), 0)
    return pl.pallas_call(
        partial(final_kernel, model=model),
        out_shape=shape(tokens.shape, BF16),
        grid=(CHUNKS * tiles,),
        in_specs=[
            pl.BlockSpec((Q_TILE, cols), lambda i: (i, 0)),
            pl.BlockSpec((1, cols), lambda i: (0, 0)),
        ]
        + [pl.BlockSpec((Q_TILE, cols), held(c)) for c in range(CHUNKS)]
        + [pl.BlockSpec((1, Q_TILE), lambda i: (0, i)) for _ in sums],
        out_specs=pl.BlockSpec((Q_TILE, cols), lambda i: (i, 0)),
        compiler_params=PARAMS,
        name="finish",
    )(tokens, out_gain, *branches, *sums)


def per_device(
    tokens, seg_ids, in_gain, q_weight, k_weight, value_weight, o_weight, out_gain, *, sizes
):
    rows, cols = tokens.shape
    model = in_gain.shape[0]
    nz, nseq = sizes["tensor"], sizes["seq"]
    plane = nseq * sizes["groups"]
    z = lax.axis_index("tensor")
    seq = lax.axis_index("seq")
    in_plane = lax.axis_index(PLANE)
    half = nz // 2
    side, within = z // half, z % half
    half_rows = half * cols

    ring = [(i, i // half * half + (i + 1) % half) for i in range(nz)]
    swap = [(i, (i + half) % nz) for i in range(nz)]
    turn = lambda k: [(i, (i + k) % nz) for i in range(nz)]
    seq_bits = [1 << b for b in range(1, nseq.bit_length() - 1)]
    group_bits = [nseq << b for b in range(sizes["groups"].bit_length() - 1)]

    share = half_rows // plane
    at = jnp.reshape((1 - side) * plane + in_plane, (1,))
    inner = seq_bits + group_bits
    masks_kv, masks_q = inner + [1], inner[::-1] + [1]
    last = len(masks_kv) - 1
    eighth = rows // 48 * 8
    counts = [eighth, rows // 2 - 2 * TAIL, rows // 2 + 2 * TAIL - eighth]
    packed_kv, packed_q, cut = pack(
        at, q_weight, k_weight, value_weight, share, tokens, counts[0]
    )
    own_kv = lax.ppermute(packed_kv, "tensor", swap)[None]
    own_q = lax.ppermute(packed_q, "tensor", swap)[None]
    received = [lax.ppermute(cut, "tensor", ring)]
    o_share = o_weight.shape[0] // plane
    columns = [(z + k) % nz * cols for k in range(1, nz)]
    pieces = cut_pieces(in_plane * o_share, columns, o_weight, o_share, cols, own_kv)
    moved = [lax.ppermute(p, "tensor", turn(k + 1)) for k, p in enumerate(pieces)]

    order_kv, order_q, first = [0], [0], counts[0]
    for step, (mask_kv, mask_q) in enumerate(zip(masks_kv, masks_q)):
        after, count = [], 0
        if step == 0:
            pairs, after = [], [own_kv, own_q, received[0]]
        else:
            pairs = [(own_kv, far_kv), (own_q, far_q)]
        if step < 2:
            count = counts[1 + step]
        if step == last:
            after = [received[1]] + moved
        outs = stage(pairs, tokens, first, count, after, HIDE if step == last else 0)
        if pairs:
            own_kv, own_q = outs[:2]
        if count:
            received.append(lax.ppermute(outs[-1], "tensor", ring))
        first += count
        far_kv = lax.ppermute(own_kv, PLANE, [(i, i ^ mask_kv) for i in range(plane)])
        far_q = lax.ppermute(own_q, PLANE, [(i, i ^ mask_q) for i in range(plane)])
        order_kv = order_kv + [k ^ mask_kv for k in order_kv]
        order_q = order_q + [k ^ mask_q for k in order_q]
    far_kv, far_q = (order_kv, own_kv, far_kv), (order_q, own_q, far_q)

    own_o = jnp.stack(moved)[None]

    def double(own, step, after):
        if step > 0:
            (own,) = stage([own], tokens, 0, 0, after)
        return own, lax.ppermute(own, PLANE, [(i, i ^ masks_kv[step]) for i in range(plane)])

    sources = (within + half - jnp.arange(half, dtype=jnp.int32)) % half
    blocks = [[tokens], received]
    for _ in range(half - 2):
        blocks.append([lax.ppermute(part, "tensor", ring) for part in blocks[-1]])
    gains = in_gain.reshape(nz, 1, cols)
    place = jnp.stack([in_plane, side * half])
    sent_kv, x, sq = far_kv_product(
        place, sources, gains, blocks, far_kv, [far_q[2]]
    )
    got_kv = lax.ppermute(sent_kv, "tensor", swap)
    pair_o = double(own_o, 0, [])
    for step in range(1, last - 1):
        pair_o = double(pair_o, step, [])
    weights = (k_weight, value_weight, q_weight)

    near = near_product(side * half + sources, x, weights, [sent_kv])

    sent_q = far_product(place, sources, x, far_q, [near])
    got_q = lax.ppermute(sent_q, "tensor", swap)
    pair_o = double(pair_o, last - 1, [sent_q])
    cosine, sine = rotation_table(seq * rows + jnp.arange(rows, dtype=jnp.int32))
    ids = seg_ids[None, :]
    own_kv, sums = keys_values(
        near, got_kv, sq, ids, cosine, sine, [sent_q, pair_o[0]], model
    )
    pair_o = double(pair_o, last, [own_kv])
    gathered_o = lay_pieces(place, order_kv, *pair_o)

    back = -(-(nseq * rows // 2 - 1) // rows)
    kv_blocks = [own_kv]
    for k in range(1, back + 1):
        earlier = [(i, i + k) for i in range(nseq - k)]
        kv_blocks.insert(0, lax.ppermute(own_kv, "seq", earlier))

    queries = finished_queries(near, got_q, sums, cosine, sine, model)
    seq_at = jnp.reshape(seq, (1,))
    early, late, after = [], [], own_kv
    for c in range(CHUNKS):
        context = attend(seq_at, queries, ids, after, kv_blocks, c)
        after = gathered_o
        if nz == 4:
            pairs = [(i, i ^ 1) for i in range(nz)]
            opposite = lax.ppermute(context, "tensor", swap)
            beside = lax.ppermute(context, "tensor", pairs)
            across = lax.ppermute(opposite, "tensor", pairs)
            early.append([context, beside])
            late.append([opposite, across])
            order = [2 - 2 * (z % 2), jnp.int32(1), 2 * (z % 2)]
        else:
            early.append([context])
            late.append([lax.ppermute(context, "tensor", turn(k)) for k in range(1, nz)])
            order = [jnp.int32(k) for k in range(nz - 1)]
    split = len(early[0]) - 1
    branches, own_sq = [], sums
    for c in range(CHUNKS):
        part = first_output(z, order[:split], o_weight, gathered_o, early[c], context)
        branch, own_sq = last_output(order[split:], part, gathered_o, late[c], own_sq, c)
        branches.append(branch)
    squares = [own_sq]
    squares += [lax.ppermute(own_sq, "tensor", turn(k)) for k in range(1, nz)]
    return finish(tokens, branches, out_gain[None, :], squares, model)


def solution(mesh):
    return jax.shard_map(
        partial(per_device, sizes=dict(mesh.shape)),
        mesh=mesh,
        in_specs=(
            P(("groups", "seq"), "tensor"),
            P(("groups", "seq")),
            P(),
            P(None, "tensor"),
            P(None, "tensor"),
            P(None, "tensor"),
            P("tensor", None),
            P("tensor"),
        ),
        out_specs=P(("groups", "seq"), "tensor"),
        check_vma=False,
    )
```

```python
import math
from functools import partial

import jax
import jax.numpy as jnp
from jax import lax
from jax.experimental import pallas as pl
from jax.experimental.pallas import tpu as pltpu
from jax.sharding import PartitionSpec as P

HEAD_SIZE = 128
PLANE = ("groups", "seq")

epsilon = 1e-06
query_scale = 144.0 ** (-0.5)
rope_base = 10000.0
NEG = -1e30
Q_TILE = 128
K_TILE = 256
CHUNKS = 2
LANES = 128
TAIL = 16
F32, BF16 = jnp.float32, jnp.bfloat16
ANY = pl.BlockSpec(memory_space=pl.ANY)
HBM = pl.BlockSpec(memory_space=pltpu.HBM)
VMEM = pl.BlockSpec(memory_space=pltpu.VMEM)
DOCUMENTS = 8
HIDE = 5 * 10**10
PARAMS = pltpu.CompilerParams(vmem_limit_bytes=48 * 1024 * 1024)
ALL_VMEM = pltpu.CompilerParams(vmem_limit_bytes=62 * 1024 * 1024)


def shape(dims, dtype):
    return jax.ShapeDtypeStruct(dims, dtype)


def to_row(column):
    return jnp.broadcast_to(column, (column.shape[0], LANES)).T[0:1, :]


def to_column(row):
    return jnp.broadcast_to(row, (LANES, row.shape[1])).T


def rotation_table(token_places):
    half_dim = HEAD_SIZE // 2
    inverse = rope_base ** (-jnp.arange(half_dim, dtype=F32) / half_dim)
    angles = token_places.astype(F32)[:, None] * inverse[None, :]
    cosine, sine = jnp.cos(angles), jnp.sin(angles)
    return jnp.concatenate([cosine, cosine], 1), jnp.concatenate([-sine, sine], 1)


def rotate(vectors, cosine, sine):
    return vectors * cosine + pltpu.roll(vectors, HEAD_SIZE // 2, 1) * sine


def pack_kernel(at_ref, q_ref, k_ref, v_ref, x_ref, kv_out, q_out, x_out, sems):
    share, width = q_out.shape[0], k_ref.shape[1]
    rows = pl.ds(pl.multiple_of(at_ref[0] * share, TAIL), share)
    copies = [
        pltpu.make_async_copy(k_ref.at[rows], kv_out.at[:, pl.ds(0, width)], sems.at[0]),
        pltpu.make_async_copy(v_ref.at[rows], kv_out.at[:, pl.ds(width, width)], sems.at[1]),
        pltpu.make_async_copy(q_ref.at[rows], q_out, sems.at[2]),
        pltpu.make_async_copy(x_ref.at[pl.ds(0, x_out.shape[0])], x_out, sems.at[3]),
    ]
    for copy in copies:
        copy.start()
    for copy in copies:
        copy.wait()


def pack(at, q_weight, k_weight, v_weight, share, tokens, rows):
    kv_width = k_weight.shape[1] + v_weight.shape[1]
    dims = [(share, kv_width), (share, q_weight.shape[1]), (rows, tokens.shape[1])]
    return pl.pallas_call(
        pack_kernel,
        out_shape=tuple(shape(d, BF16) for d in dims),
        grid_spec=pltpu.PrefetchScalarGridSpec(
            num_scalar_prefetch=1,
            grid=(1,),
            in_specs=[HBM, HBM, HBM, HBM],
            out_specs=[pl.BlockSpec(d, lambda i, at: (0, 0)) for d in dims],
            scratch_shapes=[pltpu.SemaphoreType.DMA((4,))],
        ),
        compiler_params=ALL_VMEM,
        name="pack",
    )(at, q_weight, k_weight, v_weight, tokens)


def gate_kernel(x_ref, after_ref, out_ref):
    pass


def gate(x, after):
    return pl.pallas_call(
        gate_kernel,
        out_shape=shape(x.shape, x.dtype),
        in_specs=[ANY, ANY],
        out_specs=ANY,
        input_output_aliases={0: 0},
        compiler_params=PARAMS,
        name="gate",
    )(x, after)


def stage_kernel(*refs, pairs, first, count):
    outputs = pairs + (1 if count else 0)
    ins, outs, sems = refs[: -outputs - 1], refs[-outputs - 1 : -1], refs[-1]
    copies = []
    for p in range(pairs):
        held = ins[2 * p].shape[0]
        for side in range(2):
            there = outs[p].at[pl.ds(side * held, held)]
            copies.append(
                pltpu.make_async_copy(ins[2 * p + side], there, sems.at[len(copies)])
            )
    if count:
        rows = ins[2 * pairs].at[pl.ds(first, count)]
        copies.append(pltpu.make_async_copy(rows, outs[-1], sems.at[len(copies)]))
    for copy in copies:
        copy.start()
    for copy in copies:
        copy.wait()


def stage(joined, tokens, first, count, after, flops=0):
    dims = [(2 * pair[0].shape[0],) + pair[0].shape[1:] for pair in joined]
    if count:
        dims.append((count, tokens.shape[1]))
    return pl.pallas_call(
        partial(stage_kernel, pairs=len(joined), first=first, count=count),
        out_shape=tuple(shape(d, BF16) for d in dims),
        in_specs=[ANY] * (2 * len(joined) + 1 + len(after)),
        scratch_shapes=[pltpu.SemaphoreType.DMA((2 * len(joined) + 1,))],
        compiler_params=PARAMS,
        cost_estimate=pl.CostEstimate(flops=flops, bytes_accessed=flops // 500, transcendentals=0),
        name="stage",
    )(*[piece for pair in joined for piece in pair], tokens, *after)


def cut_kernel(at_ref, o_ref, after_ref, *rest):
    outs, sems = rest[:-1], rest[-1]
    copies = []
    for i, out in enumerate(outs):
        rows = pl.ds(pl.multiple_of(at_ref[0], TAIL), out.shape[0])
        columns = pl.ds(pl.multiple_of(at_ref[1 + i], LANES), out.shape[1])
        copies.append(pltpu.make_async_copy(o_ref.at[rows, columns], out, sems.at[i]))
    for copy in copies:
        copy.start()
    for copy in copies:
        copy.wait()


def cut_pieces(row, columns, o_weight, share, cols, after):
    if cols % LANES:
        return [lax.dynamic_slice(o_weight, (row, c), (share, cols)) for c in columns]
    return pl.pallas_call(
        cut_kernel,
        out_shape=tuple(shape((share, cols), BF16) for _ in columns),
        grid_spec=pltpu.PrefetchScalarGridSpec(
            num_scalar_prefetch=1,
            grid=(1,),
            in_specs=[ANY, ANY],
            out_specs=[VMEM for _ in columns],
            scratch_shapes=[pltpu.SemaphoreType.DMA((len(columns),))],
        ),
        compiler_params=PARAMS,
        name="cut",
    )(jnp.stack([row] + columns), o_weight, after)


def lay_kernel(place_ref, own_ref, got_ref, out_ref, sems, *, order):
    held, others, share, _ = own_ref.shape
    copies = []
    for i, mask in enumerate(order):
        piece = own_ref.at[i] if i < held else got_ref.at[i - held]
        row = pl.multiple_of((place_ref[0] ^ mask) * share, TAIL)
        there = out_ref.at[:, pl.ds(row, share)]
        copies.append(pltpu.make_async_copy(piece, there, sems.at[i]))
    for copy in copies:
        copy.start()
    for copy in copies:
        copy.wait()


def lay_pieces(place, order, own, got):
    _, others, share, cols = own.shape
    dims = (others, len(order) * share, cols)
    return pl.pallas_call(
        partial(lay_kernel, order=order),
        out_shape=shape(dims, BF16),
        grid_spec=pltpu.PrefetchScalarGridSpec(
            num_scalar_prefetch=1,
            grid=(1,),
            in_specs=[ANY, ANY],
            out_specs=pl.BlockSpec(dims, lambda i, p: (0, 0, 0)),
            scratch_shapes=[pltpu.SemaphoreType.DMA((len(order),))],
        ),
        compiler_params=PARAMS,
        name="lay",
    )(place, own, got)


def place_weights(place_ref, own_ref, got_ref, weight, sems, order):
    held, share, _ = own_ref.shape
    copies = []
    for i, mask in enumerate(order):
        piece = own_ref.at[i] if i < held else got_ref.at[i - held]
        row = pl.multiple_of((place_ref[0] ^ mask) * share, TAIL)
        there = weight.at[pl.ds(row, share)]
        copies.append(pltpu.make_async_copy(piece, there, sems.at[i]))
    for copy in copies:
        copy.start()
    return copies


def far_sum(src_ref, x_ref, weight):
    count, _, cols = x_ref.shape
    total = None
    for k in range(count):
        row = pl.multiple_of(src_ref[k] * cols, TAIL)
        term = jnp.dot(x_ref[k], weight[pl.ds(row, cols), :], preferred_element_type=F32)
        total = term if total is None else total + term
    return total


def far_kv_kernel(
    place_ref, src_ref, gain_ref, own_ref, got_ref, token_ref, *rest, order, cuts, first
):
    x_refs, (out_ref, x_out, sq_ref, weight, tokens, sems) = rest[: sum(cuts)], rest[-6:]
    rows = x_out.shape[1]
    copies = place_weights(place_ref, own_ref, got_ref, weight, sems, order)
    mine = pltpu.make_async_copy(
        token_ref.at[pl.ds(first, rows)], tokens, sems.at[len(order)]
    )
    mine.start()
    columns, at = [], 0
    for k, pieces in [(k + 1, pieces) for k, pieces in enumerate(cuts)] + [(0, 1)]:
        if k == 0:
            mine.wait()
        gain = gain_ref[place_ref[1] + src_ref[k]]
        column, row = [], 0
        for x_ref in x_refs[at : at + pieces] if k else [tokens]:
            x = x_ref[...].astype(F32)
            column.append(jnp.sum(x * x, axis=1, keepdims=True))
            x_out[k, row : row + x.shape[0]] = (x * gain).astype(BF16)
            row += x.shape[0]
        columns.append(jnp.concatenate(column, axis=0))
        at += pieces
    sq = to_row(sum(columns[1:], columns[0]))
    sq_ref[...] = sq
    for copy in copies:
        copy.wait()
    out_ref[:rows, :] = far_sum(src_ref, x_out, weight).astype(BF16)
    high = sq.astype(BF16).astype(F32)
    out_ref[rows:, :] = lines_of((high, sq - high), out_ref.shape[1])


def far_kv_product(place, sources, gains, tokens, first, blocks, gathered, after):
    order, own, got = gathered
    _, share, width = own.shape
    cols = tokens.shape[1]
    rows = sum(piece.shape[0] for piece in blocks[0])
    pieces = [piece for block in blocks for piece in block]
    dims = [(rows + TAIL, width), (len(blocks) + 1, rows, cols), (1, rows)]
    whole = lambda d: pl.BlockSpec(d, lambda i, p, s: (0,) * len(d))
    return pl.pallas_call(
        partial(
            far_kv_kernel, order=order, cuts=[len(block) for block in blocks], first=first
        ),
        out_shape=tuple(shape(d, t) for d, t in zip(dims, (BF16, BF16, F32))),
        grid_spec=pltpu.PrefetchScalarGridSpec(
            num_scalar_prefetch=2,
            grid=(1,),
            in_specs=[whole(gains.shape), ANY, ANY, ANY]
            + [whole(piece.shape) for piece in pieces]
            + [ANY for _ in after],
            out_specs=[whole(d) for d in dims],
            scratch_shapes=[
                pltpu.VMEM((len(order) * share, width), BF16),
                pltpu.VMEM((rows, cols), BF16),
                pltpu.SemaphoreType.DMA((len(order) + 1,)),
            ],
        ),
        compiler_params=PARAMS,
        name="far_kv",
    )(place, sources, gains, own, got, tokens, *pieces, *after)


def far_kernel(place_ref, src_ref, own_ref, got_ref, *rest, order, groups):
    x_refs, (out_ref, weight, sems) = rest[:groups], rest[-3:]
    for copy in place_weights(place_ref, own_ref, got_ref, weight, sems, order):
        copy.wait()
    row = 0
    for x_ref in x_refs:
        rows = x_ref.shape[1]
        out_ref[row : row + rows, :] = far_sum(src_ref, x_ref, weight).astype(BF16)
        row += rows


def lines_of(rows, width):
    lines = []
    for row in rows:
        for at in range(0, row.shape[1], width):
            line = row[:, at : at + width]
            if line.shape[1] < width:
                rest = jnp.zeros((1, width - line.shape[1]), F32)
                line = jnp.concatenate([line, rest], axis=1)
            lines.append(line)
    lines.append(jnp.zeros((TAIL - len(lines), width), F32))
    return jnp.concatenate(lines, axis=0).astype(BF16)


def rows_of(tail, count, length):
    per_row = -(-length // tail.shape[1])
    rows = []
    for r in range(count):
        lines = [tail[r * per_row + i : r * per_row + i + 1, :] for i in range(per_row)]
        rows.append(jnp.concatenate(lines, axis=1)[:, :length])
    return rows


def far_product(place, sources, xs, gathered, after):
    order, own, got = gathered
    _, share, width = own.shape
    rows = sum(x.shape[1] for x in xs)
    return pl.pallas_call(
        partial(far_kernel, order=order, groups=len(xs)),
        out_shape=shape((rows, width), BF16),
        grid_spec=pltpu.PrefetchScalarGridSpec(
            num_scalar_prefetch=2,
            grid=(1,),
            in_specs=[ANY, ANY]
            + [pl.BlockSpec(x.shape, lambda i, p, s: (0, 0, 0)) for x in xs]
            + [ANY for _ in after],
            out_specs=pl.BlockSpec((rows, width), lambda i, p, s: (0, 0)),
            scratch_shapes=[
                pltpu.VMEM((len(order) * share, width), BF16),
                pltpu.SemaphoreType.DMA((len(order),)),
            ],
        ),
        compiler_params=PARAMS,
        name="far",
    )(place, sources, own, got, *xs, *after)


def near_kernel(src_ref, x_ref, k_ref, v_ref, q_ref, *rest):
    out_ref = rest[-1]
    x = x_ref[0]

    @pl.when(pl.program_id(0) == 0)
    def _():
        out_ref[...] = jnp.zeros_like(out_ref)

    column = 0
    for ref in (k_ref, v_ref, q_ref):
        at = slice(column, column + ref.shape[1])
        out_ref[:, at] += jnp.dot(x, ref[...], preferred_element_type=F32)
        column += ref.shape[1]


def near_product(sources, x, weights, after):
    count, chunk, cols = x.shape
    widths = [w.shape[1] for w in weights]
    return pl.pallas_call(
        near_kernel,
        out_shape=shape((chunk, sum(widths)), F32),
        grid_spec=pltpu.PrefetchScalarGridSpec(
            num_scalar_prefetch=1,
            grid=(count,),
            in_specs=[pl.BlockSpec((1, chunk, cols), lambda i, s: (i, 0, 0))]
            + [pl.BlockSpec((cols, w), lambda i, s: (s[i], 0)) for w in widths]
            + [ANY for _ in after],
            out_specs=pl.BlockSpec((chunk, sum(widths)), lambda i, s: (0, 0)),
        ),
        compiler_params=PARAMS,
        name="near",
    )(sources, x, *weights, *after)


def keys_kernel(id_ref, cos_ref, sin_ref, *rest, model, groups):
    near_refs, far_refs, sq_refs = (rest[g * groups : (g + 1) * groups] for g in range(3))
    out_ref, sum_ref = rest[-2:]
    width, rows = out_ref.shape[1], out_ref.shape[0] - TAIL
    keys, values = slice(0, HEAD_SIZE), slice(HEAD_SIZE, 2 * HEAD_SIZE)
    key_parts, value_parts, first = [], [], 0
    for near_ref, far_ref, sq_ref in zip(near_refs, far_refs, sq_refs):
        count = near_ref.shape[0]
        at = slice(first, first + count)
        tail = far_ref[count:, :].astype(F32)
        total = sum(rows_of(tail, 2, count), sq_ref[...])
        factor = to_column(lax.rsqrt(total / model + epsilon))
        sum_ref[:, at] = total
        part = (near_ref[:, keys] + far_ref[:count, keys].astype(F32)) * factor
        key_parts.append(rotate(part, cos_ref[at, :], sin_ref[at, :]).astype(BF16))
        part = (near_ref[:, values] + far_ref[:count, values].astype(F32)) * factor
        value_parts.append(part.T.astype(BF16))
        first += count
    part = jnp.concatenate(key_parts, axis=0)
    out_ref[: rows // 2, keys] = part[: rows // 2]
    out_ref[: rows // 2, values] = part[rows // 2 :]
    part = jnp.concatenate(value_parts, axis=1)
    for i, at in enumerate(range(0, rows, width)):
        row = rows // 2 + i * HEAD_SIZE
        out_ref[row : row + HEAD_SIZE, :] = part[:, at : at + width]
    out_ref[rows:, :] = lines_of((id_ref[...].astype(F32),), width)


def keys_values(nears, fars, sqs, ids, cosine, sine, after, model):
    rows, width = cosine.shape[0], fars[0].shape[1]
    whole = lambda i: (0, 0)
    dims = [(rows + TAIL, width), (1, rows)]
    return pl.pallas_call(
        partial(keys_kernel, model=model, groups=len(nears)),
        out_shape=tuple(shape(d, t) for d, t in zip(dims, (BF16, F32))),
        grid=(1,),
        in_specs=[pl.BlockSpec(a.shape, whole) for a in (ids, cosine, sine)]
        + [pl.BlockSpec((near.shape[0], width), whole) for near in nears]
        + [pl.BlockSpec(a.shape, whole) for a in (*fars, *sqs)]
        + [ANY for _ in after],
        out_specs=[pl.BlockSpec(d, whole) for d in dims],
        compiler_params=PARAMS,
        name="keys",
    )(ids, cosine, sine, *nears, *fars, *sqs, *after)


def queries_kernel(far_ref, sum_ref, cos_ref, sin_ref, *rest, model):
    near_refs, out_ref = rest[:-1], rest[-1]
    scale = query_scale * math.log2(math.e)
    first = 0
    for near_ref in near_refs:
        rows = slice(first, first + near_ref.shape[0])
        factor = to_column(lax.rsqrt(sum_ref[:, rows] / model + epsilon) * scale)
        for c in range(0, out_ref.shape[1], HEAD_SIZE):
            at = slice(c, c + HEAD_SIZE)
            part = (near_ref[:, at] + far_ref[rows, at].astype(F32)) * factor
            out_ref[rows, at] = rotate(part, cos_ref[rows, :], sin_ref[rows, :]).astype(BF16)
        first += near_ref.shape[0]


def finished_queries(nears, far, sums, cosine, sine, model):
    rows, width = far.shape
    last = nears[0].shape[1] // width - 1
    whole = lambda i: (0, 0)
    return pl.pallas_call(
        partial(queries_kernel, model=model),
        out_shape=shape((rows, width), BF16),
        grid=(1,),
        in_specs=[pl.BlockSpec(a.shape, whole) for a in (far, sums, cosine, sine)]
        + [pl.BlockSpec((near.shape[0], width), lambda i: (0, last)) for near in nears],
        out_specs=pl.BlockSpec((rows, width), whole),
        compiler_params=PARAMS,
        cost_estimate=pl.CostEstimate(flops=HIDE, bytes_accessed=10**8, transcendentals=0),
        name="queries",
    )(far, sums, cosine, sine, *nears)


def attention_kernel(seq_ref, q_ref, id_ref, after_ref, *rest, back, offset):
    kv_refs, (out_ref, k_scr, vt_scr, count_scr) = rest[:-4], rest[-4:]
    part_rows, message = kv_refs[0].shape[0] - TAIL, kv_refs[0].shape[1]
    group = q_ref.shape[1] // HEAD_SIZE
    tile = pl.program_id(0)

    @pl.when(tile == 0)
    def _():
        counts = [jnp.zeros((1, 1), F32) for _ in range(DOCUMENTS)]
        for b, kv_ref in enumerate(kv_refs):
            row, half = b * part_rows, part_rows // 2
            k_scr[row : row + half, :] = kv_ref[:half, :HEAD_SIZE]
            k_scr[row + half : row + part_rows, :] = kv_ref[:half, HEAD_SIZE:]
            for i, at in enumerate(range(0, part_rows, message)):
                first = half + i * HEAD_SIZE
                vt_scr[:, row + at : row + at + message] = kv_ref[first : first + HEAD_SIZE, :]
            (ids,) = rows_of(kv_ref[part_rows:, :].astype(F32), 1, part_rows)
            exists = b >= back - seq_ref[0]
            ids = jnp.where(exists, ids, -1.0)
            for d in range(DOCUMENTS):
                below = (ids < d).astype(F32)
                counts[d] = counts[d] + jnp.sum(below, axis=1, keepdims=True)
        for d in range(DOCUMENTS):
            count_scr[d : d + 1, :] = jnp.broadcast_to(counts[d], (1, LANES))

    heads = [q_ref[:, c : c + HEAD_SIZE] for c in range(0, group * HEAD_SIZE, HEAD_SIZE)]
    q2 = jnp.concatenate(heads, axis=0)
    width = group * Q_TILE

    start = jnp.zeros((1, Q_TILE), F32)
    for d in range(DOCUMENTS):
        start = jnp.where(id_ref[...] == d, count_scr[d : d + 1, :], start)
    start = start.astype(jnp.int32)
    low = jnp.min(start) // K_TILE
    start = jnp.concatenate([start] * group, axis=1)
    first = back * part_rows + offset + tile * Q_TILE
    place = first + lax.broadcasted_iota(jnp.int32, (1, Q_TILE), 1)
    place = jnp.concatenate([place] * group, axis=1)

    def score(j):
        base = pl.multiple_of(j * K_TILE, K_TILE)
        return lax.dot_general(
            k_scr[pl.ds(base, K_TILE), :],
            q2,
            (((1,), (1,)), ((), ())),
            preferred_element_type=F32,
        )

    stop = (first + Q_TILE + K_TILE - 1) // K_TILE

    def step(j, state):
        scores, run_max, run_sum, acc = state
        following = score(jnp.minimum(j + 1, stop - 1))
        base = pl.multiple_of(j * K_TILE, K_TILE)
        key_pos = base + lax.broadcasted_iota(jnp.int32, (K_TILE, width), 0)
        allowed = (key_pos >= start) & (key_pos <= place)
        scores = jnp.where(allowed, scores, NEG)
        new_max = jnp.maximum(run_max, jnp.max(scores, axis=0, keepdims=True))
        expo = jnp.exp2(scores - new_max)
        factor = jnp.exp2(run_max - new_max)
        run_sum = run_sum * factor + jnp.sum(expo, axis=0, keepdims=True)
        acc = acc * factor + jnp.dot(
            vt_scr[:, pl.ds(base, K_TILE)], expo.astype(BF16), preferred_element_type=F32
        )
        return following, new_max, run_sum, acc

    state = (
        score(low),
        jnp.full((1, width), NEG, F32),
        jnp.zeros((1, width), F32),
        jnp.zeros((HEAD_SIZE, width), F32),
    )
    _, _, run_sum, acc = lax.fori_loop(low, stop, step, state)
    context = (acc / run_sum).T
    for g in range(group):
        out_ref[:, g * HEAD_SIZE : (g + 1) * HEAD_SIZE] = context[
            g * Q_TILE : (g + 1) * Q_TILE
        ].astype(BF16)


def attend(seq, queries, ids, after, blocks, c):
    rows, width = queries.shape[0] // CHUNKS, queries.shape[1]
    back = len(blocks) - 1
    tiles = rows // Q_TILE
    keys = len(blocks) * queries.shape[0]
    return pl.pallas_call(
        partial(attention_kernel, back=back, offset=c * rows),
        out_shape=shape((rows, width), BF16),
        grid_spec=pltpu.PrefetchScalarGridSpec(
            num_scalar_prefetch=1,
            grid=(tiles,),
            in_specs=[
                pl.BlockSpec((Q_TILE, width), lambda i, s: (c * tiles + i, 0)),
                pl.BlockSpec((1, Q_TILE), lambda i, s: (0, c * tiles + i)),
                ANY,
            ]
            + [pl.BlockSpec(b.shape, lambda i, s: (0, 0)) for b in blocks],
            out_specs=pl.BlockSpec((Q_TILE, width), lambda i, s: (i, 0)),
            scratch_shapes=[
                pltpu.VMEM((keys, HEAD_SIZE), BF16),
                pltpu.VMEM((HEAD_SIZE, keys), BF16),
                pltpu.VMEM((DOCUMENTS, LANES), F32),
            ],
        ),
        compiler_params=PARAMS,
        cost_estimate=pl.CostEstimate(
            flops=4 * rows * width * keys,
            bytes_accessed=4 * keys * width,
            transcendentals=rows * keys * width // HEAD_SIZE,
        ),
        name="attend",
    )(seq, queries, ids, after, *blocks)


def first_output_kernel(at_ref, own_o_ref, o_ref, *rest):
    ctx_refs, out_ref = rest[:-2], rest[-1]
    total = jnp.dot(ctx_refs[0][...], own_o_ref[...], preferred_element_type=F32)
    for i, ctx_ref in enumerate(ctx_refs[1:]):
        total = total + jnp.dot(ctx_ref[...], o_ref[at_ref[1 + i]], preferred_element_type=F32)
    out_ref[...] = total


def last_output_kernel(at_ref, part_ref, o_ref, *rest):
    ctx_refs, (before_ref, out_ref, sq_ref, acc) = rest[:-4], rest[-4:]
    step = pl.program_id(0)
    total = part_ref[...]
    for i, ctx_ref in enumerate(ctx_refs):
        total = total + jnp.dot(ctx_ref[...], o_ref[at_ref[i]], preferred_element_type=F32)
    out_ref[...] = total
    squares = jnp.sum(total * total, axis=1, keepdims=True)
    squares = jnp.broadcast_to(squares, acc.shape)

    @pl.when(step == 0)
    def _():
        acc[...] = squares

    @pl.when(step > 0)
    def _():
        acc[...] += squares

    @pl.when(step == pl.num_programs(0) - 1)
    def _():
        done = sq_ref.shape[1] - acc.shape[0]
        if done:
            sq_ref[:, :done] = before_ref[...]
        sq_ref[:, done:] = acc[...].T[0:1, :]


def column_tiles(cols):
    tiles = 3 if cols % (3 * LANES) == 0 else 1
    return tiles, cols // tiles


def first_output(column, order, o_weight, gathered, contexts, after):
    chunk, width = contexts[0].shape
    others, _, cols = gathered.shape
    tiles, tile = column_tiles(cols)
    if cols % LANES:
        o_weight = lax.dynamic_slice_in_dim(o_weight, column * cols, cols, axis=1)
        column = jnp.int32(0)
    return pl.pallas_call(
        first_output_kernel,
        out_shape=shape((chunk, cols), F32),
        grid_spec=pltpu.PrefetchScalarGridSpec(
            num_scalar_prefetch=1,
            grid=(tiles,),
            in_specs=[
                pl.BlockSpec((width, tile), lambda i, at: (0, at[0] * tiles + i)),
                pl.BlockSpec((others, width, tile), lambda i, at: (0, 0, i)),
            ]
            + [pl.BlockSpec((chunk, width), lambda i, at: (0, 0)) for _ in contexts]
            + [ANY],
            out_specs=pl.BlockSpec((chunk, tile), lambda i, at: (0, i)),
        ),
        compiler_params=PARAMS,
        cost_estimate=pl.CostEstimate(flops=HIDE, bytes_accessed=10**8, transcendentals=0),
        name="first_output",
    )(jnp.stack([column] + order), o_weight, gathered, *contexts, after)


def last_output(order, part, gathered, contexts, before, c):
    chunk, width = contexts[0].shape
    others, _, cols = gathered.shape
    tiles, tile = column_tiles(cols)
    return pl.pallas_call(
        last_output_kernel,
        out_shape=(shape((chunk, cols), F32), shape((1, (c + 1) * chunk), F32)),
        grid_spec=pltpu.PrefetchScalarGridSpec(
            num_scalar_prefetch=1,
            grid=(tiles,),
            in_specs=[
                pl.BlockSpec((chunk, tile), lambda i, at: (0, i)),
                pl.BlockSpec((others, width, tile), lambda i, at: (0, 0, i)),
            ]
            + [pl.BlockSpec((chunk, width), lambda i, at: (0, 0)) for _ in contexts]
            + [pl.BlockSpec(before.shape, lambda i, at: (0, 0))],
            out_specs=[
                pl.BlockSpec((chunk, tile), lambda i, at: (0, i)),
                pl.BlockSpec((1, (c + 1) * chunk), lambda i, at: (0, 0)),
            ],
            scratch_shapes=[pltpu.VMEM((chunk, LANES), F32)],
        ),
        compiler_params=PARAMS,
        name="last_output",
    )(jnp.stack(order), part, gathered, *contexts, before)


def final_kernel(token_ref, gain_ref, *rest, model):
    branch_refs, sq_refs, out_ref = rest[:CHUNKS], rest[CHUNKS:-1], rest[-1]
    total = sq_refs[0][...]
    for sq_ref in sq_refs[1:]:
        total = total + sq_ref[...]
    factor = to_column(lax.rsqrt(total / model + epsilon))[:, 0:1]
    for c in range(CHUNKS):

        @pl.when(pl.program_id(0) * CHUNKS // pl.num_programs(0) == c)
        def _():
            out = token_ref[...].astype(F32) + branch_refs[c][...] * factor * gain_ref[...]
            out_ref[...] = out.astype(BF16)


def finish(tokens, branches, out_gain, sums, model):
    rows, cols = tokens.shape
    tiles = rows // CHUNKS // Q_TILE
    held = lambda c: lambda i: (jnp.clip(i - c * tiles, 0, tiles - 1), 0)
    return pl.pallas_call(
        partial(final_kernel, model=model),
        out_shape=shape(tokens.shape, BF16),
        grid=(CHUNKS * tiles,),
        in_specs=[
            pl.BlockSpec((Q_TILE, cols), lambda i: (i, 0)),
            pl.BlockSpec((1, cols), lambda i: (0, 0)),
        ]
        + [pl.BlockSpec((Q_TILE, cols), held(c)) for c in range(CHUNKS)]
        + [pl.BlockSpec((1, Q_TILE), lambda i: (0, i)) for _ in sums],
        out_specs=pl.BlockSpec((Q_TILE, cols), lambda i: (i, 0)),
        compiler_params=PARAMS,
        name="finish",
    )(tokens, out_gain, *branches, *sums)


def per_device(
    tokens, seg_ids, in_gain, q_weight, k_weight, value_weight, o_weight, out_gain, *, sizes
):
    rows, cols = tokens.shape
    model = in_gain.shape[0]
    nz, nseq = sizes["tensor"], sizes["seq"]
    plane = nseq * sizes["groups"]
    z = lax.axis_index("tensor")
    seq = lax.axis_index("seq")
    in_plane = lax.axis_index(PLANE)
    half = nz // 2
    side, within = z // half, z % half
    half_rows = half * cols

    ring = [(i, i // half * half + (i + 1) % half) for i in range(nz)]
    swap = [(i, (i + half) % nz) for i in range(nz)]
    turn = lambda k: [(i, (i + k) % nz) for i in range(nz)]
    seq_bits = [1 << b for b in range(1, nseq.bit_length() - 1)]
    group_bits = [nseq << b for b in range(sizes["groups"].bit_length() - 1)]

    share = half_rows // plane
    at = jnp.reshape((1 - side) * plane + in_plane, (1,))
    inner = seq_bits + group_bits
    masks_kv, masks_q = inner + [1], inner[::-1] + [1]
    last = len(masks_kv) - 1
    counts = [rows // 6, rows // 2 - rows // 6, rows // 2]
    packed_kv, packed_q, cut = pack(
        at, q_weight, k_weight, value_weight, share, tokens, counts[0]
    )
    own_kv = lax.ppermute(packed_kv, "tensor", swap)[None]
    own_q = lax.ppermute(packed_q, "tensor", swap)[None]
    received = [lax.ppermute(cut, "tensor", ring)]
    o_share = o_weight.shape[0] // plane
    columns = [(z + k) % nz * cols for k in range(1, nz)]
    pieces = cut_pieces(in_plane * o_share, columns, o_weight, o_share, cols, own_kv)
    moved = [lax.ppermute(p, "tensor", turn(k + 1)) for k, p in enumerate(pieces)]

    order_kv, order_q, first = [0], [0], counts[0]
    for step, (mask_kv, mask_q) in enumerate(zip(masks_kv, masks_q)):
        after, count = [], 0
        if step == 0:
            pairs, after = [], [own_kv, own_q, received[0]]
        else:
            pairs = [(own_kv, far_kv), (own_q, far_q)]
        if step < 2:
            count = counts[1 + step]
        if step == last:
            after = [received[1]] + moved
        outs = stage(pairs, tokens, first, count, after, HIDE if step == last else 0)
        if pairs:
            own_kv, own_q = outs[:2]
        if count:
            received.append(lax.ppermute(outs[-1], "tensor", ring))
        first += count
        far_kv = lax.ppermute(own_kv, PLANE, [(i, i ^ mask_kv) for i in range(plane)])
        far_q = lax.ppermute(own_q, PLANE, [(i, i ^ mask_q) for i in range(plane)])
        order_kv = order_kv + [k ^ mask_kv for k in order_kv]
        order_q = order_q + [k ^ mask_q for k in order_q]
    far_kv, far_q = (order_kv, own_kv, far_kv), (order_q, own_q, far_q)

    own_o = jnp.stack(moved)[None]

    def double(own, step, after):
        if step > 0:
            (own,) = stage([own], tokens, 0, 0, after)
        return own, lax.ppermute(own, PLANE, [(i, i ^ masks_kv[step]) for i in range(plane)])

    sources = (within + half - jnp.arange(half, dtype=jnp.int32)) % half
    gains = in_gain.reshape(nz, 1, cols)
    place = jnp.stack([in_plane, side * half])
    weights = (k_weight, value_weight, q_weight)
    pair_o = double(own_o, 0, [])
    for step in range(1, last - 1):
        pair_o = double(pair_o, step, [])
    xs, sqs, got_kv, nears, first, after = [], [], [], [], 0, [far_q[2]]
    for pieces in (received[:2], received[2:]):
        blocks = [pieces]
        for _ in range(half - 2):
            blocks.append([lax.ppermute(part, "tensor", ring) for part in blocks[-1]])
        sent_kv, x, sq = far_kv_product(
            place, sources, gains, tokens, first, blocks, far_kv, after
        )
        xs.append(x)
        sqs.append(sq)
        got_kv.append(lax.ppermute(sent_kv, "tensor", swap))
        if not first:
            nears.append(near_product(side * half + sources, x, weights, [sent_kv]))
            after = nears
        first += x.shape[1]

    after = [sent_kv, got_kv[0]]
    nears.append(near_product(side * half + sources, xs[1], weights, after))

    sent_q = far_product(place, sources, xs, far_q, [nears[1]])
    got_q = lax.ppermute(sent_q, "tensor", swap)
    pair_o = double(pair_o, last - 1, [sent_q])
    cosine, sine = rotation_table(seq * rows + jnp.arange(rows, dtype=jnp.int32))
    ids = seg_ids[None, :]
    own_kv, sums = keys_values(
        nears, got_kv, sqs, ids, cosine, sine, [sent_q, pair_o[0]], model
    )
    pair_o = double(pair_o, last, [own_kv])
    gathered_o = lay_pieces(place, order_kv, *pair_o)

    back = -(-(nseq * rows // 2 - 1) // rows)
    kv_blocks = [own_kv]
    for k in range(1, back + 1):
        earlier = [(i, i + k) for i in range(nseq - k)]
        kv_blocks.insert(0, lax.ppermute(own_kv, "seq", earlier))

    queries = finished_queries(nears, got_q, sums, cosine, sine, model)
    seq_at = jnp.reshape(seq, (1,))
    contexts, after = [], own_kv
    for c in range(CHUNKS):
        contexts.append(attend(seq_at, queries, ids, after, kv_blocks, c))
        after = gathered_o
    early, late = [], []
    for c, context in enumerate(contexts):
        if nz == 4:
            pairs = [(i, i ^ 1) for i in range(nz)]
            opposite = lax.ppermute(context, "tensor", swap)
            beside = lax.ppermute(context, "tensor", pairs)
            if c + 1 < CHUNKS:
                opposite = gate(opposite, contexts[c + 1])
            across = lax.ppermute(opposite, "tensor", pairs)
            early.append([context, beside])
            late.append([opposite, across])
            order = [2 - 2 * (z % 2), jnp.int32(1), 2 * (z % 2)]
        else:
            early.append([context])
            late.append([lax.ppermute(context, "tensor", turn(k)) for k in range(1, nz)])
            order = [jnp.int32(k) for k in range(nz - 1)]
    split = len(early[0]) - 1
    branches, own_sq = [], sums
    for c in range(CHUNKS):
        part = first_output(z, order[:split], o_weight, gathered_o, early[c], contexts[-1])
        branch, own_sq = last_output(order[split:], part, gathered_o, late[c], own_sq, c)
        branches.append(branch)
    squares = [own_sq]
    squares += [lax.ppermute(own_sq, "tensor", turn(k)) for k in range(1, nz)]
    return finish(tokens, branches, out_gain[None, :], squares, model)


def solution(mesh):
    return jax.shard_map(
        partial(per_device, sizes=dict(mesh.shape)),
        mesh=mesh,
        in_specs=(
            P(("groups", "seq"), "tensor"),
            P(("groups", "seq")),
            P(),
            P(None, "tensor"),
            P(None, "tensor"),
            P(None, "tensor"),
            P("tensor", None),
            P("tensor"),
        ),
        out_specs=P(("groups", "seq"), "tensor"),
        check_vma=False,
    )
```

```python
import math
from functools import partial

import jax
import jax.numpy as jnp
from jax import lax
from jax.experimental import pallas as pl
from jax.experimental.pallas import tpu as pltpu
from jax.sharding import PartitionSpec as P

HEAD_SIZE = 128
PLANE = ("groups", "seq")

epsilon = 1e-06
query_scale = 144.0 ** (-0.5)
rope_base = 10000.0
NEG = -1e30
Q_TILE = 128
K_TILE = 256
CHUNKS = 2
LANES = 128
TAIL = 16
F32, BF16 = jnp.float32, jnp.bfloat16
ANY = pl.BlockSpec(memory_space=pl.ANY)
HBM = pl.BlockSpec(memory_space=pltpu.HBM)
VMEM = pl.BlockSpec(memory_space=pltpu.VMEM)
DOCUMENTS = 8
HIDE = 5 * 10**10
PARAMS = pltpu.CompilerParams(vmem_limit_bytes=48 * 1024 * 1024)
ALL_VMEM = pltpu.CompilerParams(vmem_limit_bytes=62 * 1024 * 1024)


def shape(dims, dtype):
    return jax.ShapeDtypeStruct(dims, dtype)


def to_row(column):
    return jnp.broadcast_to(column, (column.shape[0], LANES)).T[0:1, :]


def to_column(row):
    return jnp.broadcast_to(row, (LANES, row.shape[1])).T


def rotation_table(token_places):
    half_dim = HEAD_SIZE // 2
    inverse = rope_base ** (-jnp.arange(half_dim, dtype=F32) / half_dim)
    angles = token_places.astype(F32)[:, None] * inverse[None, :]
    cosine, sine = jnp.cos(angles), jnp.sin(angles)
    return jnp.concatenate([cosine, cosine], 1), jnp.concatenate([-sine, sine], 1)


def rotate(vectors, cosine, sine):
    return vectors * cosine + pltpu.roll(vectors, HEAD_SIZE // 2, 1) * sine


def pack_kernel(at_ref, q_ref, k_ref, v_ref, x_ref, kv_out, q_out, x_out, sems):
    share, width = q_out.shape[0], k_ref.shape[1]
    rows = pl.ds(pl.multiple_of(at_ref[0] * share, TAIL), share)
    copies = [
        pltpu.make_async_copy(k_ref.at[rows], kv_out.at[:, pl.ds(0, width)], sems.at[0]),
        pltpu.make_async_copy(v_ref.at[rows], kv_out.at[:, pl.ds(width, width)], sems.at[1]),
        pltpu.make_async_copy(q_ref.at[rows], q_out, sems.at[2]),
        pltpu.make_async_copy(x_ref.at[pl.ds(0, x_out.shape[0])], x_out, sems.at[3]),
    ]
    for copy in copies:
        copy.start()
    for copy in copies:
        copy.wait()


def pack(at, q_weight, k_weight, v_weight, share, tokens, rows):
    kv_width = k_weight.shape[1] + v_weight.shape[1]
    dims = [(share, kv_width), (share, q_weight.shape[1]), (rows, tokens.shape[1])]
    return pl.pallas_call(
        pack_kernel,
        out_shape=tuple(shape(d, BF16) for d in dims),
        grid_spec=pltpu.PrefetchScalarGridSpec(
            num_scalar_prefetch=1,
            grid=(1,),
            in_specs=[HBM, HBM, HBM, HBM],
            out_specs=[pl.BlockSpec(d, lambda i, at: (0, 0)) for d in dims],
            scratch_shapes=[pltpu.SemaphoreType.DMA((4,))],
        ),
        compiler_params=ALL_VMEM,
        name="pack",
    )(at, q_weight, k_weight, v_weight, tokens)


def gate_kernel(x_ref, after_ref, out_ref):
    pass


def gate(x, after):
    return pl.pallas_call(
        gate_kernel,
        out_shape=shape(x.shape, x.dtype),
        in_specs=[ANY, ANY],
        out_specs=ANY,
        input_output_aliases={0: 0},
        compiler_params=PARAMS,
        name="gate",
    )(x, after)


def stage_kernel(*refs, pairs, first, count):
    outputs = pairs + (1 if count else 0)
    ins, outs, sems = refs[: -outputs - 1], refs[-outputs - 1 : -1], refs[-1]
    copies = []
    for p in range(pairs):
        held = ins[2 * p].shape[0]
        for side in range(2):
            there = outs[p].at[pl.ds(side * held, held)]
            copies.append(
                pltpu.make_async_copy(ins[2 * p + side], there, sems.at[len(copies)])
            )
    if count:
        rows = ins[2 * pairs].at[pl.ds(first, count)]
        copies.append(pltpu.make_async_copy(rows, outs[-1], sems.at[len(copies)]))
    for copy in copies:
        copy.start()
    for copy in copies:
        copy.wait()


def stage(joined, tokens, first, count, after, flops=0):
    dims = [(2 * pair[0].shape[0],) + pair[0].shape[1:] for pair in joined]
    if count:
        dims.append((count, tokens.shape[1]))
    return pl.pallas_call(
        partial(stage_kernel, pairs=len(joined), first=first, count=count),
        out_shape=tuple(shape(d, BF16) for d in dims),
        in_specs=[ANY] * (2 * len(joined) + 1 + len(after)),
        scratch_shapes=[pltpu.SemaphoreType.DMA((2 * len(joined) + 1,))],
        compiler_params=PARAMS,
        cost_estimate=pl.CostEstimate(flops=flops, bytes_accessed=flops // 500, transcendentals=0),
        name="stage",
    )(*[piece for pair in joined for piece in pair], tokens, *after)


def cut_kernel(at_ref, o_ref, after_ref, *rest):
    outs, sems = rest[:-1], rest[-1]
    copies = []
    for i, out in enumerate(outs):
        rows = pl.ds(pl.multiple_of(at_ref[0], TAIL), out.shape[0])
        columns = pl.ds(pl.multiple_of(at_ref[1 + i], LANES), out.shape[1])
        copies.append(pltpu.make_async_copy(o_ref.at[rows, columns], out, sems.at[i]))
    for copy in copies:
        copy.start()
    for copy in copies:
        copy.wait()


def cut_pieces(row, columns, o_weight, share, cols, after):
    if cols % LANES:
        return [lax.dynamic_slice(o_weight, (row, c), (share, cols)) for c in columns]
    return pl.pallas_call(
        cut_kernel,
        out_shape=tuple(shape((share, cols), BF16) for _ in columns),
        grid_spec=pltpu.PrefetchScalarGridSpec(
            num_scalar_prefetch=1,
            grid=(1,),
            in_specs=[ANY, ANY],
            out_specs=[VMEM for _ in columns],
            scratch_shapes=[pltpu.SemaphoreType.DMA((len(columns),))],
        ),
        compiler_params=PARAMS,
        name="cut",
    )(jnp.stack([row] + columns), o_weight, after)


def lay_kernel(place_ref, own_ref, got_ref, out_ref, sems, *, order):
    held, others, share, _ = own_ref.shape
    copies = []
    for i, mask in enumerate(order):
        piece = own_ref.at[i] if i < held else got_ref.at[i - held]
        row = pl.multiple_of((place_ref[0] ^ mask) * share, TAIL)
        there = out_ref.at[:, pl.ds(row, share)]
        copies.append(pltpu.make_async_copy(piece, there, sems.at[i]))
    for copy in copies:
        copy.start()
    for copy in copies:
        copy.wait()


def lay_pieces(place, order, own, got):
    _, others, share, cols = own.shape
    dims = (others, len(order) * share, cols)
    return pl.pallas_call(
        partial(lay_kernel, order=order),
        out_shape=shape(dims, BF16),
        grid_spec=pltpu.PrefetchScalarGridSpec(
            num_scalar_prefetch=1,
            grid=(1,),
            in_specs=[ANY, ANY],
            out_specs=pl.BlockSpec(dims, lambda i, p: (0, 0, 0)),
            scratch_shapes=[pltpu.SemaphoreType.DMA((len(order),))],
        ),
        compiler_params=PARAMS,
        name="lay",
    )(place, own, got)


def place_weights(place_ref, own_ref, got_ref, weight, sems, order):
    held, share, _ = own_ref.shape
    copies = []
    for i, mask in enumerate(order):
        piece = own_ref.at[i] if i < held else got_ref.at[i - held]
        row = pl.multiple_of((place_ref[0] ^ mask) * share, TAIL)
        there = weight.at[pl.ds(row, share)]
        copies.append(pltpu.make_async_copy(piece, there, sems.at[i]))
    for copy in copies:
        copy.start()
    return copies


def far_sum(src_ref, x_ref, weight):
    count, _, cols = x_ref.shape
    total = None
    for k in range(count):
        row = pl.multiple_of(src_ref[k] * cols, TAIL)
        term = jnp.dot(x_ref[k], weight[pl.ds(row, cols), :], preferred_element_type=F32)
        total = term if total is None else total + term
    return total


def far_kv_kernel(place_ref, src_ref, gain_ref, own_ref, got_ref, *rest, order, cuts):
    x_refs, (out_ref, x_out, sq_ref, weight, sems) = rest[: sum(cuts)], rest[-5:]
    copies = place_weights(place_ref, own_ref, got_ref, weight, sems, order)
    rows = x_out.shape[1]
    columns, at = [], 0
    for k, pieces in enumerate(cuts):
        gain = gain_ref[place_ref[1] + src_ref[k]]
        column, row = [], 0
        for x_ref in x_refs[at : at + pieces]:
            x = x_ref[...].astype(F32)
            column.append(jnp.sum(x * x, axis=1, keepdims=True))
            x_out[k, row : row + x.shape[0]] = (x * gain).astype(BF16)
            row += x.shape[0]
        columns.append(jnp.concatenate(column, axis=0))
        at += pieces
    sq = to_row(sum(columns[1:], columns[0]))
    sq_ref[...] = sq
    for copy in copies:
        copy.wait()
    out_ref[:rows, :] = far_sum(src_ref, x_out, weight).astype(BF16)
    high = sq.astype(BF16).astype(F32)
    out_ref[rows:, :] = lines_of((high, sq - high), out_ref.shape[1])


def far_kv_product(place, sources, gains, blocks, gathered, after):
    order, own, got = gathered
    _, share, width = own.shape
    rows, cols = blocks[0][0].shape
    pieces = [piece for block in blocks for piece in block]
    dims = [(rows + TAIL, width), (len(blocks), rows, cols), (1, rows)]
    whole = lambda d: pl.BlockSpec(d, lambda i, p, s: (0,) * len(d))
    return pl.pallas_call(
        partial(far_kv_kernel, order=order, cuts=[len(block) for block in blocks]),
        out_shape=tuple(shape(d, t) for d, t in zip(dims, (BF16, BF16, F32))),
        grid_spec=pltpu.PrefetchScalarGridSpec(
            num_scalar_prefetch=2,
            grid=(1,),
            in_specs=[whole(gains.shape), ANY, ANY]
            + [whole(piece.shape) for piece in pieces]
            + [ANY for _ in after],
            out_specs=[whole(d) for d in dims],
            scratch_shapes=[
                pltpu.VMEM((len(order) * share, width), BF16),
                pltpu.SemaphoreType.DMA((len(order),)),
            ],
        ),
        compiler_params=PARAMS,
        name="far_kv",
    )(place, sources, gains, own, got, *pieces, *after)


def far_kernel(place_ref, src_ref, x_ref, own_ref, got_ref, *rest, order):
    out_ref, weight, sems = rest[-3:]
    for copy in place_weights(place_ref, own_ref, got_ref, weight, sems, order):
        copy.wait()
    out_ref[...] = far_sum(src_ref, x_ref, weight).astype(BF16)


def lines_of(rows, width):
    lines = []
    for row in rows:
        for at in range(0, row.shape[1], width):
            line = row[:, at : at + width]
            if line.shape[1] < width:
                rest = jnp.zeros((1, width - line.shape[1]), F32)
                line = jnp.concatenate([line, rest], axis=1)
            lines.append(line)
    lines.append(jnp.zeros((TAIL - len(lines), width), F32))
    return jnp.concatenate(lines, axis=0).astype(BF16)


def rows_of(tail, count, length):
    per_row = -(-length // tail.shape[1])
    rows = []
    for r in range(count):
        lines = [tail[r * per_row + i : r * per_row + i + 1, :] for i in range(per_row)]
        rows.append(jnp.concatenate(lines, axis=1)[:, :length])
    return rows


def far_product(place, sources, x, gathered, after):
    order, own, got = gathered
    _, share, width = own.shape
    rows = x.shape[1]
    return pl.pallas_call(
        partial(far_kernel, order=order),
        out_shape=shape((rows, width), BF16),
        grid_spec=pltpu.PrefetchScalarGridSpec(
            num_scalar_prefetch=2,
            grid=(1,),
            in_specs=[pl.BlockSpec(x.shape, lambda i, p, s: (0, 0, 0)), ANY, ANY]
            + [ANY for _ in after],
            out_specs=pl.BlockSpec((rows, width), lambda i, p, s: (0, 0)),
            scratch_shapes=[
                pltpu.VMEM((len(order) * share, width), BF16),
                pltpu.SemaphoreType.DMA((len(order),)),
            ],
        ),
        compiler_params=PARAMS,
        name="far",
    )(place, sources, x, own, got, *after)


def near_kernel(src_ref, x_ref, k_ref, v_ref, q_ref, *rest):
    out_ref = rest[-1]
    x = x_ref[0]

    @pl.when(pl.program_id(0) == 0)
    def _():
        out_ref[...] = jnp.zeros_like(out_ref)

    column = 0
    for ref in (k_ref, v_ref, q_ref):
        at = slice(column, column + ref.shape[1])
        out_ref[:, at] += jnp.dot(x, ref[...], preferred_element_type=F32)
        column += ref.shape[1]


def near_product(sources, x, weights, after):
    count, chunk, cols = x.shape
    widths = [w.shape[1] for w in weights]
    return pl.pallas_call(
        near_kernel,
        out_shape=shape((chunk, sum(widths)), F32),
        grid_spec=pltpu.PrefetchScalarGridSpec(
            num_scalar_prefetch=1,
            grid=(count,),
            in_specs=[pl.BlockSpec((1, chunk, cols), lambda i, s: (i, 0, 0))]
            + [pl.BlockSpec((cols, w), lambda i, s: (s[i], 0)) for w in widths]
            + [ANY for _ in after],
            out_specs=pl.BlockSpec((chunk, sum(widths)), lambda i, s: (0, 0)),
        ),
        compiler_params=PARAMS,
        name="near",
    )(sources, x, *weights, *after)


def keys_kernel(near_ref, far_ref, sq_ref, id_ref, cos_ref, sin_ref, *rest, model):
    out_ref, sum_ref = rest[-2:]
    rows, width = near_ref.shape[0], far_ref.shape[1]
    tail = far_ref[rows:, :].astype(F32)
    total = sum(rows_of(tail, 2, rows), sq_ref[...])
    factor = to_column(lax.rsqrt(total / model + epsilon))
    sum_ref[...] = total
    keys, values = slice(0, HEAD_SIZE), slice(HEAD_SIZE, 2 * HEAD_SIZE)
    part = (near_ref[:, keys] + far_ref[:rows, keys].astype(F32)) * factor
    part = rotate(part, cos_ref[...], sin_ref[...]).astype(BF16)
    out_ref[: rows // 2, keys] = part[: rows // 2]
    out_ref[: rows // 2, values] = part[rows // 2 :]
    part = (near_ref[:, values] + far_ref[:rows, values].astype(F32)) * factor
    part = part.T.astype(BF16)
    for i, at in enumerate(range(0, rows, width)):
        row = rows // 2 + i * HEAD_SIZE
        out_ref[row : row + HEAD_SIZE, :] = part[:, at : at + width]
    out_ref[rows:, :] = lines_of((id_ref[...].astype(F32),), width)


def keys_values(near, far, sq, ids, cosine, sine, after, model):
    rows, width = near.shape[0], far.shape[1]
    whole = lambda i: (0, 0)
    return pl.pallas_call(
        partial(keys_kernel, model=model),
        out_shape=(shape(far.shape, BF16), shape(sq.shape, F32)),
        grid=(1,),
        in_specs=[pl.BlockSpec((rows, width), whole)]
        + [pl.BlockSpec(a.shape, whole) for a in (far, sq, ids, cosine, sine)]
        + [ANY for _ in after],
        out_specs=[pl.BlockSpec(far.shape, whole), pl.BlockSpec(sq.shape, whole)],
        compiler_params=PARAMS,
        name="keys",
    )(near, far, sq, ids, cosine, sine, *after)


def queries_kernel(near_ref, far_ref, sum_ref, cos_ref, sin_ref, out_ref, *, model):
    scale = query_scale * math.log2(math.e)
    factor = to_column(lax.rsqrt(sum_ref[...] / model + epsilon) * scale)
    for c in range(0, out_ref.shape[1], HEAD_SIZE):
        at = slice(c, c + HEAD_SIZE)
        part = (near_ref[:, at] + far_ref[:, at].astype(F32)) * factor
        out_ref[:, at] = rotate(part, cos_ref[...], sin_ref[...]).astype(BF16)


def finished_queries(near, far, sums, cosine, sine, model):
    rows, width = far.shape
    last = near.shape[1] // width - 1
    whole = lambda i: (0, 0)
    return pl.pallas_call(
        partial(queries_kernel, model=model),
        out_shape=shape((rows, width), BF16),
        grid=(1,),
        in_specs=[pl.BlockSpec((rows, width), lambda i: (0, last))]
        + [pl.BlockSpec(a.shape, whole) for a in (far, sums, cosine, sine)],
        out_specs=pl.BlockSpec((rows, width), whole),
        compiler_params=PARAMS,
        cost_estimate=pl.CostEstimate(flops=HIDE, bytes_accessed=10**8, transcendentals=0),
        name="queries",
    )(near, far, sums, cosine, sine)


def attention_kernel(seq_ref, q_ref, id_ref, after_ref, *rest, back, offset):
    kv_refs, (out_ref, k_scr, vt_scr, count_scr) = rest[:-4], rest[-4:]
    part_rows, message = kv_refs[0].shape[0] - TAIL, kv_refs[0].shape[1]
    group = q_ref.shape[1] // HEAD_SIZE
    tile = pl.program_id(0)

    @pl.when(tile == 0)
    def _():
        counts = [jnp.zeros((1, 1), F32) for _ in range(DOCUMENTS)]
        for b, kv_ref in enumerate(kv_refs):
            row, half = b * part_rows, part_rows // 2
            k_scr[row : row + half, :] = kv_ref[:half, :HEAD_SIZE]
            k_scr[row + half : row + part_rows, :] = kv_ref[:half, HEAD_SIZE:]
            for i, at in enumerate(range(0, part_rows, message)):
                first = half + i * HEAD_SIZE
                vt_scr[:, row + at : row + at + message] = kv_ref[first : first + HEAD_SIZE, :]
            (ids,) = rows_of(kv_ref[part_rows:, :].astype(F32), 1, part_rows)
            exists = b >= back - seq_ref[0]
            ids = jnp.where(exists, ids, -1.0)
            for d in range(DOCUMENTS):
                below = (ids < d).astype(F32)
                counts[d] = counts[d] + jnp.sum(below, axis=1, keepdims=True)
        for d in range(DOCUMENTS):
            count_scr[d : d + 1, :] = jnp.broadcast_to(counts[d], (1, LANES))

    heads = [q_ref[:, c : c + HEAD_SIZE] for c in range(0, group * HEAD_SIZE, HEAD_SIZE)]
    q2 = jnp.concatenate(heads, axis=0)
    width = group * Q_TILE

    start = jnp.zeros((1, Q_TILE), F32)
    for d in range(DOCUMENTS):
        start = jnp.where(id_ref[...] == d, count_scr[d : d + 1, :], start)
    start = start.astype(jnp.int32)
    low = jnp.min(start) // K_TILE
    start = jnp.concatenate([start] * group, axis=1)
    first = back * part_rows + offset + tile * Q_TILE
    place = first + lax.broadcasted_iota(jnp.int32, (1, Q_TILE), 1)
    place = jnp.concatenate([place] * group, axis=1)

    def score(j):
        base = pl.multiple_of(j * K_TILE, K_TILE)
        return lax.dot_general(
            k_scr[pl.ds(base, K_TILE), :],
            q2,
            (((1,), (1,)), ((), ())),
            preferred_element_type=F32,
        )

    stop = (first + Q_TILE + K_TILE - 1) // K_TILE

    def step(j, state):
        scores, run_max, run_sum, acc = state
        following = score(jnp.minimum(j + 1, stop - 1))
        base = pl.multiple_of(j * K_TILE, K_TILE)
        key_pos = base + lax.broadcasted_iota(jnp.int32, (K_TILE, width), 0)
        allowed = (key_pos >= start) & (key_pos <= place)
        scores = jnp.where(allowed, scores, NEG)
        new_max = jnp.maximum(run_max, jnp.max(scores, axis=0, keepdims=True))
        expo = jnp.exp2(scores - new_max)
        factor = jnp.exp2(run_max - new_max)
        run_sum = run_sum * factor + jnp.sum(expo, axis=0, keepdims=True)
        acc = acc * factor + jnp.dot(
            vt_scr[:, pl.ds(base, K_TILE)], expo.astype(BF16), preferred_element_type=F32
        )
        return following, new_max, run_sum, acc

    state = (
        score(low),
        jnp.full((1, width), NEG, F32),
        jnp.zeros((1, width), F32),
        jnp.zeros((HEAD_SIZE, width), F32),
    )
    _, _, run_sum, acc = lax.fori_loop(low, stop, step, state)
    context = (acc / run_sum).T
    for g in range(group):
        out_ref[:, g * HEAD_SIZE : (g + 1) * HEAD_SIZE] = context[
            g * Q_TILE : (g + 1) * Q_TILE
        ].astype(BF16)


def attend(seq, queries, ids, after, blocks, c):
    rows, width = queries.shape[0] // CHUNKS, queries.shape[1]
    back = len(blocks) - 1
    tiles = rows // Q_TILE
    keys = len(blocks) * queries.shape[0]
    return pl.pallas_call(
        partial(attention_kernel, back=back, offset=c * rows),
        out_shape=shape((rows, width), BF16),
        grid_spec=pltpu.PrefetchScalarGridSpec(
            num_scalar_prefetch=1,
            grid=(tiles,),
            in_specs=[
                pl.BlockSpec((Q_TILE, width), lambda i, s: (c * tiles + i, 0)),
                pl.BlockSpec((1, Q_TILE), lambda i, s: (0, c * tiles + i)),
                ANY,
            ]
            + [pl.BlockSpec(b.shape, lambda i, s: (0, 0)) for b in blocks],
            out_specs=pl.BlockSpec((Q_TILE, width), lambda i, s: (i, 0)),
            scratch_shapes=[
                pltpu.VMEM((keys, HEAD_SIZE), BF16),
                pltpu.VMEM((HEAD_SIZE, keys), BF16),
                pltpu.VMEM((DOCUMENTS, LANES), F32),
            ],
        ),
        compiler_params=PARAMS,
        cost_estimate=pl.CostEstimate(
            flops=4 * rows * width * keys,
            bytes_accessed=4 * keys * width,
            transcendentals=rows * keys * width // HEAD_SIZE,
        ),
        name="attend",
    )(seq, queries, ids, after, *blocks)


def first_output_kernel(at_ref, own_o_ref, o_ref, *rest):
    ctx_refs, out_ref = rest[:-2], rest[-1]
    total = jnp.dot(ctx_refs[0][...], own_o_ref[...], preferred_element_type=F32)
    for i, ctx_ref in enumerate(ctx_refs[1:]):
        total = total + jnp.dot(ctx_ref[...], o_ref[at_ref[1 + i]], preferred_element_type=F32)
    out_ref[...] = total


def last_output_kernel(at_ref, part_ref, o_ref, *rest):
    ctx_refs, (before_ref, out_ref, sq_ref, acc) = rest[:-4], rest[-4:]
    step = pl.program_id(0)
    total = part_ref[...]
    for i, ctx_ref in enumerate(ctx_refs):
        total = total + jnp.dot(ctx_ref[...], o_ref[at_ref[i]], preferred_element_type=F32)
    out_ref[...] = total
    squares = jnp.sum(total * total, axis=1, keepdims=True)
    squares = jnp.broadcast_to(squares, acc.shape)

    @pl.when(step == 0)
    def _():
        acc[...] = squares

    @pl.when(step > 0)
    def _():
        acc[...] += squares

    @pl.when(step == pl.num_programs(0) - 1)
    def _():
        done = sq_ref.shape[1] - acc.shape[0]
        if done:
            sq_ref[:, :done] = before_ref[...]
        sq_ref[:, done:] = acc[...].T[0:1, :]


def column_tiles(cols):
    tiles = 3 if cols % (3 * LANES) == 0 else 1
    return tiles, cols // tiles


def first_output(column, order, o_weight, gathered, contexts, after):
    chunk, width = contexts[0].shape
    others, _, cols = gathered.shape
    tiles, tile = column_tiles(cols)
    if cols % LANES:
        o_weight = lax.dynamic_slice_in_dim(o_weight, column * cols, cols, axis=1)
        column = jnp.int32(0)
    return pl.pallas_call(
        first_output_kernel,
        out_shape=shape((chunk, cols), F32),
        grid_spec=pltpu.PrefetchScalarGridSpec(
            num_scalar_prefetch=1,
            grid=(tiles,),
            in_specs=[
                pl.BlockSpec((width, tile), lambda i, at: (0, at[0] * tiles + i)),
                pl.BlockSpec((others, width, tile), lambda i, at: (0, 0, i)),
            ]
            + [pl.BlockSpec((chunk, width), lambda i, at: (0, 0)) for _ in contexts]
            + [ANY],
            out_specs=pl.BlockSpec((chunk, tile), lambda i, at: (0, i)),
        ),
        compiler_params=PARAMS,
        cost_estimate=pl.CostEstimate(flops=HIDE, bytes_accessed=10**8, transcendentals=0),
        name="first_output",
    )(jnp.stack([column] + order), o_weight, gathered, *contexts, after)


def last_output(order, part, gathered, contexts, before, c):
    chunk, width = contexts[0].shape
    others, _, cols = gathered.shape
    tiles, tile = column_tiles(cols)
    return pl.pallas_call(
        last_output_kernel,
        out_shape=(shape((chunk, cols), F32), shape((1, (c + 1) * chunk), F32)),
        grid_spec=pltpu.PrefetchScalarGridSpec(
            num_scalar_prefetch=1,
            grid=(tiles,),
            in_specs=[
                pl.BlockSpec((chunk, tile), lambda i, at: (0, i)),
                pl.BlockSpec((others, width, tile), lambda i, at: (0, 0, i)),
            ]
            + [pl.BlockSpec((chunk, width), lambda i, at: (0, 0)) for _ in contexts]
            + [pl.BlockSpec(before.shape, lambda i, at: (0, 0))],
            out_specs=[
                pl.BlockSpec((chunk, tile), lambda i, at: (0, i)),
                pl.BlockSpec((1, (c + 1) * chunk), lambda i, at: (0, 0)),
            ],
            scratch_shapes=[pltpu.VMEM((chunk, LANES), F32)],
        ),
        compiler_params=PARAMS,
        name="last_output",
    )(jnp.stack(order), part, gathered, *contexts, before)


def final_kernel(token_ref, gain_ref, *rest, model):
    branch_refs, sq_refs, out_ref = rest[:CHUNKS], rest[CHUNKS:-1], rest[-1]
    total = sq_refs[0][...]
    for sq_ref in sq_refs[1:]:
        total = total + sq_ref[...]
    factor = to_column(lax.rsqrt(total / model + epsilon))[:, 0:1]
    for c in range(CHUNKS):

        @pl.when(pl.program_id(0) * CHUNKS // pl.num_programs(0) == c)
        def _():
            out = token_ref[...].astype(F32) + branch_refs[c][...] * factor * gain_ref[...]
            out_ref[...] = out.astype(BF16)


def finish(tokens, branches, out_gain, sums, model):
    rows, cols = tokens.shape
    tiles = rows // CHUNKS // Q_TILE
    held = lambda c: lambda i: (jnp.clip(i - c * tiles, 0, tiles - 1), 0)
    return pl.pallas_call(
        partial(final_kernel, model=model),
        out_shape=shape(tokens.shape, BF16),
        grid=(CHUNKS * tiles,),
        in_specs=[
            pl.BlockSpec((Q_TILE, cols), lambda i: (i, 0)),
            pl.BlockSpec((1, cols), lambda i: (0, 0)),
        ]
        + [pl.BlockSpec((Q_TILE, cols), held(c)) for c in range(CHUNKS)]
        + [pl.BlockSpec((1, Q_TILE), lambda i: (0, i)) for _ in sums],
        out_specs=pl.BlockSpec((Q_TILE, cols), lambda i: (i, 0)),
        compiler_params=PARAMS,
        name="finish",
    )(tokens, out_gain, *branches, *sums)


def per_device(
    tokens, seg_ids, in_gain, q_weight, k_weight, value_weight, o_weight, out_gain, *, sizes
):
    rows, cols = tokens.shape
    model = in_gain.shape[0]
    nz, nseq = sizes["tensor"], sizes["seq"]
    plane = nseq * sizes["groups"]
    z = lax.axis_index("tensor")
    seq = lax.axis_index("seq")
    in_plane = lax.axis_index(PLANE)
    half = nz // 2
    side, within = z // half, z % half
    half_rows = half * cols

    ring = [(i, i // half * half + (i + 1) % half) for i in range(nz)]
    swap = [(i, (i + half) % nz) for i in range(nz)]
    turn = lambda k: [(i, (i + k) % nz) for i in range(nz)]
    seq_bits = [1 << b for b in range(1, nseq.bit_length() - 1)]
    group_bits = [nseq << b for b in range(sizes["groups"].bit_length() - 1)]

    share = half_rows // plane
    at = jnp.reshape((1 - side) * plane + in_plane, (1,))
    inner = seq_bits + group_bits
    masks_kv, masks_q = inner + [1], inner[::-1] + [1]
    last = len(masks_kv) - 1
    eighth = rows // 48 * 8
    counts = [eighth, rows // 2 - 2 * TAIL, rows // 2 + 2 * TAIL - eighth]
    packed_kv, packed_q, cut = pack(
        at, q_weight, k_weight, value_weight, share, tokens, counts[0]
    )
    own_kv = lax.ppermute(packed_kv, "tensor", swap)[None]
    own_q = lax.ppermute(packed_q, "tensor", swap)[None]
    received = [lax.ppermute(cut, "tensor", ring)]
    o_share = o_weight.shape[0] // plane
    columns = [(z + k) % nz * cols for k in range(1, nz)]
    pieces = cut_pieces(in_plane * o_share, columns, o_weight, o_share, cols, own_kv)
    moved = [lax.ppermute(p, "tensor", turn(k + 1)) for k, p in enumerate(pieces)]

    order_kv, order_q, first = [0], [0], counts[0]
    for step, (mask_kv, mask_q) in enumerate(zip(masks_kv, masks_q)):
        after, count = [], 0
        if step == 0:
            pairs, after = [], [own_kv, own_q, received[0]]
        else:
            pairs = [(own_kv, far_kv), (own_q, far_q)]
        if step < 2:
            count = counts[1 + step]
        if step == last:
            after = [received[1]] + moved
        outs = stage(pairs, tokens, first, count, after, HIDE if step == last else 0)
        if pairs:
            own_kv, own_q = outs[:2]
        if count:
            received.append(lax.ppermute(outs[-1], "tensor", ring))
        first += count
        far_kv = lax.ppermute(own_kv, PLANE, [(i, i ^ mask_kv) for i in range(plane)])
        far_q = lax.ppermute(own_q, PLANE, [(i, i ^ mask_q) for i in range(plane)])
        order_kv = order_kv + [k ^ mask_kv for k in order_kv]
        order_q = order_q + [k ^ mask_q for k in order_q]
    far_kv, far_q = (order_kv, own_kv, far_kv), (order_q, own_q, far_q)

    own_o = jnp.stack(moved)[None]

    def double(own, step, after):
        if step > 0:
            (own,) = stage([own], tokens, 0, 0, after)
        return own, lax.ppermute(own, PLANE, [(i, i ^ masks_kv[step]) for i in range(plane)])

    sources = (within + half - jnp.arange(half, dtype=jnp.int32)) % half
    blocks = [[tokens], received]
    for _ in range(half - 2):
        blocks.append([lax.ppermute(part, "tensor", ring) for part in blocks[-1]])
    gains = in_gain.reshape(nz, 1, cols)
    place = jnp.stack([in_plane, side * half])
    sent_kv, x, sq = far_kv_product(
        place, sources, gains, blocks, far_kv, [far_q[2]]
    )
    got_kv = lax.ppermute(sent_kv, "tensor", swap)
    pair_o = double(own_o, 0, [])
    for step in range(1, last - 1):
        pair_o = double(pair_o, step, [])
    weights = (k_weight, value_weight, q_weight)

    near = near_product(side * half + sources, x, weights, [sent_kv])

    sent_q = far_product(place, sources, x, far_q, [near])
    got_q = lax.ppermute(gate(sent_q, got_kv), "tensor", swap)
    pair_o = double(pair_o, last - 1, [sent_q])
    cosine, sine = rotation_table(seq * rows + jnp.arange(rows, dtype=jnp.int32))
    ids = seg_ids[None, :]
    own_kv, sums = keys_values(
        near, got_kv, sq, ids, cosine, sine, [sent_q, pair_o[0]], model
    )
    pair_o = double(pair_o, last, [own_kv])
    gathered_o = lay_pieces(place, order_kv, *pair_o)

    back = -(-(nseq * rows // 2 - 1) // rows)
    kv_blocks = [own_kv]
    for k in range(1, back + 1):
        earlier = [(i, i + k) for i in range(nseq - k)]
        kv_blocks.insert(0, lax.ppermute(own_kv, "seq", earlier))

    queries = finished_queries(near, got_q, sums, cosine, sine, model)
    seq_at = jnp.reshape(seq, (1,))
    contexts, after = [], own_kv
    for c in range(CHUNKS):
        contexts.append(attend(seq_at, queries, ids, after, kv_blocks, c))
        after = gathered_o
    early, late = [], []
    for c, context in enumerate(contexts):
        if nz == 4:
            pairs = [(i, i ^ 1) for i in range(nz)]
            opposite = lax.ppermute(context, "tensor", swap)
            beside = lax.ppermute(context, "tensor", pairs)
            if c + 1 < CHUNKS:
                opposite = gate(opposite, contexts[c + 1])
            across = lax.ppermute(opposite, "tensor", pairs)
            early.append([context, beside])
            late.append([opposite, across])
            order = [2 - 2 * (z % 2), jnp.int32(1), 2 * (z % 2)]
        else:
            early.append([context])
            late.append([lax.ppermute(context, "tensor", turn(k)) for k in range(1, nz)])
            order = [jnp.int32(k) for k in range(nz - 1)]
    split = len(early[0]) - 1
    branches, own_sq = [], sums
    for c in range(CHUNKS):
        part = first_output(z, order[:split], o_weight, gathered_o, early[c], contexts[-1])
        branch, own_sq = last_output(order[split:], part, gathered_o, late[c], own_sq, c)
        branches.append(branch)
    squares = [own_sq]
    squares += [lax.ppermute(own_sq, "tensor", turn(k)) for k in range(1, nz)]
    return finish(tokens, branches, out_gain[None, :], squares, model)


def solution(mesh):
    return jax.shard_map(
        partial(per_device, sizes=dict(mesh.shape)),
        mesh=mesh,
        in_specs=(
            P(("groups", "seq"), "tensor"),
            P(("groups", "seq")),
            P(),
            P(None, "tensor"),
            P(None, "tensor"),
            P(None, "tensor"),
            P("tensor", None),
            P("tensor"),
        ),
        out_specs=P(("groups", "seq"), "tensor"),
        check_vma=False,
    )
```

```python
import math
from functools import partial

import jax
import jax.numpy as jnp
from jax import lax
from jax.experimental import pallas as pl
from jax.experimental.pallas import tpu as pltpu
from jax.sharding import PartitionSpec as P

HEAD_SIZE = 128
PLANE = ("groups", "seq")

epsilon = 1e-06
query_scale = 144.0 ** (-0.5)
rope_base = 10000.0
NEG = -1e30
Q_TILE = 128
K_TILE = 256
CHUNKS = 2
LANES = 128
TAIL = 16
F32, BF16 = jnp.float32, jnp.bfloat16
ANY = pl.BlockSpec(memory_space=pl.ANY)
HBM = pl.BlockSpec(memory_space=pltpu.HBM)
VMEM = pl.BlockSpec(memory_space=pltpu.VMEM)
DOCUMENTS = 8
HIDE = 5 * 10**10
PARAMS = pltpu.CompilerParams(vmem_limit_bytes=48 * 1024 * 1024)
ALL_VMEM = pltpu.CompilerParams(vmem_limit_bytes=62 * 1024 * 1024)


def shape(dims, dtype):
    return jax.ShapeDtypeStruct(dims, dtype)


def to_row(column):
    return jnp.broadcast_to(column, (column.shape[0], LANES)).T[0:1, :]


def to_column(row):
    return jnp.broadcast_to(row, (LANES, row.shape[1])).T


def rotation_table(token_places):
    half_dim = HEAD_SIZE // 2
    inverse = rope_base ** (-jnp.arange(half_dim, dtype=F32) / half_dim)
    angles = token_places.astype(F32)[:, None] * inverse[None, :]
    cosine, sine = jnp.cos(angles), jnp.sin(angles)
    return jnp.concatenate([cosine, cosine], 1), jnp.concatenate([-sine, sine], 1)


def rotate(vectors, cosine, sine):
    return vectors * cosine + pltpu.roll(vectors, HEAD_SIZE // 2, 1) * sine


def pack_kernel(at_ref, q_ref, k_ref, v_ref, x_ref, kv_out, q_out, x_out, sems):
    share, width = q_out.shape[0], k_ref.shape[1]
    rows = pl.ds(pl.multiple_of(at_ref[0] * share, TAIL), share)
    copies = [
        pltpu.make_async_copy(k_ref.at[rows], kv_out.at[:, pl.ds(0, width)], sems.at[0]),
        pltpu.make_async_copy(v_ref.at[rows], kv_out.at[:, pl.ds(width, width)], sems.at[1]),
        pltpu.make_async_copy(q_ref.at[rows], q_out, sems.at[2]),
        pltpu.make_async_copy(x_ref.at[pl.ds(0, x_out.shape[0])], x_out, sems.at[3]),
    ]
    for copy in copies:
        copy.start()
    for copy in copies:
        copy.wait()


def pack(at, q_weight, k_weight, v_weight, share, tokens, rows):
    kv_width = k_weight.shape[1] + v_weight.shape[1]
    dims = [(share, kv_width), (share, q_weight.shape[1]), (rows, tokens.shape[1])]
    return pl.pallas_call(
        pack_kernel,
        out_shape=tuple(shape(d, BF16) for d in dims),
        grid_spec=pltpu.PrefetchScalarGridSpec(
            num_scalar_prefetch=1,
            grid=(1,),
            in_specs=[HBM, HBM, HBM, HBM],
            out_specs=[pl.BlockSpec(d, lambda i, at: (0, 0)) for d in dims],
            scratch_shapes=[pltpu.SemaphoreType.DMA((4,))],
        ),
        compiler_params=ALL_VMEM,
        name="pack",
    )(at, q_weight, k_weight, v_weight, tokens)


def gate_kernel(x_ref, after_ref, out_ref):
    pass


def gate(x, after):
    return pl.pallas_call(
        gate_kernel,
        out_shape=shape(x.shape, x.dtype),
        in_specs=[ANY, ANY],
        out_specs=ANY,
        input_output_aliases={0: 0},
        compiler_params=PARAMS,
        name="gate",
    )(x, after)


def stage_kernel(*refs, pairs, first, count):
    outputs = pairs + (1 if count else 0)
    ins, outs, sems = refs[: -outputs - 1], refs[-outputs - 1 : -1], refs[-1]
    copies = []
    for p in range(pairs):
        held = ins[2 * p].shape[0]
        for side in range(2):
            there = outs[p].at[pl.ds(side * held, held)]
            copies.append(
                pltpu.make_async_copy(ins[2 * p + side], there, sems.at[len(copies)])
            )
    if count:
        rows = ins[2 * pairs].at[pl.ds(first, count)]
        copies.append(pltpu.make_async_copy(rows, outs[-1], sems.at[len(copies)]))
    for copy in copies:
        copy.start()
    for copy in copies:
        copy.wait()


def stage(joined, tokens, first, count, after, flops=0):
    dims = [(2 * pair[0].shape[0],) + pair[0].shape[1:] for pair in joined]
    if count:
        dims.append((count, tokens.shape[1]))
    return pl.pallas_call(
        partial(stage_kernel, pairs=len(joined), first=first, count=count),
        out_shape=tuple(shape(d, BF16) for d in dims),
        in_specs=[ANY] * (2 * len(joined) + 1 + len(after)),
        scratch_shapes=[pltpu.SemaphoreType.DMA((2 * len(joined) + 1,))],
        compiler_params=PARAMS,
        cost_estimate=pl.CostEstimate(flops=flops, bytes_accessed=flops // 500, transcendentals=0),
        name="stage",
    )(*[piece for pair in joined for piece in pair], tokens, *after)


def cut_kernel(at_ref, o_ref, after_ref, *rest):
    outs, sems = rest[:-1], rest[-1]
    copies = []
    for i, out in enumerate(outs):
        rows = pl.ds(pl.multiple_of(at_ref[0], TAIL), out.shape[0])
        columns = pl.ds(pl.multiple_of(at_ref[1 + i], LANES), out.shape[1])
        copies.append(pltpu.make_async_copy(o_ref.at[rows, columns], out, sems.at[i]))
    for copy in copies:
        copy.start()
    for copy in copies:
        copy.wait()


def cut_pieces(row, columns, o_weight, share, cols, after):
    if cols % LANES:
        return [lax.dynamic_slice(o_weight, (row, c), (share, cols)) for c in columns]
    return pl.pallas_call(
        cut_kernel,
        out_shape=tuple(shape((share, cols), BF16) for _ in columns),
        grid_spec=pltpu.PrefetchScalarGridSpec(
            num_scalar_prefetch=1,
            grid=(1,),
            in_specs=[ANY, ANY],
            out_specs=[VMEM for _ in columns],
            scratch_shapes=[pltpu.SemaphoreType.DMA((len(columns),))],
        ),
        compiler_params=PARAMS,
        name="cut",
    )(jnp.stack([row] + columns), o_weight, after)


def lay_kernel(place_ref, own_ref, got_ref, out_ref, sems, *, order):
    held, others, share, _ = own_ref.shape
    copies = []
    for i, mask in enumerate(order):
        piece = own_ref.at[i] if i < held else got_ref.at[i - held]
        row = pl.multiple_of((place_ref[0] ^ mask) * share, TAIL)
        there = out_ref.at[:, pl.ds(row, share)]
        copies.append(pltpu.make_async_copy(piece, there, sems.at[i]))
    for copy in copies:
        copy.start()
    for copy in copies:
        copy.wait()


def lay_pieces(place, order, own, got):
    _, others, share, cols = own.shape
    dims = (others, len(order) * share, cols)
    return pl.pallas_call(
        partial(lay_kernel, order=order),
        out_shape=shape(dims, BF16),
        grid_spec=pltpu.PrefetchScalarGridSpec(
            num_scalar_prefetch=1,
            grid=(1,),
            in_specs=[ANY, ANY],
            out_specs=pl.BlockSpec(dims, lambda i, p: (0, 0, 0)),
            scratch_shapes=[pltpu.SemaphoreType.DMA((len(order),))],
        ),
        compiler_params=PARAMS,
        name="lay",
    )(place, own, got)


def place_weights(place_ref, own_ref, got_ref, weight, sems, order):
    held, share, _ = own_ref.shape
    copies = []
    for i, mask in enumerate(order):
        piece = own_ref.at[i] if i < held else got_ref.at[i - held]
        row = pl.multiple_of((place_ref[0] ^ mask) * share, TAIL)
        there = weight.at[pl.ds(row, share)]
        copies.append(pltpu.make_async_copy(piece, there, sems.at[i]))
    for copy in copies:
        copy.start()
    return copies


def far_sum(src_ref, x_ref, weight):
    count, _, cols = x_ref.shape
    total = None
    for k in range(count):
        row = pl.multiple_of(src_ref[k] * cols, TAIL)
        term = jnp.dot(x_ref[k], weight[pl.ds(row, cols), :], preferred_element_type=F32)
        total = term if total is None else total + term
    return total


def far_kv_kernel(place_ref, src_ref, gain_ref, own_ref, got_ref, *rest, order, cuts):
    x_refs, (out_ref, x_out, sq_ref, weight, sems) = rest[: sum(cuts)], rest[-5:]
    copies = place_weights(place_ref, own_ref, got_ref, weight, sems, order)
    rows = x_out.shape[1]
    columns, at = [], 0
    for k, pieces in enumerate(cuts):
        gain = gain_ref[place_ref[1] + src_ref[k]]
        column, row = [], 0
        for x_ref in x_refs[at : at + pieces]:
            x = x_ref[...].astype(F32)
            column.append(jnp.sum(x * x, axis=1, keepdims=True))
            x_out[k, row : row + x.shape[0]] = (x * gain).astype(BF16)
            row += x.shape[0]
        columns.append(jnp.concatenate(column, axis=0))
        at += pieces
    sq = to_row(sum(columns[1:], columns[0]))
    sq_ref[...] = sq
    for copy in copies:
        copy.wait()
    out_ref[:rows, :] = far_sum(src_ref, x_out, weight).astype(BF16)
    high = sq.astype(BF16).astype(F32)
    out_ref[rows:, :] = lines_of((high, sq - high), out_ref.shape[1])


def far_kv_product(place, sources, gains, blocks, gathered, after):
    order, own, got = gathered
    _, share, width = own.shape
    rows, cols = blocks[0][0].shape
    pieces = [piece for block in blocks for piece in block]
    dims = [(rows + TAIL, width), (len(blocks), rows, cols), (1, rows)]
    whole = lambda d: pl.BlockSpec(d, lambda i, p, s: (0,) * len(d))
    return pl.pallas_call(
        partial(far_kv_kernel, order=order, cuts=[len(block) for block in blocks]),
        out_shape=tuple(shape(d, t) for d, t in zip(dims, (BF16, BF16, F32))),
        grid_spec=pltpu.PrefetchScalarGridSpec(
            num_scalar_prefetch=2,
            grid=(1,),
            in_specs=[whole(gains.shape), ANY, ANY]
            + [whole(piece.shape) for piece in pieces]
            + [ANY for _ in after],
            out_specs=[whole(d) for d in dims],
            scratch_shapes=[
                pltpu.VMEM((len(order) * share, width), BF16),
                pltpu.SemaphoreType.DMA((len(order),)),
            ],
        ),
        compiler_params=PARAMS,
        name="far_kv",
    )(place, sources, gains, own, got, *pieces, *after)


def far_kernel(place_ref, src_ref, x_ref, own_ref, got_ref, *rest, order):
    out_ref, weight, sems = rest[-3:]
    for copy in place_weights(place_ref, own_ref, got_ref, weight, sems, order):
        copy.wait()
    out_ref[...] = far_sum(src_ref, x_ref, weight).astype(BF16)


def lines_of(rows, width):
    lines = []
    for row in rows:
        for at in range(0, row.shape[1], width):
            line = row[:, at : at + width]
            if line.shape[1] < width:
                rest = jnp.zeros((1, width - line.shape[1]), F32)
                line = jnp.concatenate([line, rest], axis=1)
            lines.append(line)
    lines.append(jnp.zeros((TAIL - len(lines), width), F32))
    return jnp.concatenate(lines, axis=0).astype(BF16)


def rows_of(tail, count, length):
    per_row = -(-length // tail.shape[1])
    rows = []
    for r in range(count):
        lines = [tail[r * per_row + i : r * per_row + i + 1, :] for i in range(per_row)]
        rows.append(jnp.concatenate(lines, axis=1)[:, :length])
    return rows


def far_product(place, sources, x, gathered, after):
    order, own, got = gathered
    _, share, width = own.shape
    rows = x.shape[1]
    return pl.pallas_call(
        partial(far_kernel, order=order),
        out_shape=shape((rows, width), BF16),
        grid_spec=pltpu.PrefetchScalarGridSpec(
            num_scalar_prefetch=2,
            grid=(1,),
            in_specs=[pl.BlockSpec(x.shape, lambda i, p, s: (0, 0, 0)), ANY, ANY]
            + [ANY for _ in after],
            out_specs=pl.BlockSpec((rows, width), lambda i, p, s: (0, 0)),
            scratch_shapes=[
                pltpu.VMEM((len(order) * share, width), BF16),
                pltpu.SemaphoreType.DMA((len(order),)),
            ],
        ),
        compiler_params=PARAMS,
        name="far",
    )(place, sources, x, own, got, *after)


def near_kernel(src_ref, x_ref, k_ref, v_ref, q_ref, *rest):
    out_ref = rest[-1]
    x = x_ref[0]

    @pl.when(pl.program_id(0) == 0)
    def _():
        out_ref[...] = jnp.zeros_like(out_ref)

    column = 0
    for ref in (k_ref, v_ref, q_ref):
        at = slice(column, column + ref.shape[1])
        out_ref[:, at] += jnp.dot(x, ref[...], preferred_element_type=F32)
        column += ref.shape[1]


def near_product(sources, x, weights, after):
    count, chunk, cols = x.shape
    widths = [w.shape[1] for w in weights]
    return pl.pallas_call(
        near_kernel,
        out_shape=shape((chunk, sum(widths)), F32),
        grid_spec=pltpu.PrefetchScalarGridSpec(
            num_scalar_prefetch=1,
            grid=(count,),
            in_specs=[pl.BlockSpec((1, chunk, cols), lambda i, s: (i, 0, 0))]
            + [pl.BlockSpec((cols, w), lambda i, s: (s[i], 0)) for w in widths]
            + [ANY for _ in after],
            out_specs=pl.BlockSpec((chunk, sum(widths)), lambda i, s: (0, 0)),
        ),
        compiler_params=PARAMS,
        name="near",
    )(sources, x, *weights, *after)


def keys_kernel(near_ref, far_ref, sq_ref, id_ref, cos_ref, sin_ref, *rest, model):
    out_ref, sum_ref = rest[-2:]
    rows, width = near_ref.shape[0], far_ref.shape[1]
    tail = far_ref[rows:, :].astype(F32)
    total = sum(rows_of(tail, 2, rows), sq_ref[...])
    factor = to_column(lax.rsqrt(total / model + epsilon))
    sum_ref[...] = total
    keys, values = slice(0, HEAD_SIZE), slice(HEAD_SIZE, 2 * HEAD_SIZE)
    part = (near_ref[:, keys] + far_ref[:rows, keys].astype(F32)) * factor
    part = rotate(part, cos_ref[...], sin_ref[...]).astype(BF16)
    out_ref[: rows // 2, keys] = part[: rows // 2]
    out_ref[: rows // 2, values] = part[rows // 2 :]
    part = (near_ref[:, values] + far_ref[:rows, values].astype(F32)) * factor
    part = part.T.astype(BF16)
    for i, at in enumerate(range(0, rows, width)):
        row = rows // 2 + i * HEAD_SIZE
        out_ref[row : row + HEAD_SIZE, :] = part[:, at : at + width]
    out_ref[rows:, :] = lines_of((id_ref[...].astype(F32),), width)


def keys_values(near, far, sq, ids, cosine, sine, after, model):
    rows, width = near.shape[0], far.shape[1]
    whole = lambda i: (0, 0)
    return pl.pallas_call(
        partial(keys_kernel, model=model),
        out_shape=(shape(far.shape, BF16), shape(sq.shape, F32)),
        grid=(1,),
        in_specs=[pl.BlockSpec((rows, width), whole)]
        + [pl.BlockSpec(a.shape, whole) for a in (far, sq, ids, cosine, sine)]
        + [ANY for _ in after],
        out_specs=[pl.BlockSpec(far.shape, whole), pl.BlockSpec(sq.shape, whole)],
        compiler_params=PARAMS,
        name="keys",
    )(near, far, sq, ids, cosine, sine, *after)


def queries_kernel(near_ref, far_ref, sum_ref, cos_ref, sin_ref, out_ref, *, model):
    scale = query_scale * math.log2(math.e)
    factor = to_column(lax.rsqrt(sum_ref[...] / model + epsilon) * scale)
    for c in range(0, out_ref.shape[1], HEAD_SIZE):
        at = slice(c, c + HEAD_SIZE)
        part = (near_ref[:, at] + far_ref[:, at].astype(F32)) * factor
        out_ref[:, at] = rotate(part, cos_ref[...], sin_ref[...]).astype(BF16)


def finished_queries(near, far, sums, cosine, sine, model):
    rows, width = far.shape
    last = near.shape[1] // width - 1
    whole = lambda i: (0, 0)
    return pl.pallas_call(
        partial(queries_kernel, model=model),
        out_shape=shape((rows, width), BF16),
        grid=(1,),
        in_specs=[pl.BlockSpec((rows, width), lambda i: (0, last))]
        + [pl.BlockSpec(a.shape, whole) for a in (far, sums, cosine, sine)],
        out_specs=pl.BlockSpec((rows, width), whole),
        compiler_params=PARAMS,
        cost_estimate=pl.CostEstimate(flops=HIDE, bytes_accessed=10**8, transcendentals=0),
        name="queries",
    )(near, far, sums, cosine, sine)


def attention_kernel(seq_ref, q_ref, id_ref, after_ref, *rest, back, offset):
    kv_refs, (out_ref, k_scr, vt_scr, count_scr) = rest[:-4], rest[-4:]
    part_rows, message = kv_refs[0].shape[0] - TAIL, kv_refs[0].shape[1]
    group = q_ref.shape[1] // HEAD_SIZE
    tile = pl.program_id(0)

    @pl.when(tile == 0)
    def _():
        counts = [jnp.zeros((1, 1), F32) for _ in range(DOCUMENTS)]
        for b, kv_ref in enumerate(kv_refs):
            row, half = b * part_rows, part_rows // 2
            k_scr[row : row + half, :] = kv_ref[:half, :HEAD_SIZE]
            k_scr[row + half : row + part_rows, :] = kv_ref[:half, HEAD_SIZE:]
            for i, at in enumerate(range(0, part_rows, message)):
                first = half + i * HEAD_SIZE
                vt_scr[:, row + at : row + at + message] = kv_ref[first : first + HEAD_SIZE, :]
            (ids,) = rows_of(kv_ref[part_rows:, :].astype(F32), 1, part_rows)
            exists = b >= back - seq_ref[0]
            ids = jnp.where(exists, ids, -1.0)
            for d in range(DOCUMENTS):
                below = (ids < d).astype(F32)
                counts[d] = counts[d] + jnp.sum(below, axis=1, keepdims=True)
        for d in range(DOCUMENTS):
            count_scr[d : d + 1, :] = jnp.broadcast_to(counts[d], (1, LANES))

    heads = [q_ref[:, c : c + HEAD_SIZE] for c in range(0, group * HEAD_SIZE, HEAD_SIZE)]
    q2 = jnp.concatenate(heads, axis=0)
    width = group * Q_TILE

    start = jnp.zeros((1, Q_TILE), F32)
    for d in range(DOCUMENTS):
        start = jnp.where(id_ref[...] == d, count_scr[d : d + 1, :], start)
    start = start.astype(jnp.int32)
    low = jnp.min(start) // K_TILE
    start = jnp.concatenate([start] * group, axis=1)
    first = back * part_rows + offset + tile * Q_TILE
    place = first + lax.broadcasted_iota(jnp.int32, (1, Q_TILE), 1)
    place = jnp.concatenate([place] * group, axis=1)

    def score(j):
        base = pl.multiple_of(j * K_TILE, K_TILE)
        return lax.dot_general(
            k_scr[pl.ds(base, K_TILE), :],
            q2,
            (((1,), (1,)), ((), ())),
            preferred_element_type=F32,
        )

    stop = (first + Q_TILE + K_TILE - 1) // K_TILE

    clear = jnp.minimum((jnp.max(start) + K_TILE - 1) // K_TILE, stop)
    edge = jnp.maximum((first + 1) // K_TILE, clear)

    def step(j, state, masked):
        scores, run_max, run_sum, acc = state
        following = score(jnp.minimum(j + 1, stop - 1))
        base = pl.multiple_of(j * K_TILE, K_TILE)
        if masked:
            key_pos = base + lax.broadcasted_iota(jnp.int32, (K_TILE, width), 0)
            allowed = (key_pos >= start) & (key_pos <= place)
            scores = jnp.where(allowed, scores, NEG)
        new_max = jnp.maximum(run_max, jnp.max(scores, axis=0, keepdims=True))
        expo = jnp.exp2(scores - new_max)
        factor = jnp.exp2(run_max - new_max)
        run_sum = run_sum * factor + jnp.sum(expo, axis=0, keepdims=True)
        acc = acc * factor + jnp.dot(
            vt_scr[:, pl.ds(base, K_TILE)], expo.astype(BF16), preferred_element_type=F32
        )
        return following, new_max, run_sum, acc

    state = (
        score(low),
        jnp.full((1, width), NEG, F32),
        jnp.zeros((1, width), F32),
        jnp.zeros((HEAD_SIZE, width), F32),
    )
    state = lax.fori_loop(low, clear, partial(step, masked=True), state)
    state = lax.fori_loop(clear, edge, partial(step, masked=False), state)
    _, _, run_sum, acc = lax.fori_loop(edge, stop, partial(step, masked=True), state)
    context = (acc / run_sum).T
    for g in range(group):
        out_ref[:, g * HEAD_SIZE : (g + 1) * HEAD_SIZE] = context[
            g * Q_TILE : (g + 1) * Q_TILE
        ].astype(BF16)


def attend(seq, queries, ids, after, blocks, c):
    rows, width = queries.shape[0] // CHUNKS, queries.shape[1]
    back = len(blocks) - 1
    tiles = rows // Q_TILE
    keys = len(blocks) * queries.shape[0]
    return pl.pallas_call(
        partial(attention_kernel, back=back, offset=c * rows),
        out_shape=shape((rows, width), BF16),
        grid_spec=pltpu.PrefetchScalarGridSpec(
            num_scalar_prefetch=1,
            grid=(tiles,),
            in_specs=[
                pl.BlockSpec((Q_TILE, width), lambda i, s: (c * tiles + i, 0)),
                pl.BlockSpec((1, Q_TILE), lambda i, s: (0, c * tiles + i)),
                ANY,
            ]
            + [pl.BlockSpec(b.shape, lambda i, s: (0, 0)) for b in blocks],
            out_specs=pl.BlockSpec((Q_TILE, width), lambda i, s: (i, 0)),
            scratch_shapes=[
                pltpu.VMEM((keys, HEAD_SIZE), BF16),
                pltpu.VMEM((HEAD_SIZE, keys), BF16),
                pltpu.VMEM((DOCUMENTS, LANES), F32),
            ],
        ),
        compiler_params=PARAMS,
        cost_estimate=pl.CostEstimate(
            flops=4 * rows * width * keys,
            bytes_accessed=4 * keys * width,
            transcendentals=rows * keys * width // HEAD_SIZE,
        ),
        name="attend",
    )(seq, queries, ids, after, *blocks)


def first_output_kernel(at_ref, own_o_ref, o_ref, *rest):
    ctx_refs, out_ref = rest[:-2], rest[-1]
    total = jnp.dot(ctx_refs[0][...], own_o_ref[...], preferred_element_type=F32)
    for i, ctx_ref in enumerate(ctx_refs[1:]):
        total = total + jnp.dot(ctx_ref[...], o_ref[at_ref[1 + i]], preferred_element_type=F32)
    out_ref[...] = total


def last_output_kernel(at_ref, part_ref, o_ref, *rest):
    ctx_refs, (before_ref, out_ref, sq_ref, acc) = rest[:-4], rest[-4:]
    step = pl.program_id(0)
    total = part_ref[...]
    for i, ctx_ref in enumerate(ctx_refs):
        total = total + jnp.dot(ctx_ref[...], o_ref[at_ref[i]], preferred_element_type=F32)
    out_ref[...] = total
    squares = jnp.sum(total * total, axis=1, keepdims=True)
    squares = jnp.broadcast_to(squares, acc.shape)

    @pl.when(step == 0)
    def _():
        acc[...] = squares

    @pl.when(step > 0)
    def _():
        acc[...] += squares

    @pl.when(step == pl.num_programs(0) - 1)
    def _():
        done = sq_ref.shape[1] - acc.shape[0]
        if done:
            sq_ref[:, :done] = before_ref[...]
        sq_ref[:, done:] = acc[...].T[0:1, :]


def column_tiles(cols):
    tiles = 3 if cols % (3 * LANES) == 0 else 1
    return tiles, cols // tiles


def first_output(column, order, o_weight, gathered, contexts, after):
    chunk, width = contexts[0].shape
    others, _, cols = gathered.shape
    tiles, tile = column_tiles(cols)
    if cols % LANES:
        o_weight = lax.dynamic_slice_in_dim(o_weight, column * cols, cols, axis=1)
        column = jnp.int32(0)
    return pl.pallas_call(
        first_output_kernel,
        out_shape=shape((chunk, cols), F32),
        grid_spec=pltpu.PrefetchScalarGridSpec(
            num_scalar_prefetch=1,
            grid=(tiles,),
            in_specs=[
                pl.BlockSpec((width, tile), lambda i, at: (0, at[0] * tiles + i)),
                pl.BlockSpec((others, width, tile), lambda i, at: (0, 0, i)),
            ]
            + [pl.BlockSpec((chunk, width), lambda i, at: (0, 0)) for _ in contexts]
            + [ANY],
            out_specs=pl.BlockSpec((chunk, tile), lambda i, at: (0, i)),
        ),
        compiler_params=PARAMS,
        cost_estimate=pl.CostEstimate(flops=HIDE, bytes_accessed=10**8, transcendentals=0),
        name="first_output",
    )(jnp.stack([column] + order), o_weight, gathered, *contexts, after)


def last_output(order, part, gathered, contexts, before, c):
    chunk, width = contexts[0].shape
    others, _, cols = gathered.shape
    tiles, tile = column_tiles(cols)
    return pl.pallas_call(
        last_output_kernel,
        out_shape=(shape((chunk, cols), F32), shape((1, (c + 1) * chunk), F32)),
        grid_spec=pltpu.PrefetchScalarGridSpec(
            num_scalar_prefetch=1,
            grid=(tiles,),
            in_specs=[
                pl.BlockSpec((chunk, tile), lambda i, at: (0, i)),
                pl.BlockSpec((others, width, tile), lambda i, at: (0, 0, i)),
            ]
            + [pl.BlockSpec((chunk, width), lambda i, at: (0, 0)) for _ in contexts]
            + [pl.BlockSpec(before.shape, lambda i, at: (0, 0))],
            out_specs=[
                pl.BlockSpec((chunk, tile), lambda i, at: (0, i)),
                pl.BlockSpec((1, (c + 1) * chunk), lambda i, at: (0, 0)),
            ],
            scratch_shapes=[pltpu.VMEM((chunk, LANES), F32)],
        ),
        compiler_params=PARAMS,
        name="last_output",
    )(jnp.stack(order), part, gathered, *contexts, before)


def final_kernel(token_ref, gain_ref, *rest, model):
    branch_refs, sq_refs, out_ref = rest[:CHUNKS], rest[CHUNKS:-1], rest[-1]
    total = sq_refs[0][...]
    for sq_ref in sq_refs[1:]:
        total = total + sq_ref[...]
    factor = to_column(lax.rsqrt(total / model + epsilon))[:, 0:1]
    for c in range(CHUNKS):

        @pl.when(pl.program_id(0) * CHUNKS // pl.num_programs(0) == c)
        def _():
            out = token_ref[...].astype(F32) + branch_refs[c][...] * factor * gain_ref[...]
            out_ref[...] = out.astype(BF16)


def finish(tokens, branches, out_gain, sums, model):
    rows, cols = tokens.shape
    tiles = rows // CHUNKS // Q_TILE
    held = lambda c: lambda i: (jnp.clip(i - c * tiles, 0, tiles - 1), 0)
    return pl.pallas_call(
        partial(final_kernel, model=model),
        out_shape=shape(tokens.shape, BF16),
        grid=(CHUNKS * tiles,),
        in_specs=[
            pl.BlockSpec((Q_TILE, cols), lambda i: (i, 0)),
            pl.BlockSpec((1, cols), lambda i: (0, 0)),
        ]
        + [pl.BlockSpec((Q_TILE, cols), held(c)) for c in range(CHUNKS)]
        + [pl.BlockSpec((1, Q_TILE), lambda i: (0, i)) for _ in sums],
        out_specs=pl.BlockSpec((Q_TILE, cols), lambda i: (i, 0)),
        compiler_params=PARAMS,
        name="finish",
    )(tokens, out_gain, *branches, *sums)


def per_device(
    tokens, seg_ids, in_gain, q_weight, k_weight, value_weight, o_weight, out_gain, *, sizes
):
    rows, cols = tokens.shape
    model = in_gain.shape[0]
    nz, nseq = sizes["tensor"], sizes["seq"]
    plane = nseq * sizes["groups"]
    z = lax.axis_index("tensor")
    seq = lax.axis_index("seq")
    in_plane = lax.axis_index(PLANE)
    half = nz // 2
    side, within = z // half, z % half
    half_rows = half * cols

    ring = [(i, i // half * half + (i + 1) % half) for i in range(nz)]
    swap = [(i, (i + half) % nz) for i in range(nz)]
    turn = lambda k: [(i, (i + k) % nz) for i in range(nz)]
    seq_bits = [1 << b for b in range(1, nseq.bit_length() - 1)]
    group_bits = [nseq << b for b in range(sizes["groups"].bit_length() - 1)]

    share = half_rows // plane
    at = jnp.reshape((1 - side) * plane + in_plane, (1,))
    inner = seq_bits + group_bits
    masks_kv, masks_q = inner + [1], inner[::-1] + [1]
    last = len(masks_kv) - 1
    eighth = rows // 48 * 8
    counts = [eighth, rows // 2 - 2 * TAIL, rows // 2 + 2 * TAIL - eighth]
    packed_kv, packed_q, cut = pack(
        at, q_weight, k_weight, value_weight, share, tokens, counts[0]
    )
    own_kv = lax.ppermute(packed_kv, "tensor", swap)[None]
    own_q = lax.ppermute(packed_q, "tensor", swap)[None]
    received = [lax.ppermute(cut, "tensor", ring)]
    o_share = o_weight.shape[0] // plane
    columns = [(z + k) % nz * cols for k in range(1, nz)]
    pieces = cut_pieces(in_plane * o_share, columns, o_weight, o_share, cols, own_kv)
    moved = [lax.ppermute(p, "tensor", turn(k + 1)) for k, p in enumerate(pieces)]

    order_kv, order_q, first = [0], [0], counts[0]
    for step, (mask_kv, mask_q) in enumerate(zip(masks_kv, masks_q)):
        after, count = [], 0
        if step == 0:
            pairs, after = [], [own_kv, own_q, received[0]]
        else:
            pairs = [(own_kv, far_kv), (own_q, far_q)]
        if step < 2:
            count = counts[1 + step]
        if step == last:
            after = [received[1]] + moved
        outs = stage(pairs, tokens, first, count, after, HIDE if step == last else 0)
        if pairs:
            own_kv, own_q = outs[:2]
        if count:
            received.append(lax.ppermute(outs[-1], "tensor", ring))
        first += count
        far_kv = lax.ppermute(own_kv, PLANE, [(i, i ^ mask_kv) for i in range(plane)])
        far_q = lax.ppermute(own_q, PLANE, [(i, i ^ mask_q) for i in range(plane)])
        order_kv = order_kv + [k ^ mask_kv for k in order_kv]
        order_q = order_q + [k ^ mask_q for k in order_q]
    far_kv, far_q = (order_kv, own_kv, far_kv), (order_q, own_q, far_q)

    own_o = jnp.stack(moved)[None]

    def double(own, step, after):
        if step > 0:
            (own,) = stage([own], tokens, 0, 0, after)
        return own, lax.ppermute(own, PLANE, [(i, i ^ masks_kv[step]) for i in range(plane)])

    sources = (within + half - jnp.arange(half, dtype=jnp.int32)) % half
    blocks = [[tokens], received]
    for _ in range(half - 2):
        blocks.append([lax.ppermute(part, "tensor", ring) for part in blocks[-1]])
    gains = in_gain.reshape(nz, 1, cols)
    place = jnp.stack([in_plane, side * half])
    sent_kv, x, sq = far_kv_product(
        place, sources, gains, blocks, far_kv, [far_q[2]]
    )
    got_kv = lax.ppermute(sent_kv, "tensor", swap)
    pair_o = double(own_o, 0, [])
    for step in range(1, last - 1):
        pair_o = double(pair_o, step, [])
    weights = (k_weight, value_weight, q_weight)

    near = near_product(side * half + sources, x, weights, [sent_kv])

    sent_q = far_product(place, sources, x, far_q, [near])
    got_q = lax.ppermute(gate(sent_q, got_kv), "tensor", swap)
    pair_o = double(pair_o, last - 1, [sent_q])
    cosine, sine = rotation_table(seq * rows + jnp.arange(rows, dtype=jnp.int32))
    ids = seg_ids[None, :]
    own_kv, sums = keys_values(
        near, got_kv, sq, ids, cosine, sine, [sent_q, pair_o[0]], model
    )
    pair_o = double(pair_o, last, [own_kv])
    gathered_o = lay_pieces(place, order_kv, *pair_o)

    back = -(-(nseq * rows // 2 - 1) // rows)
    kv_blocks = [own_kv]
    for k in range(1, back + 1):
        earlier = [(i, i + k) for i in range(nseq - k)]
        kv_blocks.insert(0, lax.ppermute(own_kv, "seq", earlier))

    queries = finished_queries(near, got_q, sums, cosine, sine, model)
    seq_at = jnp.reshape(seq, (1,))
    contexts, after = [], own_kv
    for c in range(CHUNKS):
        contexts.append(attend(seq_at, queries, ids, after, kv_blocks, c))
        after = gathered_o
    early, late = [], []
    for c, context in enumerate(contexts):
        if nz == 4:
            pairs = [(i, i ^ 1) for i in range(nz)]
            opposite = lax.ppermute(context, "tensor", swap)
            beside = lax.ppermute(context, "tensor", pairs)
            if c + 1 < CHUNKS:
                opposite = gate(opposite, contexts[c + 1])
            across = lax.ppermute(opposite, "tensor", pairs)
            early.append([context, beside])
            late.append([opposite, across])
            order = [2 - 2 * (z % 2), jnp.int32(1), 2 * (z % 2)]
        else:
            early.append([context])
            late.append([lax.ppermute(context, "tensor", turn(k)) for k in range(1, nz)])
            order = [jnp.int32(k) for k in range(nz - 1)]
    split = len(early[0]) - 1
    branches, own_sq = [], sums
    for c in range(CHUNKS):
        part = first_output(z, order[:split], o_weight, gathered_o, early[c], contexts[-1])
        branch, own_sq = last_output(order[split:], part, gathered_o, late[c], own_sq, c)
        branches.append(branch)
    squares = [own_sq]
    squares += [lax.ppermute(own_sq, "tensor", turn(k)) for k in range(1, nz)]
    return finish(tokens, branches, out_gain[None, :], squares, model)


def solution(mesh):
    return jax.shard_map(
        partial(per_device, sizes=dict(mesh.shape)),
        mesh=mesh,
        in_specs=(
            P(("groups", "seq"), "tensor"),
            P(("groups", "seq")),
            P(),
            P(None, "tensor"),
            P(None, "tensor"),
            P(None, "tensor"),
            P("tensor", None),
            P("tensor"),
        ),
        out_specs=P(("groups", "seq"), "tensor"),
        check_vma=False,
    )
```

```python
import math
from functools import partial

import jax
import jax.numpy as jnp
from jax import lax
from jax.experimental import pallas as pl
from jax.experimental.pallas import tpu as pltpu
from jax.sharding import PartitionSpec as P

HEAD_SIZE = 128
PLANE = ("groups", "seq")

epsilon = 1e-06
query_scale = 144.0 ** (-0.5)
rope_base = 10000.0
NEG = -1e30
Q_TILE = 128
K_TILE = 384
CHUNKS = 2
LANES = 128
TAIL = 16
F32, BF16 = jnp.float32, jnp.bfloat16
ANY = pl.BlockSpec(memory_space=pl.ANY)
HBM = pl.BlockSpec(memory_space=pltpu.HBM)
VMEM = pl.BlockSpec(memory_space=pltpu.VMEM)
DOCUMENTS = 8
HIDE = 5 * 10**10
PARAMS = pltpu.CompilerParams(vmem_limit_bytes=48 * 1024 * 1024)
ALL_VMEM = pltpu.CompilerParams(vmem_limit_bytes=62 * 1024 * 1024)


def shape(dims, dtype):
    return jax.ShapeDtypeStruct(dims, dtype)


def to_row(column):
    return jnp.broadcast_to(column, (column.shape[0], LANES)).T[0:1, :]


def to_column(row):
    return jnp.broadcast_to(row, (LANES, row.shape[1])).T


def rotation_table(token_places):
    half_dim = HEAD_SIZE // 2
    inverse = rope_base ** (-jnp.arange(half_dim, dtype=F32) / half_dim)
    angles = token_places.astype(F32)[:, None] * inverse[None, :]
    cosine, sine = jnp.cos(angles), jnp.sin(angles)
    return jnp.concatenate([cosine, cosine], 1), jnp.concatenate([-sine, sine], 1)


def rotate(vectors, cosine, sine):
    return vectors * cosine + pltpu.roll(vectors, HEAD_SIZE // 2, 1) * sine


def pack_kernel(at_ref, q_ref, k_ref, v_ref, x_ref, kv_out, q_out, x_out, sems):
    share, width = q_out.shape[0], k_ref.shape[1]
    rows = pl.ds(pl.multiple_of(at_ref[0] * share, TAIL), share)
    copies = [
        pltpu.make_async_copy(k_ref.at[rows], kv_out.at[:, pl.ds(0, width)], sems.at[0]),
        pltpu.make_async_copy(v_ref.at[rows], kv_out.at[:, pl.ds(width, width)], sems.at[1]),
        pltpu.make_async_copy(q_ref.at[rows], q_out, sems.at[2]),
        pltpu.make_async_copy(x_ref.at[pl.ds(0, x_out.shape[0])], x_out, sems.at[3]),
    ]
    for copy in copies:
        copy.start()
    for copy in copies:
        copy.wait()


def pack(at, q_weight, k_weight, v_weight, share, tokens, rows):
    kv_width = k_weight.shape[1] + v_weight.shape[1]
    dims = [(share, kv_width), (share, q_weight.shape[1]), (rows, tokens.shape[1])]
    return pl.pallas_call(
        pack_kernel,
        out_shape=tuple(shape(d, BF16) for d in dims),
        grid_spec=pltpu.PrefetchScalarGridSpec(
            num_scalar_prefetch=1,
            grid=(1,),
            in_specs=[HBM, HBM, HBM, HBM],
            out_specs=[pl.BlockSpec(d, lambda i, at: (0, 0)) for d in dims],
            scratch_shapes=[pltpu.SemaphoreType.DMA((4,))],
        ),
        compiler_params=ALL_VMEM,
        name="pack",
    )(at, q_weight, k_weight, v_weight, tokens)


def gate_kernel(x_ref, after_ref, out_ref):
    pass


def gate(x, after):
    return pl.pallas_call(
        gate_kernel,
        out_shape=shape(x.shape, x.dtype),
        in_specs=[ANY, ANY],
        out_specs=ANY,
        input_output_aliases={0: 0},
        compiler_params=PARAMS,
        name="gate",
    )(x, after)


def stage_kernel(*refs, pairs, first, count):
    outputs = pairs + (1 if count else 0)
    ins, outs, sems = refs[: -outputs - 1], refs[-outputs - 1 : -1], refs[-1]
    copies = []
    for p in range(pairs):
        held = ins[2 * p].shape[0]
        for side in range(2):
            there = outs[p].at[pl.ds(side * held, held)]
            copies.append(
                pltpu.make_async_copy(ins[2 * p + side], there, sems.at[len(copies)])
            )
    if count:
        rows = ins[2 * pairs].at[pl.ds(first, count)]
        copies.append(pltpu.make_async_copy(rows, outs[-1], sems.at[len(copies)]))
    for copy in copies:
        copy.start()
    for copy in copies:
        copy.wait()


def stage(joined, tokens, first, count, after, flops=0):
    dims = [(2 * pair[0].shape[0],) + pair[0].shape[1:] for pair in joined]
    if count:
        dims.append((count, tokens.shape[1]))
    return pl.pallas_call(
        partial(stage_kernel, pairs=len(joined), first=first, count=count),
        out_shape=tuple(shape(d, BF16) for d in dims),
        in_specs=[ANY] * (2 * len(joined) + 1 + len(after)),
        scratch_shapes=[pltpu.SemaphoreType.DMA((2 * len(joined) + 1,))],
        compiler_params=PARAMS,
        cost_estimate=pl.CostEstimate(flops=flops, bytes_accessed=flops // 500, transcendentals=0),
        name="stage",
    )(*[piece for pair in joined for piece in pair], tokens, *after)


def cut_kernel(at_ref, o_ref, after_ref, *rest):
    outs, sems = rest[:-1], rest[-1]
    copies = []
    for i, out in enumerate(outs):
        rows = pl.ds(pl.multiple_of(at_ref[0], TAIL), out.shape[0])
        columns = pl.ds(pl.multiple_of(at_ref[1 + i], LANES), out.shape[1])
        copies.append(pltpu.make_async_copy(o_ref.at[rows, columns], out, sems.at[i]))
    for copy in copies:
        copy.start()
    for copy in copies:
        copy.wait()


def cut_pieces(row, columns, o_weight, share, cols, after):
    if cols % LANES:
        return [lax.dynamic_slice(o_weight, (row, c), (share, cols)) for c in columns]
    return pl.pallas_call(
        cut_kernel,
        out_shape=tuple(shape((share, cols), BF16) for _ in columns),
        grid_spec=pltpu.PrefetchScalarGridSpec(
            num_scalar_prefetch=1,
            grid=(1,),
            in_specs=[ANY, ANY],
            out_specs=[VMEM for _ in columns],
            scratch_shapes=[pltpu.SemaphoreType.DMA((len(columns),))],
        ),
        compiler_params=PARAMS,
        name="cut",
    )(jnp.stack([row] + columns), o_weight, after)


def lay_kernel(place_ref, own_ref, got_ref, out_ref, sems, *, order):
    held, others, share, _ = own_ref.shape
    copies = []
    for i, mask in enumerate(order):
        piece = own_ref.at[i] if i < held else got_ref.at[i - held]
        row = pl.multiple_of((place_ref[0] ^ mask) * share, TAIL)
        there = out_ref.at[:, pl.ds(row, share)]
        copies.append(pltpu.make_async_copy(piece, there, sems.at[i]))
    for copy in copies:
        copy.start()
    for copy in copies:
        copy.wait()


def lay_pieces(place, order, own, got):
    _, others, share, cols = own.shape
    dims = (others, len(order) * share, cols)
    return pl.pallas_call(
        partial(lay_kernel, order=order),
        out_shape=shape(dims, BF16),
        grid_spec=pltpu.PrefetchScalarGridSpec(
            num_scalar_prefetch=1,
            grid=(1,),
            in_specs=[ANY, ANY],
            out_specs=pl.BlockSpec(dims, lambda i, p: (0, 0, 0)),
            scratch_shapes=[pltpu.SemaphoreType.DMA((len(order),))],
        ),
        compiler_params=PARAMS,
        name="lay",
    )(place, own, got)


def place_weights(place_ref, own_ref, got_ref, weight, sems, order):
    held, share, _ = own_ref.shape
    copies = []
    for i, mask in enumerate(order):
        piece = own_ref.at[i] if i < held else got_ref.at[i - held]
        row = pl.multiple_of((place_ref[0] ^ mask) * share, TAIL)
        there = weight.at[pl.ds(row, share)]
        copies.append(pltpu.make_async_copy(piece, there, sems.at[i]))
    for copy in copies:
        copy.start()
    return copies


def far_sum(src_ref, first, x_ref, weight):
    count, _, cols = x_ref.shape
    total = None
    for k in range(count):
        row = pl.multiple_of(src_ref[first + k] * cols, TAIL)
        term = jnp.dot(x_ref[k], weight[pl.ds(row, cols), :], preferred_element_type=F32)
        total = term if total is None else total + term
    return total


def prepare(x_refs, gain, x_out, k):
    column, row = [], 0
    for x_ref in x_refs:
        x = x_ref[...].astype(F32)
        column.append(jnp.sum(x * x, axis=1, keepdims=True))
        x_out[k, row : row + x.shape[0]] = (x * gain).astype(BF16)
        row += x.shape[0]
    return jnp.concatenate(column, axis=0)


def far_own_kernel(
    place_ref, src_ref, gain_ref, own_ref, got_ref, x_ref, x_out, sq_ref, out_ref, weight, sems,
    *, order
):
    copies = place_weights(place_ref, own_ref, got_ref, weight, sems, order)
    gain = gain_ref[place_ref[1] + src_ref[0]]
    sq_ref[...] = to_row(prepare([x_ref], gain, x_out, 0))
    for copy in copies:
        copy.wait()
    out_ref[...] = far_sum(src_ref, 0, x_out, weight)


def far_kv_kernel(
    place_ref, src_ref, gain_ref, part_ref, own_sq_ref, own_ref, got_ref, *rest, order, cuts
):
    x_refs, (out_ref, x_out, sq_ref, weight, sems) = rest[: sum(cuts)], rest[-5:]
    copies = place_weights(place_ref, own_ref, got_ref, weight, sems, order)
    rows = x_out.shape[1]
    columns, at = [], 0
    for k, pieces in enumerate(cuts):
        gain = gain_ref[place_ref[1] + src_ref[1 + k]]
        columns.append(prepare(x_refs[at : at + pieces], gain, x_out, k))
        at += pieces
    sq = to_row(sum(columns[1:], columns[0])) + own_sq_ref[...]
    sq_ref[...] = sq
    for copy in copies:
        copy.wait()
    total = part_ref[...] + far_sum(src_ref, 1, x_out, weight)
    out_ref[:rows, :] = total.astype(BF16)
    high = sq.astype(BF16).astype(F32)
    out_ref[rows:, :] = lines_of((high, sq - high), out_ref.shape[1])


def far_kv_scratch(gathered):
    order, own, _ = gathered
    return [
        pltpu.VMEM((len(order) * own.shape[1], own.shape[2]), BF16),
        pltpu.SemaphoreType.DMA((len(order),)),
    ]


def far_own_product(place, sources, gains, tokens, gathered):
    order, own, got = gathered
    rows, cols = tokens.shape
    dims = [(1, rows, cols), (1, rows), (rows, own.shape[2])]
    whole = lambda d: pl.BlockSpec(d, lambda i, p, s: (0,) * len(d))
    return pl.pallas_call(
        partial(far_own_kernel, order=order),
        out_shape=tuple(shape(d, t) for d, t in zip(dims, (BF16, F32, F32))),
        grid_spec=pltpu.PrefetchScalarGridSpec(
            num_scalar_prefetch=2,
            grid=(1,),
            in_specs=[whole(gains.shape), ANY, ANY, whole(tokens.shape)],
            out_specs=[whole(d) for d in dims],
            scratch_shapes=far_kv_scratch(gathered),
        ),
        compiler_params=PARAMS,
        name="far_own",
    )(place, sources, gains, own, got, tokens)


def far_kv_product(place, sources, gains, part, own_sq, blocks, gathered, after):
    order, own, got = gathered
    rows, width = part.shape
    cols = blocks[0][0].shape[1]
    pieces = [piece for block in blocks for piece in block]
    dims = [(rows + TAIL, width), (len(blocks), rows, cols), (1, rows)]
    whole = lambda d: pl.BlockSpec(d, lambda i, p, s: (0,) * len(d))
    return pl.pallas_call(
        partial(far_kv_kernel, order=order, cuts=[len(block) for block in blocks]),
        out_shape=tuple(shape(d, t) for d, t in zip(dims, (BF16, BF16, F32))),
        grid_spec=pltpu.PrefetchScalarGridSpec(
            num_scalar_prefetch=2,
            grid=(1,),
            in_specs=[whole(gains.shape), whole(part.shape), whole(own_sq.shape), ANY, ANY]
            + [whole(piece.shape) for piece in pieces]
            + [ANY for _ in after],
            out_specs=[whole(d) for d in dims],
            scratch_shapes=far_kv_scratch(gathered),
        ),
        compiler_params=PARAMS,
        name="far_kv",
    )(place, sources, gains, part, own_sq, own, got, *pieces, *after)


def far_kernel(place_ref, src_ref, own_x_ref, x_ref, own_ref, got_ref, *rest, order):
    out_ref, weight, sems = rest[-3:]
    for copy in place_weights(place_ref, own_ref, got_ref, weight, sems, order):
        copy.wait()
    total = far_sum(src_ref, 0, own_x_ref, weight) + far_sum(src_ref, 1, x_ref, weight)
    out_ref[...] = total.astype(BF16)


def lines_of(rows, width):
    lines = []
    for row in rows:
        for at in range(0, row.shape[1], width):
            line = row[:, at : at + width]
            if line.shape[1] < width:
                rest = jnp.zeros((1, width - line.shape[1]), F32)
                line = jnp.concatenate([line, rest], axis=1)
            lines.append(line)
    lines.append(jnp.zeros((TAIL - len(lines), width), F32))
    return jnp.concatenate(lines, axis=0).astype(BF16)


def rows_of(tail, count, length):
    per_row = -(-length // tail.shape[1])
    rows = []
    for r in range(count):
        lines = [tail[r * per_row + i : r * per_row + i + 1, :] for i in range(per_row)]
        rows.append(jnp.concatenate(lines, axis=1)[:, :length])
    return rows


def far_product(place, sources, own_x, x, gathered, after):
    order, own, got = gathered
    rows, width = x.shape[1], own.shape[2]
    return pl.pallas_call(
        partial(far_kernel, order=order),
        out_shape=shape((rows, width), BF16),
        grid_spec=pltpu.PrefetchScalarGridSpec(
            num_scalar_prefetch=2,
            grid=(1,),
            in_specs=[
                pl.BlockSpec(own_x.shape, lambda i, p, s: (0, 0, 0)),
                pl.BlockSpec(x.shape, lambda i, p, s: (0, 0, 0)),
                ANY,
                ANY,
            ]
            + [ANY for _ in after],
            out_specs=pl.BlockSpec((rows, width), lambda i, p, s: (0, 0)),
            scratch_shapes=far_kv_scratch(gathered),
        ),
        compiler_params=PARAMS,
        name="far",
    )(place, sources, own_x, x, own, got, *after)


def near_kernel(src_ref, own_x_ref, x_ref, k_ref, v_ref, q_ref, *rest):
    out_ref = rest[-1]
    step = pl.program_id(0)
    dot = partial(jnp.dot, preferred_element_type=F32)
    column = 0
    for ref in (k_ref, v_ref, q_ref):
        at = slice(column, column + ref.shape[1])

        @pl.when(step == 0)
        def _():
            out_ref[:, at] = dot(own_x_ref[0], ref[...])

        @pl.when(step > 0)
        def _():
            out_ref[:, at] += dot(x_ref[0], ref[...])

        column += ref.shape[1]


def near_product(sources, own_x, x, weights, after):
    count, rows, cols = x.shape
    widths = [w.shape[1] for w in weights]
    return pl.pallas_call(
        near_kernel,
        out_shape=shape((rows, sum(widths)), F32),
        grid_spec=pltpu.PrefetchScalarGridSpec(
            num_scalar_prefetch=1,
            grid=(count + 1,),
            in_specs=[
                pl.BlockSpec((1, rows, cols), lambda i, s: (0, 0, 0)),
                pl.BlockSpec((1, rows, cols), lambda i, s: (jnp.maximum(i - 1, 0), 0, 0)),
            ]
            + [pl.BlockSpec((cols, w), lambda i, s: (s[i], 0)) for w in widths]
            + [ANY for _ in after],
            out_specs=pl.BlockSpec((rows, sum(widths)), lambda i, s: (0, 0)),
        ),
        compiler_params=PARAMS,
        name="near",
    )(sources, own_x, x, *weights, *after)


def keys_kernel(near_ref, far_ref, sq_ref, id_ref, cos_ref, sin_ref, *rest, model):
    out_ref, sum_ref = rest[-2:]
    rows, width = near_ref.shape[0], far_ref.shape[1]
    tail = far_ref[rows:, :].astype(F32)
    total = sum(rows_of(tail, 2, rows), sq_ref[...])
    factor = to_column(lax.rsqrt(total / model + epsilon))
    sum_ref[...] = total
    keys, values = slice(0, HEAD_SIZE), slice(HEAD_SIZE, 2 * HEAD_SIZE)
    part = (near_ref[:, keys] + far_ref[:rows, keys].astype(F32)) * factor
    part = rotate(part, cos_ref[...], sin_ref[...]).astype(BF16)
    out_ref[: rows // 2, keys] = part[: rows // 2]
    out_ref[: rows // 2, values] = part[rows // 2 :]
    part = (near_ref[:, values] + far_ref[:rows, values].astype(F32)) * factor
    part = part.T.astype(BF16)
    for i, at in enumerate(range(0, rows, width)):
        row = rows // 2 + i * HEAD_SIZE
        out_ref[row : row + HEAD_SIZE, :] = part[:, at : at + width]
    out_ref[rows:, :] = lines_of((id_ref[...].astype(F32),), width)


def keys_values(near, far, sq, ids, cosine, sine, after, model):
    rows, width = near.shape[0], far.shape[1]
    whole = lambda i: (0, 0)
    return pl.pallas_call(
        partial(keys_kernel, model=model),
        out_shape=(shape(far.shape, BF16), shape(sq.shape, F32)),
        grid=(1,),
        in_specs=[pl.BlockSpec((rows, width), whole)]
        + [pl.BlockSpec(a.shape, whole) for a in (far, sq, ids, cosine, sine)]
        + [ANY for _ in after],
        out_specs=[pl.BlockSpec(far.shape, whole), pl.BlockSpec(sq.shape, whole)],
        compiler_params=PARAMS,
        name="keys",
    )(near, far, sq, ids, cosine, sine, *after)


def queries_kernel(near_ref, far_ref, sum_ref, cos_ref, sin_ref, out_ref, *, model):
    scale = query_scale * math.log2(math.e)
    factor = to_column(lax.rsqrt(sum_ref[...] / model + epsilon) * scale)
    for c in range(0, out_ref.shape[1], HEAD_SIZE):
        at = slice(c, c + HEAD_SIZE)
        part = (near_ref[:, at] + far_ref[:, at].astype(F32)) * factor
        out_ref[:, at] = rotate(part, cos_ref[...], sin_ref[...]).astype(BF16)


def finished_queries(near, far, sums, cosine, sine, model):
    rows, width = far.shape
    last = near.shape[1] // width - 1
    whole = lambda i: (0, 0)
    return pl.pallas_call(
        partial(queries_kernel, model=model),
        out_shape=shape((rows, width), BF16),
        grid=(1,),
        in_specs=[pl.BlockSpec((rows, width), lambda i: (0, last))]
        + [pl.BlockSpec(a.shape, whole) for a in (far, sums, cosine, sine)],
        out_specs=pl.BlockSpec((rows, width), whole),
        compiler_params=PARAMS,
        cost_estimate=pl.CostEstimate(flops=HIDE, bytes_accessed=10**8, transcendentals=0),
        name="queries",
    )(near, far, sums, cosine, sine)


def attention_kernel(seq_ref, q_ref, id_ref, after_ref, *rest, back, offset):
    kv_refs, (out_ref, k_scr, vt_scr, count_scr) = rest[:-4], rest[-4:]
    part_rows, message = kv_refs[0].shape[0] - TAIL, kv_refs[0].shape[1]
    group = q_ref.shape[1] // HEAD_SIZE
    tile = pl.program_id(0)

    @pl.when(tile == 0)
    def _():
        counts = [jnp.zeros((1, 1), F32) for _ in range(DOCUMENTS)]
        for b, kv_ref in enumerate(kv_refs):
            row, half = b * part_rows, part_rows // 2
            k_scr[row : row + half, :] = kv_ref[:half, :HEAD_SIZE]
            k_scr[row + half : row + part_rows, :] = kv_ref[:half, HEAD_SIZE:]
            for i, at in enumerate(range(0, part_rows, message)):
                first = half + i * HEAD_SIZE
                vt_scr[:, row + at : row + at + message] = kv_ref[first : first + HEAD_SIZE, :]
            (ids,) = rows_of(kv_ref[part_rows:, :].astype(F32), 1, part_rows)
            exists = b >= back - seq_ref[0]
            ids = jnp.where(exists, ids, -1.0)
            for d in range(DOCUMENTS):
                below = (ids < d).astype(F32)
                counts[d] = counts[d] + jnp.sum(below, axis=1, keepdims=True)
        for d in range(DOCUMENTS):
            count_scr[d : d + 1, :] = jnp.broadcast_to(counts[d], (1, LANES))

    heads = [q_ref[:, c : c + HEAD_SIZE] for c in range(0, group * HEAD_SIZE, HEAD_SIZE)]
    q2 = jnp.concatenate(heads, axis=0)
    width = group * Q_TILE

    start = jnp.zeros((1, Q_TILE), F32)
    for d in range(DOCUMENTS):
        start = jnp.where(id_ref[...] == d, count_scr[d : d + 1, :], start)
    start = start.astype(jnp.int32)
    low = jnp.min(start) // K_TILE
    start = jnp.concatenate([start] * group, axis=1)
    first = back * part_rows + offset + tile * Q_TILE
    place = first + lax.broadcasted_iota(jnp.int32, (1, Q_TILE), 1)
    place = jnp.concatenate([place] * group, axis=1)

    def score(j):
        base = pl.multiple_of(j * K_TILE, K_TILE)
        return lax.dot_general(
            k_scr[pl.ds(base, K_TILE), :],
            q2,
            (((1,), (1,)), ((), ())),
            preferred_element_type=F32,
        )

    stop = (first + Q_TILE + K_TILE - 1) // K_TILE

    def step(j, state):
        scores, run_max, run_sum, acc = state
        following = score(jnp.minimum(j + 1, stop - 1))
        base = pl.multiple_of(j * K_TILE, K_TILE)
        key_pos = base + lax.broadcasted_iota(jnp.int32, (K_TILE, width), 0)
        allowed = (key_pos >= start) & (key_pos <= place)
        scores = jnp.where(allowed, scores, NEG)
        new_max = jnp.maximum(run_max, jnp.max(scores, axis=0, keepdims=True))
        expo = jnp.exp2(scores - new_max)
        factor = jnp.exp2(run_max - new_max)
        run_sum = run_sum * factor + jnp.sum(expo, axis=0, keepdims=True)
        acc = acc * factor + jnp.dot(
            vt_scr[:, pl.ds(base, K_TILE)], expo.astype(BF16), preferred_element_type=F32
        )
        return following, new_max, run_sum, acc

    state = (
        score(low),
        jnp.full((1, width), NEG, F32),
        jnp.zeros((1, width), F32),
        jnp.zeros((HEAD_SIZE, width), F32),
    )
    _, _, run_sum, acc = lax.fori_loop(low, stop, step, state)
    context = (acc / run_sum).T
    for g in range(group):
        out_ref[:, g * HEAD_SIZE : (g + 1) * HEAD_SIZE] = context[
            g * Q_TILE : (g + 1) * Q_TILE
        ].astype(BF16)


def attend(seq, queries, ids, after, blocks, c):
    rows, width = queries.shape[0] // CHUNKS, queries.shape[1]
    back = len(blocks) - 1
    tiles = rows // Q_TILE
    keys = len(blocks) * queries.shape[0]
    return pl.pallas_call(
        partial(attention_kernel, back=back, offset=c * rows),
        out_shape=shape((rows, width), BF16),
        grid_spec=pltpu.PrefetchScalarGridSpec(
            num_scalar_prefetch=1,
            grid=(tiles,),
            in_specs=[
                pl.BlockSpec((Q_TILE, width), lambda i, s: (c * tiles + i, 0)),
                pl.BlockSpec((1, Q_TILE), lambda i, s: (0, c * tiles + i)),
                ANY,
            ]
            + [pl.BlockSpec(b.shape, lambda i, s: (0, 0)) for b in blocks],
            out_specs=pl.BlockSpec((Q_TILE, width), lambda i, s: (i, 0)),
            scratch_shapes=[
                pltpu.VMEM((keys, HEAD_SIZE), BF16),
                pltpu.VMEM((HEAD_SIZE, keys), BF16),
                pltpu.VMEM((DOCUMENTS, LANES), F32),
            ],
        ),
        compiler_params=PARAMS,
        cost_estimate=pl.CostEstimate(
            flops=4 * rows * width * keys,
            bytes_accessed=4 * keys * width,
            transcendentals=rows * keys * width // HEAD_SIZE,
        ),
        name="attend",
    )(seq, queries, ids, after, *blocks)


def first_output_kernel(at_ref, own_o_ref, o_ref, *rest):
    ctx_refs, out_ref = rest[:-2], rest[-1]
    total = jnp.dot(ctx_refs[0][...], own_o_ref[...], preferred_element_type=F32)
    for i, ctx_ref in enumerate(ctx_refs[1:]):
        total = total + jnp.dot(ctx_ref[...], o_ref[at_ref[1 + i]], preferred_element_type=F32)
    out_ref[...] = total


def last_output_kernel(at_ref, part_ref, o_ref, *rest):
    ctx_refs, (before_ref, out_ref, sq_ref, acc) = rest[:-4], rest[-4:]
    step = pl.program_id(0)
    total = part_ref[...]
    for i, ctx_ref in enumerate(ctx_refs):
        total = total + jnp.dot(ctx_ref[...], o_ref[at_ref[i]], preferred_element_type=F32)
    out_ref[...] = total
    squares = jnp.sum(total * total, axis=1, keepdims=True)
    squares = jnp.broadcast_to(squares, acc.shape)

    @pl.when(step == 0)
    def _():
        acc[...] = squares

    @pl.when(step > 0)
    def _():
        acc[...] += squares

    @pl.when(step == pl.num_programs(0) - 1)
    def _():
        done = sq_ref.shape[1] - acc.shape[0]
        if done:
            sq_ref[:, :done] = before_ref[...]
        sq_ref[:, done:] = acc[...].T[0:1, :]


def column_tiles(cols):
    tiles = 3 if cols % (3 * LANES) == 0 else 1
    return tiles, cols // tiles


def first_output(column, order, o_weight, gathered, contexts, after):
    chunk, width = contexts[0].shape
    others, _, cols = gathered.shape
    tiles, tile = column_tiles(cols)
    if cols % LANES:
        o_weight = lax.dynamic_slice_in_dim(o_weight, column * cols, cols, axis=1)
        column = jnp.int32(0)
    return pl.pallas_call(
        first_output_kernel,
        out_shape=shape((chunk, cols), F32),
        grid_spec=pltpu.PrefetchScalarGridSpec(
            num_scalar_prefetch=1,
            grid=(tiles,),
            in_specs=[
                pl.BlockSpec((width, tile), lambda i, at: (0, at[0] * tiles + i)),
                pl.BlockSpec((others, width, tile), lambda i, at: (0, 0, i)),
            ]
            + [pl.BlockSpec((chunk, width), lambda i, at: (0, 0)) for _ in contexts]
            + [ANY],
            out_specs=pl.BlockSpec((chunk, tile), lambda i, at: (0, i)),
        ),
        compiler_params=PARAMS,
        cost_estimate=pl.CostEstimate(flops=HIDE, bytes_accessed=10**8, transcendentals=0),
        name="first_output",
    )(jnp.stack([column] + order), o_weight, gathered, *contexts, after)


def last_output(order, part, gathered, contexts, before, c):
    chunk, width = contexts[0].shape
    others, _, cols = gathered.shape
    tiles, tile = column_tiles(cols)
    return pl.pallas_call(
        last_output_kernel,
        out_shape=(shape((chunk, cols), F32), shape((1, (c + 1) * chunk), F32)),
        grid_spec=pltpu.PrefetchScalarGridSpec(
            num_scalar_prefetch=1,
            grid=(tiles,),
            in_specs=[
                pl.BlockSpec((chunk, tile), lambda i, at: (0, i)),
                pl.BlockSpec((others, width, tile), lambda i, at: (0, 0, i)),
            ]
            + [pl.BlockSpec((chunk, width), lambda i, at: (0, 0)) for _ in contexts]
            + [pl.BlockSpec(before.shape, lambda i, at: (0, 0))],
            out_specs=[
                pl.BlockSpec((chunk, tile), lambda i, at: (0, i)),
                pl.BlockSpec((1, (c + 1) * chunk), lambda i, at: (0, 0)),
            ],
            scratch_shapes=[pltpu.VMEM((chunk, LANES), F32)],
        ),
        compiler_params=PARAMS,
        name="last_output",
    )(jnp.stack(order), part, gathered, *contexts, before)


def final_kernel(token_ref, gain_ref, *rest, model):
    branch_refs, sq_refs, out_ref = rest[:CHUNKS], rest[CHUNKS:-1], rest[-1]
    total = sq_refs[0][...]
    for sq_ref in sq_refs[1:]:
        total = total + sq_ref[...]
    factor = to_column(lax.rsqrt(total / model + epsilon))[:, 0:1]
    for c in range(CHUNKS):

        @pl.when(pl.program_id(0) * CHUNKS // pl.num_programs(0) == c)
        def _():
            out = token_ref[...].astype(F32) + branch_refs[c][...] * factor * gain_ref[...]
            out_ref[...] = out.astype(BF16)


def finish(tokens, branches, out_gain, sums, model):
    rows, cols = tokens.shape
    tiles = rows // CHUNKS // Q_TILE
    held = lambda c: lambda i: (jnp.clip(i - c * tiles, 0, tiles - 1), 0)
    return pl.pallas_call(
        partial(final_kernel, model=model),
        out_shape=shape(tokens.shape, BF16),
        grid=(CHUNKS * tiles,),
        in_specs=[
            pl.BlockSpec((Q_TILE, cols), lambda i: (i, 0)),
            pl.BlockSpec((1, cols), lambda i: (0, 0)),
        ]
        + [pl.BlockSpec((Q_TILE, cols), held(c)) for c in range(CHUNKS)]
        + [pl.BlockSpec((1, Q_TILE), lambda i: (0, i)) for _ in sums],
        out_specs=pl.BlockSpec((Q_TILE, cols), lambda i: (i, 0)),
        compiler_params=PARAMS,
        name="finish",
    )(tokens, out_gain, *branches, *sums)


def per_device(
    tokens, seg_ids, in_gain, q_weight, k_weight, value_weight, o_weight, out_gain, *, sizes
):
    rows, cols = tokens.shape
    model = in_gain.shape[0]
    nz, nseq = sizes["tensor"], sizes["seq"]
    plane = nseq * sizes["groups"]
    z = lax.axis_index("tensor")
    seq = lax.axis_index("seq")
    in_plane = lax.axis_index(PLANE)
    half = nz // 2
    side, within = z // half, z % half
    half_rows = half * cols

    ring = [(i, i // half * half + (i + 1) % half) for i in range(nz)]
    swap = [(i, (i + half) % nz) for i in range(nz)]
    turn = lambda k: [(i, (i + k) % nz) for i in range(nz)]
    seq_bits = [1 << b for b in range(1, nseq.bit_length() - 1)]
    group_bits = [nseq << b for b in range(sizes["groups"].bit_length() - 1)]

    share = half_rows // plane
    at = jnp.reshape((1 - side) * plane + in_plane, (1,))
    inner = seq_bits + group_bits
    masks_kv, masks_q = inner + [1], inner[::-1] + [1]
    last = len(masks_kv) - 1
    eighth = rows // 48 * 8
    counts = [eighth, rows // 2 - 2 * TAIL, rows // 2 + 2 * TAIL - eighth]
    packed_kv, packed_q, cut = pack(
        at, q_weight, k_weight, value_weight, share, tokens, counts[0]
    )
    own_kv = lax.ppermute(packed_kv, "tensor", swap)[None]
    own_q = lax.ppermute(packed_q, "tensor", swap)[None]
    received = [lax.ppermute(cut, "tensor", ring)]
    o_share = o_weight.shape[0] // plane
    columns = [(z + k) % nz * cols for k in range(1, nz)]
    pieces = cut_pieces(in_plane * o_share, columns, o_weight, o_share, cols, own_kv)
    moved = [lax.ppermute(p, "tensor", turn(k + 1)) for k, p in enumerate(pieces)]

    order_kv, order_q, first = [0], [0], counts[0]
    for step, (mask_kv, mask_q) in enumerate(zip(masks_kv, masks_q)):
        after, count = [], 0
        if step == 0:
            pairs, after = [], [own_kv, own_q, received[0]]
        else:
            pairs = [(own_kv, far_kv), (own_q, far_q)]
        if step < 2:
            count = counts[1 + step]
        if step == last:
            after = [received[1]] + moved
        outs = stage(pairs, tokens, first, count, after, HIDE if step == last else 0)
        if pairs:
            own_kv, own_q = outs[:2]
        if count:
            received.append(lax.ppermute(outs[-1], "tensor", ring))
        first += count
        far_kv = lax.ppermute(own_kv, PLANE, [(i, i ^ mask_kv) for i in range(plane)])
        far_q = lax.ppermute(own_q, PLANE, [(i, i ^ mask_q) for i in range(plane)])
        order_kv = order_kv + [k ^ mask_kv for k in order_kv]
        order_q = order_q + [k ^ mask_q for k in order_q]
    far_kv, far_q = (order_kv, own_kv, far_kv), (order_q, own_q, far_q)

    own_o = jnp.stack(moved)[None]

    def double(own, step, after):
        if step > 0:
            (own,) = stage([own], tokens, 0, 0, after)
        return own, lax.ppermute(own, PLANE, [(i, i ^ masks_kv[step]) for i in range(plane)])

    sources = (within + half - jnp.arange(half, dtype=jnp.int32)) % half
    gains = in_gain.reshape(nz, 1, cols)
    place = jnp.stack([in_plane, side * half])
    own_x, own_sq, part = far_own_product(place, sources, gains, tokens, far_kv)
    received[-1] = gate(received[-1], own_sq)
    blocks = [received]
    for _ in range(half - 2):
        blocks.append([lax.ppermute(block, "tensor", ring) for block in blocks[-1]])
    sent_kv, x, sq = far_kv_product(
        place, sources, gains, part, own_sq, blocks, far_kv, [far_q[2]]
    )
    got_kv = lax.ppermute(sent_kv, "tensor", swap)
    pair_o = double(own_o, 0, [])
    for step in range(1, last - 1):
        pair_o = double(pair_o, step, [])
    weights = (k_weight, value_weight, q_weight)

    near = near_product(side * half + sources, own_x, x, weights, [sent_kv])

    sent_q = far_product(place, sources, own_x, x, far_q, [near])
    got_q = lax.ppermute(gate(sent_q, got_kv), "tensor", swap)
    pair_o = double(pair_o, last - 1, [sent_q])
    cosine, sine = rotation_table(seq * rows + jnp.arange(rows, dtype=jnp.int32))
    ids = seg_ids[None, :]
    own_kv, sums = keys_values(
        near, got_kv, sq, ids, cosine, sine, [sent_q, pair_o[0]], model
    )
    pair_o = double(pair_o, last, [own_kv])
    gathered_o = lay_pieces(place, order_kv, *pair_o)

    back = -(-(nseq * rows // 2 - 1) // rows)
    kv_blocks = [own_kv]
    for k in range(1, back + 1):
        earlier = [(i, i + k) for i in range(nseq - k)]
        kv_blocks.insert(0, lax.ppermute(own_kv, "seq", earlier))

    queries = finished_queries(near, got_q, sums, cosine, sine, model)
    seq_at = jnp.reshape(seq, (1,))
    contexts, after = [], own_kv
    for c in range(CHUNKS):
        contexts.append(attend(seq_at, queries, ids, after, kv_blocks, c))
        after = gathered_o
    early, late = [], []
    for c, context in enumerate(contexts):
        if nz == 4:
            pairs = [(i, i ^ 1) for i in range(nz)]
            opposite = lax.ppermute(context, "tensor", swap)
            beside = lax.ppermute(context, "tensor", pairs)
            if c + 1 < CHUNKS:
                opposite = gate(opposite, contexts[c + 1])
            across = lax.ppermute(opposite, "tensor", pairs)
            early.append([context, beside])
            late.append([opposite, across])
            order = [2 - 2 * (z % 2), jnp.int32(1), 2 * (z % 2)]
        else:
            early.append([context])
            late.append([lax.ppermute(context, "tensor", turn(k)) for k in range(1, nz)])
            order = [jnp.int32(k) for k in range(nz - 1)]
    split = len(early[0]) - 1
    branches, own_sq = [], sums
    for c in range(CHUNKS):
        part = first_output(z, order[:split], o_weight, gathered_o, early[c], contexts[-1])
        branch, own_sq = last_output(order[split:], part, gathered_o, late[c], own_sq, c)
        branches.append(branch)
    squares = [own_sq]
    squares += [lax.ppermute(own_sq, "tensor", turn(k)) for k in range(1, nz)]
    return finish(tokens, branches, out_gain[None, :], squares, model)


def solution(mesh):
    return jax.shard_map(
        partial(per_device, sizes=dict(mesh.shape)),
        mesh=mesh,
        in_specs=(
            P(("groups", "seq"), "tensor"),
            P(("groups", "seq")),
            P(),
            P(None, "tensor"),
            P(None, "tensor"),
            P(None, "tensor"),
            P("tensor", None),
            P("tensor"),
        ),
        out_specs=P(("groups", "seq"), "tensor"),
        check_vma=False,
    )
```

```python
import math
from functools import partial

import jax
import jax.numpy as jnp
from jax import lax
from jax.experimental import pallas as pl
from jax.experimental.pallas import tpu as pltpu
from jax.sharding import PartitionSpec as P

HEAD_SIZE = 128
PLANE = ("groups", "seq")

epsilon = 1e-06
query_scale = 144.0 ** (-0.5)
rope_base = 10000.0
NEG = -1e30
Q_TILE = 128
K_TILE = 384
CHUNKS = 2
LANES = 128
TAIL = 16
F32, BF16 = jnp.float32, jnp.bfloat16
ANY = pl.BlockSpec(memory_space=pl.ANY)
HBM = pl.BlockSpec(memory_space=pltpu.HBM)
VMEM = pl.BlockSpec(memory_space=pltpu.VMEM)
DOCUMENTS = 8
HIDE = 5 * 10**10
PARAMS = pltpu.CompilerParams(vmem_limit_bytes=48 * 1024 * 1024)
ALL_VMEM = pltpu.CompilerParams(vmem_limit_bytes=62 * 1024 * 1024)


def shape(dims, dtype):
    return jax.ShapeDtypeStruct(dims, dtype)


def to_row(column):
    return jnp.broadcast_to(column, (column.shape[0], LANES)).T[0:1, :]


def to_column(row):
    return jnp.broadcast_to(row, (LANES, row.shape[1])).T


def rotation_table(token_places):
    half_dim = HEAD_SIZE // 2
    inverse = rope_base ** (-jnp.arange(half_dim, dtype=F32) / half_dim)
    angles = token_places.astype(F32)[:, None] * inverse[None, :]
    cosine, sine = jnp.cos(angles), jnp.sin(angles)
    return jnp.concatenate([cosine, cosine], 1), jnp.concatenate([-sine, sine], 1)


def rotate(vectors, cosine, sine):
    return vectors * cosine + pltpu.roll(vectors, HEAD_SIZE // 2, 1) * sine


def pack_kernel(at_ref, q_ref, k_ref, v_ref, x_ref, kv_out, q_out, x_out, sems):
    share, width = q_out.shape[0], k_ref.shape[1]
    rows = pl.ds(pl.multiple_of(at_ref[0] * share, TAIL), share)
    copies = [
        pltpu.make_async_copy(k_ref.at[rows], kv_out.at[:, pl.ds(0, width)], sems.at[0]),
        pltpu.make_async_copy(v_ref.at[rows], kv_out.at[:, pl.ds(width, width)], sems.at[1]),
        pltpu.make_async_copy(q_ref.at[rows], q_out, sems.at[2]),
        pltpu.make_async_copy(x_ref.at[pl.ds(0, x_out.shape[0])], x_out, sems.at[3]),
    ]
    for copy in copies:
        copy.start()
    for copy in copies:
        copy.wait()


def pack(at, q_weight, k_weight, v_weight, share, tokens, rows):
    kv_width = k_weight.shape[1] + v_weight.shape[1]
    dims = [(share, kv_width), (share, q_weight.shape[1]), (rows, tokens.shape[1])]
    return pl.pallas_call(
        pack_kernel,
        out_shape=tuple(shape(d, BF16) for d in dims),
        grid_spec=pltpu.PrefetchScalarGridSpec(
            num_scalar_prefetch=1,
            grid=(1,),
            in_specs=[HBM, HBM, HBM, HBM],
            out_specs=[pl.BlockSpec(d, lambda i, at: (0, 0)) for d in dims],
            scratch_shapes=[pltpu.SemaphoreType.DMA((4,))],
        ),
        compiler_params=ALL_VMEM,
        name="pack",
    )(at, q_weight, k_weight, v_weight, tokens)


def gate_kernel(x_ref, after_ref, out_ref):
    pass


def gate(x, after):
    return pl.pallas_call(
        gate_kernel,
        out_shape=shape(x.shape, x.dtype),
        in_specs=[ANY, ANY],
        out_specs=ANY,
        input_output_aliases={0: 0},
        compiler_params=PARAMS,
        name="gate",
    )(x, after)


def stage_kernel(*refs, pairs, first, count):
    outputs = pairs + (1 if count else 0)
    ins, outs, sems = refs[: -outputs - 1], refs[-outputs - 1 : -1], refs[-1]
    copies = []
    for p in range(pairs):
        held = ins[2 * p].shape[0]
        for side in range(2):
            there = outs[p].at[pl.ds(side * held, held)]
            copies.append(
                pltpu.make_async_copy(ins[2 * p + side], there, sems.at[len(copies)])
            )
    if count:
        rows = ins[2 * pairs].at[pl.ds(first, count)]
        copies.append(pltpu.make_async_copy(rows, outs[-1], sems.at[len(copies)]))
    for copy in copies:
        copy.start()
    for copy in copies:
        copy.wait()


def stage(joined, tokens, first, count, after, flops=0):
    dims = [(2 * pair[0].shape[0],) + pair[0].shape[1:] for pair in joined]
    if count:
        dims.append((count, tokens.shape[1]))
    return pl.pallas_call(
        partial(stage_kernel, pairs=len(joined), first=first, count=count),
        out_shape=tuple(shape(d, BF16) for d in dims),
        in_specs=[ANY] * (2 * len(joined) + 1 + len(after)),
        scratch_shapes=[pltpu.SemaphoreType.DMA((2 * len(joined) + 1,))],
        compiler_params=PARAMS,
        cost_estimate=pl.CostEstimate(flops=flops, bytes_accessed=flops // 500, transcendentals=0),
        name="stage",
    )(*[piece for pair in joined for piece in pair], tokens, *after)


def cut_kernel(at_ref, o_ref, after_ref, *rest):
    outs, sems = rest[:-1], rest[-1]
    copies = []
    for i, out in enumerate(outs):
        rows = pl.ds(pl.multiple_of(at_ref[0], TAIL), out.shape[0])
        columns = pl.ds(pl.multiple_of(at_ref[1 + i], LANES), out.shape[1])
        copies.append(pltpu.make_async_copy(o_ref.at[rows, columns], out, sems.at[i]))
    for copy in copies:
        copy.start()
    for copy in copies:
        copy.wait()


def cut_pieces(row, columns, o_weight, share, cols, after):
    if cols % LANES:
        return [lax.dynamic_slice(o_weight, (row, c), (share, cols)) for c in columns]
    return pl.pallas_call(
        cut_kernel,
        out_shape=tuple(shape((share, cols), BF16) for _ in columns),
        grid_spec=pltpu.PrefetchScalarGridSpec(
            num_scalar_prefetch=1,
            grid=(1,),
            in_specs=[ANY, ANY],
            out_specs=[VMEM for _ in columns],
            scratch_shapes=[pltpu.SemaphoreType.DMA((len(columns),))],
        ),
        compiler_params=PARAMS,
        name="cut",
    )(jnp.stack([row] + columns), o_weight, after)


def lay_kernel(place_ref, own_ref, got_ref, out_ref, sems, *, order):
    held, others, share, _ = own_ref.shape
    copies = []
    for i, mask in enumerate(order):
        piece = own_ref.at[i] if i < held else got_ref.at[i - held]
        row = pl.multiple_of((place_ref[0] ^ mask) * share, TAIL)
        there = out_ref.at[:, pl.ds(row, share)]
        copies.append(pltpu.make_async_copy(piece, there, sems.at[i]))
    for copy in copies:
        copy.start()
    for copy in copies:
        copy.wait()


def lay_pieces(place, order, own, got):
    _, others, share, cols = own.shape
    dims = (others, len(order) * share, cols)
    return pl.pallas_call(
        partial(lay_kernel, order=order),
        out_shape=shape(dims, BF16),
        grid_spec=pltpu.PrefetchScalarGridSpec(
            num_scalar_prefetch=1,
            grid=(1,),
            in_specs=[ANY, ANY],
            out_specs=pl.BlockSpec(dims, lambda i, p: (0, 0, 0)),
            scratch_shapes=[pltpu.SemaphoreType.DMA((len(order),))],
        ),
        compiler_params=PARAMS,
        name="lay",
    )(place, own, got)


def place_weights(place_ref, own_ref, got_ref, weight, sems, order):
    held, share, _ = own_ref.shape
    copies = []
    for i, mask in enumerate(order):
        piece = own_ref.at[i] if i < held else got_ref.at[i - held]
        row = pl.multiple_of((place_ref[0] ^ mask) * share, TAIL)
        there = weight.at[pl.ds(row, share)]
        copies.append(pltpu.make_async_copy(piece, there, sems.at[i]))
    for copy in copies:
        copy.start()
    return copies


def far_sum(src_ref, first, x_ref, weight):
    count, _, cols = x_ref.shape
    total = None
    for k in range(count):
        row = pl.multiple_of(src_ref[first + k] * cols, TAIL)
        term = jnp.dot(x_ref[k], weight[pl.ds(row, cols), :], preferred_element_type=F32)
        total = term if total is None else total + term
    return total


def prepare(x_refs, gain, x_out, k):
    column, row = [], 0
    for x_ref in x_refs:
        x = x_ref[...].astype(F32)
        column.append(jnp.sum(x * x, axis=1, keepdims=True))
        x_out[k, row : row + x.shape[0]] = (x * gain).astype(BF16)
        row += x.shape[0]
    return jnp.concatenate(column, axis=0)


def far_own_kernel(
    place_ref, src_ref, gain_ref, own_ref, got_ref, x_ref, x_out, sq_ref, out_ref, weight, sems,
    *, order
):
    copies = place_weights(place_ref, own_ref, got_ref, weight, sems, order)
    gain = gain_ref[place_ref[1] + src_ref[0]]
    sq_ref[...] = to_row(prepare([x_ref], gain, x_out, 0))
    for copy in copies:
        copy.wait()
    out_ref[...] = far_sum(src_ref, 0, x_out, weight)


def far_kv_kernel(
    place_ref, src_ref, gain_ref, part_ref, own_sq_ref, own_ref, got_ref, *rest, order, cuts
):
    x_refs, (out_ref, x_out, sq_ref, weight, sems) = rest[: sum(cuts)], rest[-5:]
    copies = place_weights(place_ref, own_ref, got_ref, weight, sems, order)
    rows = x_out.shape[1]
    columns, at = [], 0
    for k, pieces in enumerate(cuts):
        gain = gain_ref[place_ref[1] + src_ref[1 + k]]
        columns.append(prepare(x_refs[at : at + pieces], gain, x_out, k))
        at += pieces
    sq = to_row(sum(columns[1:], columns[0])) + own_sq_ref[...]
    sq_ref[...] = sq
    for copy in copies:
        copy.wait()
    total = part_ref[...] + far_sum(src_ref, 1, x_out, weight)
    out_ref[:rows, :] = total.astype(BF16)
    high = sq.astype(BF16).astype(F32)
    out_ref[rows:, :] = lines_of((high, sq - high), out_ref.shape[1])


def far_kv_scratch(gathered):
    order, own, _ = gathered
    return [
        pltpu.VMEM((len(order) * own.shape[1], own.shape[2]), BF16),
        pltpu.SemaphoreType.DMA((len(order),)),
    ]


def far_own_product(place, sources, gains, tokens, gathered):
    order, own, got = gathered
    rows, cols = tokens.shape
    dims = [(1, rows, cols), (1, rows), (rows, own.shape[2])]
    whole = lambda d: pl.BlockSpec(d, lambda i, p, s: (0,) * len(d))
    return pl.pallas_call(
        partial(far_own_kernel, order=order),
        out_shape=tuple(shape(d, t) for d, t in zip(dims, (BF16, F32, F32))),
        grid_spec=pltpu.PrefetchScalarGridSpec(
            num_scalar_prefetch=2,
            grid=(1,),
            in_specs=[whole(gains.shape), ANY, ANY, whole(tokens.shape)],
            out_specs=[whole(d) for d in dims],
            scratch_shapes=far_kv_scratch(gathered),
        ),
        compiler_params=PARAMS,
        name="far_own",
    )(place, sources, gains, own, got, tokens)


def far_kv_product(place, sources, gains, part, own_sq, blocks, gathered, after):
    order, own, got = gathered
    rows, width = part.shape
    cols = blocks[0][0].shape[1]
    pieces = [piece for block in blocks for piece in block]
    dims = [(rows + TAIL, width), (len(blocks), rows, cols), (1, rows)]
    whole = lambda d: pl.BlockSpec(d, lambda i, p, s: (0,) * len(d))
    return pl.pallas_call(
        partial(far_kv_kernel, order=order, cuts=[len(block) for block in blocks]),
        out_shape=tuple(shape(d, t) for d, t in zip(dims, (BF16, BF16, F32))),
        grid_spec=pltpu.PrefetchScalarGridSpec(
            num_scalar_prefetch=2,
            grid=(1,),
            in_specs=[whole(gains.shape), whole(part.shape), whole(own_sq.shape), ANY, ANY]
            + [whole(piece.shape) for piece in pieces]
            + [ANY for _ in after],
            out_specs=[whole(d) for d in dims],
            scratch_shapes=far_kv_scratch(gathered),
        ),
        compiler_params=PARAMS,
        name="far_kv",
    )(place, sources, gains, part, own_sq, own, got, *pieces, *after)


def far_kernel(place_ref, src_ref, own_x_ref, x_ref, own_ref, got_ref, *rest, order):
    out_ref, weight, sems = rest[-3:]
    for copy in place_weights(place_ref, own_ref, got_ref, weight, sems, order):
        copy.wait()
    total = far_sum(src_ref, 0, own_x_ref, weight) + far_sum(src_ref, 1, x_ref, weight)
    out_ref[...] = total.astype(BF16)


def lines_of(rows, width):
    lines = []
    for row in rows:
        for at in range(0, row.shape[1], width):
            line = row[:, at : at + width]
            if line.shape[1] < width:
                rest = jnp.zeros((1, width - line.shape[1]), F32)
                line = jnp.concatenate([line, rest], axis=1)
            lines.append(line)
    lines.append(jnp.zeros((TAIL - len(lines), width), F32))
    return jnp.concatenate(lines, axis=0).astype(BF16)


def rows_of(tail, count, length):
    per_row = -(-length // tail.shape[1])
    rows = []
    for r in range(count):
        lines = [tail[r * per_row + i : r * per_row + i + 1, :] for i in range(per_row)]
        rows.append(jnp.concatenate(lines, axis=1)[:, :length])
    return rows


def far_product(place, sources, own_x, x, gathered, after):
    order, own, got = gathered
    rows, width = x.shape[1], own.shape[2]
    return pl.pallas_call(
        partial(far_kernel, order=order),
        out_shape=shape((rows, width), BF16),
        grid_spec=pltpu.PrefetchScalarGridSpec(
            num_scalar_prefetch=2,
            grid=(1,),
            in_specs=[
                pl.BlockSpec(own_x.shape, lambda i, p, s: (0, 0, 0)),
                pl.BlockSpec(x.shape, lambda i, p, s: (0, 0, 0)),
                ANY,
                ANY,
            ]
            + [ANY for _ in after],
            out_specs=pl.BlockSpec((rows, width), lambda i, p, s: (0, 0)),
            scratch_shapes=far_kv_scratch(gathered),
        ),
        compiler_params=PARAMS,
        name="far",
    )(place, sources, own_x, x, own, got, *after)


def near_kernel(src_ref, own_x_ref, x_ref, k_ref, v_ref, q_ref, *rest):
    out_ref = rest[-1]
    step = pl.program_id(0)
    dot = partial(jnp.dot, preferred_element_type=F32)
    column = 0
    for ref in (k_ref, v_ref, q_ref):
        at = slice(column, column + ref.shape[1])

        @pl.when(step == 0)
        def _():
            out_ref[:, at] = dot(own_x_ref[0], ref[...])

        @pl.when(step > 0)
        def _():
            out_ref[:, at] += dot(x_ref[0], ref[...])

        column += ref.shape[1]


def near_product(sources, own_x, x, weights, after):
    count, rows, cols = x.shape
    widths = [w.shape[1] for w in weights]
    return pl.pallas_call(
        near_kernel,
        out_shape=shape((rows, sum(widths)), F32),
        grid_spec=pltpu.PrefetchScalarGridSpec(
            num_scalar_prefetch=1,
            grid=(count + 1,),
            in_specs=[
                pl.BlockSpec((1, rows, cols), lambda i, s: (0, 0, 0)),
                pl.BlockSpec((1, rows, cols), lambda i, s: (jnp.maximum(i - 1, 0), 0, 0)),
            ]
            + [pl.BlockSpec((cols, w), lambda i, s: (s[i], 0)) for w in widths]
            + [ANY for _ in after],
            out_specs=pl.BlockSpec((rows, sum(widths)), lambda i, s: (0, 0)),
        ),
        compiler_params=PARAMS,
        name="near",
    )(sources, own_x, x, *weights, *after)


def keys_kernel(near_ref, far_ref, sq_ref, id_ref, cos_ref, sin_ref, *rest, model):
    out_ref, sum_ref = rest[-2:]
    rows, width = near_ref.shape[0], far_ref.shape[1]
    tail = far_ref[rows:, :].astype(F32)
    total = sum(rows_of(tail, 2, rows), sq_ref[...])
    factor = to_column(lax.rsqrt(total / model + epsilon))
    sum_ref[...] = total
    keys, values = slice(0, HEAD_SIZE), slice(HEAD_SIZE, 2 * HEAD_SIZE)
    part = (near_ref[:, keys] + far_ref[:rows, keys].astype(F32)) * factor
    part = rotate(part, cos_ref[...], sin_ref[...]).astype(BF16)
    out_ref[: rows // 2, keys] = part[: rows // 2]
    out_ref[: rows // 2, values] = part[rows // 2 :]
    part = (near_ref[:, values] + far_ref[:rows, values].astype(F32)) * factor
    part = part.T.astype(BF16)
    for i, at in enumerate(range(0, rows, width)):
        row = rows // 2 + i * HEAD_SIZE
        out_ref[row : row + HEAD_SIZE, :] = part[:, at : at + width]
    out_ref[rows:, :] = lines_of((id_ref[...].astype(F32),), width)


def keys_values(near, far, sq, ids, cosine, sine, after, model):
    rows, width = near.shape[0], far.shape[1]
    whole = lambda i: (0, 0)
    return pl.pallas_call(
        partial(keys_kernel, model=model),
        out_shape=(shape(far.shape, BF16), shape(sq.shape, F32)),
        grid=(1,),
        in_specs=[pl.BlockSpec((rows, width), whole)]
        + [pl.BlockSpec(a.shape, whole) for a in (far, sq, ids, cosine, sine)]
        + [ANY for _ in after],
        out_specs=[pl.BlockSpec(far.shape, whole), pl.BlockSpec(sq.shape, whole)],
        compiler_params=PARAMS,
        name="keys",
    )(near, far, sq, ids, cosine, sine, *after)


def queries_kernel(near_ref, far_ref, sum_ref, cos_ref, sin_ref, out_ref, *, model):
    scale = query_scale * math.log2(math.e)
    factor = to_column(lax.rsqrt(sum_ref[...] / model + epsilon) * scale)
    for c in range(0, out_ref.shape[1], HEAD_SIZE):
        at = slice(c, c + HEAD_SIZE)
        part = (near_ref[:, at] + far_ref[:, at].astype(F32)) * factor
        out_ref[:, at] = rotate(part, cos_ref[...], sin_ref[...]).astype(BF16)


def finished_queries(near, far, sums, cosine, sine, model):
    rows, width = far.shape
    last = near.shape[1] // width - 1
    whole = lambda i: (0, 0)
    return pl.pallas_call(
        partial(queries_kernel, model=model),
        out_shape=shape((rows, width), BF16),
        grid=(1,),
        in_specs=[pl.BlockSpec((rows, width), lambda i: (0, last))]
        + [pl.BlockSpec(a.shape, whole) for a in (far, sums, cosine, sine)],
        out_specs=pl.BlockSpec((rows, width), whole),
        compiler_params=PARAMS,
        cost_estimate=pl.CostEstimate(flops=HIDE, bytes_accessed=10**8, transcendentals=0),
        name="queries",
    )(near, far, sums, cosine, sine)


def attention_kernel(seq_ref, q_ref, id_ref, after_ref, *rest, back, offset):
    kv_refs, (out_ref, k_scr, vt_scr, count_scr) = rest[:-4], rest[-4:]
    part_rows, message = kv_refs[0].shape[0] - TAIL, kv_refs[0].shape[1]
    group = q_ref.shape[1] // HEAD_SIZE
    tile = pl.program_id(0)

    @pl.when(tile == 0)
    def _():
        counts = [jnp.zeros((1, 1), F32) for _ in range(DOCUMENTS)]
        for b, kv_ref in enumerate(kv_refs):
            row, half = b * part_rows, part_rows // 2
            k_scr[row : row + half, :] = kv_ref[:half, :HEAD_SIZE]
            k_scr[row + half : row + part_rows, :] = kv_ref[:half, HEAD_SIZE:]
            for i, at in enumerate(range(0, part_rows, message)):
                first = half + i * HEAD_SIZE
                vt_scr[:, row + at : row + at + message] = kv_ref[first : first + HEAD_SIZE, :]
            (ids,) = rows_of(kv_ref[part_rows:, :].astype(F32), 1, part_rows)
            exists = b >= back - seq_ref[0]
            ids = jnp.where(exists, ids, -1.0)
            for d in range(DOCUMENTS):
                below = (ids < d).astype(F32)
                counts[d] = counts[d] + jnp.sum(below, axis=1, keepdims=True)
        for d in range(DOCUMENTS):
            count_scr[d : d + 1, :] = jnp.broadcast_to(counts[d], (1, LANES))

    heads = [q_ref[:, c : c + HEAD_SIZE] for c in range(0, group * HEAD_SIZE, HEAD_SIZE)]
    q2 = jnp.concatenate(heads, axis=0)
    width = group * Q_TILE

    start = jnp.zeros((1, Q_TILE), F32)
    for d in range(DOCUMENTS):
        start = jnp.where(id_ref[...] == d, count_scr[d : d + 1, :], start)
    start = start.astype(jnp.int32)
    low = jnp.min(start) // K_TILE
    start = jnp.concatenate([start] * group, axis=1)
    first = back * part_rows + offset + tile * Q_TILE
    place = first + lax.broadcasted_iota(jnp.int32, (1, Q_TILE), 1)
    place = jnp.concatenate([place] * group, axis=1)

    def score(j):
        base = pl.multiple_of(j * K_TILE, K_TILE)
        return lax.dot_general(
            k_scr[pl.ds(base, K_TILE), :],
            q2,
            (((1,), (1,)), ((), ())),
            preferred_element_type=F32,
        )

    stop = (first + Q_TILE + K_TILE - 1) // K_TILE

    def step(j, state):
        scores, run_max, run_sum, acc = state
        following = score(jnp.minimum(j + 1, stop - 1))
        base = pl.multiple_of(j * K_TILE, K_TILE)
        key_pos = base + lax.broadcasted_iota(jnp.int32, (K_TILE, width), 0)
        allowed = (key_pos >= start) & (key_pos <= place)
        scores = jnp.where(allowed, scores, NEG)
        new_max = jnp.maximum(run_max, jnp.max(scores, axis=0, keepdims=True))
        expo = jnp.exp2(scores - new_max)
        factor = jnp.exp2(run_max - new_max)
        run_sum = run_sum * factor + jnp.sum(expo, axis=0, keepdims=True)
        acc = acc * factor + jnp.dot(
            vt_scr[:, pl.ds(base, K_TILE)], expo.astype(BF16), preferred_element_type=F32
        )
        return following, new_max, run_sum, acc

    state = (
        score(low),
        jnp.full((1, width), NEG, F32),
        jnp.zeros((1, width), F32),
        jnp.zeros((HEAD_SIZE, width), F32),
    )
    _, _, run_sum, acc = lax.fori_loop(low, stop, step, state)
    context = (acc / run_sum).T
    for g in range(group):
        out_ref[:, g * HEAD_SIZE : (g + 1) * HEAD_SIZE] = context[
            g * Q_TILE : (g + 1) * Q_TILE
        ].astype(BF16)


def attend(seq, queries, ids, after, blocks, c):
    rows, width = queries.shape[0] // CHUNKS, queries.shape[1]
    back = len(blocks) - 1
    tiles = rows // Q_TILE
    keys = len(blocks) * queries.shape[0]
    return pl.pallas_call(
        partial(attention_kernel, back=back, offset=c * rows),
        out_shape=shape((rows, width), BF16),
        grid_spec=pltpu.PrefetchScalarGridSpec(
            num_scalar_prefetch=1,
            grid=(tiles,),
            in_specs=[
                pl.BlockSpec((Q_TILE, width), lambda i, s: (c * tiles + i, 0)),
                pl.BlockSpec((1, Q_TILE), lambda i, s: (0, c * tiles + i)),
                ANY,
            ]
            + [pl.BlockSpec(b.shape, lambda i, s: (0, 0)) for b in blocks],
            out_specs=pl.BlockSpec((Q_TILE, width), lambda i, s: (i, 0)),
            scratch_shapes=[
                pltpu.VMEM((keys, HEAD_SIZE), BF16),
                pltpu.VMEM((HEAD_SIZE, keys), BF16),
                pltpu.VMEM((DOCUMENTS, LANES), F32),
            ],
        ),
        compiler_params=PARAMS,
        cost_estimate=pl.CostEstimate(
            flops=4 * rows * width * keys,
            bytes_accessed=4 * keys * width,
            transcendentals=rows * keys * width // HEAD_SIZE,
        ),
        name="attend",
    )(seq, queries, ids, after, *blocks)


def first_output_kernel(at_ref, own_o_ref, o_ref, *rest):
    ctx_refs, out_ref = rest[:-2], rest[-1]
    total = jnp.dot(ctx_refs[0][...], own_o_ref[...], preferred_element_type=F32)
    for i, ctx_ref in enumerate(ctx_refs[1:]):
        total = total + jnp.dot(ctx_ref[...], o_ref[at_ref[1 + i]], preferred_element_type=F32)
    out_ref[...] = total


def last_output_kernel(at_ref, part_ref, o_ref, *rest):
    ctx_refs, (before_ref, out_ref, sq_ref, acc) = rest[:-4], rest[-4:]
    step = pl.program_id(0)
    total = part_ref[...]
    for i, ctx_ref in enumerate(ctx_refs):
        total = total + jnp.dot(ctx_ref[...], o_ref[at_ref[i]], preferred_element_type=F32)
    out_ref[...] = total
    squares = jnp.sum(total * total, axis=1, keepdims=True)
    squares = jnp.broadcast_to(squares, acc.shape)

    @pl.when(step == 0)
    def _():
        acc[...] = squares

    @pl.when(step > 0)
    def _():
        acc[...] += squares

    @pl.when(step == pl.num_programs(0) - 1)
    def _():
        done = sq_ref.shape[1] - acc.shape[0]
        if done:
            sq_ref[:, :done] = before_ref[...]
        sq_ref[:, done:] = acc[...].T[0:1, :]


def column_tiles(cols):
    tiles = 3 if cols % (3 * LANES) == 0 else 1
    return tiles, cols // tiles


def first_output(column, order, o_weight, gathered, contexts, after):
    chunk, width = contexts[0].shape
    others, _, cols = gathered.shape
    tiles, tile = column_tiles(cols)
    if cols % LANES:
        o_weight = lax.dynamic_slice_in_dim(o_weight, column * cols, cols, axis=1)
        column = jnp.int32(0)
    return pl.pallas_call(
        first_output_kernel,
        out_shape=shape((chunk, cols), F32),
        grid_spec=pltpu.PrefetchScalarGridSpec(
            num_scalar_prefetch=1,
            grid=(tiles,),
            in_specs=[
                pl.BlockSpec((width, tile), lambda i, at: (0, at[0] * tiles + i)),
                pl.BlockSpec((others, width, tile), lambda i, at: (0, 0, i)),
            ]
            + [pl.BlockSpec((chunk, width), lambda i, at: (0, 0)) for _ in contexts]
            + [ANY],
            out_specs=pl.BlockSpec((chunk, tile), lambda i, at: (0, i)),
        ),
        compiler_params=PARAMS,
        cost_estimate=pl.CostEstimate(flops=HIDE, bytes_accessed=10**8, transcendentals=0),
        name="first_output",
    )(jnp.stack([column] + order), o_weight, gathered, *contexts, after)


def last_output(order, part, gathered, contexts, before, c):
    chunk, width = contexts[0].shape
    others, _, cols = gathered.shape
    tiles, tile = column_tiles(cols)
    return pl.pallas_call(
        last_output_kernel,
        out_shape=(shape((chunk, cols), F32), shape((1, (c + 1) * chunk), F32)),
        grid_spec=pltpu.PrefetchScalarGridSpec(
            num_scalar_prefetch=1,
            grid=(tiles,),
            in_specs=[
                pl.BlockSpec((chunk, tile), lambda i, at: (0, i)),
                pl.BlockSpec((others, width, tile), lambda i, at: (0, 0, i)),
            ]
            + [pl.BlockSpec((chunk, width), lambda i, at: (0, 0)) for _ in contexts]
            + [pl.BlockSpec(before.shape, lambda i, at: (0, 0))],
            out_specs=[
                pl.BlockSpec((chunk, tile), lambda i, at: (0, i)),
                pl.BlockSpec((1, (c + 1) * chunk), lambda i, at: (0, 0)),
            ],
            scratch_shapes=[pltpu.VMEM((chunk, LANES), F32)],
        ),
        compiler_params=PARAMS,
        name="last_output",
    )(jnp.stack(order), part, gathered, *contexts, before)


def final_kernel(token_ref, gain_ref, *rest, model):
    branch_refs, sq_refs, out_ref = rest[:CHUNKS], rest[CHUNKS:-1], rest[-1]
    total = sq_refs[0][...]
    for sq_ref in sq_refs[1:]:
        total = total + sq_ref[...]
    factor = to_column(lax.rsqrt(total / model + epsilon))[:, 0:1]
    for c in range(CHUNKS):

        @pl.when(pl.program_id(0) * CHUNKS // pl.num_programs(0) == c)
        def _():
            out = token_ref[...].astype(F32) + branch_refs[c][...] * factor * gain_ref[...]
            out_ref[...] = out.astype(BF16)


def finish(tokens, branches, out_gain, sums, model):
    rows, cols = tokens.shape
    tiles = rows // CHUNKS // Q_TILE
    held = lambda c: lambda i: (jnp.clip(i - c * tiles, 0, tiles - 1), 0)
    return pl.pallas_call(
        partial(final_kernel, model=model),
        out_shape=shape(tokens.shape, BF16),
        grid=(CHUNKS * tiles,),
        in_specs=[
            pl.BlockSpec((Q_TILE, cols), lambda i: (i, 0)),
            pl.BlockSpec((1, cols), lambda i: (0, 0)),
        ]
        + [pl.BlockSpec((Q_TILE, cols), held(c)) for c in range(CHUNKS)]
        + [pl.BlockSpec((1, Q_TILE), lambda i: (0, i)) for _ in sums],
        out_specs=pl.BlockSpec((Q_TILE, cols), lambda i: (i, 0)),
        compiler_params=PARAMS,
        name="finish",
    )(tokens, out_gain, *branches, *sums)


def per_device(
    tokens, seg_ids, in_gain, q_weight, k_weight, value_weight, o_weight, out_gain, *, sizes
):
    rows, cols = tokens.shape
    model = in_gain.shape[0]
    nz, nseq = sizes["tensor"], sizes["seq"]
    plane = nseq * sizes["groups"]
    z = lax.axis_index("tensor")
    seq = lax.axis_index("seq")
    in_plane = lax.axis_index(PLANE)
    half = nz // 2
    side, within = z // half, z % half
    half_rows = half * cols

    ring = [(i, i // half * half + (i + 1) % half) for i in range(nz)]
    swap = [(i, (i + half) % nz) for i in range(nz)]
    turn = lambda k: [(i, (i + k) % nz) for i in range(nz)]
    seq_bits = [1 << b for b in range(1, nseq.bit_length() - 1)]
    group_bits = [nseq << b for b in range(sizes["groups"].bit_length() - 1)]

    share = half_rows // plane
    at = jnp.reshape((1 - side) * plane + in_plane, (1,))
    inner = seq_bits + group_bits
    masks_kv, masks_q = inner + [1], inner[::-1] + [1]
    last = len(masks_kv) - 1
    eighth = rows // 48 * 8
    counts = [eighth, rows // 2 - 2 * TAIL, rows // 2 + 2 * TAIL - eighth]
    packed_kv, packed_q, cut = pack(
        at, q_weight, k_weight, value_weight, share, tokens, counts[0]
    )
    own_kv = lax.ppermute(packed_kv, "tensor", swap)[None]
    own_q = lax.ppermute(packed_q, "tensor", swap)[None]
    received = [lax.ppermute(cut, "tensor", ring)]
    o_share = o_weight.shape[0] // plane
    columns = [(z + k) % nz * cols for k in range(1, nz)]
    pieces = cut_pieces(in_plane * o_share, columns, o_weight, o_share, cols, own_kv)
    moved = [lax.ppermute(p, "tensor", turn(k + 1)) for k, p in enumerate(pieces)]

    order_kv, order_q, first = [0], [0], counts[0]
    for step, (mask_kv, mask_q) in enumerate(zip(masks_kv, masks_q)):
        after, count = [], 0
        if step == 0:
            pairs, after = [], [own_kv, received[0]]
        else:
            pairs = [(own_kv, far_kv), (own_q, far_q)]
        if step < 2:
            count = counts[1 + step]
        if step == last:
            after = [received[1]] + moved
        outs = stage(pairs, tokens, first, count, after, HIDE if step == last else 0)
        if pairs:
            own_kv, own_q = outs[:2]
        if count:
            received.append(lax.ppermute(outs[-1], "tensor", ring))
        first += count
        far_kv = lax.ppermute(own_kv, PLANE, [(i, i ^ mask_kv) for i in range(plane)])
        far_q = lax.ppermute(own_q, PLANE, [(i, i ^ mask_q) for i in range(plane)])
        order_kv = order_kv + [k ^ mask_kv for k in order_kv]
        order_q = order_q + [k ^ mask_q for k in order_q]
    far_kv, far_q = (order_kv, own_kv, far_kv), (order_q, own_q, far_q)

    own_o = jnp.stack(moved)[None]

    def double(own, step, after):
        if step > 0:
            (own,) = stage([own], tokens, 0, 0, after)
        return own, lax.ppermute(own, PLANE, [(i, i ^ masks_kv[step]) for i in range(plane)])

    sources = (within + half - jnp.arange(half, dtype=jnp.int32)) % half
    gains = in_gain.reshape(nz, 1, cols)
    place = jnp.stack([in_plane, side * half])
    own_x, own_sq, part = far_own_product(place, sources, gains, tokens, far_kv)
    received[-1] = gate(received[-1], own_sq)
    blocks = [received]
    for _ in range(half - 2):
        blocks.append([lax.ppermute(block, "tensor", ring) for block in blocks[-1]])
    sent_kv, x, sq = far_kv_product(
        place, sources, gains, part, own_sq, blocks, far_kv, [far_q[2]]
    )
    got_kv = lax.ppermute(sent_kv, "tensor", swap)
    pair_o = double(own_o, 0, [])
    for step in range(1, last - 1):
        pair_o = double(pair_o, step, [])
    weights = (k_weight, value_weight, q_weight)

    near = near_product(side * half + sources, own_x, x, weights, [sent_kv])

    sent_q = far_product(place, sources, own_x, x, far_q, [near])
    got_q = lax.ppermute(gate(sent_q, got_kv), "tensor", swap)
    pair_o = double(pair_o, last - 1, [sent_q])
    cosine, sine = rotation_table(seq * rows + jnp.arange(rows, dtype=jnp.int32))
    ids = seg_ids[None, :]
    own_kv, sums = keys_values(
        near, got_kv, sq, ids, cosine, sine, [sent_q, pair_o[0]], model
    )
    pair_o = double(pair_o, last, [own_kv])
    gathered_o = lay_pieces(place, order_kv, *pair_o)

    back = -(-(nseq * rows // 2 - 1) // rows)
    kv_blocks = [own_kv]
    for k in range(1, back + 1):
        earlier = [(i, i + k) for i in range(nseq - k)]
        kv_blocks.insert(0, lax.ppermute(own_kv, "seq", earlier))

    queries = finished_queries(near, got_q, sums, cosine, sine, model)
    seq_at = jnp.reshape(seq, (1,))
    contexts, after = [], own_kv
    for c in range(CHUNKS):
        contexts.append(attend(seq_at, queries, ids, after, kv_blocks, c))
        after = gathered_o
    early, late = [], []
    for c, context in enumerate(contexts):
        if nz == 4:
            pairs = [(i, i ^ 1) for i in range(nz)]
            opposite = lax.ppermute(context, "tensor", swap)
            beside = lax.ppermute(context, "tensor", pairs)
            if c + 1 < CHUNKS:
                opposite = gate(opposite, contexts[c + 1])
            across = lax.ppermute(opposite, "tensor", pairs)
            early.append([context, beside])
            late.append([opposite, across])
            order = [2 - 2 * (z % 2), jnp.int32(1), 2 * (z % 2)]
        else:
            early.append([context])
            late.append([lax.ppermute(context, "tensor", turn(k)) for k in range(1, nz)])
            order = [jnp.int32(k) for k in range(nz - 1)]
    split = len(early[0]) - 1
    branches, own_sq = [], sums
    for c in range(CHUNKS):
        part = first_output(z, order[:split], o_weight, gathered_o, early[c], contexts[-1])
        branch, own_sq = last_output(order[split:], part, gathered_o, late[c], own_sq, c)
        branches.append(branch)
    squares = [own_sq]
    squares += [lax.ppermute(own_sq, "tensor", turn(k)) for k in range(1, nz)]
    return finish(tokens, branches, out_gain[None, :], squares, model)


def solution(mesh):
    return jax.shard_map(
        partial(per_device, sizes=dict(mesh.shape)),
        mesh=mesh,
        in_specs=(
            P(("groups", "seq"), "tensor"),
            P(("groups", "seq")),
            P(),
            P(None, "tensor"),
            P(None, "tensor"),
            P(None, "tensor"),
            P("tensor", None),
            P("tensor"),
        ),
        out_specs=P(("groups", "seq"), "tensor"),
        check_vma=False,
    )
```

```python
import math
from functools import partial

import jax
import jax.numpy as jnp
from jax import lax
from jax.experimental import pallas as pl
from jax.experimental.pallas import tpu as pltpu
from jax.sharding import PartitionSpec as P

HEAD_SIZE = 128
PLANE = ("groups", "seq")

epsilon = 1e-06
query_scale = 144.0 ** (-0.5)
rope_base = 10000.0
NEG = -1e30
Q_TILE = 128
K_TILE = 384
CHUNKS = 2
LANES = 128
TAIL = 16
F32, BF16 = jnp.float32, jnp.bfloat16
ANY = pl.BlockSpec(memory_space=pl.ANY)
HBM = pl.BlockSpec(memory_space=pltpu.HBM)
VMEM = pl.BlockSpec(memory_space=pltpu.VMEM)
DOCUMENTS = 8
HIDE = 5 * 10**10
PARAMS = pltpu.CompilerParams(vmem_limit_bytes=48 * 1024 * 1024)
ALL_VMEM = pltpu.CompilerParams(vmem_limit_bytes=62 * 1024 * 1024)


def shape(dims, dtype):
    return jax.ShapeDtypeStruct(dims, dtype)


def to_row(column):
    return jnp.broadcast_to(column, (column.shape[0], LANES)).T[0:1, :]


def to_column(row):
    return jnp.broadcast_to(row, (LANES, row.shape[1])).T


def rotation_table(token_places):
    half_dim = HEAD_SIZE // 2
    inverse = rope_base ** (-jnp.arange(half_dim, dtype=F32) / half_dim)
    angles = token_places.astype(F32)[:, None] * inverse[None, :]
    cosine, sine = jnp.cos(angles), jnp.sin(angles)
    return jnp.concatenate([cosine, cosine], 1), jnp.concatenate([-sine, sine], 1)


def rotate(vectors, cosine, sine):
    return vectors * cosine + pltpu.roll(vectors, HEAD_SIZE // 2, 1) * sine


def pack_kernel(at_ref, q_ref, k_ref, v_ref, x_ref, kv_out, q_out, x_out, sems):
    share, width = q_out.shape[0], k_ref.shape[1]
    rows = pl.ds(pl.multiple_of(at_ref[0] * share, TAIL), share)
    copies = [
        pltpu.make_async_copy(k_ref.at[rows], kv_out.at[:, pl.ds(0, width)], sems.at[0]),
        pltpu.make_async_copy(v_ref.at[rows], kv_out.at[:, pl.ds(width, width)], sems.at[1]),
        pltpu.make_async_copy(q_ref.at[rows], q_out, sems.at[2]),
        pltpu.make_async_copy(x_ref.at[pl.ds(0, x_out.shape[0])], x_out, sems.at[3]),
    ]
    for copy in copies:
        copy.start()
    for copy in copies:
        copy.wait()


def pack(at, q_weight, k_weight, v_weight, share, tokens, rows):
    kv_width = k_weight.shape[1] + v_weight.shape[1]
    dims = [(share, kv_width), (share, q_weight.shape[1]), (rows, tokens.shape[1])]
    return pl.pallas_call(
        pack_kernel,
        out_shape=tuple(shape(d, BF16) for d in dims),
        grid_spec=pltpu.PrefetchScalarGridSpec(
            num_scalar_prefetch=1,
            grid=(1,),
            in_specs=[HBM, HBM, HBM, HBM],
            out_specs=[pl.BlockSpec(d, lambda i, at: (0, 0)) for d in dims],
            scratch_shapes=[pltpu.SemaphoreType.DMA((4,))],
        ),
        compiler_params=ALL_VMEM,
        name="pack",
    )(at, q_weight, k_weight, v_weight, tokens)


def gate_kernel(x_ref, after_ref, out_ref):
    pass


def gate(x, after):
    return pl.pallas_call(
        gate_kernel,
        out_shape=shape(x.shape, x.dtype),
        in_specs=[ANY, ANY],
        out_specs=ANY,
        input_output_aliases={0: 0},
        compiler_params=PARAMS,
        name="gate",
    )(x, after)


def stage_kernel(*refs, pairs, first, count):
    outputs = pairs + (1 if count else 0)
    ins, outs, sems = refs[: -outputs - 1], refs[-outputs - 1 : -1], refs[-1]
    copies = []
    for p in range(pairs):
        held = ins[2 * p].shape[0]
        for side in range(2):
            there = outs[p].at[pl.ds(side * held, held)]
            copies.append(
                pltpu.make_async_copy(ins[2 * p + side], there, sems.at[len(copies)])
            )
    if count:
        rows = ins[2 * pairs].at[pl.ds(first, count)]
        copies.append(pltpu.make_async_copy(rows, outs[-1], sems.at[len(copies)]))
    for copy in copies:
        copy.start()
    for copy in copies:
        copy.wait()


def stage(joined, tokens, first, count, after, flops=0):
    dims = [(2 * pair[0].shape[0],) + pair[0].shape[1:] for pair in joined]
    if count:
        dims.append((count, tokens.shape[1]))
    return pl.pallas_call(
        partial(stage_kernel, pairs=len(joined), first=first, count=count),
        out_shape=tuple(shape(d, BF16) for d in dims),
        in_specs=[ANY] * (2 * len(joined) + 1 + len(after)),
        scratch_shapes=[pltpu.SemaphoreType.DMA((2 * len(joined) + 1,))],
        compiler_params=PARAMS,
        cost_estimate=pl.CostEstimate(flops=flops, bytes_accessed=flops // 500, transcendentals=0),
        name="stage",
    )(*[piece for pair in joined for piece in pair], tokens, *after)


def cut_kernel(at_ref, o_ref, after_ref, *rest):
    outs, sems = rest[:-1], rest[-1]
    copies = []
    for i, out in enumerate(outs):
        rows = pl.ds(pl.multiple_of(at_ref[0], TAIL), out.shape[0])
        columns = pl.ds(pl.multiple_of(at_ref[1 + i], LANES), out.shape[1])
        copies.append(pltpu.make_async_copy(o_ref.at[rows, columns], out, sems.at[i]))
    for copy in copies:
        copy.start()
    for copy in copies:
        copy.wait()


def cut_pieces(row, columns, o_weight, share, cols, after):
    if cols % LANES:
        return [lax.dynamic_slice(o_weight, (row, c), (share, cols)) for c in columns]
    return pl.pallas_call(
        cut_kernel,
        out_shape=tuple(shape((share, cols), BF16) for _ in columns),
        grid_spec=pltpu.PrefetchScalarGridSpec(
            num_scalar_prefetch=1,
            grid=(1,),
            in_specs=[ANY, ANY],
            out_specs=[VMEM for _ in columns],
            scratch_shapes=[pltpu.SemaphoreType.DMA((len(columns),))],
        ),
        compiler_params=PARAMS,
        name="cut",
    )(jnp.stack([row] + columns), o_weight, after)


def lay_kernel(place_ref, own_ref, got_ref, out_ref, sems, *, order):
    held, others, share, _ = own_ref.shape
    copies = []
    for i, mask in enumerate(order):
        piece = own_ref.at[i] if i < held else got_ref.at[i - held]
        row = pl.multiple_of((place_ref[0] ^ mask) * share, TAIL)
        there = out_ref.at[:, pl.ds(row, share)]
        copies.append(pltpu.make_async_copy(piece, there, sems.at[i]))
    for copy in copies:
        copy.start()
    for copy in copies:
        copy.wait()


def lay_pieces(place, order, own, got):
    _, others, share, cols = own.shape
    dims = (others, len(order) * share, cols)
    return pl.pallas_call(
        partial(lay_kernel, order=order),
        out_shape=shape(dims, BF16),
        grid_spec=pltpu.PrefetchScalarGridSpec(
            num_scalar_prefetch=1,
            grid=(1,),
            in_specs=[ANY, ANY],
            out_specs=pl.BlockSpec(dims, lambda i, p: (0, 0, 0)),
            scratch_shapes=[pltpu.SemaphoreType.DMA((len(order),))],
        ),
        compiler_params=PARAMS,
        name="lay",
    )(place, own, got)


def place_weights(place_ref, own_ref, got_ref, weight, sems, order):
    held, share, _ = own_ref.shape
    copies = []
    for i, mask in enumerate(order):
        piece = own_ref.at[i] if i < held else got_ref.at[i - held]
        row = pl.multiple_of((place_ref[0] ^ mask) * share, TAIL)
        there = weight.at[pl.ds(row, share)]
        copies.append(pltpu.make_async_copy(piece, there, sems.at[i]))
    for copy in copies:
        copy.start()
    return copies


def far_sum(src_ref, first, x_ref, weight):
    count, _, cols = x_ref.shape
    total = None
    for k in range(count):
        row = pl.multiple_of(src_ref[first + k] * cols, TAIL)
        term = jnp.dot(x_ref[k], weight[pl.ds(row, cols), :], preferred_element_type=F32)
        total = term if total is None else total + term
    return total


def prepare(x_refs, gain, x_out, k):
    column, row = [], 0
    for x_ref in x_refs:
        x = x_ref[...].astype(F32)
        column.append(jnp.sum(x * x, axis=1, keepdims=True))
        x_out[k, row : row + x.shape[0]] = (x * gain).astype(BF16)
        row += x.shape[0]
    return jnp.concatenate(column, axis=0)


def far_own_kernel(
    place_ref, src_ref, gain_ref, own_ref, got_ref, x_ref, x_out, sq_ref, out_ref, weight, sems,
    *, order
):
    copies = place_weights(place_ref, own_ref, got_ref, weight, sems, order)
    gain = gain_ref[place_ref[1] + src_ref[0]]
    sq_ref[...] = to_row(prepare([x_ref], gain, x_out, 0))
    for copy in copies:
        copy.wait()
    out_ref[...] = far_sum(src_ref, 0, x_out, weight)


def far_kv_kernel(
    place_ref, src_ref, gain_ref, part_ref, own_sq_ref, own_ref, got_ref, *rest, order, cuts
):
    x_refs, (out_ref, x_out, sq_ref, weight, sems) = rest[: sum(cuts)], rest[-5:]
    copies = place_weights(place_ref, own_ref, got_ref, weight, sems, order)
    rows = x_out.shape[1]
    columns, at = [], 0
    for k, pieces in enumerate(cuts):
        gain = gain_ref[place_ref[1] + src_ref[1 + k]]
        columns.append(prepare(x_refs[at : at + pieces], gain, x_out, k))
        at += pieces
    sq = to_row(sum(columns[1:], columns[0])) + own_sq_ref[...]
    sq_ref[...] = sq
    for copy in copies:
        copy.wait()
    total = part_ref[...] + far_sum(src_ref, 1, x_out, weight)
    out_ref[:rows, :] = total.astype(BF16)
    high = sq.astype(BF16).astype(F32)
    out_ref[rows:, :] = lines_of((high, sq - high), out_ref.shape[1])


def far_kv_scratch(gathered):
    order, own, _ = gathered
    return [
        pltpu.VMEM((len(order) * own.shape[1], own.shape[2]), BF16),
        pltpu.SemaphoreType.DMA((len(order),)),
    ]


def far_own_product(place, sources, gains, tokens, gathered):
    order, own, got = gathered
    rows, cols = tokens.shape
    dims = [(1, rows, cols), (1, rows), (rows, own.shape[2])]
    whole = lambda d: pl.BlockSpec(d, lambda i, p, s: (0,) * len(d))
    return pl.pallas_call(
        partial(far_own_kernel, order=order),
        out_shape=tuple(shape(d, t) for d, t in zip(dims, (BF16, F32, F32))),
        grid_spec=pltpu.PrefetchScalarGridSpec(
            num_scalar_prefetch=2,
            grid=(1,),
            in_specs=[whole(gains.shape), ANY, ANY, whole(tokens.shape)],
            out_specs=[whole(d) for d in dims],
            scratch_shapes=far_kv_scratch(gathered),
        ),
        compiler_params=PARAMS,
        name="far_own",
    )(place, sources, gains, own, got, tokens)


def far_kv_product(place, sources, gains, part, own_sq, blocks, gathered, after):
    order, own, got = gathered
    rows, width = part.shape
    cols = blocks[0][0].shape[1]
    pieces = [piece for block in blocks for piece in block]
    dims = [(rows + TAIL, width), (len(blocks), rows, cols), (1, rows)]
    whole = lambda d: pl.BlockSpec(d, lambda i, p, s: (0,) * len(d))
    return pl.pallas_call(
        partial(far_kv_kernel, order=order, cuts=[len(block) for block in blocks]),
        out_shape=tuple(shape(d, t) for d, t in zip(dims, (BF16, BF16, F32))),
        grid_spec=pltpu.PrefetchScalarGridSpec(
            num_scalar_prefetch=2,
            grid=(1,),
            in_specs=[whole(gains.shape), whole(part.shape), whole(own_sq.shape), ANY, ANY]
            + [whole(piece.shape) for piece in pieces]
            + [ANY for _ in after],
            out_specs=[whole(d) for d in dims],
            scratch_shapes=far_kv_scratch(gathered),
        ),
        compiler_params=PARAMS,
        name="far_kv",
    )(place, sources, gains, part, own_sq, own, got, *pieces, *after)


def far_kernel(place_ref, src_ref, own_x_ref, x_ref, own_ref, got_ref, *rest, order):
    out_ref, weight, sems = rest[-3:]
    for copy in place_weights(place_ref, own_ref, got_ref, weight, sems, order):
        copy.wait()
    total = far_sum(src_ref, 0, own_x_ref, weight) + far_sum(src_ref, 1, x_ref, weight)
    out_ref[...] = total.astype(BF16)


def lines_of(rows, width):
    lines = []
    for row in rows:
        for at in range(0, row.shape[1], width):
            line = row[:, at : at + width]
            if line.shape[1] < width:
                rest = jnp.zeros((1, width - line.shape[1]), F32)
                line = jnp.concatenate([line, rest], axis=1)
            lines.append(line)
    lines.append(jnp.zeros((TAIL - len(lines), width), F32))
    return jnp.concatenate(lines, axis=0).astype(BF16)


def rows_of(tail, count, length):
    per_row = -(-length // tail.shape[1])
    rows = []
    for r in range(count):
        lines = [tail[r * per_row + i : r * per_row + i + 1, :] for i in range(per_row)]
        rows.append(jnp.concatenate(lines, axis=1)[:, :length])
    return rows


def far_product(place, sources, own_x, x, gathered, after):
    order, own, got = gathered
    rows, width = x.shape[1], own.shape[2]
    return pl.pallas_call(
        partial(far_kernel, order=order),
        out_shape=shape((rows, width), BF16),
        grid_spec=pltpu.PrefetchScalarGridSpec(
            num_scalar_prefetch=2,
            grid=(1,),
            in_specs=[
                pl.BlockSpec(own_x.shape, lambda i, p, s: (0, 0, 0)),
                pl.BlockSpec(x.shape, lambda i, p, s: (0, 0, 0)),
                ANY,
                ANY,
            ]
            + [ANY for _ in after],
            out_specs=pl.BlockSpec((rows, width), lambda i, p, s: (0, 0)),
            scratch_shapes=far_kv_scratch(gathered),
        ),
        compiler_params=PARAMS,
        name="far",
    )(place, sources, own_x, x, own, got, *after)


def near_kernel(src_ref, own_x_ref, x_ref, k_ref, v_ref, q_ref, *rest):
    out_ref = rest[-1]
    step = pl.program_id(0)
    dot = partial(jnp.dot, preferred_element_type=F32)
    column = 0
    for ref in (k_ref, v_ref, q_ref):
        at = slice(column, column + ref.shape[1])

        @pl.when(step == 0)
        def _():
            out_ref[:, at] = dot(own_x_ref[0], ref[...])

        @pl.when(step > 0)
        def _():
            out_ref[:, at] += dot(x_ref[0], ref[...])

        column += ref.shape[1]


def near_product(sources, own_x, x, weights, after):
    count, rows, cols = x.shape
    widths = [w.shape[1] for w in weights]
    return pl.pallas_call(
        near_kernel,
        out_shape=shape((rows, sum(widths)), F32),
        grid_spec=pltpu.PrefetchScalarGridSpec(
            num_scalar_prefetch=1,
            grid=(count + 1,),
            in_specs=[
                pl.BlockSpec((1, rows, cols), lambda i, s: (0, 0, 0)),
                pl.BlockSpec((1, rows, cols), lambda i, s: (jnp.maximum(i - 1, 0), 0, 0)),
            ]
            + [pl.BlockSpec((cols, w), lambda i, s: (s[i], 0)) for w in widths]
            + [ANY for _ in after],
            out_specs=pl.BlockSpec((rows, sum(widths)), lambda i, s: (0, 0)),
        ),
        compiler_params=PARAMS,
        name="near",
    )(sources, own_x, x, *weights, *after)


def keys_kernel(near_ref, far_ref, sq_ref, id_ref, cos_ref, sin_ref, *rest, model):
    out_ref, sum_ref = rest[-2:]
    rows, width = near_ref.shape[0], far_ref.shape[1]
    tail = far_ref[rows:, :].astype(F32)
    total = sum(rows_of(tail, 2, rows), sq_ref[...])
    factor = to_column(lax.rsqrt(total / model + epsilon))
    sum_ref[...] = total
    keys, values = slice(0, HEAD_SIZE), slice(HEAD_SIZE, 2 * HEAD_SIZE)
    part = (near_ref[:, keys] + far_ref[:rows, keys].astype(F32)) * factor
    part = rotate(part, cos_ref[...], sin_ref[...]).astype(BF16)
    out_ref[: rows // 2, keys] = part[: rows // 2]
    out_ref[: rows // 2, values] = part[rows // 2 :]
    part = (near_ref[:, values] + far_ref[:rows, values].astype(F32)) * factor
    part = part.T.astype(BF16)
    for i, at in enumerate(range(0, rows, width)):
        row = rows // 2 + i * HEAD_SIZE
        out_ref[row : row + HEAD_SIZE, :] = part[:, at : at + width]
    out_ref[rows:, :] = lines_of((id_ref[...].astype(F32),), width)


def keys_values(near, far, sq, ids, cosine, sine, after, model):
    rows, width = near.shape[0], far.shape[1]
    whole = lambda i: (0, 0)
    return pl.pallas_call(
        partial(keys_kernel, model=model),
        out_shape=(shape(far.shape, BF16), shape(sq.shape, F32)),
        grid=(1,),
        in_specs=[pl.BlockSpec((rows, width), whole)]
        + [pl.BlockSpec(a.shape, whole) for a in (far, sq, ids, cosine, sine)]
        + [ANY for _ in after],
        out_specs=[pl.BlockSpec(far.shape, whole), pl.BlockSpec(sq.shape, whole)],
        compiler_params=PARAMS,
        name="keys",
    )(near, far, sq, ids, cosine, sine, *after)


def queries_kernel(near_ref, far_ref, sum_ref, cos_ref, sin_ref, out_ref, *, model):
    scale = query_scale * math.log2(math.e)
    factor = to_column(lax.rsqrt(sum_ref[...] / model + epsilon) * scale)
    for c in range(0, out_ref.shape[1], HEAD_SIZE):
        at = slice(c, c + HEAD_SIZE)
        part = (near_ref[:, at] + far_ref[:, at].astype(F32)) * factor
        out_ref[:, at] = rotate(part, cos_ref[...], sin_ref[...]).astype(BF16)


def finished_queries(near, far, sums, cosine, sine, model):
    rows, width = far.shape
    last = near.shape[1] // width - 1
    whole = lambda i: (0, 0)
    return pl.pallas_call(
        partial(queries_kernel, model=model),
        out_shape=shape((rows, width), BF16),
        grid=(1,),
        in_specs=[pl.BlockSpec((rows, width), lambda i: (0, last))]
        + [pl.BlockSpec(a.shape, whole) for a in (far, sums, cosine, sine)],
        out_specs=pl.BlockSpec((rows, width), whole),
        compiler_params=PARAMS,
        cost_estimate=pl.CostEstimate(flops=HIDE, bytes_accessed=10**8, transcendentals=0),
        name="queries",
    )(near, far, sums, cosine, sine)


def attention_kernel(seq_ref, q_ref, id_ref, after_ref, *rest, back, offset):
    kv_refs, (out_ref, k_scr, vt_scr, count_scr) = rest[:-4], rest[-4:]
    part_rows, message = kv_refs[0].shape[0] - TAIL, kv_refs[0].shape[1]
    group = q_ref.shape[1] // HEAD_SIZE
    tile = pl.program_id(0)

    @pl.when(tile == 0)
    def _():
        counts = [jnp.zeros((1, 1), F32) for _ in range(DOCUMENTS)]
        for b, kv_ref in enumerate(kv_refs):
            row, half = b * part_rows, part_rows // 2
            k_scr[row : row + half, :] = kv_ref[:half, :HEAD_SIZE]
            k_scr[row + half : row + part_rows, :] = kv_ref[:half, HEAD_SIZE:]
            for i, at in enumerate(range(0, part_rows, message)):
                first = half + i * HEAD_SIZE
                vt_scr[:, row + at : row + at + message] = kv_ref[first : first + HEAD_SIZE, :]
            (ids,) = rows_of(kv_ref[part_rows:, :].astype(F32), 1, part_rows)
            exists = b >= back - seq_ref[0]
            ids = jnp.where(exists, ids, -1.0)
            for d in range(DOCUMENTS):
                below = (ids < d).astype(F32)
                counts[d] = counts[d] + jnp.sum(below, axis=1, keepdims=True)
        for d in range(DOCUMENTS):
            count_scr[d : d + 1, :] = jnp.broadcast_to(counts[d], (1, LANES))

    heads = [q_ref[:, c : c + HEAD_SIZE] for c in range(0, group * HEAD_SIZE, HEAD_SIZE)]
    q2 = jnp.concatenate(heads, axis=0)
    width = group * Q_TILE

    start = jnp.zeros((1, Q_TILE), F32)
    for d in range(DOCUMENTS):
        start = jnp.where(id_ref[...] == d, count_scr[d : d + 1, :], start)
    start = start.astype(jnp.int32)
    low = jnp.min(start) // K_TILE
    start = jnp.concatenate([start] * group, axis=1)
    first = back * part_rows + offset + tile * Q_TILE
    place = first + lax.broadcasted_iota(jnp.int32, (1, Q_TILE), 1)
    place = jnp.concatenate([place] * group, axis=1)

    def score(j):
        base = pl.multiple_of(j * K_TILE, K_TILE)
        return lax.dot_general(
            k_scr[pl.ds(base, K_TILE), :],
            q2,
            (((1,), (1,)), ((), ())),
            preferred_element_type=F32,
        )

    stop = (first + Q_TILE + K_TILE - 1) // K_TILE

    def step(j, state):
        scores, run_max, run_sum, acc = state
        following = score(jnp.minimum(j + 1, stop - 1))
        base = pl.multiple_of(j * K_TILE, K_TILE)
        key_pos = base + lax.broadcasted_iota(jnp.int32, (K_TILE, width), 0)
        allowed = (key_pos >= start) & (key_pos <= place)
        scores = jnp.where(allowed, scores, NEG)
        new_max = jnp.maximum(run_max, jnp.max(scores, axis=0, keepdims=True))
        expo = jnp.exp2(scores - new_max)
        factor = jnp.exp2(run_max - new_max)
        run_sum = run_sum * factor + jnp.sum(expo, axis=0, keepdims=True)
        acc = acc * factor + jnp.dot(
            vt_scr[:, pl.ds(base, K_TILE)], expo.astype(BF16), preferred_element_type=F32
        )
        return following, new_max, run_sum, acc

    state = (
        score(low),
        jnp.full((1, width), NEG, F32),
        jnp.zeros((1, width), F32),
        jnp.zeros((HEAD_SIZE, width), F32),
    )
    _, _, run_sum, acc = lax.fori_loop(low, stop, step, state)
    context = (acc / run_sum).T
    for g in range(group):
        out_ref[:, g * HEAD_SIZE : (g + 1) * HEAD_SIZE] = context[
            g * Q_TILE : (g + 1) * Q_TILE
        ].astype(BF16)


def attend(seq, queries, ids, after, blocks, c):
    rows, width = queries.shape[0] // CHUNKS, queries.shape[1]
    back = len(blocks) - 1
    tiles = rows // Q_TILE
    keys = len(blocks) * queries.shape[0]
    return pl.pallas_call(
        partial(attention_kernel, back=back, offset=c * rows),
        out_shape=shape((rows, width), BF16),
        grid_spec=pltpu.PrefetchScalarGridSpec(
            num_scalar_prefetch=1,
            grid=(tiles,),
            in_specs=[
                pl.BlockSpec((Q_TILE, width), lambda i, s: (c * tiles + i, 0)),
                pl.BlockSpec((1, Q_TILE), lambda i, s: (0, c * tiles + i)),
                ANY,
            ]
            + [pl.BlockSpec(b.shape, lambda i, s: (0, 0)) for b in blocks],
            out_specs=pl.BlockSpec((Q_TILE, width), lambda i, s: (i, 0)),
            scratch_shapes=[
                pltpu.VMEM((keys, HEAD_SIZE), BF16),
                pltpu.VMEM((HEAD_SIZE, keys), BF16),
                pltpu.VMEM((DOCUMENTS, LANES), F32),
            ],
        ),
        compiler_params=PARAMS,
        cost_estimate=pl.CostEstimate(
            flops=4 * rows * width * keys,
            bytes_accessed=4 * keys * width,
            transcendentals=rows * keys * width // HEAD_SIZE,
        ),
        name="attend",
    )(seq, queries, ids, after, *blocks)


def first_output_kernel(at_ref, own_o_ref, o_ref, *rest):
    ctx_refs, out_ref = rest[:-2], rest[-1]
    total = jnp.dot(ctx_refs[0][...], own_o_ref[...], preferred_element_type=F32)
    for i, ctx_ref in enumerate(ctx_refs[1:]):
        total = total + jnp.dot(ctx_ref[...], o_ref[at_ref[1 + i]], preferred_element_type=F32)
    out_ref[...] = total


def last_output_kernel(at_ref, part_ref, o_ref, *rest):
    ctx_refs, (before_ref, out_ref, sq_ref, acc) = rest[:-4], rest[-4:]
    step = pl.program_id(0)
    total = part_ref[...]
    for i, ctx_ref in enumerate(ctx_refs):
        total = total + jnp.dot(ctx_ref[...], o_ref[at_ref[i]], preferred_element_type=F32)
    out_ref[...] = total
    squares = jnp.sum(total * total, axis=1, keepdims=True)
    squares = jnp.broadcast_to(squares, acc.shape)

    @pl.when(step == 0)
    def _():
        acc[...] = squares

    @pl.when(step > 0)
    def _():
        acc[...] += squares

    @pl.when(step == pl.num_programs(0) - 1)
    def _():
        done = sq_ref.shape[1] - acc.shape[0]
        if done:
            sq_ref[:, :done] = before_ref[...]
        sq_ref[:, done:] = acc[...].T[0:1, :]


def column_tiles(cols):
    tiles = 3 if cols % (3 * LANES) == 0 else 1
    return tiles, cols // tiles


def first_output(column, order, o_weight, gathered, contexts, after):
    chunk, width = contexts[0].shape
    others, _, cols = gathered.shape
    tiles, tile = column_tiles(cols)
    if cols % LANES:
        o_weight = lax.dynamic_slice_in_dim(o_weight, column * cols, cols, axis=1)
        column = jnp.int32(0)
    return pl.pallas_call(
        first_output_kernel,
        out_shape=shape((chunk, cols), F32),
        grid_spec=pltpu.PrefetchScalarGridSpec(
            num_scalar_prefetch=1,
            grid=(tiles,),
            in_specs=[
                pl.BlockSpec((width, tile), lambda i, at: (0, at[0] * tiles + i)),
                pl.BlockSpec((others, width, tile), lambda i, at: (0, 0, i)),
            ]
            + [pl.BlockSpec((chunk, width), lambda i, at: (0, 0)) for _ in contexts]
            + [ANY],
            out_specs=pl.BlockSpec((chunk, tile), lambda i, at: (0, i)),
        ),
        compiler_params=PARAMS,
        cost_estimate=pl.CostEstimate(flops=HIDE, bytes_accessed=10**8, transcendentals=0),
        name="first_output",
    )(jnp.stack([column] + order), o_weight, gathered, *contexts, after)


def last_output(order, part, gathered, contexts, before, c):
    chunk, width = contexts[0].shape
    others, _, cols = gathered.shape
    tiles, tile = column_tiles(cols)
    return pl.pallas_call(
        last_output_kernel,
        out_shape=(shape((chunk, cols), F32), shape((1, (c + 1) * chunk), F32)),
        grid_spec=pltpu.PrefetchScalarGridSpec(
            num_scalar_prefetch=1,
            grid=(tiles,),
            in_specs=[
                pl.BlockSpec((chunk, tile), lambda i, at: (0, i)),
                pl.BlockSpec((others, width, tile), lambda i, at: (0, 0, i)),
            ]
            + [pl.BlockSpec((chunk, width), lambda i, at: (0, 0)) for _ in contexts]
            + [pl.BlockSpec(before.shape, lambda i, at: (0, 0))],
            out_specs=[
                pl.BlockSpec((chunk, tile), lambda i, at: (0, i)),
                pl.BlockSpec((1, (c + 1) * chunk), lambda i, at: (0, 0)),
            ],
            scratch_shapes=[pltpu.VMEM((chunk, LANES), F32)],
        ),
        compiler_params=PARAMS,
        name="last_output",
    )(jnp.stack(order), part, gathered, *contexts, before)


def final_kernel(token_ref, gain_ref, *rest, model):
    branch_refs, sq_refs, out_ref = rest[:CHUNKS], rest[CHUNKS:-1], rest[-1]
    total = sq_refs[0][...]
    for sq_ref in sq_refs[1:]:
        total = total + sq_ref[...]
    factor = to_column(lax.rsqrt(total / model + epsilon))[:, 0:1]
    for c in range(CHUNKS):

        @pl.when(pl.program_id(0) * CHUNKS // pl.num_programs(0) == c)
        def _():
            out = token_ref[...].astype(F32) + branch_refs[c][...] * factor * gain_ref[...]
            out_ref[...] = out.astype(BF16)


def finish(tokens, branches, out_gain, sums, model):
    rows, cols = tokens.shape
    tiles = rows // CHUNKS // Q_TILE
    held = lambda c: lambda i: (jnp.clip(i - c * tiles, 0, tiles - 1), 0)
    return pl.pallas_call(
        partial(final_kernel, model=model),
        out_shape=shape(tokens.shape, BF16),
        grid=(CHUNKS * tiles,),
        in_specs=[
            pl.BlockSpec((Q_TILE, cols), lambda i: (i, 0)),
            pl.BlockSpec((1, cols), lambda i: (0, 0)),
        ]
        + [pl.BlockSpec((Q_TILE, cols), held(c)) for c in range(CHUNKS)]
        + [pl.BlockSpec((1, Q_TILE), lambda i: (0, i)) for _ in sums],
        out_specs=pl.BlockSpec((Q_TILE, cols), lambda i: (i, 0)),
        compiler_params=PARAMS,
        name="finish",
    )(tokens, out_gain, *branches, *sums)


def per_device(
    tokens, seg_ids, in_gain, q_weight, k_weight, value_weight, o_weight, out_gain, *, sizes
):
    rows, cols = tokens.shape
    model = in_gain.shape[0]
    nz, nseq = sizes["tensor"], sizes["seq"]
    plane = nseq * sizes["groups"]
    z = lax.axis_index("tensor")
    seq = lax.axis_index("seq")
    in_plane = lax.axis_index(PLANE)
    half = nz // 2
    side, within = z // half, z % half
    half_rows = half * cols

    ring = [(i, i // half * half + (i + 1) % half) for i in range(nz)]
    swap = [(i, (i + half) % nz) for i in range(nz)]
    turn = lambda k: [(i, (i + k) % nz) for i in range(nz)]
    seq_bits = [1 << b for b in range(1, nseq.bit_length() - 1)]
    group_bits = [nseq << b for b in range(sizes["groups"].bit_length() - 1)]

    share = half_rows // plane
    at = jnp.reshape((1 - side) * plane + in_plane, (1,))
    inner = seq_bits + group_bits
    masks_kv, masks_q = inner + [1], inner[::-1] + [1]
    last = len(masks_kv) - 1
    eighth = rows // 48 * 8
    counts = [eighth, rows // 2 - 2 * TAIL, rows // 2 + 2 * TAIL - eighth]
    packed_kv, packed_q, cut = pack(
        at, q_weight, k_weight, value_weight, share, tokens, counts[0]
    )
    own_kv = lax.ppermute(packed_kv, "tensor", swap)[None]
    own_q = lax.ppermute(packed_q, "tensor", swap)[None]
    received = [lax.ppermute(cut, "tensor", ring)]
    o_share = o_weight.shape[0] // plane
    columns = [(z + k) % nz * cols for k in range(1, nz)]
    pieces = cut_pieces(in_plane * o_share, columns, o_weight, o_share, cols, own_kv)
    moved = [lax.ppermute(p, "tensor", turn(k + 1)) for k, p in enumerate(pieces)]

    order_kv, order_q, first = [0], [0], counts[0]
    for step, (mask_kv, mask_q) in enumerate(zip(masks_kv, masks_q)):
        after, count = [], 0
        if step == 0:
            pairs, after = [], [own_kv, own_q, received[0]]
        else:
            pairs = [(own_kv, far_kv), (own_q, far_q)]
        if step < 2:
            count = counts[1 + step]
        if step == last:
            after = [received[1]] + moved
        outs = stage(pairs, tokens, first, count, after, HIDE if step == last else 0)
        if pairs:
            own_kv, own_q = outs[:2]
        if count:
            received.append(lax.ppermute(outs[-1], "tensor", ring))
        first += count
        far_kv = lax.ppermute(own_kv, PLANE, [(i, i ^ mask_kv) for i in range(plane)])
        far_q = lax.ppermute(own_q, PLANE, [(i, i ^ mask_q) for i in range(plane)])
        order_kv = order_kv + [k ^ mask_kv for k in order_kv]
        order_q = order_q + [k ^ mask_q for k in order_q]
    far_kv, far_q = (order_kv, own_kv, far_kv), (order_q, own_q, far_q)

    own_o = jnp.stack(moved)[None]

    def double(own, step, after):
        if step > 0:
            (own,) = stage([own], tokens, 0, 0, after)
        return own, lax.ppermute(own, PLANE, [(i, i ^ masks_kv[step]) for i in range(plane)])

    sources = (within + half - jnp.arange(half, dtype=jnp.int32)) % half
    gains = in_gain.reshape(nz, 1, cols)
    place = jnp.stack([in_plane, side * half])
    own_x, own_sq, part = far_own_product(place, sources, gains, tokens, far_kv)
    received[-1] = gate(received[-1], own_sq)
    blocks = [received]
    for _ in range(half - 2):
        blocks.append([lax.ppermute(block, "tensor", ring) for block in blocks[-1]])
    sent_kv, x, sq = far_kv_product(
        place, sources, gains, part, own_sq, blocks, far_kv, [far_q[2]]
    )
    got_kv = lax.ppermute(sent_kv, "tensor", swap)
    pair_o = double(own_o, 0, [])
    for step in range(1, last - 1):
        pair_o = double(pair_o, step, [])
    weights = (k_weight, value_weight, q_weight)

    near = near_product(side * half + sources, own_x, x, weights, [sent_kv])

    sent_q = far_product(place, sources, own_x, x, far_q, [near])
    got_q = lax.ppermute(gate(sent_q, got_kv), "tensor", swap)
    pair_o = double(pair_o, last - 1, [sent_q])
    cosine, sine = rotation_table(seq * rows + jnp.arange(rows, dtype=jnp.int32))
    ids = seg_ids[None, :]
    own_kv, sums = keys_values(
        near, got_kv, sq, ids, cosine, sine, [sent_q, pair_o[0]], model
    )
    pair_o = double(pair_o, last, [own_kv])
    gathered_o = lay_pieces(place, order_kv, *pair_o)

    back = -(-(nseq * rows // 2 - 1) // rows)
    kv_blocks = [own_kv]
    for k in range(1, back + 1):
        earlier = [(i, i + k) for i in range(nseq - k)]
        kv_blocks.insert(0, lax.ppermute(own_kv, "seq", earlier))

    queries = finished_queries(near, got_q, sums, cosine, sine, model)
    seq_at = jnp.reshape(seq, (1,))
    contexts, after = [], own_kv
    for c in range(CHUNKS):
        contexts.append(attend(seq_at, queries, ids, after, kv_blocks, c))
        after = contexts[-1]
    early, late = [], []
    for c, context in enumerate(contexts):
        if nz == 4:
            pairs = [(i, i ^ 1) for i in range(nz)]
            opposite = lax.ppermute(context, "tensor", swap)
            beside = lax.ppermute(context, "tensor", pairs)
            if c + 1 < CHUNKS:
                opposite = gate(opposite, contexts[c + 1])
            across = lax.ppermute(opposite, "tensor", pairs)
            early.append([context, beside])
            late.append([opposite, across])
            order = [2 - 2 * (z % 2), jnp.int32(1), 2 * (z % 2)]
        else:
            early.append([context])
            late.append([lax.ppermute(context, "tensor", turn(k)) for k in range(1, nz)])
            order = [jnp.int32(k) for k in range(nz - 1)]
    split = len(early[0]) - 1
    branches, own_sq = [], sums
    for c in range(CHUNKS):
        part = first_output(z, order[:split], o_weight, gathered_o, early[c], contexts[-1])
        branch, own_sq = last_output(order[split:], part, gathered_o, late[c], own_sq, c)
        branches.append(branch)
    squares = [own_sq]
    squares += [lax.ppermute(own_sq, "tensor", turn(k)) for k in range(1, nz)]
    return finish(tokens, branches, out_gain[None, :], squares, model)


def solution(mesh):
    return jax.shard_map(
        partial(per_device, sizes=dict(mesh.shape)),
        mesh=mesh,
        in_specs=(
            P(("groups", "seq"), "tensor"),
            P(("groups", "seq")),
            P(),
            P(None, "tensor"),
            P(None, "tensor"),
            P(None, "tensor"),
            P("tensor", None),
            P("tensor"),
        ),
        out_specs=P(("groups", "seq"), "tensor"),
        check_vma=False,
    )
```

```python
import math
from functools import partial

import jax
import jax.numpy as jnp
from jax import lax
from jax.experimental import pallas as pl
from jax.experimental.pallas import tpu as pltpu
from jax.sharding import PartitionSpec as P

HEAD_SIZE = 128
PLANE = ("groups", "seq")

epsilon = 1e-06
query_scale = 144.0 ** (-0.5)
rope_base = 10000.0
NEG = -1e30
Q_TILE = 128
K_TILE = 384
CHUNKS = 2
LANES = 128
TAIL = 16
F32, BF16 = jnp.float32, jnp.bfloat16
ANY = pl.BlockSpec(memory_space=pl.ANY)
HBM = pl.BlockSpec(memory_space=pltpu.HBM)
VMEM = pl.BlockSpec(memory_space=pltpu.VMEM)
DOCUMENTS = 8
HIDE = 5 * 10**10
PARAMS = pltpu.CompilerParams(vmem_limit_bytes=48 * 1024 * 1024)
ALL_VMEM = pltpu.CompilerParams(vmem_limit_bytes=62 * 1024 * 1024)


def shape(dims, dtype):
    return jax.ShapeDtypeStruct(dims, dtype)


def to_row(column):
    return jnp.broadcast_to(column, (column.shape[0], LANES)).T[0:1, :]


def to_column(row):
    return jnp.broadcast_to(row, (LANES, row.shape[1])).T


def rotation_table(token_places):
    half_dim = HEAD_SIZE // 2
    inverse = rope_base ** (-jnp.arange(half_dim, dtype=F32) / half_dim)
    angles = token_places.astype(F32)[:, None] * inverse[None, :]
    cosine, sine = jnp.cos(angles), jnp.sin(angles)
    return jnp.concatenate([cosine, cosine], 1), jnp.concatenate([-sine, sine], 1)


def rotate(vectors, cosine, sine):
    return vectors * cosine + pltpu.roll(vectors, HEAD_SIZE // 2, 1) * sine


def pack_kernel(at_ref, q_ref, k_ref, v_ref, x_ref, kv_out, q_out, x_out, sems):
    share, width = q_out.shape[0], k_ref.shape[1]
    rows = pl.ds(pl.multiple_of(at_ref[0] * share, TAIL), share)
    copies = [
        pltpu.make_async_copy(k_ref.at[rows], kv_out.at[:, pl.ds(0, width)], sems.at[0]),
        pltpu.make_async_copy(v_ref.at[rows], kv_out.at[:, pl.ds(width, width)], sems.at[1]),
        pltpu.make_async_copy(q_ref.at[rows], q_out, sems.at[2]),
        pltpu.make_async_copy(x_ref.at[pl.ds(0, x_out.shape[0])], x_out, sems.at[3]),
    ]
    for copy in copies:
        copy.start()
    for copy in copies:
        copy.wait()


def pack(at, q_weight, k_weight, v_weight, share, tokens, rows):
    kv_width = k_weight.shape[1] + v_weight.shape[1]
    dims = [(share, kv_width), (share, q_weight.shape[1]), (rows, tokens.shape[1])]
    return pl.pallas_call(
        pack_kernel,
        out_shape=tuple(shape(d, BF16) for d in dims),
        grid_spec=pltpu.PrefetchScalarGridSpec(
            num_scalar_prefetch=1,
            grid=(1,),
            in_specs=[HBM, HBM, HBM, HBM],
            out_specs=[pl.BlockSpec(d, lambda i, at: (0, 0)) for d in dims],
            scratch_shapes=[pltpu.SemaphoreType.DMA((4,))],
        ),
        compiler_params=ALL_VMEM,
        name="pack",
    )(at, q_weight, k_weight, v_weight, tokens)


def gate_kernel(x_ref, after_ref, out_ref):
    pass


def gate(x, after):
    return pl.pallas_call(
        gate_kernel,
        out_shape=shape(x.shape, x.dtype),
        in_specs=[ANY, ANY],
        out_specs=ANY,
        input_output_aliases={0: 0},
        compiler_params=PARAMS,
        name="gate",
    )(x, after)


def stage_kernel(*refs, pairs, first, count):
    outputs = pairs + (1 if count else 0)
    ins, outs, sems = refs[: -outputs - 1], refs[-outputs - 1 : -1], refs[-1]
    copies = []
    for p in range(pairs):
        held = ins[2 * p].shape[0]
        for side in range(2):
            there = outs[p].at[pl.ds(side * held, held)]
            copies.append(
                pltpu.make_async_copy(ins[2 * p + side], there, sems.at[len(copies)])
            )
    if count:
        rows = ins[2 * pairs].at[pl.ds(first, count)]
        copies.append(pltpu.make_async_copy(rows, outs[-1], sems.at[len(copies)]))
    for copy in copies:
        copy.start()
    for copy in copies:
        copy.wait()


def stage(joined, tokens, first, count, after, flops=0):
    dims = [(2 * pair[0].shape[0],) + pair[0].shape[1:] for pair in joined]
    if count:
        dims.append((count, tokens.shape[1]))
    return pl.pallas_call(
        partial(stage_kernel, pairs=len(joined), first=first, count=count),
        out_shape=tuple(shape(d, BF16) for d in dims),
        in_specs=[ANY] * (2 * len(joined) + 1 + len(after)),
        scratch_shapes=[pltpu.SemaphoreType.DMA((2 * len(joined) + 1,))],
        compiler_params=PARAMS,
        cost_estimate=pl.CostEstimate(flops=flops, bytes_accessed=flops // 500, transcendentals=0),
        name="stage",
    )(*[piece for pair in joined for piece in pair], tokens, *after)


def cut_kernel(at_ref, o_ref, after_ref, *rest):
    outs, sems = rest[:-1], rest[-1]
    copies = []
    for i, out in enumerate(outs):
        rows = pl.ds(pl.multiple_of(at_ref[0], TAIL), out.shape[0])
        columns = pl.ds(pl.multiple_of(at_ref[1 + i], LANES), out.shape[1])
        copies.append(pltpu.make_async_copy(o_ref.at[rows, columns], out, sems.at[i]))
    for copy in copies:
        copy.start()
    for copy in copies:
        copy.wait()


def cut_pieces(row, columns, o_weight, share, cols, after):
    if cols % LANES:
        return [lax.dynamic_slice(o_weight, (row, c), (share, cols)) for c in columns]
    return pl.pallas_call(
        cut_kernel,
        out_shape=tuple(shape((share, cols), BF16) for _ in columns),
        grid_spec=pltpu.PrefetchScalarGridSpec(
            num_scalar_prefetch=1,
            grid=(1,),
            in_specs=[ANY, ANY],
            out_specs=[VMEM for _ in columns],
            scratch_shapes=[pltpu.SemaphoreType.DMA((len(columns),))],
        ),
        compiler_params=PARAMS,
        name="cut",
    )(jnp.stack([row] + columns), o_weight, after)


def lay_kernel(place_ref, own_ref, got_ref, out_ref, sems, *, order):
    held, others, share, _ = own_ref.shape
    copies = []
    for i, mask in enumerate(order):
        piece = own_ref.at[i] if i < held else got_ref.at[i - held]
        row = pl.multiple_of((place_ref[0] ^ mask) * share, TAIL)
        there = out_ref.at[:, pl.ds(row, share)]
        copies.append(pltpu.make_async_copy(piece, there, sems.at[i]))
    for copy in copies:
        copy.start()
    for copy in copies:
        copy.wait()


def lay_pieces(place, order, own, got):
    _, others, share, cols = own.shape
    dims = (others, len(order) * share, cols)
    return pl.pallas_call(
        partial(lay_kernel, order=order),
        out_shape=shape(dims, BF16),
        grid_spec=pltpu.PrefetchScalarGridSpec(
            num_scalar_prefetch=1,
            grid=(1,),
            in_specs=[ANY, ANY],
            out_specs=pl.BlockSpec(dims, lambda i, p: (0, 0, 0)),
            scratch_shapes=[pltpu.SemaphoreType.DMA((len(order),))],
        ),
        compiler_params=PARAMS,
        name="lay",
    )(place, own, got)


def place_weights(place_ref, own_ref, got_ref, weight, sems, order):
    held, share, _ = own_ref.shape
    copies = []
    for i, mask in enumerate(order):
        piece = own_ref.at[i] if i < held else got_ref.at[i - held]
        row = pl.multiple_of((place_ref[0] ^ mask) * share, TAIL)
        there = weight.at[pl.ds(row, share)]
        copies.append(pltpu.make_async_copy(piece, there, sems.at[i]))
    for copy in copies:
        copy.start()
    return copies


def far_sum(src_ref, first, x_ref, weight):
    count, _, cols = x_ref.shape
    total = None
    for k in range(count):
        row = pl.multiple_of(src_ref[first + k] * cols, TAIL)
        term = jnp.dot(x_ref[k], weight[pl.ds(row, cols), :], preferred_element_type=F32)
        total = term if total is None else total + term
    return total


def prepare(x_refs, gain, x_out, k):
    column, row = [], 0
    for x_ref in x_refs:
        x = x_ref[...].astype(F32)
        column.append(jnp.sum(x * x, axis=1, keepdims=True))
        x_out[k, row : row + x.shape[0]] = (x * gain).astype(BF16)
        row += x.shape[0]
    return jnp.concatenate(column, axis=0)


def far_own_kernel(
    place_ref, src_ref, gain_ref, own_ref, got_ref, x_ref, x_out, sq_ref, out_ref, weight, sems,
    *, order
):
    copies = place_weights(place_ref, own_ref, got_ref, weight, sems, order)
    gain = gain_ref[place_ref[1] + src_ref[0]]
    sq_ref[...] = to_row(prepare([x_ref], gain, x_out, 0))
    for copy in copies:
        copy.wait()
    out_ref[...] = far_sum(src_ref, 0, x_out, weight)


def far_kv_kernel(
    place_ref, src_ref, gain_ref, part_ref, own_sq_ref, own_ref, got_ref, *rest, order, cuts, first
):
    x_refs, (out_ref, x_out, sq_ref, weight, sems) = rest[: sum(cuts)], rest[-5:]
    copies = place_weights(place_ref, own_ref, got_ref, weight, sems, order)
    rows = x_out.shape[1]
    columns, at = [], 0
    for k, pieces in enumerate(cuts):
        gain = gain_ref[place_ref[1] + src_ref[1 + k]]
        columns.append(prepare(x_refs[at : at + pieces], gain, x_out, k))
        at += pieces
    mine = slice(first, first + rows)
    sq = to_row(sum(columns[1:], columns[0])) + own_sq_ref[:, mine]
    sq_ref[...] = sq
    for copy in copies:
        copy.wait()
    total = part_ref[mine, :] + far_sum(src_ref, 1, x_out, weight)
    out_ref[:rows, :] = total.astype(BF16)
    high = sq.astype(BF16).astype(F32)
    out_ref[rows:, :] = lines_of((high, sq - high), out_ref.shape[1])


def far_kv_scratch(gathered):
    order, own, _ = gathered
    return [
        pltpu.VMEM((len(order) * own.shape[1], own.shape[2]), BF16),
        pltpu.SemaphoreType.DMA((len(order),)),
    ]


def far_own_product(place, sources, gains, tokens, gathered):
    order, own, got = gathered
    rows, cols = tokens.shape
    dims = [(1, rows, cols), (1, rows), (rows, own.shape[2])]
    whole = lambda d: pl.BlockSpec(d, lambda i, p, s: (0,) * len(d))
    return pl.pallas_call(
        partial(far_own_kernel, order=order),
        out_shape=tuple(shape(d, t) for d, t in zip(dims, (BF16, F32, F32))),
        grid_spec=pltpu.PrefetchScalarGridSpec(
            num_scalar_prefetch=2,
            grid=(1,),
            in_specs=[whole(gains.shape), ANY, ANY, whole(tokens.shape)],
            out_specs=[whole(d) for d in dims],
            scratch_shapes=far_kv_scratch(gathered),
        ),
        compiler_params=PARAMS,
        name="far_own",
    )(place, sources, gains, own, got, tokens)


def far_kv_product(place, sources, gains, part, own_sq, first, blocks, gathered, after):
    order, own, got = gathered
    rows, width = sum(piece.shape[0] for piece in blocks[0]), part.shape[1]
    cols = blocks[0][0].shape[1]
    pieces = [piece for block in blocks for piece in block]
    dims = [(rows + TAIL, width), (len(blocks), rows, cols), (1, rows)]
    whole = lambda d: pl.BlockSpec(d, lambda i, p, s: (0,) * len(d))
    return pl.pallas_call(
        partial(
            far_kv_kernel, order=order, cuts=[len(block) for block in blocks], first=first
        ),
        out_shape=tuple(shape(d, t) for d, t in zip(dims, (BF16, BF16, F32))),
        grid_spec=pltpu.PrefetchScalarGridSpec(
            num_scalar_prefetch=2,
            grid=(1,),
            in_specs=[whole(gains.shape), whole(part.shape), whole(own_sq.shape), ANY, ANY]
            + [whole(piece.shape) for piece in pieces]
            + [ANY for _ in after],
            out_specs=[whole(d) for d in dims],
            scratch_shapes=far_kv_scratch(gathered),
        ),
        compiler_params=PARAMS,
        name="far_kv",
    )(place, sources, gains, part, own_sq, own, got, *pieces, *after)


def far_kernel(place_ref, src_ref, own_x_ref, own_ref, got_ref, *rest, order, groups):
    x_refs, (out_ref, weight, sems) = rest[:groups], rest[-3:]
    for copy in place_weights(place_ref, own_ref, got_ref, weight, sems, order):
        copy.wait()
    total = far_sum(src_ref, 0, own_x_ref, weight)
    first = 0
    for x_ref in x_refs:
        mine = slice(first, first + x_ref.shape[1])
        part = total[mine, :] + far_sum(src_ref, 1, x_ref, weight)
        out_ref[mine, :] = part.astype(BF16)
        first += x_ref.shape[1]


def lines_of(rows, width):
    lines = []
    for row in rows:
        for at in range(0, row.shape[1], width):
            line = row[:, at : at + width]
            if line.shape[1] < width:
                rest = jnp.zeros((1, width - line.shape[1]), F32)
                line = jnp.concatenate([line, rest], axis=1)
            lines.append(line)
    lines.append(jnp.zeros((TAIL - len(lines), width), F32))
    return jnp.concatenate(lines, axis=0).astype(BF16)


def rows_of(tail, count, length):
    per_row = -(-length // tail.shape[1])
    rows = []
    for r in range(count):
        lines = [tail[r * per_row + i : r * per_row + i + 1, :] for i in range(per_row)]
        rows.append(jnp.concatenate(lines, axis=1)[:, :length])
    return rows


def far_product(place, sources, own_x, xs, gathered, after):
    order, own, got = gathered
    rows, width = own_x.shape[1], own.shape[2]
    whole = lambda d: pl.BlockSpec(d, lambda i, p, s: (0,) * len(d))
    return pl.pallas_call(
        partial(far_kernel, order=order, groups=len(xs)),
        out_shape=shape((rows, width), BF16),
        grid_spec=pltpu.PrefetchScalarGridSpec(
            num_scalar_prefetch=2,
            grid=(1,),
            in_specs=[whole(own_x.shape), ANY, ANY]
            + [whole(x.shape) for x in xs]
            + [ANY for _ in after],
            out_specs=whole((rows, width)),
            scratch_shapes=far_kv_scratch(gathered),
        ),
        compiler_params=PARAMS,
        name="far",
    )(place, sources, own_x, own, got, *xs, *after)


def near_kernel(src_ref, own_x_ref, k_ref, v_ref, q_ref, *rest, groups):
    x_refs, out_ref = rest[:groups], rest[-1]
    step = pl.program_id(0)
    dot = partial(jnp.dot, preferred_element_type=F32)
    column = 0
    for ref in (k_ref, v_ref, q_ref):
        at = slice(column, column + ref.shape[1])

        @pl.when(step == 0)
        def _():
            out_ref[:, at] = dot(own_x_ref[0], ref[...])

        @pl.when(step > 0)
        def _():
            first = 0
            for x_ref in x_refs:
                mine = slice(first, first + x_ref.shape[1])
                out_ref[mine, at] += dot(x_ref[0], ref[...])
                first += x_ref.shape[1]

        column += ref.shape[1]


def near_product(sources, own_x, xs, weights, after):
    count, rows, cols = own_x.shape[0] + xs[0].shape[0], own_x.shape[1], own_x.shape[2]
    widths = [w.shape[1] for w in weights]
    return pl.pallas_call(
        partial(near_kernel, groups=len(xs)),
        out_shape=shape((rows, sum(widths)), F32),
        grid_spec=pltpu.PrefetchScalarGridSpec(
            num_scalar_prefetch=1,
            grid=(count,),
            in_specs=[pl.BlockSpec((1, rows, cols), lambda i, s: (0, 0, 0))]
            + [pl.BlockSpec((cols, w), lambda i, s: (s[i], 0)) for w in widths]
            + [
                pl.BlockSpec((1,) + x.shape[1:], lambda i, s: (jnp.maximum(i - 1, 0), 0, 0))
                for x in xs
            ]
            + [ANY for _ in after],
            out_specs=pl.BlockSpec((rows, sum(widths)), lambda i, s: (0, 0)),
        ),
        compiler_params=PARAMS,
        name="near",
    )(sources, own_x, *weights, *xs, *after)


def keys_kernel(near_ref, id_ref, cos_ref, sin_ref, *rest, model, groups):
    far_refs, sq_refs = rest[:groups], rest[groups : 2 * groups]
    out_ref, sum_ref = rest[-2:]
    rows, width = near_ref.shape[0], out_ref.shape[1]
    keys, values = slice(0, HEAD_SIZE), slice(HEAD_SIZE, 2 * HEAD_SIZE)
    key_parts, value_parts, first = [], [], 0
    for far_ref, sq_ref in zip(far_refs, sq_refs):
        count = sq_ref.shape[1]
        at = slice(first, first + count)
        tail = far_ref[count:, :].astype(F32)
        total = sum(rows_of(tail, 2, count), sq_ref[...])
        factor = to_column(lax.rsqrt(total / model + epsilon))
        sum_ref[:, at] = total
        part = (near_ref[at, keys] + far_ref[:count, keys].astype(F32)) * factor
        key_parts.append(rotate(part, cos_ref[at, :], sin_ref[at, :]).astype(BF16))
        part = (near_ref[at, values] + far_ref[:count, values].astype(F32)) * factor
        value_parts.append(part.T.astype(BF16))
        first += count
    part = jnp.concatenate(key_parts, axis=0)
    out_ref[: rows // 2, keys] = part[: rows // 2]
    out_ref[: rows // 2, values] = part[rows // 2 :]
    part = jnp.concatenate(value_parts, axis=1)
    for i, at in enumerate(range(0, rows, width)):
        row = rows // 2 + i * HEAD_SIZE
        out_ref[row : row + HEAD_SIZE, :] = part[:, at : at + width]
    out_ref[rows:, :] = lines_of((id_ref[...].astype(F32),), width)


def keys_values(near, fars, sqs, ids, cosine, sine, after, model):
    rows, width = near.shape[0], fars[0].shape[1]
    whole = lambda i: (0, 0)
    dims = [(rows + TAIL, width), (1, rows)]
    return pl.pallas_call(
        partial(keys_kernel, model=model, groups=len(fars)),
        out_shape=tuple(shape(d, t) for d, t in zip(dims, (BF16, F32))),
        grid=(1,),
        in_specs=[pl.BlockSpec((rows, width), whole)]
        + [pl.BlockSpec(a.shape, whole) for a in (ids, cosine, sine, *fars, *sqs)]
        + [ANY for _ in after],
        out_specs=[pl.BlockSpec(d, whole) for d in dims],
        compiler_params=PARAMS,
        name="keys",
    )(near, ids, cosine, sine, *fars, *sqs, *after)


def queries_kernel(near_ref, far_ref, sum_ref, cos_ref, sin_ref, out_ref, *, model):
    scale = query_scale * math.log2(math.e)
    factor = to_column(lax.rsqrt(sum_ref[...] / model + epsilon) * scale)
    for c in range(0, out_ref.shape[1], HEAD_SIZE):
        at = slice(c, c + HEAD_SIZE)
        part = (near_ref[:, at] + far_ref[:, at].astype(F32)) * factor
        out_ref[:, at] = rotate(part, cos_ref[...], sin_ref[...]).astype(BF16)


def finished_queries(near, far, sums, cosine, sine, model):
    rows, width = far.shape
    last = near.shape[1] // width - 1
    whole = lambda i: (0, 0)
    return pl.pallas_call(
        partial(queries_kernel, model=model),
        out_shape=shape((rows, width), BF16),
        grid=(1,),
        in_specs=[pl.BlockSpec((rows, width), lambda i: (0, last))]
        + [pl.BlockSpec(a.shape, whole) for a in (far, sums, cosine, sine)],
        out_specs=pl.BlockSpec((rows, width), whole),
        compiler_params=PARAMS,
        cost_estimate=pl.CostEstimate(flops=HIDE, bytes_accessed=10**8, transcendentals=0),
        name="queries",
    )(near, far, sums, cosine, sine)


def attention_kernel(seq_ref, q_ref, id_ref, after_ref, *rest, back, offset):
    kv_refs, (out_ref, k_scr, vt_scr, count_scr) = rest[:-4], rest[-4:]
    part_rows, message = kv_refs[0].shape[0] - TAIL, kv_refs[0].shape[1]
    group = q_ref.shape[1] // HEAD_SIZE
    tile = pl.program_id(0)

    @pl.when(tile == 0)
    def _():
        counts = [jnp.zeros((1, 1), F32) for _ in range(DOCUMENTS)]
        for b, kv_ref in enumerate(kv_refs):
            row, half = b * part_rows, part_rows // 2
            k_scr[row : row + half, :] = kv_ref[:half, :HEAD_SIZE]
            k_scr[row + half : row + part_rows, :] = kv_ref[:half, HEAD_SIZE:]
            for i, at in enumerate(range(0, part_rows, message)):
                first = half + i * HEAD_SIZE
                vt_scr[:, row + at : row + at + message] = kv_ref[first : first + HEAD_SIZE, :]
            (ids,) = rows_of(kv_ref[part_rows:, :].astype(F32), 1, part_rows)
            exists = b >= back - seq_ref[0]
            ids = jnp.where(exists, ids, -1.0)
            for d in range(DOCUMENTS):
                below = (ids < d).astype(F32)
                counts[d] = counts[d] + jnp.sum(below, axis=1, keepdims=True)
        for d in range(DOCUMENTS):
            count_scr[d : d + 1, :] = jnp.broadcast_to(counts[d], (1, LANES))

    heads = [q_ref[:, c : c + HEAD_SIZE] for c in range(0, group * HEAD_SIZE, HEAD_SIZE)]
    q2 = jnp.concatenate(heads, axis=0)
    width = group * Q_TILE

    start = jnp.zeros((1, Q_TILE), F32)
    for d in range(DOCUMENTS):
        start = jnp.where(id_ref[...] == d, count_scr[d : d + 1, :], start)
    start = start.astype(jnp.int32)
    low = jnp.min(start) // K_TILE
    start = jnp.concatenate([start] * group, axis=1)
    first = back * part_rows + offset + tile * Q_TILE
    place = first + lax.broadcasted_iota(jnp.int32, (1, Q_TILE), 1)
    place = jnp.concatenate([place] * group, axis=1)

    def score(j):
        base = pl.multiple_of(j * K_TILE, K_TILE)
        return lax.dot_general(
            k_scr[pl.ds(base, K_TILE), :],
            q2,
            (((1,), (1,)), ((), ())),
            preferred_element_type=F32,
        )

    stop = (first + Q_TILE + K_TILE - 1) // K_TILE

    def step(j, state):
        scores, run_max, run_sum, acc = state
        following = score(jnp.minimum(j + 1, stop - 1))
        base = pl.multiple_of(j * K_TILE, K_TILE)
        key_pos = base + lax.broadcasted_iota(jnp.int32, (K_TILE, width), 0)
        allowed = (key_pos >= start) & (key_pos <= place)
        scores = jnp.where(allowed, scores, NEG)
        new_max = jnp.maximum(run_max, jnp.max(scores, axis=0, keepdims=True))
        expo = jnp.exp2(scores - new_max)
        factor = jnp.exp2(run_max - new_max)
        run_sum = run_sum * factor + jnp.sum(expo, axis=0, keepdims=True)
        acc = acc * factor + jnp.dot(
            vt_scr[:, pl.ds(base, K_TILE)], expo.astype(BF16), preferred_element_type=F32
        )
        return following, new_max, run_sum, acc

    state = (
        score(low),
        jnp.full((1, width), NEG, F32),
        jnp.zeros((1, width), F32),
        jnp.zeros((HEAD_SIZE, width), F32),
    )
    _, _, run_sum, acc = lax.fori_loop(low, stop, step, state)
    context = (acc / run_sum).T
    for g in range(group):
        out_ref[:, g * HEAD_SIZE : (g + 1) * HEAD_SIZE] = context[
            g * Q_TILE : (g + 1) * Q_TILE
        ].astype(BF16)


def attend(seq, queries, ids, after, blocks, c):
    rows, width = queries.shape[0] // CHUNKS, queries.shape[1]
    back = len(blocks) - 1
    tiles = rows // Q_TILE
    keys = len(blocks) * queries.shape[0]
    return pl.pallas_call(
        partial(attention_kernel, back=back, offset=c * rows),
        out_shape=shape((rows, width), BF16),
        grid_spec=pltpu.PrefetchScalarGridSpec(
            num_scalar_prefetch=1,
            grid=(tiles,),
            in_specs=[
                pl.BlockSpec((Q_TILE, width), lambda i, s: (c * tiles + i, 0)),
                pl.BlockSpec((1, Q_TILE), lambda i, s: (0, c * tiles + i)),
                ANY,
            ]
            + [pl.BlockSpec(b.shape, lambda i, s: (0, 0)) for b in blocks],
            out_specs=pl.BlockSpec((Q_TILE, width), lambda i, s: (i, 0)),
            scratch_shapes=[
                pltpu.VMEM((keys, HEAD_SIZE), BF16),
                pltpu.VMEM((HEAD_SIZE, keys), BF16),
                pltpu.VMEM((DOCUMENTS, LANES), F32),
            ],
        ),
        compiler_params=PARAMS,
        cost_estimate=pl.CostEstimate(
            flops=4 * rows * width * keys,
            bytes_accessed=4 * keys * width,
            transcendentals=rows * keys * width // HEAD_SIZE,
        ),
        name="attend",
    )(seq, queries, ids, after, *blocks)


def first_output_kernel(at_ref, own_o_ref, o_ref, *rest):
    ctx_refs, out_ref = rest[:-2], rest[-1]
    total = jnp.dot(ctx_refs[0][...], own_o_ref[...], preferred_element_type=F32)
    for i, ctx_ref in enumerate(ctx_refs[1:]):
        total = total + jnp.dot(ctx_ref[...], o_ref[at_ref[1 + i]], preferred_element_type=F32)
    out_ref[...] = total


def last_output_kernel(at_ref, part_ref, o_ref, *rest):
    ctx_refs, (before_ref, out_ref, sq_ref, acc) = rest[:-4], rest[-4:]
    step = pl.program_id(0)
    total = part_ref[...]
    for i, ctx_ref in enumerate(ctx_refs):
        total = total + jnp.dot(ctx_ref[...], o_ref[at_ref[i]], preferred_element_type=F32)
    out_ref[...] = total
    squares = jnp.sum(total * total, axis=1, keepdims=True)
    squares = jnp.broadcast_to(squares, acc.shape)

    @pl.when(step == 0)
    def _():
        acc[...] = squares

    @pl.when(step > 0)
    def _():
        acc[...] += squares

    @pl.when(step == pl.num_programs(0) - 1)
    def _():
        done = sq_ref.shape[1] - acc.shape[0]
        if done:
            sq_ref[:, :done] = before_ref[...]
        sq_ref[:, done:] = acc[...].T[0:1, :]


def column_tiles(cols):
    tiles = 3 if cols % (3 * LANES) == 0 else 1
    return tiles, cols // tiles


def first_output(column, order, o_weight, gathered, contexts, after):
    chunk, width = contexts[0].shape
    others, _, cols = gathered.shape
    tiles, tile = column_tiles(cols)
    if cols % LANES:
        o_weight = lax.dynamic_slice_in_dim(o_weight, column * cols, cols, axis=1)
        column = jnp.int32(0)
    return pl.pallas_call(
        first_output_kernel,
        out_shape=shape((chunk, cols), F32),
        grid_spec=pltpu.PrefetchScalarGridSpec(
            num_scalar_prefetch=1,
            grid=(tiles,),
            in_specs=[
                pl.BlockSpec((width, tile), lambda i, at: (0, at[0] * tiles + i)),
                pl.BlockSpec((others, width, tile), lambda i, at: (0, 0, i)),
            ]
            + [pl.BlockSpec((chunk, width), lambda i, at: (0, 0)) for _ in contexts]
            + [ANY],
            out_specs=pl.BlockSpec((chunk, tile), lambda i, at: (0, i)),
        ),
        compiler_params=PARAMS,
        cost_estimate=pl.CostEstimate(flops=HIDE, bytes_accessed=10**8, transcendentals=0),
        name="first_output",
    )(jnp.stack([column] + order), o_weight, gathered, *contexts, after)


def last_output(order, part, gathered, contexts, before, c):
    chunk, width = contexts[0].shape
    others, _, cols = gathered.shape
    tiles, tile = column_tiles(cols)
    return pl.pallas_call(
        last_output_kernel,
        out_shape=(shape((chunk, cols), F32), shape((1, (c + 1) * chunk), F32)),
        grid_spec=pltpu.PrefetchScalarGridSpec(
            num_scalar_prefetch=1,
            grid=(tiles,),
            in_specs=[
                pl.BlockSpec((chunk, tile), lambda i, at: (0, i)),
                pl.BlockSpec((others, width, tile), lambda i, at: (0, 0, i)),
            ]
            + [pl.BlockSpec((chunk, width), lambda i, at: (0, 0)) for _ in contexts]
            + [pl.BlockSpec(before.shape, lambda i, at: (0, 0))],
            out_specs=[
                pl.BlockSpec((chunk, tile), lambda i, at: (0, i)),
                pl.BlockSpec((1, (c + 1) * chunk), lambda i, at: (0, 0)),
            ],
            scratch_shapes=[pltpu.VMEM((chunk, LANES), F32)],
        ),
        compiler_params=PARAMS,
        name="last_output",
    )(jnp.stack(order), part, gathered, *contexts, before)


def final_kernel(token_ref, gain_ref, *rest, model):
    branch_refs, sq_refs, out_ref = rest[:CHUNKS], rest[CHUNKS:-1], rest[-1]
    total = sq_refs[0][...]
    for sq_ref in sq_refs[1:]:
        total = total + sq_ref[...]
    factor = to_column(lax.rsqrt(total / model + epsilon))[:, 0:1]
    for c in range(CHUNKS):

        @pl.when(pl.program_id(0) * CHUNKS // pl.num_programs(0) == c)
        def _():
            out = token_ref[...].astype(F32) + branch_refs[c][...] * factor * gain_ref[...]
            out_ref[...] = out.astype(BF16)


def finish(tokens, branches, out_gain, sums, model):
    rows, cols = tokens.shape
    tiles = rows // CHUNKS // Q_TILE
    held = lambda c: lambda i: (jnp.clip(i - c * tiles, 0, tiles - 1), 0)
    return pl.pallas_call(
        partial(final_kernel, model=model),
        out_shape=shape(tokens.shape, BF16),
        grid=(CHUNKS * tiles,),
        in_specs=[
            pl.BlockSpec((Q_TILE, cols), lambda i: (i, 0)),
            pl.BlockSpec((1, cols), lambda i: (0, 0)),
        ]
        + [pl.BlockSpec((Q_TILE, cols), held(c)) for c in range(CHUNKS)]
        + [pl.BlockSpec((1, Q_TILE), lambda i: (0, i)) for _ in sums],
        out_specs=pl.BlockSpec((Q_TILE, cols), lambda i: (i, 0)),
        compiler_params=PARAMS,
        name="finish",
    )(tokens, out_gain, *branches, *sums)


def per_device(
    tokens, seg_ids, in_gain, q_weight, k_weight, value_weight, o_weight, out_gain, *, sizes
):
    rows, cols = tokens.shape
    model = in_gain.shape[0]
    nz, nseq = sizes["tensor"], sizes["seq"]
    plane = nseq * sizes["groups"]
    z = lax.axis_index("tensor")
    seq = lax.axis_index("seq")
    in_plane = lax.axis_index(PLANE)
    half = nz // 2
    side, within = z // half, z % half
    half_rows = half * cols

    ring = [(i, i // half * half + (i + 1) % half) for i in range(nz)]
    swap = [(i, (i + half) % nz) for i in range(nz)]
    turn = lambda k: [(i, (i + k) % nz) for i in range(nz)]
    seq_bits = [1 << b for b in range(1, nseq.bit_length() - 1)]
    group_bits = [nseq << b for b in range(sizes["groups"].bit_length() - 1)]

    share = half_rows // plane
    at = jnp.reshape((1 - side) * plane + in_plane, (1,))
    inner = seq_bits + group_bits
    masks_kv, masks_q = inner + [1], inner[::-1] + [1]
    last = len(masks_kv) - 1
    eighth = rows // 48 * 8
    counts = [eighth, rows // 2 - eighth, rows // 2]
    packed_kv, packed_q, cut = pack(
        at, q_weight, k_weight, value_weight, share, tokens, counts[0]
    )
    own_kv = lax.ppermute(packed_kv, "tensor", swap)[None]
    own_q = lax.ppermute(packed_q, "tensor", swap)[None]
    received = [lax.ppermute(cut, "tensor", ring)]
    o_share = o_weight.shape[0] // plane
    columns = [(z + k) % nz * cols for k in range(1, nz)]
    pieces = cut_pieces(in_plane * o_share, columns, o_weight, o_share, cols, own_kv)
    moved = [lax.ppermute(p, "tensor", turn(k + 1)) for k, p in enumerate(pieces)]

    order_kv, order_q, first = [0], [0], counts[0]
    for step, (mask_kv, mask_q) in enumerate(zip(masks_kv, masks_q)):
        after, count = [], 0
        if step == 0:
            pairs, after = [], [own_kv, own_q, received[0]]
        else:
            pairs = [(own_kv, far_kv), (own_q, far_q)]
        if step < 2:
            count = counts[1 + step]
        if step == last:
            after = [received[1]]
        outs = stage(pairs, tokens, first, count, after, HIDE if step == last else 0)
        if pairs:
            own_kv, own_q = outs[:2]
        if count:
            received.append(lax.ppermute(outs[-1], "tensor", ring))
        first += count
        far_kv = lax.ppermute(own_kv, PLANE, [(i, i ^ mask_kv) for i in range(plane)])
        far_q = lax.ppermute(own_q, PLANE, [(i, i ^ mask_q) for i in range(plane)])
        order_kv = order_kv + [k ^ mask_kv for k in order_kv]
        order_q = order_q + [k ^ mask_q for k in order_q]
    far_kv, far_q = (order_kv, own_kv, far_kv), (order_q, own_q, far_q)

    own_o = jnp.stack(moved)[None]

    def double(own, step, after):
        if step > 0:
            (own,) = stage([own], tokens, 0, 0, after)
        return own, lax.ppermute(own, PLANE, [(i, i ^ masks_kv[step]) for i in range(plane)])

    sources = (within + half - jnp.arange(half, dtype=jnp.int32)) % half
    gains = in_gain.reshape(nz, 1, cols)
    place = jnp.stack([in_plane, side * half])
    own_x, own_sq, part = far_own_product(place, sources, gains, tokens, far_kv)
    received[-1] = gate(received[-1], own_sq)
    weights = (k_weight, value_weight, q_weight)
    pair_o = double(own_o, 0, [])
    for step in range(1, last - 1):
        pair_o = double(pair_o, step, [])
    xs, sqs, got_kv, first, after = [], [], [], 0, [far_q[2]] + moved
    for pieces in (received[:2], received[2:]):
        blocks = [pieces]
        for _ in range(half - 2):
            blocks.append([lax.ppermute(block, "tensor", ring) for block in blocks[-1]])
        sent_kv, x, sq = far_kv_product(
            place, sources, gains, part, own_sq, first, blocks, far_kv, after
        )
        xs.append(x)
        sqs.append(sq)
        got_kv.append(lax.ppermute(sent_kv, "tensor", swap))
        first, after = first + x.shape[1], [sent_kv]

    sent_q = far_product(place, sources, own_x, xs, far_q, [sent_kv, got_kv[0]])
    got_q = lax.ppermute(gate(sent_q, got_kv[1]), "tensor", swap)
    near = near_product(side * half + sources, own_x, xs, weights, [sent_q])
    pair_o = double(pair_o, last - 1, [sent_q])
    cosine, sine = rotation_table(seq * rows + jnp.arange(rows, dtype=jnp.int32))
    ids = seg_ids[None, :]
    own_kv, sums = keys_values(
        near, got_kv, sqs, ids, cosine, sine, [sent_q, pair_o[0]], model
    )
    pair_o = double(pair_o, last, [own_kv])
    gathered_o = lay_pieces(place, order_kv, *pair_o)

    back = -(-(nseq * rows // 2 - 1) // rows)
    kv_blocks = [own_kv]
    for k in range(1, back + 1):
        earlier = [(i, i + k) for i in range(nseq - k)]
        kv_blocks.insert(0, lax.ppermute(own_kv, "seq", earlier))

    queries = finished_queries(near, got_q, sums, cosine, sine, model)
    seq_at = jnp.reshape(seq, (1,))
    contexts, after = [], own_kv
    for c in range(CHUNKS):
        contexts.append(attend(seq_at, queries, ids, after, kv_blocks, c))
        after = gathered_o
    early, late = [], []
    for c, context in enumerate(contexts):
        if nz == 4:
            pairs = [(i, i ^ 1) for i in range(nz)]
            opposite = lax.ppermute(context, "tensor", swap)
            beside = lax.ppermute(context, "tensor", pairs)
            if c + 1 < CHUNKS:
                opposite = gate(opposite, contexts[c + 1])
            across = lax.ppermute(opposite, "tensor", pairs)
            early.append([context, beside])
            late.append([opposite, across])
            order = [2 - 2 * (z % 2), jnp.int32(1), 2 * (z % 2)]
        else:
            early.append([context])
            late.append([lax.ppermute(context, "tensor", turn(k)) for k in range(1, nz)])
            order = [jnp.int32(k) for k in range(nz - 1)]
    split = len(early[0]) - 1
    branches, own_sq = [], sums
    for c in range(CHUNKS):
        part = first_output(z, order[:split], o_weight, gathered_o, early[c], contexts[-1])
        branch, own_sq = last_output(order[split:], part, gathered_o, late[c], own_sq, c)
        branches.append(branch)
    squares = [own_sq]
    squares += [lax.ppermute(own_sq, "tensor", turn(k)) for k in range(1, nz)]
    return finish(tokens, branches, out_gain[None, :], squares, model)


def solution(mesh):
    return jax.shard_map(
        partial(per_device, sizes=dict(mesh.shape)),
        mesh=mesh,
        in_specs=(
            P(("groups", "seq"), "tensor"),
            P(("groups", "seq")),
            P(),
            P(None, "tensor"),
            P(None, "tensor"),
            P(None, "tensor"),
            P("tensor", None),
            P("tensor"),
        ),
        out_specs=P(("groups", "seq"), "tensor"),
        check_vma=False,
    )
```

```python
import math
from functools import partial

import jax
import jax.numpy as jnp
from jax import lax
from jax.experimental import pallas as pl
from jax.experimental.pallas import tpu as pltpu
from jax.sharding import PartitionSpec as P

HEAD_SIZE = 128
PLANE = ("groups", "seq")

epsilon = 1e-06
query_scale = 144.0 ** (-0.5)
rope_base = 10000.0
NEG = -1e30
Q_TILE = 128
K_TILE = 384
CHUNKS = 2
LANES = 128
TAIL = 16
F32, BF16 = jnp.float32, jnp.bfloat16
ANY = pl.BlockSpec(memory_space=pl.ANY)
HBM = pl.BlockSpec(memory_space=pltpu.HBM)
VMEM = pl.BlockSpec(memory_space=pltpu.VMEM)
DOCUMENTS = 8
HIDE = 5 * 10**10
PARAMS = pltpu.CompilerParams(vmem_limit_bytes=48 * 1024 * 1024)
ALL_VMEM = pltpu.CompilerParams(vmem_limit_bytes=62 * 1024 * 1024)


def shape(dims, dtype):
    return jax.ShapeDtypeStruct(dims, dtype)


def to_row(column):
    return jnp.broadcast_to(column, (column.shape[0], LANES)).T[0:1, :]


def to_column(row):
    return jnp.broadcast_to(row, (LANES, row.shape[1])).T


def rotation_table(token_places):
    half_dim = HEAD_SIZE // 2
    inverse = rope_base ** (-jnp.arange(half_dim, dtype=F32) / half_dim)
    angles = token_places.astype(F32)[:, None] * inverse[None, :]
    cosine, sine = jnp.cos(angles), jnp.sin(angles)
    return jnp.concatenate([cosine, cosine], 1), jnp.concatenate([-sine, sine], 1)


def rotate(vectors, cosine, sine):
    return vectors * cosine + pltpu.roll(vectors, HEAD_SIZE // 2, 1) * sine


def pack_kernel(at_ref, q_ref, k_ref, v_ref, x_ref, kv_out, q_out, x_out, sems):
    share, width = q_out.shape[0], k_ref.shape[1]
    rows = pl.ds(pl.multiple_of(at_ref[0] * share, TAIL), share)
    copies = [
        pltpu.make_async_copy(k_ref.at[rows], kv_out.at[:, pl.ds(0, width)], sems.at[0]),
        pltpu.make_async_copy(v_ref.at[rows], kv_out.at[:, pl.ds(width, width)], sems.at[1]),
        pltpu.make_async_copy(q_ref.at[rows], q_out, sems.at[2]),
        pltpu.make_async_copy(x_ref.at[pl.ds(0, x_out.shape[0])], x_out, sems.at[3]),
    ]
    for copy in copies:
        copy.start()
    for copy in copies:
        copy.wait()


def pack(at, q_weight, k_weight, v_weight, share, tokens, rows):
    kv_width = k_weight.shape[1] + v_weight.shape[1]
    dims = [(share, kv_width), (share, q_weight.shape[1]), (rows, tokens.shape[1])]
    return pl.pallas_call(
        pack_kernel,
        out_shape=tuple(shape(d, BF16) for d in dims),
        grid_spec=pltpu.PrefetchScalarGridSpec(
            num_scalar_prefetch=1,
            grid=(1,),
            in_specs=[HBM, HBM, HBM, HBM],
            out_specs=[pl.BlockSpec(d, lambda i, at: (0, 0)) for d in dims],
            scratch_shapes=[pltpu.SemaphoreType.DMA((4,))],
        ),
        compiler_params=ALL_VMEM,
        name="pack",
    )(at, q_weight, k_weight, v_weight, tokens)


def gate_kernel(x_ref, after_ref, out_ref):
    pass


def gate(x, after):
    return pl.pallas_call(
        gate_kernel,
        out_shape=shape(x.shape, x.dtype),
        in_specs=[ANY, ANY],
        out_specs=ANY,
        input_output_aliases={0: 0},
        compiler_params=PARAMS,
        name="gate",
    )(x, after)


def stage_kernel(*refs, pairs, first, count):
    outputs = pairs + (1 if count else 0)
    ins, outs, sems = refs[: -outputs - 1], refs[-outputs - 1 : -1], refs[-1]
    copies = []
    for p in range(pairs):
        held = ins[2 * p].shape[0]
        for side in range(2):
            there = outs[p].at[pl.ds(side * held, held)]
            copies.append(
                pltpu.make_async_copy(ins[2 * p + side], there, sems.at[len(copies)])
            )
    if count:
        rows = ins[2 * pairs].at[pl.ds(first, count)]
        copies.append(pltpu.make_async_copy(rows, outs[-1], sems.at[len(copies)]))
    for copy in copies:
        copy.start()
    for copy in copies:
        copy.wait()


def stage(joined, tokens, first, count, after, flops=0):
    dims = [(2 * pair[0].shape[0],) + pair[0].shape[1:] for pair in joined]
    if count:
        dims.append((count, tokens.shape[1]))
    return pl.pallas_call(
        partial(stage_kernel, pairs=len(joined), first=first, count=count),
        out_shape=tuple(shape(d, BF16) for d in dims),
        in_specs=[ANY] * (2 * len(joined) + 1 + len(after)),
        scratch_shapes=[pltpu.SemaphoreType.DMA((2 * len(joined) + 1,))],
        compiler_params=PARAMS,
        cost_estimate=pl.CostEstimate(flops=flops, bytes_accessed=flops // 500, transcendentals=0),
        name="stage",
    )(*[piece for pair in joined for piece in pair], tokens, *after)


def cut_kernel(at_ref, o_ref, after_ref, *rest):
    outs, sems = rest[:-1], rest[-1]
    copies = []
    for i, out in enumerate(outs):
        rows = pl.ds(pl.multiple_of(at_ref[0], TAIL), out.shape[0])
        columns = pl.ds(pl.multiple_of(at_ref[1 + i], LANES), out.shape[1])
        copies.append(pltpu.make_async_copy(o_ref.at[rows, columns], out, sems.at[i]))
    for copy in copies:
        copy.start()
    for copy in copies:
        copy.wait()


def cut_pieces(row, columns, o_weight, share, cols, after):
    if cols % LANES:
        return [lax.dynamic_slice(o_weight, (row, c), (share, cols)) for c in columns]
    return pl.pallas_call(
        cut_kernel,
        out_shape=tuple(shape((share, cols), BF16) for _ in columns),
        grid_spec=pltpu.PrefetchScalarGridSpec(
            num_scalar_prefetch=1,
            grid=(1,),
            in_specs=[ANY, ANY],
            out_specs=[VMEM for _ in columns],
            scratch_shapes=[pltpu.SemaphoreType.DMA((len(columns),))],
        ),
        compiler_params=PARAMS,
        name="cut",
    )(jnp.stack([row] + columns), o_weight, after)


def lay_kernel(place_ref, own_ref, got_ref, out_ref, sems, *, order):
    held, others, share, _ = own_ref.shape
    copies = []
    for i, mask in enumerate(order):
        piece = own_ref.at[i] if i < held else got_ref.at[i - held]
        row = pl.multiple_of((place_ref[0] ^ mask) * share, TAIL)
        there = out_ref.at[:, pl.ds(row, share)]
        copies.append(pltpu.make_async_copy(piece, there, sems.at[i]))
    for copy in copies:
        copy.start()
    for copy in copies:
        copy.wait()


def lay_pieces(place, order, own, got):
    _, others, share, cols = own.shape
    dims = (others, len(order) * share, cols)
    return pl.pallas_call(
        partial(lay_kernel, order=order),
        out_shape=shape(dims, BF16),
        grid_spec=pltpu.PrefetchScalarGridSpec(
            num_scalar_prefetch=1,
            grid=(1,),
            in_specs=[ANY, ANY],
            out_specs=pl.BlockSpec(dims, lambda i, p: (0, 0, 0)),
            scratch_shapes=[pltpu.SemaphoreType.DMA((len(order),))],
        ),
        compiler_params=PARAMS,
        name="lay",
    )(place, own, got)


def place_weights(place_ref, own_ref, got_ref, weight, sems, order):
    held, share, _ = own_ref.shape
    copies = []
    for i, mask in enumerate(order):
        piece = own_ref.at[i] if i < held else got_ref.at[i - held]
        row = pl.multiple_of((place_ref[0] ^ mask) * share, TAIL)
        there = weight.at[pl.ds(row, share)]
        copies.append(pltpu.make_async_copy(piece, there, sems.at[i]))
    for copy in copies:
        copy.start()
    return copies


def far_sum(src_ref, first, x_ref, weight):
    count, _, cols = x_ref.shape
    total = None
    for k in range(count):
        row = pl.multiple_of(src_ref[first + k] * cols, TAIL)
        term = jnp.dot(x_ref[k], weight[pl.ds(row, cols), :], preferred_element_type=F32)
        total = term if total is None else total + term
    return total


def prepare(x_refs, gain, x_out, k):
    column, row = [], 0
    for x_ref in x_refs:
        x = x_ref[...].astype(F32)
        column.append(jnp.sum(x * x, axis=1, keepdims=True))
        x_out[k, row : row + x.shape[0]] = (x * gain).astype(BF16)
        row += x.shape[0]
    return jnp.concatenate(column, axis=0)


def far_own_kernel(
    place_ref, src_ref, gain_ref, own_ref, got_ref, x_ref, x_out, sq_ref, out_ref, weight, sems,
    *, order
):
    copies = place_weights(place_ref, own_ref, got_ref, weight, sems, order)
    gain = gain_ref[place_ref[1] + src_ref[0]]
    sq_ref[...] = to_row(prepare([x_ref], gain, x_out, 0))
    for copy in copies:
        copy.wait()
    out_ref[...] = far_sum(src_ref, 0, x_out, weight)


def far_kv_kernel(
    place_ref, src_ref, gain_ref, part_ref, own_sq_ref, own_ref, got_ref, *rest, order, cuts, first
):
    x_refs, (out_ref, x_out, sq_ref, weight, sems) = rest[: sum(cuts)], rest[-5:]
    copies = place_weights(place_ref, own_ref, got_ref, weight, sems, order)
    rows = x_out.shape[1]
    columns, at = [], 0
    for k, pieces in enumerate(cuts):
        gain = gain_ref[place_ref[1] + src_ref[1 + k]]
        columns.append(prepare(x_refs[at : at + pieces], gain, x_out, k))
        at += pieces
    mine = slice(first, first + rows)
    sq = to_row(sum(columns[1:], columns[0])) + own_sq_ref[:, mine]
    sq_ref[...] = sq
    for copy in copies:
        copy.wait()
    total = part_ref[mine, :] + far_sum(src_ref, 1, x_out, weight)
    out_ref[:rows, :] = total.astype(BF16)
    high = sq.astype(BF16).astype(F32)
    out_ref[rows:, :] = lines_of((high, sq - high), out_ref.shape[1])


def far_kv_scratch(gathered):
    order, own, _ = gathered
    return [
        pltpu.VMEM((len(order) * own.shape[1], own.shape[2]), BF16),
        pltpu.SemaphoreType.DMA((len(order),)),
    ]


def far_own_product(place, sources, gains, tokens, gathered):
    order, own, got = gathered
    rows, cols = tokens.shape
    dims = [(1, rows, cols), (1, rows), (rows, own.shape[2])]
    whole = lambda d: pl.BlockSpec(d, lambda i, p, s: (0,) * len(d))
    return pl.pallas_call(
        partial(far_own_kernel, order=order),
        out_shape=tuple(shape(d, t) for d, t in zip(dims, (BF16, F32, F32))),
        grid_spec=pltpu.PrefetchScalarGridSpec(
            num_scalar_prefetch=2,
            grid=(1,),
            in_specs=[whole(gains.shape), ANY, ANY, whole(tokens.shape)],
            out_specs=[whole(d) for d in dims],
            scratch_shapes=far_kv_scratch(gathered),
        ),
        compiler_params=PARAMS,
        name="far_own",
    )(place, sources, gains, own, got, tokens)


def far_kv_product(place, sources, gains, part, own_sq, first, blocks, gathered, after):
    order, own, got = gathered
    rows, width = sum(piece.shape[0] for piece in blocks[0]), part.shape[1]
    cols = blocks[0][0].shape[1]
    pieces = [piece for block in blocks for piece in block]
    dims = [(rows + TAIL, width), (len(blocks), rows, cols), (1, rows)]
    whole = lambda d: pl.BlockSpec(d, lambda i, p, s: (0,) * len(d))
    return pl.pallas_call(
        partial(
            far_kv_kernel, order=order, cuts=[len(block) for block in blocks], first=first
        ),
        out_shape=tuple(shape(d, t) for d, t in zip(dims, (BF16, BF16, F32))),
        grid_spec=pltpu.PrefetchScalarGridSpec(
            num_scalar_prefetch=2,
            grid=(1,),
            in_specs=[whole(gains.shape), whole(part.shape), whole(own_sq.shape), ANY, ANY]
            + [whole(piece.shape) for piece in pieces]
            + [ANY for _ in after],
            out_specs=[whole(d) for d in dims],
            scratch_shapes=far_kv_scratch(gathered),
        ),
        compiler_params=PARAMS,
        name="far_kv",
    )(place, sources, gains, part, own_sq, own, got, *pieces, *after)


def far_kernel(place_ref, src_ref, own_x_ref, own_ref, got_ref, *rest, order, groups):
    x_refs, (out_ref, weight, sems) = rest[:groups], rest[-3:]
    for copy in place_weights(place_ref, own_ref, got_ref, weight, sems, order):
        copy.wait()
    total = far_sum(src_ref, 0, own_x_ref, weight)
    first = 0
    for x_ref in x_refs:
        mine = slice(first, first + x_ref.shape[1])
        part = total[mine, :] + far_sum(src_ref, 1, x_ref, weight)
        out_ref[mine, :] = part.astype(BF16)
        first += x_ref.shape[1]


def lines_of(rows, width):
    lines = []
    for row in rows:
        for at in range(0, row.shape[1], width):
            line = row[:, at : at + width]
            if line.shape[1] < width:
                rest = jnp.zeros((1, width - line.shape[1]), F32)
                line = jnp.concatenate([line, rest], axis=1)
            lines.append(line)
    lines.append(jnp.zeros((TAIL - len(lines), width), F32))
    return jnp.concatenate(lines, axis=0).astype(BF16)


def rows_of(tail, count, length):
    per_row = -(-length // tail.shape[1])
    rows = []
    for r in range(count):
        lines = [tail[r * per_row + i : r * per_row + i + 1, :] for i in range(per_row)]
        rows.append(jnp.concatenate(lines, axis=1)[:, :length])
    return rows


def far_product(place, sources, own_x, xs, gathered, after):
    order, own, got = gathered
    rows, width = own_x.shape[1], own.shape[2]
    whole = lambda d: pl.BlockSpec(d, lambda i, p, s: (0,) * len(d))
    return pl.pallas_call(
        partial(far_kernel, order=order, groups=len(xs)),
        out_shape=shape((rows, width), BF16),
        grid_spec=pltpu.PrefetchScalarGridSpec(
            num_scalar_prefetch=2,
            grid=(1,),
            in_specs=[whole(own_x.shape), ANY, ANY]
            + [whole(x.shape) for x in xs]
            + [ANY for _ in after],
            out_specs=whole((rows, width)),
            scratch_shapes=far_kv_scratch(gathered),
        ),
        compiler_params=PARAMS,
        name="far",
    )(place, sources, own_x, own, got, *xs, *after)


def near_kernel(src_ref, own_x_ref, k_ref, v_ref, q_ref, *rest, groups):
    x_refs, out_ref = rest[:groups], rest[-1]
    step = pl.program_id(0)
    dot = partial(jnp.dot, preferred_element_type=F32)
    column = 0
    for ref in (k_ref, v_ref, q_ref):
        at = slice(column, column + ref.shape[1])

        @pl.when(step == 0)
        def _():
            out_ref[:, at] = dot(own_x_ref[0], ref[...])

        @pl.when(step > 0)
        def _():
            first = 0
            for x_ref in x_refs:
                mine = slice(first, first + x_ref.shape[1])
                out_ref[mine, at] += dot(x_ref[0], ref[...])
                first += x_ref.shape[1]

        column += ref.shape[1]


def near_product(sources, own_x, xs, weights, after):
    count, rows, cols = own_x.shape[0] + xs[0].shape[0], own_x.shape[1], own_x.shape[2]
    widths = [w.shape[1] for w in weights]
    return pl.pallas_call(
        partial(near_kernel, groups=len(xs)),
        out_shape=shape((rows, sum(widths)), F32),
        grid_spec=pltpu.PrefetchScalarGridSpec(
            num_scalar_prefetch=1,
            grid=(count,),
            in_specs=[pl.BlockSpec((1, rows, cols), lambda i, s: (0, 0, 0))]
            + [pl.BlockSpec((cols, w), lambda i, s: (s[i], 0)) for w in widths]
            + [
                pl.BlockSpec((1,) + x.shape[1:], lambda i, s: (jnp.maximum(i - 1, 0), 0, 0))
                for x in xs
            ]
            + [ANY for _ in after],
            out_specs=pl.BlockSpec((rows, sum(widths)), lambda i, s: (0, 0)),
        ),
        compiler_params=PARAMS,
        name="near",
    )(sources, own_x, *weights, *xs, *after)


def keys_kernel(near_ref, id_ref, cos_ref, sin_ref, *rest, model, groups):
    far_refs, sq_refs = rest[:groups], rest[groups : 2 * groups]
    out_ref, sum_ref = rest[-2:]
    rows, width = near_ref.shape[0], out_ref.shape[1]
    keys, values = slice(0, HEAD_SIZE), slice(HEAD_SIZE, 2 * HEAD_SIZE)
    key_parts, value_parts, first = [], [], 0
    for far_ref, sq_ref in zip(far_refs, sq_refs):
        count = sq_ref.shape[1]
        at = slice(first, first + count)
        tail = far_ref[count:, :].astype(F32)
        total = sum(rows_of(tail, 2, count), sq_ref[...])
        factor = to_column(lax.rsqrt(total / model + epsilon))
        sum_ref[:, at] = total
        part = (near_ref[at, keys] + far_ref[:count, keys].astype(F32)) * factor
        key_parts.append(rotate(part, cos_ref[at, :], sin_ref[at, :]).astype(BF16))
        part = (near_ref[at, values] + far_ref[:count, values].astype(F32)) * factor
        value_parts.append(part.T.astype(BF16))
        first += count
    part = jnp.concatenate(key_parts, axis=0)
    out_ref[: rows // 2, keys] = part[: rows // 2]
    out_ref[: rows // 2, values] = part[rows // 2 :]
    part = jnp.concatenate(value_parts, axis=1)
    for i, at in enumerate(range(0, rows, width)):
        row = rows // 2 + i * HEAD_SIZE
        out_ref[row : row + HEAD_SIZE, :] = part[:, at : at + width]
    out_ref[rows:, :] = lines_of((id_ref[...].astype(F32),), width)


def keys_values(near, fars, sqs, ids, cosine, sine, after, model):
    rows, width = near.shape[0], fars[0].shape[1]
    whole = lambda i: (0, 0)
    dims = [(rows + TAIL, width), (1, rows)]
    return pl.pallas_call(
        partial(keys_kernel, model=model, groups=len(fars)),
        out_shape=tuple(shape(d, t) for d, t in zip(dims, (BF16, F32))),
        grid=(1,),
        in_specs=[pl.BlockSpec((rows, width), whole)]
        + [pl.BlockSpec(a.shape, whole) for a in (ids, cosine, sine, *fars, *sqs)]
        + [ANY for _ in after],
        out_specs=[pl.BlockSpec(d, whole) for d in dims],
        compiler_params=PARAMS,
        name="keys",
    )(near, ids, cosine, sine, *fars, *sqs, *after)


def queries_kernel(near_ref, far_ref, sum_ref, cos_ref, sin_ref, out_ref, *, model):
    scale = query_scale * math.log2(math.e)
    factor = to_column(lax.rsqrt(sum_ref[...] / model + epsilon) * scale)
    for c in range(0, out_ref.shape[1], HEAD_SIZE):
        at = slice(c, c + HEAD_SIZE)
        part = (near_ref[:, at] + far_ref[:, at].astype(F32)) * factor
        out_ref[:, at] = rotate(part, cos_ref[...], sin_ref[...]).astype(BF16)


def finished_queries(near, far, sums, cosine, sine, model):
    rows, width = far.shape
    last = near.shape[1] // width - 1
    whole = lambda i: (0, 0)
    return pl.pallas_call(
        partial(queries_kernel, model=model),
        out_shape=shape((rows, width), BF16),
        grid=(1,),
        in_specs=[pl.BlockSpec((rows, width), lambda i: (0, last))]
        + [pl.BlockSpec(a.shape, whole) for a in (far, sums, cosine, sine)],
        out_specs=pl.BlockSpec((rows, width), whole),
        compiler_params=PARAMS,
        cost_estimate=pl.CostEstimate(flops=HIDE, bytes_accessed=10**8, transcendentals=0),
        name="queries",
    )(near, far, sums, cosine, sine)


def attention_kernel(seq_ref, q_ref, id_ref, after_ref, *rest, back, offset):
    kv_refs, (out_ref, k_scr, vt_scr, count_scr) = rest[:-4], rest[-4:]
    part_rows, message = kv_refs[0].shape[0] - TAIL, kv_refs[0].shape[1]
    group = q_ref.shape[1] // HEAD_SIZE
    tile = pl.program_id(0)

    @pl.when(tile == 0)
    def _():
        counts = [jnp.zeros((1, 1), F32) for _ in range(DOCUMENTS)]
        for b, kv_ref in enumerate(kv_refs):
            row, half = b * part_rows, part_rows // 2
            k_scr[row : row + half, :] = kv_ref[:half, :HEAD_SIZE]
            k_scr[row + half : row + part_rows, :] = kv_ref[:half, HEAD_SIZE:]
            for i, at in enumerate(range(0, part_rows, message)):
                first = half + i * HEAD_SIZE
                vt_scr[:, row + at : row + at + message] = kv_ref[first : first + HEAD_SIZE, :]
            (ids,) = rows_of(kv_ref[part_rows:, :].astype(F32), 1, part_rows)
            exists = b >= back - seq_ref[0]
            ids = jnp.where(exists, ids, -1.0)
            for d in range(DOCUMENTS):
                below = (ids < d).astype(F32)
                counts[d] = counts[d] + jnp.sum(below, axis=1, keepdims=True)
        for d in range(DOCUMENTS):
            count_scr[d : d + 1, :] = jnp.broadcast_to(counts[d], (1, LANES))

    heads = [q_ref[:, c : c + HEAD_SIZE] for c in range(0, group * HEAD_SIZE, HEAD_SIZE)]
    q2 = jnp.concatenate(heads, axis=0)
    width = group * Q_TILE

    start = jnp.zeros((1, Q_TILE), F32)
    for d in range(DOCUMENTS):
        start = jnp.where(id_ref[...] == d, count_scr[d : d + 1, :], start)
    start = start.astype(jnp.int32)
    low = jnp.min(start) // K_TILE
    start = jnp.concatenate([start] * group, axis=1)
    first = back * part_rows + offset + tile * Q_TILE
    place = first + lax.broadcasted_iota(jnp.int32, (1, Q_TILE), 1)
    place = jnp.concatenate([place] * group, axis=1)

    def score(j):
        base = pl.multiple_of(j * K_TILE, K_TILE)
        return lax.dot_general(
            k_scr[pl.ds(base, K_TILE), :],
            q2,
            (((1,), (1,)), ((), ())),
            preferred_element_type=F32,
        )

    stop = (first + Q_TILE + K_TILE - 1) // K_TILE

    def step(j, state):
        scores, run_max, run_sum, acc = state
        following = score(jnp.minimum(j + 1, stop - 1))
        base = pl.multiple_of(j * K_TILE, K_TILE)
        key_pos = base + lax.broadcasted_iota(jnp.int32, (K_TILE, width), 0)
        allowed = (key_pos >= start) & (key_pos <= place)
        scores = jnp.where(allowed, scores, NEG)
        new_max = jnp.maximum(run_max, jnp.max(scores, axis=0, keepdims=True))
        expo = jnp.exp2(scores - new_max)
        factor = jnp.exp2(run_max - new_max)
        run_sum = run_sum * factor + jnp.sum(expo, axis=0, keepdims=True)
        acc = acc * factor + jnp.dot(
            vt_scr[:, pl.ds(base, K_TILE)], expo.astype(BF16), preferred_element_type=F32
        )
        return following, new_max, run_sum, acc

    state = (
        score(low),
        jnp.full((1, width), NEG, F32),
        jnp.zeros((1, width), F32),
        jnp.zeros((HEAD_SIZE, width), F32),
    )
    _, _, run_sum, acc = lax.fori_loop(low, stop, step, state)
    context = (acc / run_sum).T
    for g in range(group):
        out_ref[:, g * HEAD_SIZE : (g + 1) * HEAD_SIZE] = context[
            g * Q_TILE : (g + 1) * Q_TILE
        ].astype(BF16)


def attend(seq, queries, ids, after, blocks, c):
    rows, width = queries.shape[0] // CHUNKS, queries.shape[1]
    back = len(blocks) - 1
    tiles = rows // Q_TILE
    keys = len(blocks) * queries.shape[0]
    return pl.pallas_call(
        partial(attention_kernel, back=back, offset=c * rows),
        out_shape=shape((rows, width), BF16),
        grid_spec=pltpu.PrefetchScalarGridSpec(
            num_scalar_prefetch=1,
            grid=(tiles,),
            in_specs=[
                pl.BlockSpec((Q_TILE, width), lambda i, s: (c * tiles + i, 0)),
                pl.BlockSpec((1, Q_TILE), lambda i, s: (0, c * tiles + i)),
                ANY,
            ]
            + [pl.BlockSpec(b.shape, lambda i, s: (0, 0)) for b in blocks],
            out_specs=pl.BlockSpec((Q_TILE, width), lambda i, s: (i, 0)),
            scratch_shapes=[
                pltpu.VMEM((keys, HEAD_SIZE), BF16),
                pltpu.VMEM((HEAD_SIZE, keys), BF16),
                pltpu.VMEM((DOCUMENTS, LANES), F32),
            ],
        ),
        compiler_params=PARAMS,
        cost_estimate=pl.CostEstimate(
            flops=4 * rows * width * keys,
            bytes_accessed=4 * keys * width,
            transcendentals=rows * keys * width // HEAD_SIZE,
        ),
        name="attend",
    )(seq, queries, ids, after, *blocks)


def first_output_kernel(at_ref, own_o_ref, o_ref, *rest):
    ctx_refs, out_ref = rest[:-2], rest[-1]
    total = jnp.dot(ctx_refs[0][...], own_o_ref[...], preferred_element_type=F32)
    for i, ctx_ref in enumerate(ctx_refs[1:]):
        total = total + jnp.dot(ctx_ref[...], o_ref[at_ref[1 + i]], preferred_element_type=F32)
    out_ref[...] = total


def last_output_kernel(at_ref, part_ref, o_ref, *rest):
    ctx_refs, (before_ref, out_ref, sq_ref, acc) = rest[:-4], rest[-4:]
    step = pl.program_id(0)
    total = part_ref[...]
    for i, ctx_ref in enumerate(ctx_refs):
        total = total + jnp.dot(ctx_ref[...], o_ref[at_ref[i]], preferred_element_type=F32)
    out_ref[...] = total
    squares = jnp.sum(total * total, axis=1, keepdims=True)
    squares = jnp.broadcast_to(squares, acc.shape)

    @pl.when(step == 0)
    def _():
        acc[...] = squares

    @pl.when(step > 0)
    def _():
        acc[...] += squares

    @pl.when(step == pl.num_programs(0) - 1)
    def _():
        done = sq_ref.shape[1] - acc.shape[0]
        if done:
            sq_ref[:, :done] = before_ref[...]
        sq_ref[:, done:] = acc[...].T[0:1, :]


def column_tiles(cols):
    tiles = 3 if cols % (3 * LANES) == 0 else 1
    return tiles, cols // tiles


def first_output(column, order, o_weight, gathered, contexts, after):
    chunk, width = contexts[0].shape
    others, _, cols = gathered.shape
    tiles, tile = column_tiles(cols)
    if cols % LANES:
        o_weight = lax.dynamic_slice_in_dim(o_weight, column * cols, cols, axis=1)
        column = jnp.int32(0)
    return pl.pallas_call(
        first_output_kernel,
        out_shape=shape((chunk, cols), F32),
        grid_spec=pltpu.PrefetchScalarGridSpec(
            num_scalar_prefetch=1,
            grid=(tiles,),
            in_specs=[
                pl.BlockSpec((width, tile), lambda i, at: (0, at[0] * tiles + i)),
                pl.BlockSpec((others, width, tile), lambda i, at: (0, 0, i)),
            ]
            + [pl.BlockSpec((chunk, width), lambda i, at: (0, 0)) for _ in contexts]
            + [ANY],
            out_specs=pl.BlockSpec((chunk, tile), lambda i, at: (0, i)),
        ),
        compiler_params=PARAMS,
        cost_estimate=pl.CostEstimate(flops=HIDE, bytes_accessed=10**8, transcendentals=0),
        name="first_output",
    )(jnp.stack([column] + order), o_weight, gathered, *contexts, after)


def last_output(order, part, gathered, contexts, before, c):
    chunk, width = contexts[0].shape
    others, _, cols = gathered.shape
    tiles, tile = column_tiles(cols)
    return pl.pallas_call(
        last_output_kernel,
        out_shape=(shape((chunk, cols), F32), shape((1, (c + 1) * chunk), F32)),
        grid_spec=pltpu.PrefetchScalarGridSpec(
            num_scalar_prefetch=1,
            grid=(tiles,),
            in_specs=[
                pl.BlockSpec((chunk, tile), lambda i, at: (0, i)),
                pl.BlockSpec((others, width, tile), lambda i, at: (0, 0, i)),
            ]
            + [pl.BlockSpec((chunk, width), lambda i, at: (0, 0)) for _ in contexts]
            + [pl.BlockSpec(before.shape, lambda i, at: (0, 0))],
            out_specs=[
                pl.BlockSpec((chunk, tile), lambda i, at: (0, i)),
                pl.BlockSpec((1, (c + 1) * chunk), lambda i, at: (0, 0)),
            ],
            scratch_shapes=[pltpu.VMEM((chunk, LANES), F32)],
        ),
        compiler_params=PARAMS,
        name="last_output",
    )(jnp.stack(order), part, gathered, *contexts, before)


def final_kernel(token_ref, gain_ref, *rest, model):
    branch_refs, sq_refs, out_ref = rest[:CHUNKS], rest[CHUNKS:-1], rest[-1]
    total = sq_refs[0][...]
    for sq_ref in sq_refs[1:]:
        total = total + sq_ref[...]
    factor = to_column(lax.rsqrt(total / model + epsilon))[:, 0:1]
    for c in range(CHUNKS):

        @pl.when(pl.program_id(0) * CHUNKS // pl.num_programs(0) == c)
        def _():
            out = token_ref[...].astype(F32) + branch_refs[c][...] * factor * gain_ref[...]
            out_ref[...] = out.astype(BF16)


def finish(tokens, branches, out_gain, sums, model):
    rows, cols = tokens.shape
    tiles = rows // CHUNKS // Q_TILE
    held = lambda c: lambda i: (jnp.clip(i - c * tiles, 0, tiles - 1), 0)
    return pl.pallas_call(
        partial(final_kernel, model=model),
        out_shape=shape(tokens.shape, BF16),
        grid=(CHUNKS * tiles,),
        in_specs=[
            pl.BlockSpec((Q_TILE, cols), lambda i: (i, 0)),
            pl.BlockSpec((1, cols), lambda i: (0, 0)),
        ]
        + [pl.BlockSpec((Q_TILE, cols), held(c)) for c in range(CHUNKS)]
        + [pl.BlockSpec((1, Q_TILE), lambda i: (0, i)) for _ in sums],
        out_specs=pl.BlockSpec((Q_TILE, cols), lambda i: (i, 0)),
        compiler_params=PARAMS,
        name="finish",
    )(tokens, out_gain, *branches, *sums)


def per_device(
    tokens, seg_ids, in_gain, q_weight, k_weight, value_weight, o_weight, out_gain, *, sizes
):
    rows, cols = tokens.shape
    model = in_gain.shape[0]
    nz, nseq = sizes["tensor"], sizes["seq"]
    plane = nseq * sizes["groups"]
    z = lax.axis_index("tensor")
    seq = lax.axis_index("seq")
    in_plane = lax.axis_index(PLANE)
    half = nz // 2
    side, within = z // half, z % half
    half_rows = half * cols

    ring = [(i, i // half * half + (i + 1) % half) for i in range(nz)]
    swap = [(i, (i + half) % nz) for i in range(nz)]
    turn = lambda k: [(i, (i + k) % nz) for i in range(nz)]
    seq_bits = [1 << b for b in range(1, nseq.bit_length() - 1)]
    group_bits = [nseq << b for b in range(sizes["groups"].bit_length() - 1)]

    share = half_rows // plane
    at = jnp.reshape((1 - side) * plane + in_plane, (1,))
    inner = seq_bits + group_bits
    masks_kv, masks_q = inner + [1], inner[::-1] + [1]
    last = len(masks_kv) - 1
    eighth = rows // 48 * 8
    counts = [eighth, rows // 2 - eighth, rows // 2]
    packed_kv, packed_q, cut = pack(
        at, q_weight, k_weight, value_weight, share, tokens, counts[0]
    )
    own_kv = lax.ppermute(packed_kv, "tensor", swap)[None]
    own_q = lax.ppermute(packed_q, "tensor", swap)[None]
    received = [lax.ppermute(cut, "tensor", ring)]
    o_share = o_weight.shape[0] // plane
    columns = [(z + k) % nz * cols for k in range(1, nz)]
    pieces = cut_pieces(in_plane * o_share, columns, o_weight, o_share, cols, own_kv)
    moved = [lax.ppermute(p, "tensor", turn(k + 1)) for k, p in enumerate(pieces)]

    order_kv, order_q, first = [0], [0], counts[0]
    for step, (mask_kv, mask_q) in enumerate(zip(masks_kv, masks_q)):
        after, count = [], 0
        if step == 0:
            pairs, after = [], [own_kv, own_q, received[0]]
        else:
            pairs = [(own_kv, far_kv), (own_q, far_q)]
        if step < 2:
            count = counts[1 + step]
        if step == last:
            after = [received[1]]
        outs = stage(pairs, tokens, first, count, after, HIDE if step == last else 0)
        if pairs:
            own_kv, own_q = outs[:2]
        if count:
            received.append(lax.ppermute(outs[-1], "tensor", ring))
        first += count
        far_kv = lax.ppermute(own_kv, PLANE, [(i, i ^ mask_kv) for i in range(plane)])
        far_q = lax.ppermute(own_q, PLANE, [(i, i ^ mask_q) for i in range(plane)])
        order_kv = order_kv + [k ^ mask_kv for k in order_kv]
        order_q = order_q + [k ^ mask_q for k in order_q]
    far_kv, far_q = (order_kv, own_kv, far_kv), (order_q, own_q, far_q)

    own_o = jnp.stack(moved)[None]

    def double(own, step, after):
        if step > 0:
            (own,) = stage([own], tokens, 0, 0, after)
        return own, lax.ppermute(own, PLANE, [(i, i ^ masks_kv[step]) for i in range(plane)])

    sources = (within + half - jnp.arange(half, dtype=jnp.int32)) % half
    gains = in_gain.reshape(nz, 1, cols)
    place = jnp.stack([in_plane, side * half])
    own_x, own_sq, part = far_own_product(place, sources, gains, tokens, far_kv)
    received[-1] = gate(received[-1], own_sq)
    weights = (k_weight, value_weight, q_weight)
    pair_o = double(own_o, 0, [])
    for step in range(1, last - 1):
        pair_o = double(pair_o, step, [])
    xs, sqs, got_kv, first, after = [], [], [], 0, [far_q[2]]
    for pieces in (received[:2], received[2:]):
        blocks = [pieces]
        for _ in range(half - 2):
            blocks.append([lax.ppermute(block, "tensor", ring) for block in blocks[-1]])
        sent_kv, x, sq = far_kv_product(
            place, sources, gains, part, own_sq, first, blocks, far_kv, after
        )
        xs.append(x)
        sqs.append(sq)
        got_kv.append(lax.ppermute(sent_kv, "tensor", swap))
        first, after = first + x.shape[1], [sent_kv]

    sent_q = far_product(place, sources, own_x, xs, far_q, [sent_kv, got_kv[0]])
    got_q = lax.ppermute(gate(sent_q, got_kv[1]), "tensor", swap)
    near = near_product(side * half + sources, own_x, xs, weights, [sent_q])
    pair_o = double(pair_o, last - 1, [sent_q])
    cosine, sine = rotation_table(seq * rows + jnp.arange(rows, dtype=jnp.int32))
    ids = seg_ids[None, :]
    own_kv, sums = keys_values(
        near, got_kv, sqs, ids, cosine, sine, [sent_q, pair_o[0]], model
    )
    pair_o = double(pair_o, last, [own_kv])
    gathered_o = lay_pieces(place, order_kv, *pair_o)

    back = -(-(nseq * rows // 2 - 1) // rows)
    kv_blocks = [own_kv]
    for k in range(1, back + 1):
        earlier = [(i, i + k) for i in range(nseq - k)]
        kv_blocks.insert(0, lax.ppermute(own_kv, "seq", earlier))

    queries = finished_queries(near, got_q, sums, cosine, sine, model)
    seq_at = jnp.reshape(seq, (1,))
    contexts, after = [], own_kv
    for c in range(CHUNKS):
        contexts.append(attend(seq_at, queries, ids, after, kv_blocks, c))
        after = gathered_o
    early, late = [], []
    for c, context in enumerate(contexts):
        if nz == 4:
            pairs = [(i, i ^ 1) for i in range(nz)]
            opposite = lax.ppermute(context, "tensor", swap)
            beside = lax.ppermute(context, "tensor", pairs)
            if c + 1 < CHUNKS:
                opposite = gate(opposite, contexts[c + 1])
            across = lax.ppermute(opposite, "tensor", pairs)
            early.append([context, beside])
            late.append([opposite, across])
            order = [2 - 2 * (z % 2), jnp.int32(1), 2 * (z % 2)]
        else:
            early.append([context])
            late.append([lax.ppermute(context, "tensor", turn(k)) for k in range(1, nz)])
            order = [jnp.int32(k) for k in range(nz - 1)]
    split = len(early[0]) - 1
    branches, own_sq = [], sums
    for c in range(CHUNKS):
        part = first_output(z, order[:split], o_weight, gathered_o, early[c], contexts[-1])
        branch, own_sq = last_output(order[split:], part, gathered_o, late[c], own_sq, c)
        branches.append(branch)
    squares = [own_sq]
    squares += [lax.ppermute(own_sq, "tensor", turn(k)) for k in range(1, nz)]
    return finish(tokens, branches, out_gain[None, :], squares, model)


def solution(mesh):
    return jax.shard_map(
        partial(per_device, sizes=dict(mesh.shape)),
        mesh=mesh,
        in_specs=(
            P(("groups", "seq"), "tensor"),
            P(("groups", "seq")),
            P(),
            P(None, "tensor"),
            P(None, "tensor"),
            P(None, "tensor"),
            P("tensor", None),
            P("tensor"),
        ),
        out_specs=P(("groups", "seq"), "tensor"),
        check_vma=False,
    )
```

```python
import math
from functools import partial

import jax
import jax.numpy as jnp
from jax import lax
from jax.experimental import pallas as pl
from jax.experimental.pallas import tpu as pltpu
from jax.sharding import PartitionSpec as P

HEAD_SIZE = 128
PLANE = ("groups", "seq")

epsilon = 1e-06
query_scale = 144.0 ** (-0.5)
rope_base = 10000.0
NEG = -1e30
Q_TILE = 128
K_TILE = 256
CHUNKS = 2
LANES = 128
TAIL = 16
F32, BF16 = jnp.float32, jnp.bfloat16
ANY = pl.BlockSpec(memory_space=pl.ANY)
HBM = pl.BlockSpec(memory_space=pltpu.HBM)
VMEM = pl.BlockSpec(memory_space=pltpu.VMEM)
DOCUMENTS = 8
HIDE = 5 * 10**10
PARAMS = pltpu.CompilerParams(vmem_limit_bytes=48 * 1024 * 1024)
ALL_VMEM = pltpu.CompilerParams(vmem_limit_bytes=62 * 1024 * 1024)


def shape(dims, dtype):
    return jax.ShapeDtypeStruct(dims, dtype)


def to_row(column):
    return jnp.broadcast_to(column, (column.shape[0], LANES)).T[0:1, :]


def to_column(row):
    return jnp.broadcast_to(row, (LANES, row.shape[1])).T


def rotation_table(token_places):
    half_dim = HEAD_SIZE // 2
    inverse = rope_base ** (-jnp.arange(half_dim, dtype=F32) / half_dim)
    angles = token_places.astype(F32)[:, None] * inverse[None, :]
    cosine, sine = jnp.cos(angles), jnp.sin(angles)
    return jnp.concatenate([cosine, cosine], 1), jnp.concatenate([-sine, sine], 1)


def rotate(vectors, cosine, sine):
    return vectors * cosine + pltpu.roll(vectors, HEAD_SIZE // 2, 1) * sine


def pack_kernel(at_ref, q_ref, k_ref, v_ref, x_ref, kv_out, q_out, x_out, sems):
    share, width = q_out.shape[0], k_ref.shape[1]
    rows = pl.ds(pl.multiple_of(at_ref[0] * share, TAIL), share)
    copies = [
        pltpu.make_async_copy(k_ref.at[rows], kv_out.at[:, pl.ds(0, width)], sems.at[0]),
        pltpu.make_async_copy(v_ref.at[rows], kv_out.at[:, pl.ds(width, width)], sems.at[1]),
        pltpu.make_async_copy(q_ref.at[rows], q_out, sems.at[2]),
        pltpu.make_async_copy(x_ref.at[pl.ds(0, x_out.shape[0])], x_out, sems.at[3]),
    ]
    for copy in copies:
        copy.start()
    for copy in copies:
        copy.wait()


def pack(at, q_weight, k_weight, v_weight, share, tokens, rows):
    kv_width = k_weight.shape[1] + v_weight.shape[1]
    dims = [(share, kv_width), (share, q_weight.shape[1]), (rows, tokens.shape[1])]
    return pl.pallas_call(
        pack_kernel,
        out_shape=tuple(shape(d, BF16) for d in dims),
        grid_spec=pltpu.PrefetchScalarGridSpec(
            num_scalar_prefetch=1,
            grid=(1,),
            in_specs=[HBM, HBM, HBM, HBM],
            out_specs=[pl.BlockSpec(d, lambda i, at: (0, 0)) for d in dims],
            scratch_shapes=[pltpu.SemaphoreType.DMA((4,))],
        ),
        compiler_params=ALL_VMEM,
        name="pack",
    )(at, q_weight, k_weight, v_weight, tokens)


def gate_kernel(x_ref, after_ref, out_ref):
    pass


def gate(x, after):
    return pl.pallas_call(
        gate_kernel,
        out_shape=shape(x.shape, x.dtype),
        in_specs=[ANY, ANY],
        out_specs=ANY,
        input_output_aliases={0: 0},
        compiler_params=PARAMS,
        name="gate",
    )(x, after)


def stage_kernel(*refs, pairs, first, count):
    outputs = pairs + (1 if count else 0)
    ins, outs, sems = refs[: -outputs - 1], refs[-outputs - 1 : -1], refs[-1]
    copies = []
    for p in range(pairs):
        held = ins[2 * p].shape[0]
        for side in range(2):
            there = outs[p].at[pl.ds(side * held, held)]
            copies.append(
                pltpu.make_async_copy(ins[2 * p + side], there, sems.at[len(copies)])
            )
    if count:
        rows = ins[2 * pairs].at[pl.ds(first, count)]
        copies.append(pltpu.make_async_copy(rows, outs[-1], sems.at[len(copies)]))
    for copy in copies:
        copy.start()
    for copy in copies:
        copy.wait()


def stage(joined, tokens, first, count, after, flops=0):
    dims = [(2 * pair[0].shape[0],) + pair[0].shape[1:] for pair in joined]
    if count:
        dims.append((count, tokens.shape[1]))
    return pl.pallas_call(
        partial(stage_kernel, pairs=len(joined), first=first, count=count),
        out_shape=tuple(shape(d, BF16) for d in dims),
        in_specs=[ANY] * (2 * len(joined) + 1 + len(after)),
        scratch_shapes=[pltpu.SemaphoreType.DMA((2 * len(joined) + 1,))],
        compiler_params=PARAMS,
        cost_estimate=pl.CostEstimate(flops=flops, bytes_accessed=flops // 500, transcendentals=0),
        name="stage",
    )(*[piece for pair in joined for piece in pair], tokens, *after)


def cut_kernel(at_ref, o_ref, after_ref, *rest):
    outs, sems = rest[:-1], rest[-1]
    copies = []
    for i, out in enumerate(outs):
        rows = pl.ds(pl.multiple_of(at_ref[0], TAIL), out.shape[0])
        columns = pl.ds(pl.multiple_of(at_ref[1 + i], LANES), out.shape[1])
        copies.append(pltpu.make_async_copy(o_ref.at[rows, columns], out, sems.at[i]))
    for copy in copies:
        copy.start()
    for copy in copies:
        copy.wait()


def cut_pieces(row, columns, o_weight, share, cols, after):
    if cols % LANES:
        return [lax.dynamic_slice(o_weight, (row, c), (share, cols)) for c in columns]
    return pl.pallas_call(
        cut_kernel,
        out_shape=tuple(shape((share, cols), BF16) for _ in columns),
        grid_spec=pltpu.PrefetchScalarGridSpec(
            num_scalar_prefetch=1,
            grid=(1,),
            in_specs=[ANY, ANY],
            out_specs=[VMEM for _ in columns],
            scratch_shapes=[pltpu.SemaphoreType.DMA((len(columns),))],
        ),
        compiler_params=PARAMS,
        name="cut",
    )(jnp.stack([row] + columns), o_weight, after)


def lay_kernel(place_ref, own_ref, got_ref, out_ref, sems, *, order):
    held, others, share, _ = own_ref.shape
    copies = []
    for i, mask in enumerate(order):
        piece = own_ref.at[i] if i < held else got_ref.at[i - held]
        row = pl.multiple_of((place_ref[0] ^ mask) * share, TAIL)
        there = out_ref.at[:, pl.ds(row, share)]
        copies.append(pltpu.make_async_copy(piece, there, sems.at[i]))
    for copy in copies:
        copy.start()
    for copy in copies:
        copy.wait()


def lay_pieces(place, order, own, got):
    _, others, share, cols = own.shape
    dims = (others, len(order) * share, cols)
    return pl.pallas_call(
        partial(lay_kernel, order=order),
        out_shape=shape(dims, BF16),
        grid_spec=pltpu.PrefetchScalarGridSpec(
            num_scalar_prefetch=1,
            grid=(1,),
            in_specs=[ANY, ANY],
            out_specs=pl.BlockSpec(dims, lambda i, p: (0, 0, 0)),
            scratch_shapes=[pltpu.SemaphoreType.DMA((len(order),))],
        ),
        compiler_params=PARAMS,
        name="lay",
    )(place, own, got)


def place_weights(place_ref, own_ref, got_ref, weight, sems, order):
    held, share, _ = own_ref.shape
    copies = []
    for i, mask in enumerate(order):
        piece = own_ref.at[i] if i < held else got_ref.at[i - held]
        row = pl.multiple_of((place_ref[0] ^ mask) * share, TAIL)
        there = weight.at[pl.ds(row, share)]
        copies.append(pltpu.make_async_copy(piece, there, sems.at[i]))
    for copy in copies:
        copy.start()
    return copies


def far_sum(src_ref, first, x_ref, weight):
    count, _, cols = x_ref.shape
    total = None
    for k in range(count):
        row = pl.multiple_of(src_ref[first + k] * cols, TAIL)
        term = jnp.dot(x_ref[k], weight[pl.ds(row, cols), :], preferred_element_type=F32)
        total = term if total is None else total + term
    return total


def prepare(x_refs, gain, x_out, k):
    column, row = [], 0
    for x_ref in x_refs:
        x = x_ref[...].astype(F32)
        column.append(jnp.sum(x * x, axis=1, keepdims=True))
        x_out[k, row : row + x.shape[0]] = (x * gain).astype(BF16)
        row += x.shape[0]
    return jnp.concatenate(column, axis=0)


def far_own_kernel(
    place_ref, src_ref, gain_ref, own_ref, got_ref, x_ref, x_out, sq_ref, out_ref, weight, sems,
    *, order
):
    copies = place_weights(place_ref, own_ref, got_ref, weight, sems, order)
    gain = gain_ref[place_ref[1] + src_ref[0]]
    sq_ref[...] = to_row(prepare([x_ref], gain, x_out, 0))
    for copy in copies:
        copy.wait()
    out_ref[...] = far_sum(src_ref, 0, x_out, weight)


def far_kv_kernel(
    place_ref, src_ref, gain_ref, part_ref, own_sq_ref, own_ref, got_ref, *rest, order, cuts
):
    x_refs, (out_ref, x_out, sq_ref, weight, sems) = rest[: sum(cuts)], rest[-5:]
    copies = place_weights(place_ref, own_ref, got_ref, weight, sems, order)
    rows = x_out.shape[1]
    columns, at = [], 0
    for k, pieces in enumerate(cuts):
        gain = gain_ref[place_ref[1] + src_ref[1 + k]]
        columns.append(prepare(x_refs[at : at + pieces], gain, x_out, k))
        at += pieces
    sq = to_row(sum(columns[1:], columns[0])) + own_sq_ref[...]
    sq_ref[...] = sq
    for copy in copies:
        copy.wait()
    total = part_ref[...] + far_sum(src_ref, 1, x_out, weight)
    out_ref[:rows, :] = total.astype(BF16)
    high = sq.astype(BF16).astype(F32)
    out_ref[rows:, :] = lines_of((high, sq - high), out_ref.shape[1])


def far_kv_scratch(gathered):
    order, own, _ = gathered
    return [
        pltpu.VMEM((len(order) * own.shape[1], own.shape[2]), BF16),
        pltpu.SemaphoreType.DMA((len(order),)),
    ]


def far_own_product(place, sources, gains, tokens, gathered):
    order, own, got = gathered
    rows, cols = tokens.shape
    dims = [(1, rows, cols), (1, rows), (rows, own.shape[2])]
    whole = lambda d: pl.BlockSpec(d, lambda i, p, s: (0,) * len(d))
    return pl.pallas_call(
        partial(far_own_kernel, order=order),
        out_shape=tuple(shape(d, t) for d, t in zip(dims, (BF16, F32, F32))),
        grid_spec=pltpu.PrefetchScalarGridSpec(
            num_scalar_prefetch=2,
            grid=(1,),
            in_specs=[whole(gains.shape), ANY, ANY, whole(tokens.shape)],
            out_specs=[whole(d) for d in dims],
            scratch_shapes=far_kv_scratch(gathered),
        ),
        compiler_params=PARAMS,
        name="far_own",
    )(place, sources, gains, own, got, tokens)


def far_kv_product(place, sources, gains, part, own_sq, blocks, gathered, after):
    order, own, got = gathered
    rows, width = part.shape
    cols = blocks[0][0].shape[1]
    pieces = [piece for block in blocks for piece in block]
    dims = [(rows + TAIL, width), (len(blocks), rows, cols), (1, rows)]
    whole = lambda d: pl.BlockSpec(d, lambda i, p, s: (0,) * len(d))
    return pl.pallas_call(
        partial(far_kv_kernel, order=order, cuts=[len(block) for block in blocks]),
        out_shape=tuple(shape(d, t) for d, t in zip(dims, (BF16, BF16, F32))),
        grid_spec=pltpu.PrefetchScalarGridSpec(
            num_scalar_prefetch=2,
            grid=(1,),
            in_specs=[whole(gains.shape), whole(part.shape), whole(own_sq.shape), ANY, ANY]
            + [whole(piece.shape) for piece in pieces]
            + [ANY for _ in after],
            out_specs=[whole(d) for d in dims],
            scratch_shapes=far_kv_scratch(gathered),
        ),
        compiler_params=PARAMS,
        name="far_kv",
    )(place, sources, gains, part, own_sq, own, got, *pieces, *after)


def far_kernel(place_ref, src_ref, own_x_ref, x_ref, own_ref, got_ref, *rest, order):
    out_ref, weight, sems = rest[-3:]
    for copy in place_weights(place_ref, own_ref, got_ref, weight, sems, order):
        copy.wait()
    total = far_sum(src_ref, 0, own_x_ref, weight) + far_sum(src_ref, 1, x_ref, weight)
    out_ref[...] = total.astype(BF16)


def lines_of(rows, width):
    lines = []
    for row in rows:
        for at in range(0, row.shape[1], width):
            line = row[:, at : at + width]
            if line.shape[1] < width:
                rest = jnp.zeros((1, width - line.shape[1]), F32)
                line = jnp.concatenate([line, rest], axis=1)
            lines.append(line)
    lines.append(jnp.zeros((TAIL - len(lines), width), F32))
    return jnp.concatenate(lines, axis=0).astype(BF16)


def rows_of(tail, count, length):
    per_row = -(-length // tail.shape[1])
    rows = []
    for r in range(count):
        lines = [tail[r * per_row + i : r * per_row + i + 1, :] for i in range(per_row)]
        rows.append(jnp.concatenate(lines, axis=1)[:, :length])
    return rows


def far_product(place, sources, own_x, x, gathered, after):
    order, own, got = gathered
    rows, width = x.shape[1], own.shape[2]
    return pl.pallas_call(
        partial(far_kernel, order=order),
        out_shape=shape((rows, width), BF16),
        grid_spec=pltpu.PrefetchScalarGridSpec(
            num_scalar_prefetch=2,
            grid=(1,),
            in_specs=[
                pl.BlockSpec(own_x.shape, lambda i, p, s: (0, 0, 0)),
                pl.BlockSpec(x.shape, lambda i, p, s: (0, 0, 0)),
                ANY,
                ANY,
            ]
            + [ANY for _ in after],
            out_specs=pl.BlockSpec((rows, width), lambda i, p, s: (0, 0)),
            scratch_shapes=far_kv_scratch(gathered),
        ),
        compiler_params=PARAMS,
        name="far",
    )(place, sources, own_x, x, own, got, *after)


def near_kernel(src_ref, own_x_ref, x_ref, k_ref, v_ref, q_ref, *rest):
    out_ref = rest[-1]
    step = pl.program_id(0)
    dot = partial(jnp.dot, preferred_element_type=F32)
    column = 0
    for ref in (k_ref, v_ref, q_ref):
        at = slice(column, column + ref.shape[1])

        @pl.when(step == 0)
        def _():
            out_ref[:, at] = dot(own_x_ref[0], ref[...])

        @pl.when(step > 0)
        def _():
            out_ref[:, at] += dot(x_ref[0], ref[...])

        column += ref.shape[1]


def near_product(sources, own_x, x, weights, after):
    count, rows, cols = x.shape
    widths = [w.shape[1] for w in weights]
    return pl.pallas_call(
        near_kernel,
        out_shape=shape((rows, sum(widths)), F32),
        grid_spec=pltpu.PrefetchScalarGridSpec(
            num_scalar_prefetch=1,
            grid=(count + 1,),
            in_specs=[
                pl.BlockSpec((1, rows, cols), lambda i, s: (0, 0, 0)),
                pl.BlockSpec((1, rows, cols), lambda i, s: (jnp.maximum(i - 1, 0), 0, 0)),
            ]
            + [pl.BlockSpec((cols, w), lambda i, s: (s[i], 0)) for w in widths]
            + [ANY for _ in after],
            out_specs=pl.BlockSpec((rows, sum(widths)), lambda i, s: (0, 0)),
        ),
        compiler_params=PARAMS,
        name="near",
    )(sources, own_x, x, *weights, *after)


def keys_kernel(near_ref, far_ref, sq_ref, id_ref, cos_ref, sin_ref, *rest, model):
    out_ref, sum_ref = rest[-2:]
    rows, width = near_ref.shape[0], far_ref.shape[1]
    tail = far_ref[rows:, :].astype(F32)
    total = sum(rows_of(tail, 2, rows), sq_ref[...])
    factor = to_column(lax.rsqrt(total / model + epsilon))
    sum_ref[...] = total
    keys, values = slice(0, HEAD_SIZE), slice(HEAD_SIZE, 2 * HEAD_SIZE)
    part = (near_ref[:, keys] + far_ref[:rows, keys].astype(F32)) * factor
    part = rotate(part, cos_ref[...], sin_ref[...]).astype(BF16)
    out_ref[: rows // 2, keys] = part[: rows // 2]
    out_ref[: rows // 2, values] = part[rows // 2 :]
    part = (near_ref[:, values] + far_ref[:rows, values].astype(F32)) * factor
    part = part.T.astype(BF16)
    for i, at in enumerate(range(0, rows, width)):
        row = rows // 2 + i * HEAD_SIZE
        out_ref[row : row + HEAD_SIZE, :] = part[:, at : at + width]
    out_ref[rows:, :] = lines_of((id_ref[...].astype(F32),), width)


def keys_values(near, far, sq, ids, cosine, sine, after, model):
    rows, width = near.shape[0], far.shape[1]
    whole = lambda i: (0, 0)
    return pl.pallas_call(
        partial(keys_kernel, model=model),
        out_shape=(shape(far.shape, BF16), shape(sq.shape, F32)),
        grid=(1,),
        in_specs=[pl.BlockSpec((rows, width), whole)]
        + [pl.BlockSpec(a.shape, whole) for a in (far, sq, ids, cosine, sine)]
        + [ANY for _ in after],
        out_specs=[pl.BlockSpec(far.shape, whole), pl.BlockSpec(sq.shape, whole)],
        compiler_params=PARAMS,
        name="keys",
    )(near, far, sq, ids, cosine, sine, *after)


def queries_kernel(near_ref, far_ref, sum_ref, cos_ref, sin_ref, out_ref, *, model):
    scale = query_scale * math.log2(math.e)
    factor = to_column(lax.rsqrt(sum_ref[...] / model + epsilon) * scale)
    for c in range(0, out_ref.shape[1], HEAD_SIZE):
        at = slice(c, c + HEAD_SIZE)
        part = (near_ref[:, at] + far_ref[:, at].astype(F32)) * factor
        out_ref[:, at] = rotate(part, cos_ref[...], sin_ref[...]).astype(BF16)


def finished_queries(near, far, sums, cosine, sine, model):
    rows, width = far.shape
    last = near.shape[1] // width - 1
    whole = lambda i: (0, 0)
    return pl.pallas_call(
        partial(queries_kernel, model=model),
        out_shape=shape((rows, width), BF16),
        grid=(1,),
        in_specs=[pl.BlockSpec((rows, width), lambda i: (0, last))]
        + [pl.BlockSpec(a.shape, whole) for a in (far, sums, cosine, sine)],
        out_specs=pl.BlockSpec((rows, width), whole),
        compiler_params=PARAMS,
        cost_estimate=pl.CostEstimate(flops=HIDE, bytes_accessed=10**8, transcendentals=0),
        name="queries",
    )(near, far, sums, cosine, sine)


def attention_kernel(seq_ref, q_ref, id_ref, after_ref, *rest, back, offset):
    kv_refs, (out_ref, k_scr, vt_scr, count_scr) = rest[:-4], rest[-4:]
    part_rows, message = kv_refs[0].shape[0] - TAIL, kv_refs[0].shape[1]
    group = q_ref.shape[1] // HEAD_SIZE
    tile = pl.program_id(0)

    @pl.when(tile == 0)
    def _():
        counts = [jnp.zeros((1, 1), F32) for _ in range(DOCUMENTS)]
        for b, kv_ref in enumerate(kv_refs):
            row, half = b * part_rows, part_rows // 2
            k_scr[row : row + half, :] = kv_ref[:half, :HEAD_SIZE]
            k_scr[row + half : row + part_rows, :] = kv_ref[:half, HEAD_SIZE:]
            for i, at in enumerate(range(0, part_rows, message)):
                first = half + i * HEAD_SIZE
                vt_scr[:, row + at : row + at + message] = kv_ref[first : first + HEAD_SIZE, :]
            (ids,) = rows_of(kv_ref[part_rows:, :].astype(F32), 1, part_rows)
            exists = b >= back - seq_ref[0]
            ids = jnp.where(exists, ids, -1.0)
            for d in range(DOCUMENTS):
                below = (ids < d).astype(F32)
                counts[d] = counts[d] + jnp.sum(below, axis=1, keepdims=True)
        for d in range(DOCUMENTS):
            count_scr[d : d + 1, :] = jnp.broadcast_to(counts[d], (1, LANES))

    heads = [q_ref[:, c : c + HEAD_SIZE] for c in range(0, group * HEAD_SIZE, HEAD_SIZE)]
    q2 = jnp.concatenate(heads, axis=0)
    width = group * Q_TILE

    start = jnp.zeros((1, Q_TILE), F32)
    for d in range(DOCUMENTS):
        start = jnp.where(id_ref[...] == d, count_scr[d : d + 1, :], start)
    start = start.astype(jnp.int32)
    low = jnp.min(start) // K_TILE
    start = jnp.concatenate([start] * group, axis=1)
    first = back * part_rows + offset + tile * Q_TILE
    place = first + lax.broadcasted_iota(jnp.int32, (1, Q_TILE), 1)
    place = jnp.concatenate([place] * group, axis=1)

    def score(j):
        base = pl.multiple_of(j * K_TILE, K_TILE)
        return lax.dot_general(
            k_scr[pl.ds(base, K_TILE), :],
            q2,
            (((1,), (1,)), ((), ())),
            preferred_element_type=F32,
        )

    stop = (first + Q_TILE + K_TILE - 1) // K_TILE

    def step(j, state):
        scores, run_max, run_sum, acc = state
        following = score(jnp.minimum(j + 1, stop - 1))
        base = pl.multiple_of(j * K_TILE, K_TILE)
        key_pos = base + lax.broadcasted_iota(jnp.int32, (K_TILE, width), 0)
        allowed = (key_pos >= start) & (key_pos <= place)
        scores = jnp.where(allowed, scores, NEG)
        new_max = jnp.maximum(run_max, jnp.max(scores, axis=0, keepdims=True))
        expo = jnp.exp2(scores - new_max)
        factor = jnp.exp2(run_max - new_max)
        run_sum = run_sum * factor + jnp.sum(expo, axis=0, keepdims=True)
        acc = acc * factor + jnp.dot(
            vt_scr[:, pl.ds(base, K_TILE)], expo.astype(BF16), preferred_element_type=F32
        )
        return following, new_max, run_sum, acc

    state = (
        score(low),
        jnp.full((1, width), NEG, F32),
        jnp.zeros((1, width), F32),
        jnp.zeros((HEAD_SIZE, width), F32),
    )
    _, _, run_sum, acc = lax.fori_loop(low, stop, step, state)
    context = (acc / run_sum).T
    for g in range(group):
        out_ref[:, g * HEAD_SIZE : (g + 1) * HEAD_SIZE] = context[
            g * Q_TILE : (g + 1) * Q_TILE
        ].astype(BF16)


def attend(seq, queries, ids, after, blocks, c):
    rows, width = queries.shape[0] // CHUNKS, queries.shape[1]
    back = len(blocks) - 1
    tiles = rows // Q_TILE
    keys = len(blocks) * queries.shape[0]
    return pl.pallas_call(
        partial(attention_kernel, back=back, offset=c * rows),
        out_shape=shape((rows, width), BF16),
        grid_spec=pltpu.PrefetchScalarGridSpec(
            num_scalar_prefetch=1,
            grid=(tiles,),
            in_specs=[
                pl.BlockSpec((Q_TILE, width), lambda i, s: (c * tiles + i, 0)),
                pl.BlockSpec((1, Q_TILE), lambda i, s: (0, c * tiles + i)),
                ANY,
            ]
            + [pl.BlockSpec(b.shape, lambda i, s: (0, 0)) for b in blocks],
            out_specs=pl.BlockSpec((Q_TILE, width), lambda i, s: (i, 0)),
            scratch_shapes=[
                pltpu.VMEM((keys, HEAD_SIZE), BF16),
                pltpu.VMEM((HEAD_SIZE, keys), BF16),
                pltpu.VMEM((DOCUMENTS, LANES), F32),
            ],
        ),
        compiler_params=PARAMS,
        cost_estimate=pl.CostEstimate(
            flops=4 * rows * width * keys,
            bytes_accessed=4 * keys * width,
            transcendentals=rows * keys * width // HEAD_SIZE,
        ),
        name="attend",
    )(seq, queries, ids, after, *blocks)


def first_output_kernel(at_ref, own_o_ref, o_ref, *rest):
    ctx_refs, out_ref = rest[:-2], rest[-1]
    total = jnp.dot(ctx_refs[0][...], own_o_ref[...], preferred_element_type=F32)
    for i, ctx_ref in enumerate(ctx_refs[1:]):
        total = total + jnp.dot(ctx_ref[...], o_ref[at_ref[1 + i]], preferred_element_type=F32)
    out_ref[...] = total


def last_output_kernel(at_ref, part_ref, o_ref, *rest):
    ctx_refs, (before_ref, out_ref, sq_ref, acc) = rest[:-4], rest[-4:]
    step = pl.program_id(0)
    total = part_ref[...]
    for i, ctx_ref in enumerate(ctx_refs):
        total = total + jnp.dot(ctx_ref[...], o_ref[at_ref[i]], preferred_element_type=F32)
    out_ref[...] = total
    squares = jnp.sum(total * total, axis=1, keepdims=True)
    squares = jnp.broadcast_to(squares, acc.shape)

    @pl.when(step == 0)
    def _():
        acc[...] = squares

    @pl.when(step > 0)
    def _():
        acc[...] += squares

    @pl.when(step == pl.num_programs(0) - 1)
    def _():
        done = sq_ref.shape[1] - acc.shape[0]
        if done:
            sq_ref[:, :done] = before_ref[...]
        sq_ref[:, done:] = acc[...].T[0:1, :]


def column_tiles(cols):
    tiles = 3 if cols % (3 * LANES) == 0 else 1
    return tiles, cols // tiles


def first_output(column, order, o_weight, gathered, contexts, after):
    chunk, width = contexts[0].shape
    others, _, cols = gathered.shape
    tiles, tile = column_tiles(cols)
    if cols % LANES:
        o_weight = lax.dynamic_slice_in_dim(o_weight, column * cols, cols, axis=1)
        column = jnp.int32(0)
    return pl.pallas_call(
        first_output_kernel,
        out_shape=shape((chunk, cols), F32),
        grid_spec=pltpu.PrefetchScalarGridSpec(
            num_scalar_prefetch=1,
            grid=(tiles,),
            in_specs=[
                pl.BlockSpec((width, tile), lambda i, at: (0, at[0] * tiles + i)),
                pl.BlockSpec((others, width, tile), lambda i, at: (0, 0, i)),
            ]
            + [pl.BlockSpec((chunk, width), lambda i, at: (0, 0)) for _ in contexts]
            + [ANY],
            out_specs=pl.BlockSpec((chunk, tile), lambda i, at: (0, i)),
        ),
        compiler_params=PARAMS,
        cost_estimate=pl.CostEstimate(flops=HIDE, bytes_accessed=10**8, transcendentals=0),
        name="first_output",
    )(jnp.stack([column] + order), o_weight, gathered, *contexts, after)


def last_output(order, part, gathered, contexts, before, c):
    chunk, width = contexts[0].shape
    others, _, cols = gathered.shape
    tiles, tile = column_tiles(cols)
    return pl.pallas_call(
        last_output_kernel,
        out_shape=(shape((chunk, cols), F32), shape((1, (c + 1) * chunk), F32)),
        grid_spec=pltpu.PrefetchScalarGridSpec(
            num_scalar_prefetch=1,
            grid=(tiles,),
            in_specs=[
                pl.BlockSpec((chunk, tile), lambda i, at: (0, i)),
                pl.BlockSpec((others, width, tile), lambda i, at: (0, 0, i)),
            ]
            + [pl.BlockSpec((chunk, width), lambda i, at: (0, 0)) for _ in contexts]
            + [pl.BlockSpec(before.shape, lambda i, at: (0, 0))],
            out_specs=[
                pl.BlockSpec((chunk, tile), lambda i, at: (0, i)),
                pl.BlockSpec((1, (c + 1) * chunk), lambda i, at: (0, 0)),
            ],
            scratch_shapes=[pltpu.VMEM((chunk, LANES), F32)],
        ),
        compiler_params=PARAMS,
        name="last_output",
    )(jnp.stack(order), part, gathered, *contexts, before)


def final_kernel(token_ref, gain_ref, *rest, model):
    branch_refs, sq_refs, out_ref = rest[:CHUNKS], rest[CHUNKS:-1], rest[-1]
    total = sq_refs[0][...]
    for sq_ref in sq_refs[1:]:
        total = total + sq_ref[...]
    factor = to_column(lax.rsqrt(total / model + epsilon))[:, 0:1]
    for c in range(CHUNKS):

        @pl.when(pl.program_id(0) * CHUNKS // pl.num_programs(0) == c)
        def _():
            out = token_ref[...].astype(F32) + branch_refs[c][...] * factor * gain_ref[...]
            out_ref[...] = out.astype(BF16)


def finish(tokens, branches, out_gain, sums, model):
    rows, cols = tokens.shape
    tiles = rows // CHUNKS // Q_TILE
    held = lambda c: lambda i: (jnp.clip(i - c * tiles, 0, tiles - 1), 0)
    return pl.pallas_call(
        partial(final_kernel, model=model),
        out_shape=shape(tokens.shape, BF16),
        grid=(CHUNKS * tiles,),
        in_specs=[
            pl.BlockSpec((Q_TILE, cols), lambda i: (i, 0)),
            pl.BlockSpec((1, cols), lambda i: (0, 0)),
        ]
        + [pl.BlockSpec((Q_TILE, cols), held(c)) for c in range(CHUNKS)]
        + [pl.BlockSpec((1, Q_TILE), lambda i: (0, i)) for _ in sums],
        out_specs=pl.BlockSpec((Q_TILE, cols), lambda i: (i, 0)),
        compiler_params=PARAMS,
        name="finish",
    )(tokens, out_gain, *branches, *sums)


def per_device(
    tokens, seg_ids, in_gain, q_weight, k_weight, value_weight, o_weight, out_gain, *, sizes
):
    rows, cols = tokens.shape
    model = in_gain.shape[0]
    nz, nseq = sizes["tensor"], sizes["seq"]
    plane = nseq * sizes["groups"]
    z = lax.axis_index("tensor")
    seq = lax.axis_index("seq")
    in_plane = lax.axis_index(PLANE)
    half = nz // 2
    side, within = z // half, z % half
    half_rows = half * cols

    ring = [(i, i // half * half + (i + 1) % half) for i in range(nz)]
    swap = [(i, (i + half) % nz) for i in range(nz)]
    turn = lambda k: [(i, (i + k) % nz) for i in range(nz)]
    seq_bits = [1 << b for b in range(1, nseq.bit_length() - 1)]
    group_bits = [nseq << b for b in range(sizes["groups"].bit_length() - 1)]

    share = half_rows // plane
    at = jnp.reshape((1 - side) * plane + in_plane, (1,))
    inner = seq_bits + group_bits
    masks_kv, masks_q = inner + [1], inner[::-1] + [1]
    last = len(masks_kv) - 1
    eighth = rows // 48 * 8
    counts = [eighth, rows // 2 - 2 * TAIL, rows // 2 + 2 * TAIL - eighth]
    packed_kv, packed_q, cut = pack(
        at, q_weight, k_weight, value_weight, share, tokens, counts[0]
    )
    own_kv = lax.ppermute(packed_kv, "tensor", swap)[None]
    own_q = lax.ppermute(packed_q, "tensor", swap)[None]
    received = [lax.ppermute(cut, "tensor", ring)]
    o_share = o_weight.shape[0] // plane
    columns = [(z + k) % nz * cols for k in range(1, nz)]
    pieces = cut_pieces(in_plane * o_share, columns, o_weight, o_share, cols, own_kv)
    moved = [lax.ppermute(p, "tensor", turn(k + 1)) for k, p in enumerate(pieces)]

    order_kv, order_q, first = [0], [0], counts[0]
    for step, (mask_kv, mask_q) in enumerate(zip(masks_kv, masks_q)):
        after, count = [], 0
        if step == 0:
            pairs, after = [], [own_kv, own_q, received[0]]
        else:
            pairs = [(own_kv, far_kv), (own_q, far_q)]
        if step < 2:
            count = counts[1 + step]
        if step == last:
            after = [received[1]] + moved
        outs = stage(pairs, tokens, first, count, after, HIDE if step == last else 0)
        if pairs:
            own_kv, own_q = outs[:2]
        if count:
            received.append(lax.ppermute(outs[-1], "tensor", ring))
        first += count
        far_kv = lax.ppermute(own_kv, PLANE, [(i, i ^ mask_kv) for i in range(plane)])
        far_q = lax.ppermute(own_q, PLANE, [(i, i ^ mask_q) for i in range(plane)])
        order_kv = order_kv + [k ^ mask_kv for k in order_kv]
        order_q = order_q + [k ^ mask_q for k in order_q]
    far_kv, far_q = (order_kv, own_kv, far_kv), (order_q, own_q, far_q)

    own_o = jnp.stack(moved)[None]

    def double(own, step, after):
        if step > 0:
            (own,) = stage([own], tokens, 0, 0, after)
        return own, lax.ppermute(own, PLANE, [(i, i ^ masks_kv[step]) for i in range(plane)])

    sources = (within + half - jnp.arange(half, dtype=jnp.int32)) % half
    gains = in_gain.reshape(nz, 1, cols)
    place = jnp.stack([in_plane, side * half])
    own_x, own_sq, part = far_own_product(place, sources, gains, tokens, far_kv)
    received[-1] = gate(received[-1], own_sq)
    blocks = [received]
    for _ in range(half - 2):
        blocks.append([lax.ppermute(block, "tensor", ring) for block in blocks[-1]])
    sent_kv, x, sq = far_kv_product(
        place, sources, gains, part, own_sq, blocks, far_kv, [far_q[2]]
    )
    got_kv = lax.ppermute(sent_kv, "tensor", swap)
    pair_o = double(own_o, 0, [])
    for step in range(1, last - 1):
        pair_o = double(pair_o, step, [])
    weights = (k_weight, value_weight, q_weight)

    near = near_product(side * half + sources, own_x, x, weights, [sent_kv])

    sent_q = far_product(place, sources, own_x, x, far_q, [near])
    got_q = lax.ppermute(gate(sent_q, got_kv), "tensor", swap)
    pair_o = double(pair_o, last - 1, [sent_q])
    cosine, sine = rotation_table(seq * rows + jnp.arange(rows, dtype=jnp.int32))
    ids = seg_ids[None, :]
    own_kv, sums = keys_values(
        near, got_kv, sq, ids, cosine, sine, [sent_q, pair_o[0]], model
    )
    pair_o = double(pair_o, last, [own_kv])
    gathered_o = lay_pieces(place, order_kv, *pair_o)

    back = -(-(nseq * rows // 2 - 1) // rows)
    kv_blocks = [own_kv]
    for k in range(1, back + 1):
        earlier = [(i, i + k) for i in range(nseq - k)]
        kv_blocks.insert(0, lax.ppermute(own_kv, "seq", earlier))

    queries = finished_queries(near, got_q, sums, cosine, sine, model)
    seq_at = jnp.reshape(seq, (1,))
    contexts, after = [], own_kv
    for c in range(CHUNKS):
        contexts.append(attend(seq_at, queries, ids, after, kv_blocks, c))
        after = gathered_o
    early, late = [], []
    for c, context in enumerate(contexts):
        if nz == 4:
            pairs = [(i, i ^ 1) for i in range(nz)]
            opposite = lax.ppermute(context, "tensor", swap)
            beside = lax.ppermute(context, "tensor", pairs)
            if c + 1 < CHUNKS:
                opposite = gate(opposite, contexts[c + 1])
            across = lax.ppermute(opposite, "tensor", pairs)
            early.append([context, beside])
            late.append([opposite, across])
            order = [2 - 2 * (z % 2), jnp.int32(1), 2 * (z % 2)]
        else:
            early.append([context])
            late.append([lax.ppermute(context, "tensor", turn(k)) for k in range(1, nz)])
            order = [jnp.int32(k) for k in range(nz - 1)]
    split = len(early[0]) - 1
    branches, own_sq = [], sums
    for c in range(CHUNKS):
        part = first_output(z, order[:split], o_weight, gathered_o, early[c], contexts[-1])
        branch, own_sq = last_output(order[split:], part, gathered_o, late[c], own_sq, c)
        branches.append(branch)
    squares = [own_sq]
    squares += [lax.ppermute(own_sq, "tensor", turn(k)) for k in range(1, nz)]
    return finish(tokens, branches, out_gain[None, :], squares, model)


def solution(mesh):
    return jax.shard_map(
        partial(per_device, sizes=dict(mesh.shape)),
        mesh=mesh,
        in_specs=(
            P(("groups", "seq"), "tensor"),
            P(("groups", "seq")),
            P(),
            P(None, "tensor"),
            P(None, "tensor"),
            P(None, "tensor"),
            P("tensor", None),
            P("tensor"),
        ),
        out_specs=P(("groups", "seq"), "tensor"),
        check_vma=False,
    )
```
